32 devices in a mesh: ha: 8 (over y, x, core), wa: 4 (over z).
Axes of the slice: x: 2, y: 2, z: 4, core: 2. Of those that a mesh axis runs over, the one named last changes fastest.
Arguments:
- block_input: bfloat16 [16, 64, 128, 128], P(None, 'ha', 'wa'), may hold values from -18 to 18
- timesteps: int32 [16], replicated, may hold values from 0 to 999
- aug_levels: int32 [16], replicated, may hold values from 0 to 999
- text_pooled: bfloat16 [16, 4096], replicated, may hold values from -6 to 6
- gain_one: bfloat16 [128], replicated, may hold values from 0.25 to 1.75
- bias_one: bfloat16 [128], replicated, may hold values from -3 to 3
- conv_one: bfloat16 [3, 3, 128, 128], replicated, may hold values from -0.1875 to 0.1875
- conv_one_bias: bfloat16 [128], replicated, may hold values from -3 to 3
- gain_two: bfloat16 [128], replicated, may hold values from 0.25 to 1.75
- bias_two: bfloat16 [128], replicated, may hold values from -3 to 3
- film_weight: bfloat16 [4608, 256], replicated, may hold values from -0.125 to 0.125
- film_bias: bfloat16 [256], replicated, may hold values from -2 to 2
- conv_two: bfloat16 [3, 3, 128, 128], replicated, may hold values from -0.1875 to 0.1875
- conv_two_bias: bfloat16 [128], replicated, may hold values from -3 to 3
- cotangent: bfloat16 [16, 64, 128, 128], P(None, 'ha', 'wa'), may hold values from -6 to 6
Outputs:
- mixed: bfloat16 [16, 64, 128, 128], P(None, 'ha', 'wa')
- input_grad: bfloat16 [16, 64, 128, 128], P(None, 'ha', 'wa')
- text_grad: float32 [16, 4096], replicated
- gain_one_grad: float32 [128], replicated
- bias_one_grad: float32 [128], replicated
- conv_one_grad: float32 [3, 3, 128, 128], replicated
- conv_one_bias_grad: float32 [128], replicated
- gain_two_grad: float32 [128], replicated
- bias_two_grad: float32 [128], replicated
- film_weight_grad: float32 [4608, 256], replicated
- film_bias_grad: float32 [256], replicated
- conv_two_grad: float32 [3, 3, 128, 128], replicated
- conv_two_bias_grad: float32 [128], replicated
The draws below stay inside these ranges and needn't reach their ends.
All inputs are finite; a program needn't handle non-finite values.
Results may differ from the reference program's by a relative error of at most 0.0051.
Values may be sent and summed in bfloat16 or wider, within the bound.
No kernel may reach another device: no remote copies, remote signals or barrier semaphores. Data moves between devices by JAX's collectives and lax.ppermute only.
A program may use at most 128 MiB of HBM per device.

```python
import math
import jax
import jax.numpy as jnp
import numpy as np
from jax import lax

C = 128
GROUPS = 32
TEXT = 4096
TEMB = 256
IMGS = 16
HEIGHT = 64
WIDTH = 128
COND = 4608


def width_wave(key, images):
    phase = jax.random.uniform(key, (images, 1), minval=-math.pi, maxval=math.pi)
    cols = jnp.arange(WIDTH, dtype=jnp.float32) / WIDTH
    return jnp.cos(2.0 * math.pi * cols[None, :] + phase)


def height_wave(key, images):
    phase = jax.random.uniform(key, (images, 1), minval=-math.pi, maxval=math.pi)
    rows = jnp.arange(HEIGHT, dtype=jnp.float32) / HEIGHT
    return jnp.cos(2.0 * math.pi * rows[None, :] + phase)


def group_spread(key, images, reach):
    per_group = jax.random.uniform(key, (images, GROUPS), minval=-reach, maxval=reach)
    return jnp.repeat(per_group, C // GROUPS, axis=1)


def draw_block_input(key, part):
    key = jax.random.fold_in(key, 11)
    key_base = jax.random.fold_in(key, 0)
    key_rough = jax.random.fold_in(key, 1)
    key_group = jax.random.fold_in(key, 3)
    key_amp = jax.random.fold_in(key, 4)
    key_phase = jax.random.fold_in(key, 5)
    shape = (IMGS, HEIGHT, WIDTH, C)
    rows = jnp.arange(HEIGHT, dtype=jnp.float32) / max(HEIGHT - 1, 1)
    ramp = (1.0 + 2.0 * rows)[None, :, None, None]
    rough = jnp.exp(jax.random.uniform(key_rough, (IMGS, HEIGHT, WIDTH, 1), minval=-0.35, maxval=0.35))
    base = jnp.clip(jax.random.normal(key_base, shape), -4.0, 4.0)
    amplitude = group_spread(key_group, IMGS, 1.5) + jax.random.uniform(key_amp, (IMGS, C), minval=-0.6, maxval=0.6)
    wave = width_wave(key_phase, IMGS)
    wide = amplitude[:, None, None, :] * wave[:, None, :, None]
    return jnp.clip(base * ramp * rough + wide, -18.0, 18.0).astype(jnp.bfloat16)


def draw_cotangent(key, part):
    key = jax.random.fold_in(key, 23)
    key_noise, key_group, key_chan, key_wide, key_phase, key_tall, key_tphase = jax.random.split(key, 7)
    shape = (IMGS, HEIGHT, WIDTH, C)
    noise = jnp.clip(jax.random.normal(key_noise, shape), -4.0, 4.0)
    offset = group_spread(key_group, IMGS, 1.0) + jax.random.uniform(key_chan, (IMGS, C), minval=-1.2, maxval=1.2)
    wide_amp = jax.random.uniform(key_wide, (IMGS, C), minval=-1.2, maxval=1.2)
    tall_amp = jax.random.uniform(key_tall, (IMGS, C), minval=-0.8, maxval=0.8)
    wide = wide_amp[:, None, None, :] * width_wave(key_phase, IMGS)[:, None, :, None]
    tall = tall_amp[:, None, None, :] * height_wave(key_tphase, IMGS)[:, :, None, None]
    return jnp.clip(noise + offset[:, None, None, :] + wide + tall, -6.0, 6.0).astype(jnp.bfloat16)


def touch_ends(values, stream_key, least, top_value):
    shape = values.shape
    index_at = [jax.random.randint(jax.random.fold_in(stream_key, axis), (), 0, shape[axis]) for axis in range(len(shape))]
    values = values.at[tuple(index_at)].set(least)
    longest = shape.index(max(shape))
    index_at[longest] = (index_at[longest] + 1) % shape[longest]
    return values.at[tuple(index_at)].set(top_value)


def cumulative_ranks(number_of, slope):
    loads = [(1 << 20) // math.isqrt(standing ** slope) + 1 for standing in range(1, number_of + 1)]
    scale = 1 + sum(loads) // (1 << 30)
    return np.cumsum(np.array([max(1, weight // scale) for weight in loads]))


def skewed_ids(stream_key, extent, count, lean):
    listing = cumulative_ranks(count, lean)
    ticket = jax.random.randint(jax.random.fold_in(stream_key, 1), extent, 0, int(listing[count - 1]))
    standing = jnp.searchsorted(jnp.asarray(listing, jnp.int32), ticket, side="right")
    return jax.random.permutation(jax.random.fold_in(stream_key, 2), count)[standing].astype(jnp.int32)


def bell_draw(rng, extent, scale, most, held_as=jnp.bfloat16):
    values = scale * jax.random.normal(rng, extent, jnp.float32)
    return jnp.clip(values, min=-most, max=most).astype(held_as)


def setup_inputs(seed: int = 0) -> dict:
    splits = jax.random.split(jax.random.key(seed), 16)
    block_input = draw_block_input(jax.random.fold_in(splits[15], 71), 0)
    timesteps = touch_ends(skewed_ids(splits[1], (IMGS,), 1000, 2), jax.random.fold_in(splits[1], 3), 0, 999).astype(jnp.int32)
    aug_levels = touch_ends(jax.random.randint(splits[2], (IMGS,), 0, 1000), jax.random.fold_in(splits[2], 1), 0, 999).astype(jnp.int32)
    text_pooled = bell_draw(splits[3], (IMGS, TEXT), 1.0, 6.0)
    gain_one = jnp.clip(1.0 + 0.15 * jax.random.normal(splits[4], (C,), jnp.float32), 0.25, 1.75).astype(jnp.bfloat16)
    bias_one = bell_draw(splits[5], (C,), 0.5, 3.0)
    conv_one = bell_draw(splits[6], (3, 3, C, C), (9 * C) ** -0.5, 0.1875)
    conv_one_bias = bell_draw(splits[7], (C,), 0.5, 3.0)
    gain_two = jnp.clip(1.0 + 0.15 * jax.random.normal(splits[8], (C,), jnp.float32), 0.25, 1.75).astype(jnp.bfloat16)
    bias_two = bell_draw(splits[9], (C,), 0.5, 3.0)
    film_weight = bell_draw(splits[10], (COND, 2 * C), (COND // 2) ** -0.5, 0.125)
    film_bias = bell_draw(splits[11], (2 * C,), 0.4, 2.0)
    conv_two = bell_draw(splits[12], (3, 3, C, C), (9 * C) ** -0.5, 0.1875)
    conv_two_bias = bell_draw(splits[13], (C,), 0.5, 3.0)
    cotangent = draw_cotangent(jax.random.fold_in(splits[15], 71), 0)
    return dict(block_input=block_input, timesteps=timesteps, aug_levels=aug_levels, text_pooled=text_pooled, gain_one=gain_one, bias_one=bias_one, conv_one=conv_one, conv_one_bias=conv_one_bias, gain_two=gain_two, bias_two=bias_two, film_weight=film_weight, film_bias=film_bias, conv_two=conv_two, conv_two_bias=conv_two_bias, cotangent=cotangent)


@jax.custom_vjp
def low(v):
    return lax.optimization_barrier(v.astype(jnp.bfloat16)).astype(jnp.float32)

@jax.custom_vjp
def low_back(v):
    return v

def low_keep(v):
    return (low(v), None)

def low_pass(kept, grad):
    return (grad,)

def back_keep(v):
    return (v, None)

def back_low(kept, grad):
    return (low(grad),)
low.defvjp(low_keep, low_pass)
low_back.defvjp(back_keep, back_low)
epsilon = 1e-05

def sinusoid(values):
    half = TEMB // 2
    freqs = jnp.exp(-math.log(10000.0) * jnp.arange(half, dtype=jnp.float32) / half)
    angles = values.astype(jnp.float32)[:, None] * freqs[None, :]
    return jnp.concatenate([jnp.sin(angles), jnp.cos(angles)], axis=1)

def group_norm(values, gain, shift):
    images, height, width, chans = values.shape
    grouped = values.reshape(images, height, width, GROUPS, chans // GROUPS)
    center = lax.optimization_barrier(jnp.mean(grouped, axis=(1, 2, 4), keepdims=True))
    spread = lax.optimization_barrier(jnp.mean((grouped - center) * (grouped - center), axis=(1, 2, 4), keepdims=True))
    normed = (grouped - center) * lax.rsqrt(spread + epsilon)
    return normed.reshape(values.shape) * gain + shift

def convolve(inputs, kernel):
    return lax.conv_general_dilated(inputs, kernel, (1, 1), ((1, 1), (1, 1)), dimension_numbers=('NHWC', 'HWIO', 'NHWC'), precision=lax.Precision.HIGHEST)

def reference(block_input, timesteps, aug_levels, text_pooled, gain_one, bias_one, conv_one, conv_one_bias, gain_two, bias_two, film_weight, film_bias, conv_two, conv_two_bias, cotangent):
    embed_ints = jnp.concatenate([sinusoid(timesteps), sinusoid(aug_levels)], axis=1)
    chans = block_input.shape[3]
    inv_root = 1.0 / math.sqrt(2.0)

    def forward(inputs, pooled, gain_a, bias_a, kernel_a, kbias_a, gain_b, bias_b, film_w, film_b, kernel_b, kbias_b):
        normed = group_norm(inputs, gain_a, bias_a)
        act_one = low(jax.nn.silu(normed))
        middle = low_back(convolve(act_one, kernel_a) + kbias_a)
        embed = jnp.concatenate([embed_ints, pooled], axis=1)
        cond_act = low(jax.nn.silu(embed))
        film = jnp.dot(cond_act, film_w, precision=lax.Precision.HIGHEST) + film_b
        scale = film[:, :chans][:, None, None, :]
        shift = film[:, chans:][:, None, None, :]
        norm_two = group_norm(middle, gain_b, bias_b)
        pre_two = norm_two * (1.0 + scale) + shift
        act_two = low(jax.nn.silu(pre_two))
        branch = low_back(convolve(act_two, kernel_b) + kbias_b)
        return (inputs + branch) * inv_root
    primals = tuple((a.astype(jnp.float32) for a in (block_input, text_pooled, gain_one, bias_one, conv_one, conv_one_bias, gain_two, bias_two, film_weight, film_bias, conv_two, conv_two_bias)))
    output, pullback = jax.vjp(forward, *primals)
    grads = pullback(cotangent.astype(jnp.float32))
    return (output.astype(jnp.bfloat16), grads[0].astype(jnp.bfloat16), grads[1], grads[2], grads[3], grads[4], grads[5], grads[6], grads[7], grads[8], grads[9], grads[10], grads[11])
```

```python
import functools
import math

import jax
import jax.numpy as jnp
from jax import lax
from jax.experimental import pallas as pl
from jax.experimental.pallas import tpu as pltpu
from jax.sharding import PartitionSpec as P

GROUPS = 32
TEMB = 256
EPSILON = 1e-05
INV_ROOT = 1.0 / math.sqrt(2.0)
AXES = ("ha", "wa")
F32 = jnp.float32
BF16 = jnp.bfloat16
VMEM = pl.BlockSpec(memory_space=pltpu.VMEM)
MIB = 1 << 20


def kernel_call(body, outs, *args, scratch=(), limit=40):
    return pl.pallas_call(
        body,
        out_shape=outs,
        in_specs=[VMEM] * len(args),
        out_specs=jax.tree.map(lambda _: VMEM, outs),
        scratch_shapes=scratch,
        compiler_params=pltpu.CompilerParams(vmem_limit_bytes=limit * MIB),
    )(*args)


def shaped(shape, dtype):
    return jax.ShapeDtypeStruct(shape, dtype)


def lanes_of(shape):
    return lax.broadcasted_iota(jnp.int32, shape, 1)


def group_total(values):
    chans = values.shape[1]
    lane = lanes_of(values.shape)
    step = 1
    while step < chans // GROUPS:
        up = pltpu.roll(values, chans - step, 1)
        down = pltpu.roll(values, step, 1)
        values = values + jnp.where((lane & step) == 0, up, down)
        step *= 2
    return values


def pack_pair(first, second):
    half = first.shape[0] // 2
    lane = lanes_of((half, first.shape[1])) & 3
    return jnp.where(
        lane == 0,
        first[:half],
        jnp.where(lane == 1, second[:half], jnp.where(lane == 2, first[half:], second[half:])),
    )


def unpack_at(packed, place):
    lane = lanes_of(packed.shape) & 3
    top = group_total(jnp.where(lane == place, packed, 0.0))
    low = group_total(jnp.where(lane == place + 2, packed, 0.0))
    return jnp.concatenate([top, low], axis=0)


def merge_moments(gathered_ref, local_count):
    parts = gathered_ref.shape[0]
    chans = gathered_ref.shape[2]
    every = gathered_ref[...]
    total = jnp.sum(every, axis=0)
    mean = total * (1.0 / parts)
    apart = every - mean[None]
    between = jnp.sum(apart * apart, axis=0)
    square = pltpu.roll(total, chans - 1, 1) + local_count * between
    inv = lax.rsqrt(square * (1.0 / (local_count * parts)) + EPSILON)
    return unpack_at(mean, 0), unpack_at(inv, 0)


def local_moments(total, square, pilot, pixels, per):
    off = total * (1.0 / pixels)
    mean = pilot + off
    apart = square - total * off
    group_mean = group_total(mean) * (1.0 / per)
    shift = mean - group_mean
    return group_mean, group_total(apart + pixels * shift * shift)


def sigmoid(values):
    return 0.5 + 0.5 * jnp.tanh(0.5 * values)


def forward_weights(kernel_ref, pair_ref):
    chans = kernel_ref.shape[2]
    zero = jnp.zeros((chans, chans), BF16)
    for row in range(3):
        for col in range(4):
            at = (row * 4 + col) * chans
            pair_ref[at : at + chans, 0:chans] = kernel_ref[row, col] if col < 3 else zero
            pair_ref[at : at + chans, chans:] = kernel_ref[row, col - 1] if col > 0 else zero


def backward_weights(kernel_ref, pair_ref):
    chans = kernel_ref.shape[2]
    zero = jnp.zeros((chans, chans), BF16)
    for row in range(3):
        for col in range(4):
            at = (row * 4 + col) * chans
            pair_ref[0:chans, at : at + chans] = kernel_ref[2 - row, 2 - col] if col < 3 else zero
            pair_ref[chans:, at : at + chans] = kernel_ref[2 - row, 3 - col] if col > 0 else zero


def convolve(cells_ref, pair_ref, out_ref, transposed, bias=None):
    cols, rows, images, chans = out_ref.shape
    pairs = cols // 2
    parts = []
    for row in range(3):
        for col in range(4):
            window = [cells_ref[2 * q + col, row : row + rows] for q in range(pairs)]
            parts.append(jnp.stack(window).reshape(pairs * rows * images, chans))
    wide = jnp.concatenate(parts, axis=1)
    contract = ((1,), (1,)) if transposed else ((1,), (0,))
    made = lax.dot_general(wide, pair_ref[...], (contract, ((), ())), preferred_element_type=F32)
    for side in range(2):
        piece = made[:, side * chans : (side + 1) * chans]
        if bias is not None:
            piece = piece + bias
        piece = piece.reshape(pairs, rows, images, chans)
        for q in range(pairs):
            out_ref[2 * q + side] = piece[q]


def kernel_grad(cells_ref, grads_ref, out_ref):
    cols, rows, images, chans = grads_ref.shape
    wide = grads_ref[...].reshape(cols * rows * images, chans)
    for row in range(3):
        for col in range(3):
            window = cells_ref[col : col + cols, row : row + rows]
            at = (row * 3 + col) * chans
            out_ref[at : at + chans, :] = lax.dot_general(
                window.reshape(cols * rows * images, chans),
                wide,
                (((0,), (0,)), ((), ())),
                preferred_element_type=F32,
            )


def at_edges():
    tall = lax.axis_index("ha")
    wide = lax.axis_index("wa")
    return (
        tall == 0,
        tall == lax.axis_size("ha") - 1,
        wide == 0,
        wide == lax.axis_size("wa") - 1,
    )


def clear_border(cells_ref, width):
    top, bottom, left, right = at_edges()
    cols, rows, images, chans = cells_ref.shape

    @pl.when(top)
    def _():
        cells_ref[:, 0:width] = jnp.zeros((cols, width, images, chans), cells_ref.dtype)

    @pl.when(bottom)
    def _():
        cells_ref[:, rows - width :] = jnp.zeros((cols, width, images, chans), cells_ref.dtype)

    @pl.when(left)
    def _():
        cells_ref[0:width] = jnp.zeros((width, rows, images, chans), cells_ref.dtype)

    @pl.when(right)
    def _():
        cells_ref[cols - width :] = jnp.zeros((width, rows, images, chans), cells_ref.dtype)


def prepare(x_ref, c_ref, xt_ref, gt_ref, pay_ref, bias_ref, down_ref, up_ref, right_ref, left_ref):
    images, rows, cols, chans = x_ref.shape
    per = chans // GROUPS

    pilot = x_ref[:, 0, 0].astype(F32)
    zero = jnp.zeros((images, chans), F32)

    def one_row(row, carry):
        total, square, bias = carry
        x = jnp.swapaxes(x_ref[:, pl.ds(row, 1)].reshape(images, cols, chans).astype(F32), 0, 1)
        xt_ref[:, pl.ds(row, 1)] = x.astype(BF16).reshape(cols, 1, images, chans)
        apart = x - pilot[None]
        total = total + jnp.sum(apart, axis=0)
        square = square + jnp.sum(apart * apart, axis=0)
        grad = c_ref[:, pl.ds(row, 1)].reshape(images, cols, chans).astype(F32) * INV_ROOT
        grad = jnp.swapaxes(grad, 0, 1).astype(BF16)
        gt_ref[:, pl.ds(row, 1)] = grad.reshape(cols, 1, images, chans)
        return total, square, bias + jnp.sum(grad.astype(F32), axis=0)

    total, square, bias = lax.fori_loop(0, rows, one_row, (zero, zero, zero))
    mean, spread = local_moments(total, square, pilot, rows * cols, per)
    packed = pack_pair(mean, spread)
    pay_ref[...] = jnp.broadcast_to(packed[None], pay_ref.shape)
    bias_ref[...] = bias
    for at, ref in enumerate((xt_ref, gt_ref)):
        down_ref[at] = ref[:, rows - 2 :]
        up_ref[at] = ref[:, 0:2]
        right_ref[at] = ref[cols - 2 :]
        left_ref[at] = ref[0:2]


def assemble(at, cells_ref, mid_ref, top_ref, bottom_ref, left_ref, right_ref, corner_l, corner_r, change):
    cols, rows, images, chans = mid_ref.shape

    def column(col, _):
        cells_ref[pl.ds(col + 2, 1), 2 : rows + 2] = change(mid_ref[pl.ds(col, 1)])
        cells_ref[pl.ds(col + 2, 1), 0:2] = change(top_ref[at, pl.ds(col, 1)])
        cells_ref[pl.ds(col + 2, 1), rows + 2 :] = change(bottom_ref[at, pl.ds(col, 1)])
        return 0

    lax.fori_loop(0, cols, column, 0, unroll=2)
    for side, edge, corner in ((0, left_ref, corner_l), (cols + 2, right_ref, corner_r)):
        cells_ref[side : side + 2, 2 : rows + 2] = change(edge[at])
        cells_ref[side : side + 2, 0:2] = change(corner[at, :, 0:2])
        cells_ref[side : side + 2, rows + 2 :] = change(corner[at, :, 2:4])
    clear_border(cells_ref, 2)


def first_half(
    xt_ref, top_ref, bottom_ref, left_ref, right_ref, corner_l, corner_r, gathered_ref, gain_ref, bias_ref,
    kernel_ref, kbias_ref, act_ref, mid_ref, pay_ref, stat_ref, pair_ref,
):
    cols, rows, images, chans = xt_ref.shape
    per = chans // GROUPS
    mean, inv = merge_moments(gathered_ref, rows * cols * per)
    stat_ref[0] = mean
    stat_ref[1] = inv
    slope = inv * gain_ref[...].astype(F32)
    offset = bias_ref[...].astype(F32)

    def act(cells):
        value = (cells.astype(F32) - mean) * slope + offset
        return (value * sigmoid(value)).astype(BF16)

    assemble(0, act_ref, xt_ref, top_ref, bottom_ref, left_ref, right_ref, corner_l, corner_r, act)
    forward_weights(kernel_ref, pair_ref)
    convolve(act_ref, pair_ref, mid_ref, False, kbias_ref[...].astype(F32))

    pilot = mid_ref[1, 1]
    zero = jnp.zeros((images, chans), F32)

    def column(col, carry):
        total, square = carry
        apart = mid_ref[pl.ds(col, 1), 1 : rows + 1].reshape(rows, images, chans) - pilot[None]
        return total + jnp.sum(apart, axis=0), square + jnp.sum(apart * apart, axis=0)

    total, square = lax.fori_loop(1, cols + 1, column, (zero, zero), unroll=4)
    mean, spread = local_moments(total, square, pilot, rows * cols, per)
    pay_ref[...] = jnp.broadcast_to(pack_pair(mean, spread)[None], pay_ref.shape)


def back_two(
    gt_ref, top_ref, bottom_ref, left_ref, right_ref, corner_l, corner_r, kernel_ref, out_ref, cells_ref, pair_ref
):
    assemble(
        1, cells_ref, gt_ref, top_ref, bottom_ref, left_ref, right_ref, corner_l, corner_r, lambda cells: cells
    )
    backward_weights(kernel_ref, pair_ref)
    convolve(cells_ref, pair_ref, out_ref, True)


def second_norm(
    mid_ref, back_ref, gathered_ref, gain_ref, bias_ref, film_ref, act_ref, pre_ref, pay_ref, sums_ref, stat_ref
):
    wide, tall, images, chans = mid_ref.shape
    cols, rows = wide - 2, tall - 2
    per = chans // GROUPS
    mean, inv = merge_moments(gathered_ref, rows * cols * per)
    stat_ref[0] = mean
    stat_ref[1] = inv
    gain = gain_ref[...].astype(F32)
    scale = 1.0 + film_ref[:, 0:chans]
    slope = gain * scale
    offset = bias_ref[...].astype(F32) * scale + film_ref[:, chans:]

    def column(col, inner):
        hat = (mid_ref[pl.ds(col, 1)].reshape(tall, images, chans) - mean) * inv
        pre = hat * slope + offset
        sigma = sigmoid(pre)
        act = pre * sigma
        act_ref[pl.ds(col, 1)] = act.astype(BF16).reshape(1, tall, images, chans)
        grad = back_ref[pl.ds(col, 1)].reshape(tall, images, chans) * (sigma + act * (1.0 - sigma))
        pre_ref[pl.ds(col, 1)] = grad.reshape(1, tall, images, chans)
        if inner is None:
            return None
        own = grad[1 : rows + 1]
        plain, cross = inner
        return plain + jnp.sum(own, axis=0), cross + jnp.sum(own * hat[1 : rows + 1], axis=0)

    zero = jnp.zeros((images, chans), F32)
    column(0, None)
    column(wide - 1, None)
    plain, cross = lax.fori_loop(1, cols + 1, column, (zero, zero))
    clear_border(act_ref, 1)
    sums_ref[0] = plain
    sums_ref[1] = cross
    packed = pack_pair(group_total(plain * slope), group_total(cross * slope))
    pay_ref[...] = jnp.broadcast_to(packed[None], pay_ref.shape)


def kernel_two(act_ref, gt_ref, sums_ref, bias_ref, out_ref):
    kernel_grad(act_ref, gt_ref, out_ref)
    images, chans = bias_ref.shape
    at = 9 * chans
    out_ref[at : at + images] = sums_ref[0]
    out_ref[at + images : at + 2 * images] = sums_ref[1]
    last = at + 2 * images
    total = jnp.sum(bias_ref[...], axis=0, keepdims=True)
    out_ref[last:] = jnp.broadcast_to(total, (out_ref.shape[0] - last, chans))


def mix(act_ref, kernel_ref, kbias_ref, xt_ref, out_ref, pair_ref, branch_ref):
    images, rows, cols, chans = out_ref.shape
    forward_weights(kernel_ref, pair_ref)
    convolve(act_ref, pair_ref, branch_ref, False, kbias_ref[...].astype(F32))

    def one_row(row, _):
        branch = branch_ref[:, pl.ds(row, 1)].reshape(cols, images, chans)
        x = xt_ref[:, pl.ds(row, 1)].reshape(cols, images, chans).astype(F32)
        mixed = jnp.swapaxes((x + branch) * INV_ROOT, 0, 1)
        out_ref[:, pl.ds(row, 1)] = mixed.astype(BF16).reshape(images, 1, cols, chans)
        return 0

    lax.fori_loop(0, rows, one_row, 0)


def middle_grad(
    mid_ref, pre_ref, gathered_ref, stat_ref, gain_ref, film_ref, act_ref, low_ref, kgrad_ref, bias_ref
):
    wide, tall, images, chans = mid_ref.shape
    cols, rows = wide - 2, tall - 2
    parts = gathered_ref.shape[0]
    count = parts * rows * cols * (chans // GROUPS)
    packed = jnp.sum(gathered_ref[...], axis=0) * (1.0 / count)
    plain = unpack_at(packed, 0)
    cross = unpack_at(packed, 1)
    mean = stat_ref[0]
    inv = stat_ref[1]
    slope = gain_ref[...].astype(F32) * (1.0 + film_ref[:, 0:chans])

    def column(col, total):
        hat = (mid_ref[pl.ds(col, 1)].reshape(tall, images, chans) - mean) * inv
        grad = pre_ref[pl.ds(col, 1)].reshape(tall, images, chans) * slope
        low = (inv * (grad - plain - hat * cross)).astype(BF16)
        low_ref[pl.ds(col, 1)] = low.reshape(1, tall, images, chans)
        if total is None:
            return None
        return total + jnp.sum(low[1 : rows + 1].astype(F32), axis=0)

    column(0, None)
    column(wide - 1, None)
    bias_ref[...] = lax.fori_loop(1, cols + 1, column, jnp.zeros((images, chans), F32))
    clear_border(low_ref, 1)
    kernel_grad(act_ref.at[1 : wide + 1, 1 : tall + 1], low_ref.at[1 : wide - 1, 1 : tall - 1], kgrad_ref)


def back_one(
    low_ref, kernel_ref, xt_ref, stat_ref, gain_ref, bias_ref, kbias_ref, out_ref, pay_ref, pair_ref
):
    cols, rows, images, chans = xt_ref.shape
    backward_weights(kernel_ref, pair_ref)
    convolve(low_ref, pair_ref, out_ref, True)
    mean = stat_ref[0]
    inv = stat_ref[1]
    gain = gain_ref[...].astype(F32)
    bias = bias_ref[...].astype(F32)

    def column(col, carry):
        plain, cross = carry
        hat = (xt_ref[pl.ds(col, 1)].reshape(rows, images, chans).astype(F32) - mean) * inv
        norm = hat * gain + bias
        sigma = sigmoid(norm)
        grad = out_ref[pl.ds(col, 1)].reshape(rows, images, chans)
        grad = grad * (sigma * (1.0 + norm * (1.0 - sigma)))
        out_ref[pl.ds(col, 1)] = grad.reshape(1, rows, images, chans)
        return plain + jnp.sum(grad, axis=0), cross + jnp.sum(grad * hat, axis=0)

    zero = jnp.zeros((images, chans), F32)
    plain, cross = lax.fori_loop(0, cols, column, (zero, zero))
    packed = pack_pair(group_total(plain * gain), group_total(cross * gain))
    half = packed.shape[0]
    parts = pay_ref.shape[0]
    pay_ref[:, 0:half] = jnp.broadcast_to(packed[None], (parts, half, chans))
    rest = jnp.concatenate(
        [
            jnp.sum(cross, axis=0, keepdims=True),
            jnp.sum(plain, axis=0, keepdims=True),
            jnp.sum(kbias_ref[...], axis=0, keepdims=True),
            jnp.zeros((half - 3, chans), F32),
        ],
        axis=0,
    )
    pay_ref[:, half:] = jnp.broadcast_to(rest[None], (parts, half, chans))


def finish(grad_ref, xt_ref, gathered_ref, stat_ref, gain_ref, c_ref, out_ref, sums_ref):
    images, rows, cols, chans = out_ref.shape
    parts = gathered_ref.shape[0]
    half = images // 2
    total = jnp.sum(gathered_ref[...], axis=0)
    packed = total[0:half] * (1.0 / (parts * rows * cols * (chans // GROUPS)))
    sums_ref[...] = total[half:]
    plain = unpack_at(packed, 0)
    cross = unpack_at(packed, 1)
    mean = stat_ref[0]
    inv = stat_ref[1]
    gain = gain_ref[...].astype(F32)

    def one_row(row, _):
        hat = (xt_ref[:, pl.ds(row, 1)].reshape(cols, images, chans).astype(F32) - mean) * inv
        grad = grad_ref[:, pl.ds(row, 1)].reshape(cols, images, chans) * gain
        path = jnp.swapaxes(inv * (grad - plain - hat * cross), 0, 1)
        skip = c_ref[:, pl.ds(row, 1)].reshape(images, cols, chans).astype(F32) * INV_ROOT
        out_ref[:, pl.ds(row, 1)] = (skip + path).astype(BF16).reshape(images, 1, cols, chans)
        return 0

    lax.fori_loop(0, rows, one_row, 0)


def add_shards(gathered_ref, out_ref):
    total = jnp.sum(gathered_ref[...], axis=0).astype(out_ref.dtype)
    out_ref[...] = jnp.broadcast_to(total[None], out_ref.shape)


def to_all(payload):
    return lax.all_to_all(payload, AXES, 0, 0)


def shifted(cells, axis, step):
    count = lax.axis_size(axis)
    if step > 0:
        pairs = [(i, i + 1) for i in range(count - 1)]
    else:
        pairs = [(i + 1, i) for i in range(count - 1)]
    return lax.ppermute(cells, axis, pairs)


def summed_over_devices(rows_of, gather_dtype):
    parts = lax.axis_size("ha") * lax.axis_size("wa")
    rows, chans = rows_of.shape
    share = rows // parts
    pieces = to_all(rows_of.reshape(parts, share, chans))
    added = kernel_call(add_shards, shaped((parts, share, chans), gather_dtype), pieces)
    return to_all(added).reshape(rows, chans)


def sinusoid(values):
    half = TEMB // 2
    freqs = jnp.exp(-math.log(10000.0) * jnp.arange(half, dtype=F32) / half)
    angles = values.astype(F32)[:, None] * freqs[None, :]
    return jnp.concatenate([jnp.sin(angles), jnp.cos(angles)], axis=1)


def local(
    block_input,
    timesteps,
    aug_levels,
    text_pooled,
    gain_one,
    bias_one,
    conv_one,
    conv_one_bias,
    gain_two,
    bias_two,
    film_weight,
    film_bias,
    conv_two,
    conv_two_bias,
    cotangent,
):
    images, rows, cols, chans = block_input.shape
    parts = lax.axis_size("ha") * lax.axis_size("wa")
    half = images // 2
    gain_one, bias_one, conv_one_bias, gain_two, bias_two, conv_two_bias = (
        v.reshape(1, chans) for v in (gain_one, bias_one, conv_one_bias, gain_two, bias_two, conv_two_bias)
    )
    payload = shaped((parts, half, chans), F32)
    per_image = shaped((images, chans), F32)
    two_images = shaped((2, images, chans), F32)
    block = (cols, rows, images, chans)
    rim_block = (cols + 2, rows + 2, images, chans)
    far_block = (cols + 4, rows + 4, images, chans)
    row_halo = shaped((2, cols, 2, images, chans), BF16)
    col_halo = shaped((2, 2, rows, images, chans), BF16)

    xt, gt, pay_one, kbias_two_local, down, up, right, left = kernel_call(
        prepare,
        (shaped(block, BF16), shaped(block, BF16), payload, per_image, row_halo, row_halo, col_halo, col_halo),
        block_input,
        cotangent,
    )
    top = shifted(down, "ha", 1)
    bottom = shifted(up, "ha", -1)
    from_left = shifted(right, "wa", 1)
    from_right = shifted(left, "wa", -1)
    moments_one = to_all(pay_one)
    ends = jnp.concatenate([top, bottom], axis=2)
    corner_l = shifted(ends[:, cols - 2 :], "wa", 1)
    corner_r = shifted(ends[:, 0:2], "wa", -1)

    embed = jnp.concatenate([sinusoid(timesteps), sinusoid(aug_levels), text_pooled.astype(F32)], axis=1)
    embed_sigma = jax.nn.sigmoid(embed)
    cond_act = (embed * embed_sigma).astype(BF16)
    film = jnp.dot(cond_act, film_weight, preferred_element_type=F32) + film_bias.astype(F32)

    pair = pltpu.VMEM((12 * chans, 2 * chans), BF16)
    pair_back = pltpu.VMEM((2 * chans, 12 * chans), BF16)
    act_one, mid, pay_two, stat_one = kernel_call(
        first_half,
        (shaped(far_block, BF16), shaped(rim_block, F32), payload, two_images),
        xt, top, bottom, from_left, from_right, corner_l, corner_r, moments_one,
        gain_one, bias_one, conv_one, conv_one_bias,
        scratch=(pair,),
    )
    moments_two = to_all(pay_two)
    act_two_grad = kernel_call(
        back_two,
        shaped(rim_block, F32),
        gt, top, bottom, from_left, from_right, corner_l, corner_r, conv_two,
        scratch=(pltpu.VMEM(far_block, BF16), pair_back),
    )
    act_two, pre_two_grad, pay_three, sums_two, stat_two = kernel_call(
        second_norm,
        (shaped(rim_block, BF16), shaped(rim_block, F32), payload, two_images, two_images),
        mid, act_two_grad, moments_two, gain_two, bias_two, film,
    )
    moments_three = to_all(pay_three)

    unit = 8 * parts
    two_rows = -(-(9 * chans + 2 * images + 1) // unit) * unit
    bundle_two = kernel_call(
        kernel_two, shaped((two_rows, chans), F32), act_two, gt, sums_two, kbias_two_local
    )
    mixed = kernel_call(
        mix,
        shaped((images, rows, cols, chans), BF16),
        act_two, conv_two, conv_two_bias, xt,
        scratch=(pair, pltpu.VMEM(block, F32)),
    )
    total_two = summed_over_devices(bundle_two, F32)

    middle_low, bundle_one, kbias_one_local = kernel_call(
        middle_grad,
        (shaped(rim_block, BF16), shaped((9 * chans, chans), F32), per_image),
        mid, pre_two_grad, moments_three, stat_two, gain_two, film, act_one,
    )
    norm_one_grad, pay_four = kernel_call(
        back_one,
        (shaped(block, F32), shaped((parts, 2 * half, chans), F32)),
        middle_low, conv_one, xt, stat_one, gain_one, bias_one, kbias_one_local,
        scratch=(pair_back,),
    )
    moments_four = to_all(pay_four)
    one_rows = -(-9 * chans // parts) * parts
    if one_rows != 9 * chans:
        bundle_one = jnp.pad(bundle_one, ((0, one_rows - 9 * chans), (0, 0)))
    total_one = summed_over_devices(bundle_one, BF16)
    input_grad, sums_one = kernel_call(
        finish,
        (shaped((images, rows, cols, chans), BF16), shaped((half, chans), F32)),
        norm_one_grad, xt, moments_four, stat_one, gain_one, cotangent,
    )

    taps = 9 * chans
    kernel_two_grad = total_two[:taps].reshape(3, 3, chans, chans)
    plain_two = total_two[taps : taps + images]
    cross_two = total_two[taps + images : taps + 2 * images]
    kbias_two_grad = total_two[taps + 2 * images]
    kernel_one_grad = total_one[:taps].astype(F32).reshape(3, 3, chans, chans)
    scale = 1.0 + film[:, :chans]
    gain_two_grad = jnp.sum(scale * cross_two, axis=0)
    bias_two_grad = jnp.sum(scale * plain_two, axis=0)
    scale_grad = gain_two.astype(F32) * cross_two + bias_two.astype(F32) * plain_two
    film_grad = jnp.concatenate([scale_grad, plain_two], axis=1)
    film_weight_grad = jnp.dot(cond_act.astype(F32).T, film_grad, precision=lax.Precision.HIGHEST)
    film_bias_grad = jnp.sum(film_grad, axis=0)
    text_weight = film_weight[2 * TEMB :].astype(F32)
    cond_grad = jnp.dot(film_grad, text_weight.T, precision=lax.Precision.HIGHEST)
    text = embed[:, 2 * TEMB :]
    sigma = embed_sigma[:, 2 * TEMB :]
    text_grad = cond_grad * (sigma * (1.0 + text * (1.0 - sigma)))
    return (
        mixed,
        input_grad,
        text_grad,
        sums_one[0],
        sums_one[1],
        kernel_one_grad,
        sums_one[2],
        gain_two_grad,
        bias_two_grad,
        film_weight_grad,
        film_bias_grad,
        kernel_two_grad,
        kbias_two_grad,
    )


def solution(mesh):
    split = P(None, "ha", "wa", None)
    return jax.shard_map(
        local,
        mesh=mesh,
        in_specs=(split,) + (P(),) * 13 + (split,),
        out_specs=(split, split) + (P(),) * 11,
        check_vma=False,
    )
```

```python
import functools
import math

import jax
import jax.numpy as jnp
from jax import lax
from jax.experimental import pallas as pl
from jax.experimental.pallas import tpu as pltpu
from jax.sharding import PartitionSpec as P

GROUPS = 32
TEMB = 256
EPSILON = 1e-05
INV_ROOT = 1.0 / math.sqrt(2.0)
AXES = ("ha", "wa")
F32 = jnp.float32
BF16 = jnp.bfloat16
NEAR = pl.BlockSpec(memory_space=pltpu.VMEM)
FAR = pl.BlockSpec(memory_space=pl.ANY)
MIB = 1 << 20


def shaped(shape, dtype):
    return jax.ShapeDtypeStruct(shape, dtype)


def kernel_call(body, far, near, far_out, near_out=(), scratch=(), sems=0, cost=1.0, after=(), limit=48):
    given = len(far) + len(near)
    far = [pltpu.with_memory_space_constraint(array, pltpu.HBM) for array in far]
    far_out = [pltpu.HBM(out.shape, out.dtype) for out in far_out]

    def run(*refs):
        body(*refs[:given], *refs[given + len(after) :])

    return pl.pallas_call(
        run,
        out_shape=tuple(far_out) + tuple(near_out),
        in_specs=[FAR] * len(far) + [NEAR] * len(near) + [FAR] * len(after),
        out_specs=(FAR,) * len(far_out) + (NEAR,) * len(near_out),
        scratch_shapes=tuple(scratch) + ((pltpu.SemaphoreType.DMA((sems,)),) if sems else ()),
        compiler_params=pltpu.CompilerParams(vmem_limit_bytes=limit * MIB),
        name=getattr(body, "func", body).__name__,
        cost_estimate=pl.CostEstimate(flops=int(cost * 1.1e9), bytes_accessed=0, transcendentals=0),
    )(*far, *near, *after)


class Mover:
    def __init__(self, sems):
        self.sems = sems
        self.used = 0
        self.open = []

    def start(self, source, target):
        copy = pltpu.make_async_copy(source, target, self.sems.at[self.used])
        self.used += 1
        copy.start()
        return copy

    def put(self, source, target):
        self.open.append(self.start(source, target))

    def finish(self):
        for copy in self.open:
            copy.wait()


def pieces(count, size):
    return [(at, min(at + size, count)) for at in range(0, count, size)]


def lanes_of(shape):
    return lax.broadcasted_iota(jnp.int32, shape, 1)


def group_total(values):
    chans = values.shape[1]
    lane = lanes_of(values.shape)
    step = 1
    while step < chans // GROUPS:
        up = pltpu.roll(values, chans - step, 1)
        down = pltpu.roll(values, step, 1)
        values = values + jnp.where((lane & step) == 0, up, down)
        step *= 2
    return values


def pack_pair(first, second):
    half = first.shape[0] // 2
    lane = lanes_of((half, first.shape[1])) & 3
    return jnp.where(
        lane == 0,
        first[:half],
        jnp.where(lane == 1, second[:half], jnp.where(lane == 2, first[half:], second[half:])),
    )


def unpack_at(packed, place):
    lane = lanes_of(packed.shape) & 3
    top = group_total(jnp.where(lane == place, packed, 0.0))
    low = group_total(jnp.where(lane == place + 2, packed, 0.0))
    return jnp.concatenate([top, low], axis=0)


def merge_moments(gathered_ref, local_count):
    parts = gathered_ref.shape[0]
    chans = gathered_ref.shape[2]
    every = gathered_ref[...]
    total = jnp.sum(every, axis=0)
    mean = total * (1.0 / parts)
    apart = every - mean[None]
    between = jnp.sum(apart * apart, axis=0)
    square = pltpu.roll(total, chans - 1, 1) + local_count * between
    inv = lax.rsqrt(square * (1.0 / (local_count * parts)) + EPSILON)
    return unpack_at(mean, 0), unpack_at(inv, 0)


def local_moments(total, square, pilot, pixels, per):
    off = total * (1.0 / pixels)
    mean = pilot + off
    apart = square - total * off
    group_mean = group_total(mean) * (1.0 / per)
    shift = mean - group_mean
    return group_mean, group_total(apart + pixels * shift * shift)


def sigmoid(values):
    return 0.5 + 0.5 * jnp.tanh(0.5 * values)


def forward_weights(kernel_ref, pair_ref):
    chans = kernel_ref.shape[2]
    zero = jnp.zeros((chans, chans), BF16)
    for row in range(3):
        for col in range(4):
            at = (row * 4 + col) * chans
            pair_ref[at : at + chans, 0:chans] = kernel_ref[row, col] if col < 3 else zero
            pair_ref[at : at + chans, chans:] = kernel_ref[row, col - 1] if col > 0 else zero


def backward_weights(kernel_ref, pair_ref):
    chans = kernel_ref.shape[2]
    zero = jnp.zeros((chans, chans), BF16)
    for row in range(3):
        for col in range(4):
            at = (row * 4 + col) * chans
            pair_ref[0:chans, at : at + chans] = kernel_ref[2 - row, 2 - col] if col < 3 else zero
            pair_ref[chans:, at : at + chans] = kernel_ref[2 - row, 3 - col] if col > 0 else zero


def convolve(cells_ref, pair_ref, out_ref, transposed, first, last, bias=None):
    cols, rows, images, chans = out_ref.shape
    pairs = (last - first) // 2
    parts = []
    for row in range(3):
        for col in range(4):
            window = [cells_ref[first + 2 * q + col, row : row + rows] for q in range(pairs)]
            parts.append(jnp.stack(window).reshape(pairs * rows * images, chans))
    wide = jnp.concatenate(parts, axis=1)
    contract = ((1,), (1,)) if transposed else ((1,), (0,))
    made = lax.dot_general(wide, pair_ref[...], (contract, ((), ())), preferred_element_type=F32)
    for side in range(2):
        piece = made[:, side * chans : (side + 1) * chans]
        if bias is not None:
            piece = piece + bias
        piece = piece.reshape(pairs, rows, images, chans)
        for q in range(pairs):
            out_ref[first + 2 * q + side] = piece[q]


def kernel_grad(cells_ref, grads_ref, keep_ref, send_ref):
    cols, rows, images, chans = grads_ref.shape
    half = chans // 2
    first = lax.axis_index("ha") % 2 == 0
    wide = grads_ref[...].reshape(cols * rows * images, chans)
    for row in range(3):
        for col in range(3):
            window = cells_ref[col : col + cols, row : row + rows]
            made = lax.dot_general(
                window.reshape(cols * rows * images, chans),
                wide,
                (((0,), (0,)), ((), ())),
                preferred_element_type=F32,
            )
            at = (row * 3 + col) * half
            keep_ref[at : at + half, :] = jnp.where(first, made[:half], made[half:])
            send_ref[at : at + half, :] = jnp.where(first, made[half:], made[:half])


def at_edges():
    tall = lax.axis_index("ha")
    wide = lax.axis_index("wa")
    return (
        tall == 0,
        tall == lax.axis_size("ha") - 1,
        wide == 0,
        wide == lax.axis_size("wa") - 1,
    )


def clear_border(cells_ref, width, first=0, last=None):
    top, bottom, left, right = at_edges()
    cols, rows, images, chans = cells_ref.shape
    last = cols if last is None else last
    dtype = cells_ref.dtype

    @pl.when(top)
    def _():
        cells_ref[first:last, 0:width] = jnp.zeros((last - first, width, images, chans), dtype)

    @pl.when(bottom)
    def _():
        cells_ref[first:last, rows - width :] = jnp.zeros((last - first, width, images, chans), dtype)

    if first == 0:

        @pl.when(left)
        def _():
            cells_ref[0:width] = jnp.zeros((width, rows, images, chans), dtype)

    if last == cols:

        @pl.when(right)
        def _():
            cells_ref[cols - width :] = jnp.zeros((width, rows, images, chans), dtype)


def send_payload(mover, packed, pay_ref, stage_ref):
    stage_ref[...] = jnp.broadcast_to(packed[None], stage_ref.shape)
    mover.put(stage_ref, pay_ref)


def prepare(
    x_far, c_far, xt_far, gt_far, pay_far,
    x_down, x_up, x_sides, g_down, g_up, g_sides, bias_ref,
    x_ref, c_ref, xt_ref, gt_ref, stage_ref, sems,
):
    images, rows, cols, chans = x_ref.shape
    mover = Mover(sems)
    steps = pieces(rows, 2)
    loads = [mover.start(x_far.at[:, a:b], x_ref.at[:, a:b]) for a, b in steps]
    late = [mover.start(c_far.at[:, a:b], c_ref.at[:, a:b]) for a, b in steps]
    total = jnp.zeros((images, chans), F32)
    square = total
    for (a, b), load in zip(steps, loads):
        load.wait()
        if a == 0:
            pilot = x_ref[:, 0, 0].astype(F32)
        for row in range(a, b):
            x = jnp.swapaxes(x_ref[:, row].astype(F32), 0, 1)
            xt_ref[:, row] = x.astype(BF16)
            apart = x - pilot[None]
            total = total + jnp.sum(apart, axis=0)
            square = square + jnp.sum(apart * apart, axis=0)
        mover.put(xt_ref.at[:, a:b], xt_far.at[:, a:b])
    mean, spread = local_moments(total, square, pilot, rows * cols, chans // GROUPS)
    send_payload(mover, pack_pair(mean, spread), pay_far, stage_ref)
    bias = jnp.zeros((images, chans), F32)
    for (a, b), load in zip(steps, late):
        load.wait()
        for row in range(a, b):
            grad = jnp.swapaxes(c_ref[:, row].astype(F32) * INV_ROOT, 0, 1).astype(BF16)
            gt_ref[:, row] = grad
            bias = bias + jnp.sum(grad.astype(F32), axis=0)
        mover.put(gt_ref.at[:, a:b], gt_far.at[:, a:b])
    bias_ref[...] = bias
    for cells, down, up, sides in ((xt_ref, x_down, x_up, x_sides), (gt_ref, g_down, g_up, g_sides)):
        down[...] = cells[:, rows - 2 :]
        up[...] = cells[:, 0:2]
        sides[0:2] = cells[0:2]
        sides[2:4] = cells[cols - 2 :]
    mover.finish()


def edge_columns(sides_ref, top_ref, bottom_ref, *refs, passed):
    right_ref, left_ref = refs[passed : passed + 2]
    cols, rows = top_ref.shape[0], sides_ref.shape[1]
    for ref, side, at in ((left_ref, 0, 0), (right_ref, 2, cols - 2)):
        ref[:, 0:2] = top_ref[at : at + 2]
        ref[:, 2 : rows + 2] = sides_ref[side : side + 2]
        ref[:, rows + 2 :] = bottom_ref[at : at + 2]
    for source, target in zip(refs[0:passed], refs[passed + 2 : 2 * passed + 2]):
        target[...] = source[...]


def assemble(mover, own_far, own_ref, top_ref, bottom_ref, left_ref, right_ref, cells_ref, change):
    cols, rows, images, chans = own_ref.shape
    steps = pieces(cols, 8)
    loads = [mover.start(own_far.at[a:b], own_ref.at[a:b]) for a, b in steps]

    def fill():
        def halo_column(col, _):
            cells_ref[pl.ds(col + 2, 1), 0:2] = change(top_ref[pl.ds(col, 1)])
            cells_ref[pl.ds(col + 2, 1), rows + 2 :] = change(bottom_ref[pl.ds(col, 1)])
            return 0

        def column(col, _):
            cells_ref[pl.ds(col + 2, 1), 2 : rows + 2] = change(own_ref[pl.ds(col, 1)])
            return 0

        cells_ref[0:2] = change(left_ref[...])
        cells_ref[cols + 2 :] = change(right_ref[...])
        lax.fori_loop(0, cols, halo_column, 0, unroll=4)
        for (a, b), load in zip(steps, loads):
            load.wait()
            lax.fori_loop(a, b, column, 0, unroll=2)
        clear_border(cells_ref, 2)

    return fill


def first_half(
    xt_far, kernel_far, top_ref, bottom_ref, left_ref, right_ref, gathered_ref, vecs_ref,
    act_far, mid_far, pay_far, stat_ref,
    xt_ref, kernel_ref, act_ref, mid_ref, stage_ref, pair_ref, sems,
):
    cols, rows, images, chans = xt_ref.shape
    per = chans // GROUPS
    mover = Mover(sems)
    load = mover.start(kernel_far, kernel_ref)
    mean, inv = merge_moments(gathered_ref, rows * cols * per)
    stat_ref[0] = mean
    stat_ref[1] = inv
    slope = inv * vecs_ref[0:1]
    offset = vecs_ref[1:2]

    def act(cells):
        value = (cells.astype(F32) - mean) * slope + offset
        return (value * sigmoid(value)).astype(BF16)

    fill = assemble(mover, xt_far, xt_ref, top_ref, bottom_ref, left_ref, right_ref, act_ref, act)
    fill()
    load.wait()
    forward_weights(kernel_ref, pair_ref)
    mover.put(act_ref, act_far)

    pilot = None
    total = jnp.zeros((images, chans), F32)
    square = total
    wide = cols + 2
    cut = wide // 4 * 2
    for a, b in ((0, cut), (cut, wide)):
        convolve(act_ref, pair_ref, mid_ref, False, a, b, vecs_ref[2:3])
        mover.put(mid_ref.at[a:b], mid_far.at[a:b])
        if pilot is None:
            pilot = mid_ref[1, 1]

        def column(col, carry):
            total, square = carry
            apart = mid_ref[pl.ds(col, 1), 1 : rows + 1].reshape(rows, images, chans) - pilot[None]
            return total + jnp.sum(apart, axis=0), square + jnp.sum(apart * apart, axis=0)

        total, square = lax.fori_loop(max(a, 1), min(b, cols + 1), column, (total, square))
    mean, spread = local_moments(total, square, pilot, rows * cols, per)
    send_payload(mover, pack_pair(mean, spread), pay_far, stage_ref)
    mover.finish()


def back_two(
    gt_far, kernel_far, top_ref, bottom_ref, left_ref, right_ref, out_far,
    gt_ref, kernel_ref, cells_ref, out_ref, pair_ref, sems,
):
    mover = Mover(sems)
    load = mover.start(kernel_far, kernel_ref)
    fill = assemble(mover, gt_far, gt_ref, top_ref, bottom_ref, left_ref, right_ref, cells_ref, lambda cells: cells)
    load.wait()
    backward_weights(kernel_ref, pair_ref)
    fill()
    wide = out_ref.shape[0]
    cut = wide // 4 * 2
    for a, b in ((0, cut), (cut, wide)):
        convolve(cells_ref, pair_ref, out_ref, True, a, b)
        mover.put(out_ref.at[a:b], out_far.at[a:b])
    mover.finish()


def second_norm(
    mid_far, back_far, gathered_ref, vecs_ref, film_ref,
    act_far, pre_far, pay_far, sums_ref, stat_ref,
    mid_ref, back_ref, act_ref, pre_ref, stage_ref, sems,
):
    wide, tall, images, chans = mid_ref.shape
    cols, rows = wide - 2, tall - 2
    per = chans // GROUPS
    mover = Mover(sems)
    steps = pieces(wide, 9)
    loads = []
    for a, b in steps:
        loads.append(
            [mover.start(f.at[a:b], n.at[a:b]) for f, n in ((mid_far, mid_ref), (back_far, back_ref))]
        )
    mean, inv = merge_moments(gathered_ref, rows * cols * per)
    stat_ref[0] = mean
    stat_ref[1] = inv
    scale = 1.0 + film_ref[:, 0:chans]
    slope = vecs_ref[3:4] * scale
    offset = vecs_ref[4:5] * scale + film_ref[:, chans:]

    def column(col, inner):
        hat = (mid_ref[pl.ds(col, 1)].reshape(tall, images, chans) - mean) * inv
        pre = hat * slope + offset
        sigma = sigmoid(pre)
        act = pre * sigma
        act_ref[pl.ds(col, 1)] = act.astype(BF16).reshape(1, tall, images, chans)
        grad = back_ref[pl.ds(col, 1)].reshape(tall, images, chans) * (sigma + act * (1.0 - sigma))
        pre_ref[pl.ds(col, 1)] = grad.reshape(1, tall, images, chans)
        if inner is None:
            return None
        own = grad[1 : rows + 1]
        plain, cross = inner
        return plain + jnp.sum(own, axis=0), cross + jnp.sum(own * hat[1 : rows + 1], axis=0)

    zero = jnp.zeros((images, chans), F32)
    inner = (zero, zero)
    for (a, b), pair in zip(steps, loads):
        for load in pair:
            load.wait()
        if a == 0:
            column(0, None)
        inner = lax.fori_loop(max(a, 1), min(b, cols + 1), column, inner)
        if b == wide:
            column(wide - 1, None)
        clear_border(act_ref, 1, a, b)
        mover.put(act_ref.at[a:b], act_far.at[a:b])
        mover.put(pre_ref.at[a:b], pre_far.at[a:b])
    plain, cross = inner
    sums_ref[0] = plain
    sums_ref[1] = cross
    send_payload(mover, pack_pair(group_total(plain * slope), group_total(cross * slope)), pay_far, stage_ref)
    mover.finish()


def kernel_two(
    act_far, gt_far, sums_ref, bias_ref, keep_far, send_far, act_ref, gt_ref, keep_ref, send_ref, sems
):
    mover = Mover(sems)
    for load in [mover.start(act_far, act_ref), mover.start(gt_far, gt_ref)]:
        load.wait()
    kernel_grad(act_ref, gt_ref, keep_ref, send_ref)
    images, chans = bias_ref.shape
    at = 9 * (chans // 2)
    total = jnp.sum(bias_ref[...], axis=0, keepdims=True)
    for ref in (keep_ref, send_ref):
        ref[at : at + images] = sums_ref[0]
        ref[at + images : at + 2 * images] = sums_ref[1]
        ref[at + 2 * images :] = jnp.broadcast_to(total, (ref.shape[0] - at - 2 * images, chans))
    mover.put(keep_ref, keep_far)
    mover.put(send_ref, send_far)
    mover.finish()


def mix(
    act_far, kernel_far, xt_far, vecs_ref, out_far, act_ref, kernel_ref, xt_ref, branch_ref, out_ref, pair_ref, sems
):
    images, rows, cols, chans = out_ref.shape
    mover = Mover(sems)
    loads = [mover.start(f, n) for f, n in ((kernel_far, kernel_ref), (act_far, act_ref), (xt_far, xt_ref))]
    for load in loads:
        load.wait()
    forward_weights(kernel_ref, pair_ref)
    convolve(act_ref, pair_ref, branch_ref, False, 0, cols, vecs_ref[5:6])
    for a, b in pieces(rows, 4):
        for row in range(a, b):
            mixed = jnp.swapaxes((xt_ref[:, row].astype(F32) + branch_ref[:, row]) * INV_ROOT, 0, 1)
            out_ref[:, row] = mixed.astype(BF16)
        mover.put(out_ref.at[:, a:b], out_far.at[:, a:b])
    mover.finish()


def middle_back(
    mid_far, pre_far, act_far, xt_far, kernel_far, gathered_ref, stat_two_ref, stat_one_ref, vecs_ref, film_ref,
    keep_far, send_far, grad_far,
    mid_ref, pre_ref, act_ref, xt_ref, kernel_ref, low_ref, keep_ref, send_ref, out_ref, pair_ref, sems,
):
    wide, tall, images, chans = mid_ref.shape
    cols, rows = wide - 2, tall - 2
    mover = Mover(sems)
    steps = pieces(wide, 9)
    loads = []
    for a, b in steps:
        loads.append([mover.start(f.at[a:b], n.at[a:b]) for f, n in ((mid_far, mid_ref), (pre_far, pre_ref))])
    late = [mover.start(f, n) for f, n in ((act_far, act_ref), (kernel_far, kernel_ref), (xt_far, xt_ref))]
    count = lax.axis_size("ha") * lax.axis_size("wa") * rows * cols * (chans // GROUPS)
    packed = jnp.sum(gathered_ref[...], axis=0) * (1.0 / count)
    plain = unpack_at(packed, 0)
    cross = unpack_at(packed, 1)
    mean = stat_two_ref[0]
    inv = stat_two_ref[1]
    slope = vecs_ref[3:4] * (1.0 + film_ref[:, 0:chans])

    def low_column(col, total):
        hat = (mid_ref[pl.ds(col, 1)].reshape(tall, images, chans) - mean) * inv
        grad = pre_ref[pl.ds(col, 1)].reshape(tall, images, chans) * slope
        low = (inv * (grad - plain - hat * cross)).astype(BF16)
        low_ref[pl.ds(col, 1)] = low.reshape(1, tall, images, chans)
        if total is None:
            return None
        return total + jnp.sum(low[1 : rows + 1].astype(F32), axis=0)

    kbias = jnp.zeros((images, chans), F32)
    for (a, b), pair in zip(steps, loads):
        for load in pair:
            load.wait()
        if a == 0:
            low_column(0, None)
        kbias = lax.fori_loop(max(a, 1), min(b, cols + 1), low_column, kbias)
        if b == wide:
            low_column(wide - 1, None)
    clear_border(low_ref, 1)
    for load in late:
        load.wait()
    own = low_ref.at[1 : wide - 1, 1 : tall - 1]
    kernel_grad(act_ref.at[1 : wide + 1, 1 : tall + 1], own, keep_ref, send_ref)
    backward_weights(kernel_ref, pair_ref)
    convolve(low_ref, pair_ref, out_ref, True, 0, cols)
    mean_one = stat_one_ref[0]
    inv_one = stat_one_ref[1]
    gain = vecs_ref[0:1]
    bias = vecs_ref[1:2]

    def column(col, carry):
        plain, cross = carry
        hat = (xt_ref[pl.ds(col, 1)].reshape(rows, images, chans).astype(F32) - mean_one) * inv_one
        norm = hat * gain + bias
        sigma = sigmoid(norm)
        grad = out_ref[pl.ds(col, 1)].reshape(rows, images, chans)
        grad = grad * (sigma * (1.0 + norm * (1.0 - sigma)))
        out_ref[pl.ds(col, 1)] = grad.reshape(1, rows, images, chans)
        return plain + jnp.sum(grad, axis=0), cross + jnp.sum(grad * hat, axis=0)

    zero = jnp.zeros((images, chans), F32)
    inner = (zero, zero)
    for a, b in pieces(cols, 8):
        inner = lax.fori_loop(a, b, column, inner)
        mover.put(out_ref.at[a:b], grad_far.at[a:b])
    plain_one, cross_one = inner
    rest = [jnp.sum(v, axis=0, keepdims=True) for v in (cross_one, plain_one, kbias)]
    rest = jnp.concatenate(rest + [jnp.zeros((5, chans), F32)], axis=0)
    packed = pack_pair(group_total(plain_one * gain), group_total(cross_one * gain))
    at = 9 * (chans // 2)
    half = images // 2
    for ref, far in ((keep_ref, keep_far), (send_ref, send_far)):
        ref[at : at + 8] = rest
        ref[at + 8 : at + 8 + half] = packed
        mover.put(ref, far)
    mover.finish()


def pack_terms(keep_far, came_ref, out_far, keep_ref, half_ref, out_ref, sems, extras, whole):
    chips, rows, chans = out_ref.shape
    mover = Mover(sems)
    mover.start(keep_far, keep_ref).wait()
    taps = 9 * (chans // 2)
    share = -(-taps // chips)
    more = -(-extras // chips)
    half_ref[...] = keep_ref[...] + came_ref[...]
    for chip in range(chips):
        a, b = chip * share, min((chip + 1) * share, taps)
        if a < b:
            out_ref[chip, 0 : b - a] = half_ref[a:b]
        a, b = chip * more, min((chip + 1) * more, extras)
        if a < b:
            out_ref[chip, share : share + b - a] = half_ref[taps + a : taps + b]
    if whole:
        kept = half_ref[half_ref.shape[0] - whole :]
        out_ref[:, rows - whole :] = jnp.broadcast_to(kept[None], (chips, whole, chans))
    mover.put(out_ref, out_far)
    mover.finish()


def add_terms(one_ref, two_ref, out_far, small_ref, out_ref, sems, extras_one, extras_two):
    chips, rows, chans = one_ref.shape
    mover = Mover(sems)
    share = -(-9 * (chans // 2) // chips)
    whole = small_ref.shape[0]
    one = jnp.sum(one_ref[...], axis=0)
    two = jnp.sum(two_ref[...], axis=0)
    small_ref[...] = one[rows - whole :]
    extra = jnp.concatenate(
        [two[share : share - (-extras_two // chips)], one[share : share - (-extras_one // chips)]], axis=0
    )
    high = extra.astype(BF16).astype(F32)
    both = jnp.concatenate([one[0:share], two[0:share], high, extra - high], axis=0)
    short = out_ref.shape[1] - both.shape[0]
    if short:
        both = jnp.concatenate([both, jnp.zeros((short, chans), F32)], axis=0)
    out_ref[...] = jnp.broadcast_to(both.astype(BF16)[None], out_ref.shape)
    mover.put(out_ref, out_far)
    mover.finish()


def three_terms(values):
    high = values.astype(BF16)
    rest = values - high.astype(F32)
    mid = rest.astype(BF16)
    low = (rest - mid.astype(F32)).astype(BF16)
    return jnp.concatenate([high, mid, low], axis=0)


def last_grads(
    weight_far, own_ref, other_ref, film_ref, vecs_ref, ints_ref, text_ref,
    one_far, two_far, weight_grad_far, text_grad_far, vec_ref, bias_ref,
    weight_ref, one_ref, two_ref, weight_grad_ref, text_grad_ref, half_ref, extra_ref, sems,
    extras_one, extras_two,
):
    chips, rows, chans = own_ref.shape
    images = film_ref.shape[0]
    mover = Mover(sems)
    load = mover.start(weight_far, weight_ref)
    half = chans // 2
    taps = 9 * half
    share = -(-taps // chips)
    more_two = -(-extras_two // chips)
    more_one = -(-extras_one // chips)
    more = more_two + more_one
    for chip in range(chips):
        piece = own_ref[chip].astype(F32)
        piece = piece[2 * share : 2 * share + more] + piece[2 * share + more : 2 * share + 2 * more]
        extra_ref[chip * more_two : (chip + 1) * more_two] = piece[0:more_two]
        if chip < extras_one:
            at = chips * more_two + chip * more_one
            extra_ref[at : at + more_one] = piece[more_two:]
    plain = extra_ref[0:images]
    cross = extra_ref[images : 2 * images]
    scale = 1.0 + film_ref[:, 0:chans]
    scale_grad = vecs_ref[3:4] * cross + vecs_ref[4:5] * plain
    film_grad = jnp.concatenate([scale_grad, plain], axis=1)
    bias_ref[...] = jnp.sum(film_grad, axis=0, keepdims=True)
    vec_ref[0:1] = jnp.sum(scale * cross, axis=0, keepdims=True)
    vec_ref[1:2] = jnp.sum(scale * plain, axis=0, keepdims=True)
    vec_ref[2:3] = extra_ref[2 * images : 2 * images + 1]
    at = chips * more_two
    vec_ref[3:6] = extra_ref[at : at + 3]
    vec_ref[6:8] = jnp.zeros((2, chans), F32)
    terms = three_terms(film_grad)
    ints = ints_ref.shape[1]
    depth = weight_grad_ref.shape[0]
    load.wait()
    for start in range(0, depth, 512):
        stop = start + 512
        if start < ints:
            act = ints_ref[:, start:stop]
        else:
            embed = text_ref[:, start - ints : stop - ints].astype(F32)
            sigma = sigmoid(embed)
            act = (embed * sigma).astype(BF16)
        weight_grad_ref[start:stop] = lax.dot_general(
            jnp.concatenate([act, act, act], axis=0), terms, (((0,), (0,)), ((), ())), preferred_element_type=F32
        )
        mover.put(weight_grad_ref.at[start:stop], weight_grad_far.at[start:stop])
        if start >= ints:
            made = lax.dot_general(
                terms, weight_ref[start:stop], (((1,), (1,)), ((), ())), preferred_element_type=F32
            )
            cond_grad = made[0:images] + made[images : 2 * images] + made[2 * images :]
            slope = sigma * (1.0 + embed * (1.0 - sigma))
            text_grad_ref[:, start - ints : stop - ints] = cond_grad * slope
    mover.put(text_grad_ref, text_grad_far)
    core = lax.axis_index("ha") % 2
    for source, place in ((own_ref, core), (other_ref, 1 - core)):
        for at, out_ref in enumerate((one_ref, two_ref)):
            for chip in range(chips):
                piece = source[chip].astype(F32)[at * share : (at + 1) * share]
                half_ref[chip * share : (chip + 1) * share] = piece
            for tap in range(9):
                rows_at = pl.ds(pl.multiple_of(place * half, half), half)
                out_ref[tap, rows_at] = half_ref[tap * half : (tap + 1) * half]
    mover.put(one_ref, one_far)
    mover.put(two_ref, two_far)
    mover.finish()


def finish(
    grad_far, xt_far, c_far, small_ref, stat_ref, vecs_ref, out_far, grad_ref, xt_ref, c_ref, out_ref, sems
):
    images, rows, cols, chans = out_ref.shape
    mover = Mover(sems)
    steps = pieces(rows, 2)
    loads = []
    for a, b in steps:
        both = [mover.start(f.at[:, a:b], n.at[:, a:b]) for f, n in ((grad_far, grad_ref), (xt_far, xt_ref))]
        loads.append(both + [mover.start(c_far.at[:, a:b], c_ref.at[:, a:b])])
    count = lax.axis_size("ha") * lax.axis_size("wa") * rows * cols * (chans // GROUPS)
    packed = small_ref[...] * (1.0 / count)
    plain = unpack_at(packed, 0)
    cross = unpack_at(packed, 1)
    mean = stat_ref[0]
    inv = stat_ref[1]
    gain = vecs_ref[0:1]
    for (a, b), group in zip(steps, loads):
        for load in group:
            load.wait()
        for row in range(a, b):
            hat = (xt_ref[:, row].astype(F32) - mean) * inv
            path = jnp.swapaxes(inv * (grad_ref[:, row] * gain - plain - hat * cross), 0, 1)
            out_ref[:, row] = (c_ref[:, row].astype(F32) * INV_ROOT + path).astype(BF16)
        mover.put(out_ref.at[:, a:b], out_far.at[:, a:b])
    mover.finish()


def to_all(payload):
    return lax.all_to_all(payload, AXES, 0, 0)


def to_chips(payload):
    tall, wide = lax.axis_size("ha"), lax.axis_size("wa")
    groups = [[h * wide + w for h in range(core, tall, 2) for w in range(wide)] for core in range(2)]
    return lax.all_to_all(payload, AXES, 0, 0, axis_index_groups=groups)


def to_sibling(payload):
    return lax.ppermute(payload, "ha", [(i, i ^ 1) for i in range(lax.axis_size("ha"))])


def shifted(cells, axis, step):
    count = lax.axis_size(axis)
    return lax.ppermute(cells, axis, [(i, (i + step) % count) for i in range(count)])


def halo(sides, down, up, after=(), passed=()):
    four, rows, images, chans = sides.shape
    top = shifted(down, "ha", 1)
    bottom = shifted(up, "ha", -1)
    edge = shaped((2, rows + 4, images, chans), sides.dtype)
    right, left, *rest = kernel_call(
        functools.partial(edge_columns, passed=len(passed)), (), (sides, top, bottom, *passed),
        (), (edge, edge) + tuple(shaped(p.shape, p.dtype) for p in passed), cost=0.4, after=after, limit=16,
    )
    return (top, bottom, shifted(right, "wa", 1), shifted(left, "wa", -1)), rest


def sinusoids(first, second):
    half = TEMB // 2
    freqs = jnp.exp(-math.log(10000.0) * jnp.arange(half, dtype=F32) / half)
    times = jnp.stack([first, second], axis=1).astype(F32)
    angles = times[:, :, None, None] * freqs[None, None, None, :]
    which = lax.broadcasted_iota(jnp.int32, (first.shape[0], 2, 2, half), 2)
    made = jnp.where(which == 0, jnp.sin(angles), jnp.cos(angles))
    return made.reshape(first.shape[0], 2 * TEMB)


def buffers(*arrays):
    return tuple(pltpu.VMEM(a.shape, a.dtype) for a in arrays)


def local(
    block_input,
    timesteps,
    aug_levels,
    text_pooled,
    gain_one,
    bias_one,
    conv_one,
    conv_one_bias,
    gain_two,
    bias_two,
    film_weight,
    film_bias,
    conv_two,
    conv_two_bias,
    cotangent,
):
    images, rows, cols, chans = block_input.shape
    parts = lax.axis_size("ha") * lax.axis_size("wa")
    chips = parts // 2
    half = images // 2
    vecs = (gain_one, bias_one, conv_one_bias, gain_two, bias_two, conv_two_bias, gain_one, gain_one)
    vecs = jnp.stack(vecs).astype(F32)
    payload = shaped((parts, half, chans), F32)
    per_image = shaped((images, chans), F32)
    two_images = shaped((2, images, chans), F32)
    block = shaped((cols, rows, images, chans), BF16)
    block_wide = shaped((cols, rows, images, chans), F32)
    rim = shaped((cols + 2, rows + 2, images, chans), BF16)
    rim_wide = shaped((cols + 2, rows + 2, images, chans), F32)
    far_rim = shaped((cols + 4, rows + 4, images, chans), BF16)
    row_halo = shaped((cols, 2, images, chans), BF16)
    given = shaped((images, rows, cols, chans), BF16)
    pair = pltpu.VMEM((12 * chans, 2 * chans), BF16)
    pair_back = pltpu.VMEM((2 * chans, 12 * chans), BF16)

    sides = shaped((4, rows, images, chans), BF16)
    xt, gt, pay_one, x_down, x_up, x_sides, g_down, g_up, g_sides, kbias_two_local = kernel_call(
        prepare, (block_input, cotangent), (), (block, block, payload),
        (row_halo, row_halo, sides, row_halo, row_halo, sides, per_image),
        scratch=buffers(given, given, block, block, payload), sems=24, cost=3.5,
    )
    moments_one = to_all(pay_one)
    x_halo, (g_down, g_up) = halo(x_sides, x_down, x_up, passed=(g_down, g_up))

    embed_ints = sinusoids(timesteps, aug_levels)
    act_ints = jax.nn.silu(embed_ints).astype(BF16)
    act_text = jax.nn.silu(text_pooled.astype(F32)).astype(BF16)
    film = (
        jnp.dot(act_ints, film_weight[: 2 * TEMB], preferred_element_type=F32)
        + jnp.dot(act_text, film_weight[2 * TEMB :], preferred_element_type=F32)
        + film_bias.astype(F32)
    )

    act_one, mid, pay_two, stat_one = kernel_call(
        first_half, (xt, conv_one), (*x_halo, moments_one, vecs), (far_rim, rim_wide, payload), (two_images,),
        scratch=buffers(xt, conv_one, far_rim, rim_wide, payload) + (pair,), sems=16, cost=5.5,
    )
    moments_two = to_all(pay_two)
    g_halo, _ = halo(g_sides, g_down, g_up, after=(act_one,))
    (act_two_grad,) = kernel_call(
        back_two, (gt, conv_two), g_halo, (rim_wide,),
        scratch=buffers(gt, conv_two, far_rim, rim_wide) + (pair_back,), sems=16, cost=3.7,
    )
    act_two, pre_two_grad, pay_three, sums_two, stat_two = kernel_call(
        second_norm, (mid, act_two_grad), (moments_two, vecs, film), (rim, rim_wide, payload), (two_images, two_images),
        scratch=buffers(rim_wide, rim_wide, rim, rim_wide, payload), sems=24, cost=3.2,
    )
    moments_three = to_all(pay_three)

    taps = 9 * (chans // 2)
    share = -(-taps // chips)
    extras_two = 2 * images + 1
    extras_one = 3
    halves_two = shaped((taps + 2 * images + 8, chans), F32)
    halves_one = shaped((taps + 8 + half, chans), F32)
    keep_two, send_two = kernel_call(
        kernel_two, (act_two, gt), (sums_two, kbias_two_local), (halves_two, halves_two),
        scratch=buffers(act_two, gt, halves_two, halves_two), sems=4, cost=3.0,
    )
    came_two = to_sibling(send_two)
    terms_shape = shaped((chips, -(-(share - (-extras_two // chips)) // 8) * 8, chans), F32)
    (terms_two,) = kernel_call(
        functools.partial(pack_terms, extras=extras_two, whole=0), (keep_two,), (came_two,), (terms_shape,),
        scratch=buffers(halves_two, halves_two, terms_shape), sems=3, cost=1.0,
    )
    gathered_two = to_chips(terms_two)

    keep_one, send_one, norm_one_grad = kernel_call(
        middle_back,
        (mid, pre_two_grad, act_one, xt, conv_one),
        (moments_three, stat_two, stat_one, vecs, film),
        (halves_one, halves_one, block_wide),
        scratch=buffers(mid, pre_two_grad, act_one, xt, conv_one, rim, halves_one, halves_one, block_wide)
        + (pair_back,),
        sems=24, cost=8.0, after=(terms_two,),
    )
    came_one = to_sibling(send_one)
    terms_shape = shaped((chips, -(-(share - (-extras_one // chips)) // 8) * 8 + half, chans), F32)
    (terms_one,) = kernel_call(
        functools.partial(pack_terms, extras=extras_one, whole=half), (keep_one,), (came_one,), (terms_shape,),
        scratch=buffers(halves_one, halves_one, terms_shape), sems=3, cost=1.0,
    )
    gathered_one = to_chips(terms_one)
    (mixed,) = kernel_call(
        mix, (act_two, conv_two, xt), (vecs,), (given,),
        scratch=buffers(act_two, conv_two, xt, block_wide, given) + (pair,), sems=8, cost=3.6, after=(terms_one,),
    )
    more = -(-extras_one // chips) - (-extras_two // chips)
    shares_shape = shaped((chips, -(-(2 * share + 2 * more) // 16) * 16, chans), BF16)
    shares, small = kernel_call(
        functools.partial(add_terms, extras_one=extras_one, extras_two=extras_two),
        (), (gathered_one, gathered_two), (shares_shape,), (shaped((half, chans), F32),),
        scratch=buffers(shares_shape), sems=1, cost=1.0,
    )
    own_half = to_chips(shares)
    other_half = to_sibling(own_half)
    (input_grad,) = kernel_call(
        finish, (norm_one_grad, xt, cotangent), (small, stat_one, vecs), (given,),
        scratch=buffers(norm_one_grad, xt, cotangent, given), sems=16, cost=3.3,
    )
    full = shaped((9, chans, chans), F32)
    weight_grad = shaped(film_weight.shape, F32)
    text_shape = shaped(text_pooled.shape, F32)
    kernel_one_grad, kernel_two_grad, film_weight_grad, text_grad, vec_grads, film_bias_grad = kernel_call(
        functools.partial(last_grads, extras_one=extras_one, extras_two=extras_two),
        (film_weight,),
        (own_half, other_half, film, vecs, act_ints, text_pooled),
        (full, full, weight_grad, text_shape),
        (shaped((8, chans), F32), shaped((1, 2 * chans), F32)),
        scratch=buffers(film_weight, full, full, weight_grad, text_shape)
        + (
            pltpu.VMEM((chips * share, chans), F32),
            pltpu.VMEM((chips * (-(-extras_two // chips)) + 8, chans), F32),
        ),
        sems=24, cost=4.0,
    )
    return (
        mixed,
        input_grad,
        text_grad,
        vec_grads[3],
        vec_grads[4],
        kernel_one_grad.reshape(3, 3, chans, chans),
        vec_grads[5],
        vec_grads[0],
        vec_grads[1],
        film_weight_grad,
        film_bias_grad.reshape(2 * chans),
        kernel_two_grad.reshape(3, 3, chans, chans),
        vec_grads[2],
    )


def solution(mesh):
    split = P(None, "ha", "wa", None)
    return jax.shard_map(
        local,
        mesh=mesh,
        in_specs=(split,) + (P(),) * 13 + (split,),
        out_specs=(split, split) + (P(),) * 11,
        check_vma=False,
    )
```

```python
import functools
import math

import jax
import jax.numpy as jnp
from jax import lax
from jax.experimental import pallas as pl
from jax.experimental.pallas import tpu as pltpu
from jax.sharding import PartitionSpec as P

GROUPS = 32
TEMB = 256
EPSILON = 1e-05
INV_ROOT = 1.0 / math.sqrt(2.0)
AXES = ("ha", "wa")
F32 = jnp.float32
BF16 = jnp.bfloat16
NEAR = pl.BlockSpec(memory_space=pltpu.VMEM)
FAR = pl.BlockSpec(memory_space=pl.ANY)
MIB = 1 << 20


def shaped(shape, dtype):
    return jax.ShapeDtypeStruct(shape, dtype)


def kernel_call(body, far, near, far_out, near_out=(), scratch=(), sems=0, cost=1.0, after=(), limit=48):
    given = len(far) + len(near)
    far = [pltpu.with_memory_space_constraint(array, pltpu.HBM) for array in far]
    far_out = [pltpu.HBM(out.shape, out.dtype) for out in far_out]

    def run(*refs):
        body(*refs[:given], *refs[given + len(after) :])

    return pl.pallas_call(
        run,
        out_shape=tuple(far_out) + tuple(near_out),
        in_specs=[FAR] * len(far) + [NEAR] * len(near) + [FAR] * len(after),
        out_specs=(FAR,) * len(far_out) + (NEAR,) * len(near_out),
        scratch_shapes=tuple(scratch) + ((pltpu.SemaphoreType.DMA((sems,)),) if sems else ()),
        compiler_params=pltpu.CompilerParams(vmem_limit_bytes=limit * MIB),
        name=getattr(body, "func", body).__name__,
        cost_estimate=pl.CostEstimate(flops=int(cost * 1.1e9), bytes_accessed=0, transcendentals=0),
    )(*far, *near, *after)


class Mover:
    def __init__(self, sems):
        self.sems = sems
        self.used = 0
        self.open = []

    def start(self, source, target):
        copy = pltpu.make_async_copy(source, target, self.sems.at[self.used])
        self.used += 1
        copy.start()
        return copy

    def put(self, source, target):
        self.open.append(self.start(source, target))

    def finish(self):
        for copy in self.open:
            copy.wait()


def pieces(count, size):
    return [(at, min(at + size, count)) for at in range(0, count, size)]


def lanes_of(shape):
    return lax.broadcasted_iota(jnp.int32, shape, 1)


def group_total(values):
    chans = values.shape[1]
    lane = lanes_of(values.shape)
    step = 1
    while step < chans // GROUPS:
        up = pltpu.roll(values, chans - step, 1)
        down = pltpu.roll(values, step, 1)
        values = values + jnp.where((lane & step) == 0, up, down)
        step *= 2
    return values


def pack_pair(first, second):
    half = first.shape[0] // 2
    lane = lanes_of((half, first.shape[1])) & 3
    return jnp.where(
        lane == 0,
        first[:half],
        jnp.where(lane == 1, second[:half], jnp.where(lane == 2, first[half:], second[half:])),
    )


def unpack_at(packed, place):
    lane = lanes_of(packed.shape) & 3
    top = group_total(jnp.where(lane == place, packed, 0.0))
    low = group_total(jnp.where(lane == place + 2, packed, 0.0))
    return jnp.concatenate([top, low], axis=0)


def merge_moments(gathered_ref, local_count):
    parts = gathered_ref.shape[0]
    chans = gathered_ref.shape[2]
    every = gathered_ref[...]
    total = jnp.sum(every, axis=0)
    mean = total * (1.0 / parts)
    apart = every - mean[None]
    between = jnp.sum(apart * apart, axis=0)
    square = pltpu.roll(total, chans - 1, 1) + local_count * between
    inv = lax.rsqrt(square * (1.0 / (local_count * parts)) + EPSILON)
    return unpack_at(mean, 0), unpack_at(inv, 0)


def local_moments(total, square, pilot, pixels, per):
    off = total * (1.0 / pixels)
    mean = pilot + off
    apart = square - total * off
    group_mean = group_total(mean) * (1.0 / per)
    shift = mean - group_mean
    return group_mean, group_total(apart + pixels * shift * shift)


def sigmoid(values):
    return 0.5 + 0.5 * jnp.tanh(0.5 * values)


def forward_weights(kernel_ref, pair_ref):
    chans = kernel_ref.shape[2]
    zero = jnp.zeros((chans, chans), BF16)
    for row in range(3):
        for col in range(4):
            at = (row * 4 + col) * chans
            pair_ref[at : at + chans, 0:chans] = kernel_ref[row, col] if col < 3 else zero
            pair_ref[at : at + chans, chans:] = kernel_ref[row, col - 1] if col > 0 else zero


def backward_weights(kernel_ref, pair_ref):
    chans = kernel_ref.shape[2]
    zero = jnp.zeros((chans, chans), BF16)
    for row in range(3):
        for col in range(4):
            at = (row * 4 + col) * chans
            pair_ref[0:chans, at : at + chans] = kernel_ref[2 - row, 2 - col] if col < 3 else zero
            pair_ref[chans:, at : at + chans] = kernel_ref[2 - row, 3 - col] if col > 0 else zero


def convolve(cells_ref, pair_ref, out_ref, transposed, first, last, bias=None):
    cols, rows, images, chans = out_ref.shape
    pairs = (last - first) // 2
    parts = []
    for row in range(3):
        for col in range(4):
            window = [cells_ref[first + 2 * q + col, row : row + rows] for q in range(pairs)]
            parts.append(jnp.stack(window).reshape(pairs * rows * images, chans))
    wide = jnp.concatenate(parts, axis=1)
    contract = ((1,), (1,)) if transposed else ((1,), (0,))
    made = lax.dot_general(wide, pair_ref[...], (contract, ((), ())), preferred_element_type=F32)
    for side in range(2):
        piece = made[:, side * chans : (side + 1) * chans]
        if bias is not None:
            piece = piece + bias
        piece = piece.reshape(pairs, rows, images, chans)
        for q in range(pairs):
            out_ref[first + 2 * q + side] = piece[q]


def kernel_grad(cells_ref, grads_ref, keep_ref, send_ref):
    cols, rows, images, chans = grads_ref.shape
    half = chans // 2
    first = lax.axis_index("ha") % 2 == 0
    wide = grads_ref[...].reshape(cols * rows * images, chans)
    for row in range(3):
        for col in range(3):
            window = cells_ref[col : col + cols, row : row + rows]
            made = lax.dot_general(
                window.reshape(cols * rows * images, chans),
                wide,
                (((0,), (0,)), ((), ())),
                preferred_element_type=F32,
            )
            at = (row * 3 + col) * half
            keep_ref[at : at + half, :] = jnp.where(first, made[:half], made[half:])
            send_ref[at : at + half, :] = jnp.where(first, made[half:], made[:half])


def at_edges():
    tall = lax.axis_index("ha")
    wide = lax.axis_index("wa")
    return (
        tall == 0,
        tall == lax.axis_size("ha") - 1,
        wide == 0,
        wide == lax.axis_size("wa") - 1,
    )


def clear_border(cells_ref, width, first=0, last=None):
    top, bottom, left, right = at_edges()
    cols, rows, images, chans = cells_ref.shape
    last = cols if last is None else last
    dtype = cells_ref.dtype

    @pl.when(top)
    def _():
        cells_ref[first:last, 0:width] = jnp.zeros((last - first, width, images, chans), dtype)

    @pl.when(bottom)
    def _():
        cells_ref[first:last, rows - width :] = jnp.zeros((last - first, width, images, chans), dtype)

    if first == 0:

        @pl.when(left)
        def _():
            cells_ref[0:width] = jnp.zeros((width, rows, images, chans), dtype)

    if last == cols:

        @pl.when(right)
        def _():
            cells_ref[cols - width :] = jnp.zeros((width, rows, images, chans), dtype)


def send_payload(mover, packed, pay_ref, stage_ref):
    stage_ref[...] = jnp.broadcast_to(packed[None], stage_ref.shape)
    mover.put(stage_ref, pay_ref)


def prepare_x(x_far, xt_far, down_ref, up_ref, sides_ref, moments_ref, x_ref, xt_ref, sems):
    images, rows, cols, chans = x_ref.shape
    mover = Mover(sems)
    steps = pieces(rows, 2)
    loads = [mover.start(x_far.at[:, a:b], x_ref.at[:, a:b]) for a, b in steps]
    total = jnp.zeros((images, chans), F32)
    square = total
    for (a, b), load in zip(steps, loads):
        load.wait()
        if a == 0:
            pilot = x_ref[:, 0, 0].astype(F32)
        for row in range(a, b):
            x = jnp.swapaxes(x_ref[:, row].astype(F32), 0, 1)
            xt_ref[:, row] = x.astype(BF16)
            apart = x - pilot[None]
            total = total + jnp.sum(apart, axis=0)
            square = square + jnp.sum(apart * apart, axis=0)
        mover.put(xt_ref.at[:, a:b], xt_far.at[:, a:b])
    mean, spread = local_moments(total, square, pilot, rows * cols, chans // GROUPS)
    moments_ref[...] = pack_pair(mean, spread)
    outer(xt_ref, down_ref, up_ref, sides_ref)
    mover.finish()


def outer(cells, down_ref, up_ref, sides_ref):
    cols, rows = cells.shape[0:2]
    down_ref[...] = cells[:, rows - 2 :]
    up_ref[...] = cells[:, 0:2]
    sides_ref[0:2] = cells[0:2]
    sides_ref[2:4] = cells[cols - 2 :]


def prepare_g(c_far, moments_ref, gt_far, pay_far, down_ref, up_ref, sides_ref, bias_ref, c_ref, gt_ref, stage_ref, sems):
    images, rows, cols, chans = c_ref.shape
    mover = Mover(sems)
    steps = pieces(rows, 2)
    loads = [mover.start(c_far.at[:, a:b], c_ref.at[:, a:b]) for a, b in steps]
    send_payload(mover, moments_ref[...], pay_far, stage_ref)
    bias = jnp.zeros((images, chans), F32)
    for (a, b), load in zip(steps, loads):
        load.wait()
        for row in range(a, b):
            grad = jnp.swapaxes(c_ref[:, row].astype(F32) * INV_ROOT, 0, 1).astype(BF16)
            gt_ref[:, row] = grad
            bias = bias + jnp.sum(grad.astype(F32), axis=0)
        mover.put(gt_ref.at[:, a:b], gt_far.at[:, a:b])
    bias_ref[...] = bias
    outer(gt_ref, down_ref, up_ref, sides_ref)
    mover.finish()


def edge_columns(sides_ref, top_ref, bottom_ref, *refs, passed):
    right_ref, left_ref = refs[passed : passed + 2]
    cols, rows = top_ref.shape[0], sides_ref.shape[1]
    for ref, side, at in ((left_ref, 0, 0), (right_ref, 2, cols - 2)):
        ref[:, 0:2] = top_ref[at : at + 2]
        ref[:, 2 : rows + 2] = sides_ref[side : side + 2]
        ref[:, rows + 2 :] = bottom_ref[at : at + 2]
    for source, target in zip(refs[0:passed], refs[passed + 2 : 2 * passed + 2]):
        target[...] = source[...]


def assemble(mover, own_far, own_ref, top_ref, bottom_ref, left_ref, right_ref, cells_ref, change):
    cols, rows, images, chans = own_ref.shape
    steps = pieces(cols, 8)
    loads = [mover.start(own_far.at[a:b], own_ref.at[a:b]) for a, b in steps]

    def fill():
        def halo_column(col, _):
            cells_ref[pl.ds(col + 2, 1), 0:2] = change(top_ref[pl.ds(col, 1)])
            cells_ref[pl.ds(col + 2, 1), rows + 2 :] = change(bottom_ref[pl.ds(col, 1)])
            return 0

        def column(col, _):
            cells_ref[pl.ds(col + 2, 1), 2 : rows + 2] = change(own_ref[pl.ds(col, 1)])
            return 0

        cells_ref[0:2] = change(left_ref[...])
        cells_ref[cols + 2 :] = change(right_ref[...])
        lax.fori_loop(0, cols, halo_column, 0, unroll=4)
        for (a, b), load in zip(steps, loads):
            load.wait()
            lax.fori_loop(a, b, column, 0, unroll=2)
        clear_border(cells_ref, 2)

    return fill


def first_half(
    xt_far, kernel_far, top_ref, bottom_ref, left_ref, right_ref, gathered_ref, vecs_ref,
    act_far, mid_far, pay_far, stat_ref,
    xt_ref, kernel_ref, act_ref, mid_ref, stage_ref, pair_ref, sems,
):
    cols, rows, images, chans = xt_ref.shape
    per = chans // GROUPS
    mover = Mover(sems)
    load = mover.start(kernel_far, kernel_ref)
    mean, inv = merge_moments(gathered_ref, rows * cols * per)
    stat_ref[0] = mean
    stat_ref[1] = inv
    slope = inv * vecs_ref[0:1]
    offset = vecs_ref[1:2]

    def act(cells):
        value = (cells.astype(F32) - mean) * slope + offset
        return (value * sigmoid(value)).astype(BF16)

    fill = assemble(mover, xt_far, xt_ref, top_ref, bottom_ref, left_ref, right_ref, act_ref, act)
    fill()
    load.wait()
    forward_weights(kernel_ref, pair_ref)
    mover.put(act_ref, act_far)

    pilot = None
    total = jnp.zeros((images, chans), F32)
    square = total
    wide = cols + 2
    cut = wide // 4 * 2
    for a, b in ((0, cut), (cut, wide)):
        convolve(act_ref, pair_ref, mid_ref, False, a, b, vecs_ref[2:3])
        mover.put(mid_ref.at[a:b], mid_far.at[a:b])
        if pilot is None:
            pilot = mid_ref[1, 1]

        def column(col, carry):
            total, square = carry
            apart = mid_ref[pl.ds(col, 1), 1 : rows + 1].reshape(rows, images, chans) - pilot[None]
            return total + jnp.sum(apart, axis=0), square + jnp.sum(apart * apart, axis=0)

        total, square = lax.fori_loop(max(a, 1), min(b, cols + 1), column, (total, square))
    mean, spread = local_moments(total, square, pilot, rows * cols, per)
    send_payload(mover, pack_pair(mean, spread), pay_far, stage_ref)
    mover.finish()


def back_two(
    gt_far, kernel_far, weight_far, top_ref, bottom_ref, left_ref, right_ref, ints_ref, text_ref, fbias_ref,
    out_far, film_ref,
    gt_ref, kernel_ref, weight_ref, cells_ref, out_ref, pair_ref, sems,
):
    mover = Mover(sems)
    load = mover.start(kernel_far, kernel_ref)
    fill = assemble(mover, gt_far, gt_ref, top_ref, bottom_ref, left_ref, right_ref, cells_ref, lambda cells: cells)
    late = mover.start(weight_far, weight_ref)
    load.wait()
    backward_weights(kernel_ref, pair_ref)
    fill()
    wide = out_ref.shape[0]
    cut = wide // 4 * 2
    for a, b in ((0, cut), (cut, wide)):
        convolve(cells_ref, pair_ref, out_ref, True, a, b)
        mover.put(out_ref.at[a:b], out_far.at[a:b])
    text = text_ref[...].astype(F32)
    act = jnp.concatenate([ints_ref[...], (text * sigmoid(text)).astype(BF16)], axis=1)
    late.wait()
    film_ref[...] = jnp.dot(act, weight_ref[...], preferred_element_type=F32) + fbias_ref[...].astype(F32)
    mover.finish()


def second_norm(
    mid_far, back_far, gathered_ref, vecs_ref, film_ref,
    act_far, pre_far, pay_far, sums_ref, stat_ref,
    mid_ref, back_ref, act_ref, pre_ref, stage_ref, sems,
):
    wide, tall, images, chans = mid_ref.shape
    cols, rows = wide - 2, tall - 2
    per = chans // GROUPS
    mover = Mover(sems)
    steps = pieces(wide, 9)
    loads = []
    for a, b in steps:
        loads.append(
            [mover.start(f.at[a:b], n.at[a:b]) for f, n in ((mid_far, mid_ref), (back_far, back_ref))]
        )
    mean, inv = merge_moments(gathered_ref, rows * cols * per)
    stat_ref[0] = mean
    stat_ref[1] = inv
    scale = 1.0 + film_ref[:, 0:chans]
    slope = vecs_ref[3:4] * scale
    offset = vecs_ref[4:5] * scale + film_ref[:, chans:]

    def column(col, inner):
        hat = (mid_ref[pl.ds(col, 1)].reshape(tall, images, chans) - mean) * inv
        pre = hat * slope + offset
        sigma = sigmoid(pre)
        act = pre * sigma
        act_ref[pl.ds(col, 1)] = act.astype(BF16).reshape(1, tall, images, chans)
        grad = back_ref[pl.ds(col, 1)].reshape(tall, images, chans) * (sigma + act * (1.0 - sigma))
        pre_ref[pl.ds(col, 1)] = grad.reshape(1, tall, images, chans)
        if inner is None:
            return None
        own = grad[1 : rows + 1]
        plain, cross = inner
        return plain + jnp.sum(own, axis=0), cross + jnp.sum(own * hat[1 : rows + 1], axis=0)

    zero = jnp.zeros((images, chans), F32)
    inner = (zero, zero)
    for (a, b), pair in zip(steps, loads):
        for load in pair:
            load.wait()
        if a == 0:
            column(0, None)
        inner = lax.fori_loop(max(a, 1), min(b, cols + 1), column, inner)
        if b == wide:
            column(wide - 1, None)
        clear_border(act_ref, 1, a, b)
        mover.put(act_ref.at[a:b], act_far.at[a:b])
        mover.put(pre_ref.at[a:b], pre_far.at[a:b])
    plain, cross = inner
    sums_ref[0] = plain
    sums_ref[1] = cross
    send_payload(mover, pack_pair(group_total(plain * slope), group_total(cross * slope)), pay_far, stage_ref)
    mover.finish()


def kernel_two(
    act_far, gt_far, sums_ref, bias_ref, keep_far, send_far, act_ref, gt_ref, keep_ref, send_ref, sems
):
    mover = Mover(sems)
    for load in [mover.start(act_far, act_ref), mover.start(gt_far, gt_ref)]:
        load.wait()
    kernel_grad(act_ref, gt_ref, keep_ref, send_ref)
    images, chans = bias_ref.shape
    at = 9 * (chans // 2)
    total = jnp.sum(bias_ref[...], axis=0, keepdims=True)
    for ref in (keep_ref, send_ref):
        ref[at : at + images] = sums_ref[0]
        ref[at + images : at + 2 * images] = sums_ref[1]
        ref[at + 2 * images :] = jnp.broadcast_to(total, (ref.shape[0] - at - 2 * images, chans))
    mover.put(keep_ref, keep_far)
    mover.put(send_ref, send_far)
    mover.finish()


def mix(
    act_far, kernel_far, xt_far, vecs_ref, out_far, act_ref, kernel_ref, xt_ref, branch_ref, out_ref, pair_ref, sems
):
    images, rows, cols, chans = out_ref.shape
    mover = Mover(sems)
    loads = [mover.start(f, n) for f, n in ((kernel_far, kernel_ref), (act_far, act_ref), (xt_far, xt_ref))]
    for load in loads:
        load.wait()
    forward_weights(kernel_ref, pair_ref)
    convolve(act_ref, pair_ref, branch_ref, False, 0, cols, vecs_ref[5:6])
    for a, b in pieces(rows, 4):
        for row in range(a, b):
            mixed = jnp.swapaxes((xt_ref[:, row].astype(F32) + branch_ref[:, row]) * INV_ROOT, 0, 1)
            out_ref[:, row] = mixed.astype(BF16)
        mover.put(out_ref.at[:, a:b], out_far.at[:, a:b])
    mover.finish()


def middle_back(
    mid_far, pre_far, act_far, xt_far, kernel_far, gathered_ref, stat_two_ref, stat_one_ref, vecs_ref, film_ref,
    keep_far, send_far, grad_far,
    mid_ref, pre_ref, act_ref, xt_ref, kernel_ref, low_ref, keep_ref, send_ref, out_ref, pair_ref, sems,
):
    wide, tall, images, chans = mid_ref.shape
    cols, rows = wide - 2, tall - 2
    mover = Mover(sems)
    steps = pieces(wide, 9)
    loads = []
    for a, b in steps:
        loads.append([mover.start(f.at[a:b], n.at[a:b]) for f, n in ((mid_far, mid_ref), (pre_far, pre_ref))])
    late = [mover.start(f, n) for f, n in ((act_far, act_ref), (kernel_far, kernel_ref), (xt_far, xt_ref))]
    count = lax.axis_size("ha") * lax.axis_size("wa") * rows * cols * (chans // GROUPS)
    packed = jnp.sum(gathered_ref[...], axis=0) * (1.0 / count)
    plain = unpack_at(packed, 0)
    cross = unpack_at(packed, 1)
    mean = stat_two_ref[0]
    inv = stat_two_ref[1]
    slope = vecs_ref[3:4] * (1.0 + film_ref[:, 0:chans])

    def low_column(col, total):
        hat = (mid_ref[pl.ds(col, 1)].reshape(tall, images, chans) - mean) * inv
        grad = pre_ref[pl.ds(col, 1)].reshape(tall, images, chans) * slope
        low = (inv * (grad - plain - hat * cross)).astype(BF16)
        low_ref[pl.ds(col, 1)] = low.reshape(1, tall, images, chans)
        if total is None:
            return None
        return total + jnp.sum(low[1 : rows + 1].astype(F32), axis=0)

    kbias = jnp.zeros((images, chans), F32)
    for (a, b), pair in zip(steps, loads):
        for load in pair:
            load.wait()
        if a == 0:
            low_column(0, None)
        kbias = lax.fori_loop(max(a, 1), min(b, cols + 1), low_column, kbias)
        if b == wide:
            low_column(wide - 1, None)
    clear_border(low_ref, 1)
    for load in late:
        load.wait()
    own = low_ref.at[1 : wide - 1, 1 : tall - 1]
    kernel_grad(act_ref.at[1 : wide + 1, 1 : tall + 1], own, keep_ref, send_ref)
    backward_weights(kernel_ref, pair_ref)
    convolve(low_ref, pair_ref, out_ref, True, 0, cols)
    mean_one = stat_one_ref[0]
    inv_one = stat_one_ref[1]
    gain = vecs_ref[0:1]
    bias = vecs_ref[1:2]

    def column(col, carry):
        plain, cross = carry
        hat = (xt_ref[pl.ds(col, 1)].reshape(rows, images, chans).astype(F32) - mean_one) * inv_one
        norm = hat * gain + bias
        sigma = sigmoid(norm)
        grad = out_ref[pl.ds(col, 1)].reshape(rows, images, chans)
        grad = grad * (sigma * (1.0 + norm * (1.0 - sigma)))
        out_ref[pl.ds(col, 1)] = grad.reshape(1, rows, images, chans)
        return plain + jnp.sum(grad, axis=0), cross + jnp.sum(grad * hat, axis=0)

    zero = jnp.zeros((images, chans), F32)
    inner = (zero, zero)
    for a, b in pieces(cols, 8):
        inner = lax.fori_loop(a, b, column, inner)
        mover.put(out_ref.at[a:b], grad_far.at[a:b])
    plain_one, cross_one = inner
    rest = [jnp.sum(v, axis=0, keepdims=True) for v in (cross_one, plain_one, kbias)]
    rest = jnp.concatenate(rest + [jnp.zeros((5, chans), F32)], axis=0)
    packed = pack_pair(group_total(plain_one * gain), group_total(cross_one * gain))
    at = 9 * (chans // 2)
    half = images // 2
    for ref, far in ((keep_ref, keep_far), (send_ref, send_far)):
        ref[at : at + 8] = rest
        ref[at + 8 : at + 8 + half] = packed
        mover.put(ref, far)
    mover.finish()


def pack_terms(
    keep_one_far, keep_two_far, came_one_ref, came_two_ref, out_far, token_ref,
    one_ref, two_ref, out_ref, sems, extras_one, extras_two, whole,
):
    chips, rows, chans = out_ref.shape
    mover = Mover(sems)
    loads = [mover.start(keep_two_far, two_ref), mover.start(keep_one_far, one_ref)]
    taps = 9 * (chans // 2)
    share = -(-taps // chips)
    start = 2 * share
    for load, at, ref, came_ref, extras in (
        (loads[0], share, two_ref, came_two_ref, extras_two),
        (loads[1], 0, one_ref, came_one_ref, extras_one),
    ):
        load.wait()
        ref[...] = ref[...] + came_ref[...]
        more = -(-extras // chips)
        for chip in range(chips):
            a, b = chip * share, min((chip + 1) * share, taps)
            if a < b:
                out_ref[chip, at : at + b - a] = ref[a:b]
            a, b = chip * more, min((chip + 1) * more, extras)
            if a < b:
                out_ref[chip, start : start + b - a] = ref[taps + a : taps + b]
        start += more
    kept = one_ref[one_ref.shape[0] - whole :]
    token_ref[...] = kept
    out_ref[:, rows - whole :] = jnp.broadcast_to(kept[None], (chips, whole, chans))
    mover.put(out_ref, out_far)
    mover.finish()


def add_terms(gathered_ref, out_far, small_ref, out_ref, sems, extras_one, extras_two):
    chips, rows, chans = gathered_ref.shape
    mover = Mover(sems)
    share = -(-9 * (chans // 2) // chips)
    whole = small_ref.shape[0]
    more = -(-extras_one // chips) - (-extras_two // chips)
    total = jnp.sum(gathered_ref[...], axis=0)
    small_ref[...] = total[rows - whole :]
    extra = total[2 * share : 2 * share + more]
    high = extra.astype(BF16).astype(F32)
    both = jnp.concatenate([total[0 : 2 * share], high, extra - high], axis=0)
    short = out_ref.shape[1] - both.shape[0]
    if short:
        both = jnp.concatenate([both, jnp.zeros((short, chans), F32)], axis=0)
    out_ref[...] = jnp.broadcast_to(both.astype(BF16)[None], out_ref.shape)
    mover.put(out_ref, out_far)
    mover.finish()


def three_terms(values):
    high = values.astype(BF16)
    rest = values - high.astype(F32)
    mid = rest.astype(BF16)
    low = (rest - mid.astype(F32)).astype(BF16)
    return jnp.concatenate([high, mid, low], axis=0)


def last_grads(
    weight_far, own_ref, other_ref, film_ref, vecs_ref, ints_ref, text_ref,
    one_far, two_far, weight_grad_far, text_grad_far, vec_ref, bias_ref,
    weight_ref, one_ref, two_ref, weight_grad_ref, text_grad_ref, half_ref, extra_ref, sems,
    extras_one, extras_two,
):
    chips, rows, chans = own_ref.shape
    images = film_ref.shape[0]
    mover = Mover(sems)
    load = mover.start(weight_far, weight_ref)
    half = chans // 2
    taps = 9 * half
    share = -(-taps // chips)
    more_two = -(-extras_two // chips)
    more_one = -(-extras_one // chips)
    more = more_two + more_one
    for chip in range(chips):
        piece = own_ref[chip].astype(F32)
        piece = piece[2 * share : 2 * share + more] + piece[2 * share + more : 2 * share + 2 * more]
        extra_ref[chip * more_two : (chip + 1) * more_two] = piece[0:more_two]
        if chip < extras_one:
            at = chips * more_two + chip * more_one
            extra_ref[at : at + more_one] = piece[more_two:]
    plain = extra_ref[0:images]
    cross = extra_ref[images : 2 * images]
    scale = 1.0 + film_ref[:, 0:chans]
    scale_grad = vecs_ref[3:4] * cross + vecs_ref[4:5] * plain
    film_grad = jnp.concatenate([scale_grad, plain], axis=1)
    bias_ref[...] = jnp.sum(film_grad, axis=0, keepdims=True)
    vec_ref[0:1] = jnp.sum(scale * cross, axis=0, keepdims=True)
    vec_ref[1:2] = jnp.sum(scale * plain, axis=0, keepdims=True)
    vec_ref[2:3] = extra_ref[2 * images : 2 * images + 1]
    at = chips * more_two
    vec_ref[3:6] = extra_ref[at : at + 3]
    vec_ref[6:8] = jnp.zeros((2, chans), F32)
    terms = three_terms(film_grad)
    ints = ints_ref.shape[1]
    depth = weight_grad_ref.shape[0]
    load.wait()
    for start in range(0, depth, 512):
        stop = start + 512
        if start < ints:
            act = ints_ref[:, start:stop]
        else:
            embed = text_ref[:, start - ints : stop - ints].astype(F32)
            sigma = sigmoid(embed)
            act = (embed * sigma).astype(BF16)
        weight_grad_ref[start:stop] = lax.dot_general(
            jnp.concatenate([act, act, act], axis=0), terms, (((0,), (0,)), ((), ())), preferred_element_type=F32
        )
        mover.put(weight_grad_ref.at[start:stop], weight_grad_far.at[start:stop])
        if start >= ints:
            made = lax.dot_general(
                terms, weight_ref[start:stop], (((1,), (1,)), ((), ())), preferred_element_type=F32
            )
            cond_grad = made[0:images] + made[images : 2 * images] + made[2 * images :]
            slope = sigma * (1.0 + embed * (1.0 - sigma))
            text_grad_ref[:, start - ints : stop - ints] = cond_grad * slope
    mover.put(text_grad_ref, text_grad_far)
    core = lax.axis_index("ha") % 2
    for source, place in ((own_ref, core), (other_ref, 1 - core)):
        for at, out_ref in enumerate((one_ref, two_ref)):
            for chip in range(chips):
                piece = source[chip].astype(F32)[at * share : (at + 1) * share]
                half_ref[chip * share : (chip + 1) * share] = piece
            for tap in range(9):
                rows_at = pl.ds(pl.multiple_of(place * half, half), half)
                out_ref[tap, rows_at] = half_ref[tap * half : (tap + 1) * half]
    mover.put(one_ref, one_far)
    mover.put(two_ref, two_far)
    mover.finish()


def finish(
    grad_far, xt_far, c_far, small_ref, stat_ref, vecs_ref, out_far, grad_ref, xt_ref, c_ref, out_ref, sems
):
    images, rows, cols, chans = out_ref.shape
    mover = Mover(sems)
    steps = pieces(rows, 2)
    loads = []
    for a, b in steps:
        both = [mover.start(f.at[:, a:b], n.at[:, a:b]) for f, n in ((grad_far, grad_ref), (xt_far, xt_ref))]
        loads.append(both + [mover.start(c_far.at[:, a:b], c_ref.at[:, a:b])])
    count = lax.axis_size("ha") * lax.axis_size("wa") * rows * cols * (chans // GROUPS)
    packed = small_ref[...] * (1.0 / count)
    plain = unpack_at(packed, 0)
    cross = unpack_at(packed, 1)
    mean = stat_ref[0]
    inv = stat_ref[1]
    gain = vecs_ref[0:1]
    for (a, b), group in zip(steps, loads):
        for load in group:
            load.wait()
        for row in range(a, b):
            hat = (xt_ref[:, row].astype(F32) - mean) * inv
            path = jnp.swapaxes(inv * (grad_ref[:, row] * gain - plain - hat * cross), 0, 1)
            out_ref[:, row] = (c_ref[:, row].astype(F32) * INV_ROOT + path).astype(BF16)
        mover.put(out_ref.at[:, a:b], out_far.at[:, a:b])
    mover.finish()


def to_all(payload):
    return lax.all_to_all(payload, AXES, 0, 0)


def to_chips(payload):
    tall, wide = lax.axis_size("ha"), lax.axis_size("wa")
    groups = [[h * wide + w for h in range(core, tall, 2) for w in range(wide)] for core in range(2)]
    return lax.all_to_all(payload, AXES, 0, 0, axis_index_groups=groups)


def to_sibling(payload):
    return lax.ppermute(payload, "ha", [(i, i ^ 1) for i in range(lax.axis_size("ha"))])


def shifted(cells, axis, step):
    count = lax.axis_size(axis)
    return lax.ppermute(cells, axis, [(i, (i + step) % count) for i in range(count)])


def halo(sides, down, up, after=(), passed=()):
    four, rows, images, chans = sides.shape
    top = shifted(down, "ha", 1)
    bottom = shifted(up, "ha", -1)
    edge = shaped((2, rows + 4, images, chans), sides.dtype)
    right, left, *rest = kernel_call(
        functools.partial(edge_columns, passed=len(passed)), (), (sides, top, bottom, *passed),
        (), (edge, edge) + tuple(shaped(p.shape, p.dtype) for p in passed), cost=0.4, after=after, limit=16,
    )
    return (top, bottom, shifted(right, "wa", 1), shifted(left, "wa", -1)), rest or right


def sinusoids(first, second):
    half = TEMB // 2
    freqs = jnp.exp(-math.log(10000.0) * jnp.arange(half, dtype=F32) / half)
    times = jnp.stack([first, second], axis=1).astype(F32)
    angles = times[:, :, None, None] * freqs[None, None, None, :]
    which = lax.broadcasted_iota(jnp.int32, (first.shape[0], 2, 2, half), 2)
    made = jnp.where(which == 0, jnp.sin(angles), jnp.cos(angles))
    return made.reshape(first.shape[0], 2 * TEMB)


def buffers(*arrays):
    return tuple(pltpu.VMEM(a.shape, a.dtype) for a in arrays)


def local(
    block_input,
    timesteps,
    aug_levels,
    text_pooled,
    gain_one,
    bias_one,
    conv_one,
    conv_one_bias,
    gain_two,
    bias_two,
    film_weight,
    film_bias,
    conv_two,
    conv_two_bias,
    cotangent,
):
    images, rows, cols, chans = block_input.shape
    parts = lax.axis_size("ha") * lax.axis_size("wa")
    chips = parts // 2
    half = images // 2
    vecs = (gain_one, bias_one, conv_one_bias, gain_two, bias_two, conv_two_bias, gain_one, gain_one)
    vecs = jnp.stack(vecs).astype(F32)
    payload = shaped((parts, half, chans), F32)
    per_image = shaped((images, chans), F32)
    two_images = shaped((2, images, chans), F32)
    block = shaped((cols, rows, images, chans), BF16)
    block_wide = shaped((cols, rows, images, chans), F32)
    rim = shaped((cols + 2, rows + 2, images, chans), BF16)
    rim_wide = shaped((cols + 2, rows + 2, images, chans), F32)
    far_rim = shaped((cols + 4, rows + 4, images, chans), BF16)
    row_halo = shaped((cols, 2, images, chans), BF16)
    given = shaped((images, rows, cols, chans), BF16)
    pair = pltpu.VMEM((12 * chans, 2 * chans), BF16)
    pair_back = pltpu.VMEM((2 * chans, 12 * chans), BF16)

    sides = shaped((4, rows, images, chans), BF16)
    xt, x_down, x_up, x_sides, moments = kernel_call(
        prepare_x, (block_input,), (), (block,), (row_halo, row_halo, sides, shaped((half, chans), F32)),
        scratch=buffers(given, block), sems=16, cost=2.3,
    )
    gt, pay_one, g_down, g_up, g_sides, kbias_two_local = kernel_call(
        prepare_g, (cotangent,), (moments,), (block, payload), (row_halo, row_halo, sides, per_image),
        scratch=buffers(given, block, payload), sems=16, cost=2.0,
    )
    moments_one = to_all(pay_one)
    x_halo, (g_down, g_up) = halo(x_sides, x_down, x_up, passed=(g_down, g_up))

    embed_ints = sinusoids(timesteps, aug_levels)
    act_ints = jax.nn.silu(embed_ints).astype(BF16)
    g_halo, g_edge = halo(g_sides, g_down, g_up)
    act_one, mid, pay_two, stat_one = kernel_call(
        first_half, (xt, conv_one), (*x_halo, moments_one, vecs), (far_rim, rim_wide, payload), (two_images,),
        scratch=buffers(xt, conv_one, far_rim, rim_wide, payload) + (pair,), sems=16, cost=5.5, after=(g_edge,),
    )
    moments_two = to_all(pay_two)
    act_two_grad, film = kernel_call(
        back_two,
        (gt, conv_two, film_weight),
        (*g_halo, act_ints, text_pooled, film_bias.reshape(1, 2 * chans)),
        (rim_wide,),
        (shaped((images, 2 * chans), F32),),
        scratch=buffers(gt, conv_two, film_weight, far_rim, rim_wide) + (pair_back,), sems=16, cost=5.0,
    )
    act_two, pre_two_grad, pay_three, sums_two, stat_two = kernel_call(
        second_norm, (mid, act_two_grad), (moments_two, vecs, film), (rim, rim_wide, payload), (two_images, two_images),
        scratch=buffers(rim_wide, rim_wide, rim, rim_wide, payload), sems=24, cost=3.2,
    )
    moments_three = to_all(pay_three)

    taps = 9 * (chans // 2)
    share = -(-taps // chips)
    extras_two = 2 * images + 1
    extras_one = 3
    halves_two = shaped((taps + 2 * images + 8, chans), F32)
    halves_one = shaped((taps + 8 + half, chans), F32)
    keep_two, send_two = kernel_call(
        kernel_two, (act_two, gt), (sums_two, kbias_two_local), (halves_two, halves_two),
        scratch=buffers(act_two, gt, halves_two, halves_two), sems=4, cost=3.0,
    )
    came_two = to_sibling(send_two)
    terms_shape = shaped((chips, -(-(share - (-extras_two // chips)) // 8) * 8, chans), F32)
    keep_one, send_one, norm_one_grad = kernel_call(
        middle_back,
        (mid, pre_two_grad, act_one, xt, conv_one),
        (moments_three, stat_two, stat_one, vecs, film),
        (halves_one, halves_one, block_wide),
        scratch=buffers(mid, pre_two_grad, act_one, xt, conv_one, rim, halves_one, halves_one, block_wide)
        + (pair_back,),
        sems=24, cost=8.0, after=(keep_two,),
    )
    came_one = to_sibling(send_one)
    more = -(-extras_one // chips) - (-extras_two // chips)
    terms_shape = shaped((chips, -(-(2 * share + more) // 8) * 8 + half, chans), F32)
    terms, packed = kernel_call(
        functools.partial(pack_terms, extras_one=extras_one, extras_two=extras_two, whole=half),
        (keep_one, keep_two), (came_one, came_two), (terms_shape,), (shaped((half, chans), F32),),
        scratch=buffers(halves_one, halves_two, terms_shape), sems=3, cost=1.0,
    )
    gathered = to_chips(terms)
    (mixed,) = kernel_call(
        mix, (act_two, conv_two, xt), (vecs,), (given,),
        scratch=buffers(act_two, conv_two, xt, block_wide, given) + (pair,), sems=8, cost=3.6,
        after=(to_sibling(packed),),
    )
    shares_shape = shaped((chips, -(-(2 * share + 2 * more) // 16) * 16, chans), BF16)
    shares, small = kernel_call(
        functools.partial(add_terms, extras_one=extras_one, extras_two=extras_two),
        (), (gathered,), (shares_shape,), (shaped((half, chans), F32),),
        scratch=buffers(shares_shape), sems=1, cost=1.0, after=(mixed,),
    )
    own_half = to_chips(shares)
    (input_grad,) = kernel_call(
        finish, (norm_one_grad, xt, cotangent), (to_sibling(small), stat_one, vecs), (given,),
        scratch=buffers(norm_one_grad, xt, cotangent, given), sems=16, cost=3.3,
    )
    own_half, _ = lax.optimization_barrier((own_half, input_grad))
    other_half = to_sibling(own_half)
    full = shaped((9, chans, chans), F32)
    weight_grad = shaped(film_weight.shape, F32)
    text_shape = shaped(text_pooled.shape, F32)
    kernel_one_grad, kernel_two_grad, film_weight_grad, text_grad, vec_grads, film_bias_grad = kernel_call(
        functools.partial(last_grads, extras_one=extras_one, extras_two=extras_two),
        (film_weight,),
        (own_half, other_half, film, vecs, act_ints, text_pooled),
        (full, full, weight_grad, text_shape),
        (shaped((8, chans), F32), shaped((1, 2 * chans), F32)),
        scratch=buffers(film_weight, full, full, weight_grad, text_shape)
        + (
            pltpu.VMEM((chips * share, chans), F32),
            pltpu.VMEM((chips * (-(-extras_two // chips)) + 8, chans), F32),
        ),
        sems=24, cost=4.0, after=(input_grad,),
    )
    return (
        mixed,
        input_grad,
        text_grad,
        vec_grads[3],
        vec_grads[4],
        kernel_one_grad.reshape(3, 3, chans, chans),
        vec_grads[5],
        vec_grads[0],
        vec_grads[1],
        film_weight_grad,
        film_bias_grad.reshape(2 * chans),
        kernel_two_grad.reshape(3, 3, chans, chans),
        vec_grads[2],
    )


def solution(mesh):
    split = P(None, "ha", "wa", None)
    return jax.shard_map(
        local,
        mesh=mesh,
        in_specs=(split,) + (P(),) * 13 + (split,),
        out_specs=(split, split) + (P(),) * 11,
        check_vma=False,
    )
```

```python
import functools
import math

import jax
import jax.numpy as jnp
from jax import lax
from jax.experimental import pallas as pl
from jax.experimental.pallas import tpu as pltpu
from jax.sharding import PartitionSpec as P

GROUPS = 32
TEMB = 256
EPSILON = 1e-05
INV_ROOT = 1.0 / math.sqrt(2.0)
AXES = ("ha", "wa")
F32 = jnp.float32
BF16 = jnp.bfloat16
NEAR = pl.BlockSpec(memory_space=pltpu.VMEM)
FAR = pl.BlockSpec(memory_space=pl.ANY)
MIB = 1 << 20


def shaped(shape, dtype):
    return jax.ShapeDtypeStruct(shape, dtype)


def kernel_call(body, far, near, far_out, near_out=(), scratch=(), sems=0, cost=1.0, after=(), after_near=(), limit=48):
    given = len(far) + len(near)
    far = [pltpu.with_memory_space_constraint(array, pltpu.HBM) for array in far]
    after = [pltpu.with_memory_space_constraint(array, pltpu.HBM) for array in after] + list(after_near)
    far_out = [pltpu.HBM(out.shape, out.dtype) for out in far_out]

    def run(*refs):
        body(*refs[:given], *refs[given + len(after) :])

    return pl.pallas_call(
        run,
        out_shape=tuple(far_out) + tuple(near_out),
        in_specs=[FAR] * len(far) + [NEAR] * len(near) + [FAR] * len(after),
        out_specs=(FAR,) * len(far_out) + (NEAR,) * len(near_out),
        scratch_shapes=tuple(scratch) + ((pltpu.SemaphoreType.DMA((sems,)),) if sems else ()),
        compiler_params=pltpu.CompilerParams(vmem_limit_bytes=limit * MIB),
        name=getattr(body, "func", body).__name__,
        cost_estimate=pl.CostEstimate(flops=int(cost * 1.1e9), bytes_accessed=0, transcendentals=0),
    )(*far, *near, *after)


class Mover:
    def __init__(self, sems):
        self.sems = sems
        self.used = 0
        self.open = []

    def start(self, source, target):
        copy = pltpu.make_async_copy(source, target, self.sems.at[self.used])
        self.used += 1
        copy.start()
        return copy

    def put(self, source, target):
        self.open.append(self.start(source, target))

    def finish(self):
        for copy in self.open:
            copy.wait()


def pieces(count, size):
    return [(at, min(at + size, count)) for at in range(0, count, size)]


def lanes_of(shape):
    return lax.broadcasted_iota(jnp.int32, shape, 1)


def group_total(values):
    chans = values.shape[1]
    lane = lanes_of(values.shape)
    step = 1
    while step < chans // GROUPS:
        up = pltpu.roll(values, chans - step, 1)
        down = pltpu.roll(values, step, 1)
        values = values + jnp.where((lane & step) == 0, up, down)
        step *= 2
    return values


def pack_pair(first, second):
    half = first.shape[0] // 2
    lane = lanes_of((half, first.shape[1])) & 3
    return jnp.where(
        lane == 0,
        first[:half],
        jnp.where(lane == 1, second[:half], jnp.where(lane == 2, first[half:], second[half:])),
    )


def unpack_at(packed, place):
    lane = lanes_of(packed.shape) & 3
    top = group_total(jnp.where(lane == place, packed, 0.0))
    low = group_total(jnp.where(lane == place + 2, packed, 0.0))
    return jnp.concatenate([top, low], axis=0)


def merge_moments(gathered_ref, local_count):
    parts = gathered_ref.shape[0]
    chans = gathered_ref.shape[2]
    every = gathered_ref[...]
    total = jnp.sum(every, axis=0)
    mean = total * (1.0 / parts)
    apart = every - mean[None]
    between = jnp.sum(apart * apart, axis=0)
    square = pltpu.roll(total, chans - 1, 1) + local_count * between
    inv = lax.rsqrt(square * (1.0 / (local_count * parts)) + EPSILON)
    return unpack_at(mean, 0), unpack_at(inv, 0)


def local_moments(total, square, pilot, pixels, per):
    off = total * (1.0 / pixels)
    mean = pilot + off
    apart = square - total * off
    group_mean = group_total(mean) * (1.0 / per)
    shift = mean - group_mean
    return group_mean, group_total(apart + pixels * shift * shift)


def sigmoid(values):
    return 0.5 + 0.5 * jnp.tanh(0.5 * values)


def forward_weights(kernel_ref, pair_ref):
    chans = kernel_ref.shape[2]
    zero = jnp.zeros((chans, chans), BF16)
    for row in range(3):
        for col in range(4):
            at = (row * 4 + col) * chans
            pair_ref[at : at + chans, 0:chans] = kernel_ref[row, col] if col < 3 else zero
            pair_ref[at : at + chans, chans:] = kernel_ref[row, col - 1] if col > 0 else zero


def backward_weights(kernel_ref, pair_ref):
    chans = kernel_ref.shape[2]
    zero = jnp.zeros((chans, chans), BF16)
    for row in range(3):
        for col in range(4):
            at = (row * 4 + col) * chans
            pair_ref[0:chans, at : at + chans] = kernel_ref[2 - row, 2 - col] if col < 3 else zero
            pair_ref[chans:, at : at + chans] = kernel_ref[2 - row, 3 - col] if col > 0 else zero


def convolve(cells_ref, pair_ref, out_ref, transposed, first, last, bias=None):
    cols, rows, images, chans = out_ref.shape
    pairs = (last - first) // 2
    parts = []
    for row in range(3):
        for col in range(4):
            window = [cells_ref[first + 2 * q + col, row : row + rows] for q in range(pairs)]
            parts.append(jnp.stack(window).reshape(pairs * rows * images, chans))
    wide = jnp.concatenate(parts, axis=1)
    contract = ((1,), (1,)) if transposed else ((1,), (0,))
    made = lax.dot_general(wide, pair_ref[...], (contract, ((), ())), preferred_element_type=F32)
    for side in range(2):
        piece = made[:, side * chans : (side + 1) * chans]
        if bias is not None:
            piece = piece + bias
        piece = piece.reshape(pairs, rows, images, chans)
        for q in range(pairs):
            out_ref[first + 2 * q + side] = piece[q]


def kernel_grad(cells_ref, grads_ref, keep_ref, send_ref):
    cols, rows, images, chans = grads_ref.shape
    half = chans // 2
    first = lax.axis_index("ha") % 2 == 0
    pixels = cols * rows * images
    windows = [
        cells_ref[col : col + cols, row : row + rows].reshape(pixels, chans) for row in range(3) for col in range(3)
    ]
    every = lax.dot_general(
        grads_ref[...].reshape(pixels, chans),
        jnp.concatenate(windows, axis=1),
        (((0,), (0,)), ((), ())),
        preferred_element_type=F32,
    )
    for tap in range(9):
        made = every[:, tap * chans : (tap + 1) * chans].T
        at = tap * half
        keep_ref[at : at + half, :] = jnp.where(first, made[:half], made[half:])
        send_ref[at : at + half, :] = jnp.where(first, made[half:], made[:half])


def at_edges():
    tall = lax.axis_index("ha")
    wide = lax.axis_index("wa")
    return (
        tall == 0,
        tall == lax.axis_size("ha") - 1,
        wide == 0,
        wide == lax.axis_size("wa") - 1,
    )


def clear_border(cells_ref, width, first=0, last=None):
    top, bottom, left, right = at_edges()
    cols, rows, images, chans = cells_ref.shape
    last = cols if last is None else last
    dtype = cells_ref.dtype

    @pl.when(top)
    def _():
        cells_ref[first:last, 0:width] = jnp.zeros((last - first, width, images, chans), dtype)

    @pl.when(bottom)
    def _():
        cells_ref[first:last, rows - width :] = jnp.zeros((last - first, width, images, chans), dtype)

    if first == 0:

        @pl.when(left)
        def _():
            cells_ref[0:width] = jnp.zeros((width, rows, images, chans), dtype)

    if last == cols:

        @pl.when(right)
        def _():
            cells_ref[cols - width :] = jnp.zeros((width, rows, images, chans), dtype)


def send_payload(mover, packed, pay_ref, stage_ref):
    stage_ref[...] = jnp.broadcast_to(packed[None], stage_ref.shape)
    mover.put(stage_ref, pay_ref)


def prepare_x(x_far, xt_far, down_ref, up_ref, sides_ref, moments_ref, x_ref, xt_ref, sems):
    images, rows, cols, chans = x_ref.shape
    mover = Mover(sems)
    steps = pieces(rows, 2)
    loads = [mover.start(x_far.at[:, a:b], x_ref.at[:, a:b]) for a, b in steps]
    total = jnp.zeros((images, chans), F32)
    square = total
    for (a, b), load in zip(steps, loads):
        load.wait()
        if a == 0:
            pilot = x_ref[:, 0, 0].astype(F32)
        for row in range(a, b):
            x = jnp.swapaxes(x_ref[:, row].astype(F32), 0, 1)
            xt_ref[:, row] = x.astype(BF16)
            apart = x - pilot[None]
            total = total + jnp.sum(apart, axis=0)
            square = square + jnp.sum(apart * apart, axis=0)
        mover.put(xt_ref.at[:, a:b], xt_far.at[:, a:b])
    mean, spread = local_moments(total, square, pilot, rows * cols, chans // GROUPS)
    moments_ref[...] = pack_pair(mean, spread)
    outer(xt_ref, down_ref, up_ref, sides_ref)
    mover.finish()


def outer(cells, down_ref, up_ref, sides_ref):
    cols, rows = cells.shape[0:2]
    down_ref[...] = cells[:, rows - 2 :]
    up_ref[...] = cells[:, 0:2]
    sides_ref[0:2] = cells[0:2]
    sides_ref[2:4] = cells[cols - 2 :]


def prepare_g(c_far, gt_far, down_ref, up_ref, sides_ref, bias_ref, c_ref, gt_ref, sems):
    images, rows, cols, chans = c_ref.shape
    mover = Mover(sems)
    steps = pieces(rows, 2)
    loads = [mover.start(c_far.at[:, a:b], c_ref.at[:, a:b]) for a, b in steps]
    bias = jnp.zeros((images, chans), F32)
    for (a, b), load in zip(steps, loads):
        load.wait()
        for row in range(a, b):
            grad = jnp.swapaxes(c_ref[:, row].astype(F32) * INV_ROOT, 0, 1).astype(BF16)
            gt_ref[:, row] = grad
            bias = bias + jnp.sum(grad.astype(F32), axis=0)
        mover.put(gt_ref.at[:, a:b], gt_far.at[:, a:b])
    bias_ref[...] = bias
    outer(gt_ref, down_ref, up_ref, sides_ref)
    mover.finish()


def write_payload(packed_ref, pay_far, stage_ref, sems):
    mover = Mover(sems)
    send_payload(mover, packed_ref[...], pay_far, stage_ref)
    mover.finish()


def edge_columns(sides_ref, top_ref, bottom_ref, right_ref, left_ref):
    cols, rows = top_ref.shape[0], sides_ref.shape[1]
    for ref, side, col in ((left_ref, 0, 0), (right_ref, 2, cols - 2)):
        ref[:, 0:2] = top_ref[col : col + 2]
        ref[:, 2 : rows + 2] = sides_ref[side : side + 2]
        ref[:, rows + 2 :] = bottom_ref[col : col + 2]


def assemble(mover, own_far, own_ref, top_ref, bottom_ref, left_ref, right_ref, cells_ref, change):
    cols, rows, images, chans = own_ref.shape
    steps = pieces(cols, 8)
    loads = [mover.start(own_far.at[a:b], own_ref.at[a:b]) for a, b in steps]

    def fill():
        def halo_column(col, _):
            cells_ref[pl.ds(col + 2, 1), 0:2] = change(top_ref[pl.ds(col, 1)])
            cells_ref[pl.ds(col + 2, 1), rows + 2 :] = change(bottom_ref[pl.ds(col, 1)])
            return 0

        def column(col, _):
            cells_ref[pl.ds(col + 2, 1), 2 : rows + 2] = change(own_ref[pl.ds(col, 1)])
            return 0

        cells_ref[0:2] = change(left_ref[...])
        cells_ref[cols + 2 :] = change(right_ref[...])
        lax.fori_loop(0, cols, halo_column, 0, unroll=4)
        for (a, b), load in zip(steps, loads):
            load.wait()
            lax.fori_loop(a, b, column, 0, unroll=2)
        clear_border(cells_ref, 2)

    return fill


def first_half(
    xt_far, kernel_far, top_ref, bottom_ref, left_ref, right_ref, gathered_ref, vecs_ref,
    act_far, mid_far, pay_far, stat_ref,
    xt_ref, kernel_ref, act_ref, mid_ref, stage_ref, pair_ref, sems,
):
    cols, rows, images, chans = xt_ref.shape
    per = chans // GROUPS
    mover = Mover(sems)
    load = mover.start(kernel_far, kernel_ref)
    mean, inv = merge_moments(gathered_ref, rows * cols * per)
    stat_ref[0] = mean
    stat_ref[1] = inv
    slope = 0.5 * inv * vecs_ref[0:1]
    offset = 0.5 * vecs_ref[1:2]

    def act(cells):
        value = (cells.astype(F32) - mean) * slope + offset
        return (value + value * jnp.tanh(value)).astype(BF16)

    fill = assemble(mover, xt_far, xt_ref, top_ref, bottom_ref, left_ref, right_ref, act_ref, act)
    fill()
    load.wait()
    forward_weights(kernel_ref, pair_ref)
    mover.put(act_ref, act_far)

    pilot = None
    total = jnp.zeros((images, chans), F32)
    square = total
    wide = cols + 2
    for a, b in pieces(wide, 10):
        convolve(act_ref, pair_ref, mid_ref, False, a, b, vecs_ref[2:3])
        mover.put(mid_ref.at[a:b], mid_far.at[a:b])
        if pilot is None:
            pilot = mid_ref[1, 1]

        def column(col, carry):
            total, square = carry
            apart = mid_ref[pl.ds(col, 1), 1 : rows + 1].reshape(rows, images, chans) - pilot[None]
            return total + jnp.sum(apart, axis=0), square + jnp.sum(apart * apart, axis=0)

        total, square = lax.fori_loop(max(a, 1), min(b, cols + 1), column, (total, square))
    mean, spread = local_moments(total, square, pilot, rows * cols, per)
    send_payload(mover, pack_pair(mean, spread), pay_far, stage_ref)
    mover.finish()


def back_two(
    gt_far, kernel_far, weight_far, top_ref, bottom_ref, left_ref, right_ref, ints_ref, text_ref, fbias_ref,
    out_far, film_ref,
    gt_ref, kernel_ref, weight_ref, cells_ref, out_ref, pair_ref, sems,
):
    mover = Mover(sems)
    load = mover.start(kernel_far, kernel_ref)
    fill = assemble(
        mover, gt_far, gt_ref, top_ref, bottom_ref, left_ref, right_ref, cells_ref, lambda cells: cells
    )
    late = mover.start(weight_far, weight_ref)
    load.wait()
    backward_weights(kernel_ref, pair_ref)
    fill()
    wide = out_ref.shape[0]
    for a, b in pieces(wide, 10):
        convolve(cells_ref, pair_ref, out_ref, True, a, b)
        mover.put(out_ref.at[a:b], out_far.at[a:b])
    text = text_ref[...].astype(F32)
    act = jnp.concatenate([ints_ref[...], (text * sigmoid(text)).astype(BF16)], axis=1)
    late.wait()
    film_ref[...] = jnp.dot(act, weight_ref[...], preferred_element_type=F32) + fbias_ref[...].astype(F32)
    mover.finish()


def second_norm(
    mid_far, back_far, gathered_ref, vecs_ref, film_ref,
    act_far, pre_far, pay_far, sums_ref, stat_ref,
    mid_ref, back_ref, act_ref, pre_ref, stage_ref, sems,
):
    wide, tall, images, chans = mid_ref.shape
    cols, rows = wide - 2, tall - 2
    per = chans // GROUPS
    mover = Mover(sems)
    steps = pieces(wide, 9)
    loads = []
    for a, b in steps:
        loads.append(
            [mover.start(f.at[a:b], n.at[a:b]) for f, n in ((mid_far, mid_ref), (back_far, back_ref))]
        )
    mean, inv = merge_moments(gathered_ref, rows * cols * per)
    stat_ref[0] = mean
    stat_ref[1] = inv
    scale = 1.0 + film_ref[:, 0:chans]
    slope = vecs_ref[3:4] * scale
    offset = vecs_ref[4:5] * scale + film_ref[:, chans:]

    def column(col, inner):
        hat = (mid_ref[pl.ds(col, 1)].reshape(tall, images, chans) - mean) * inv
        pre = hat * slope + offset
        sigma = sigmoid(pre)
        act = pre * sigma
        act_ref[pl.ds(col, 1)] = act.astype(BF16).reshape(1, tall, images, chans)
        grad = back_ref[pl.ds(col, 1)].reshape(tall, images, chans) * (sigma + act * (1.0 - sigma))
        pre_ref[pl.ds(col, 1)] = grad.reshape(1, tall, images, chans)
        if inner is None:
            return None
        own = grad[1 : rows + 1]
        plain, cross = inner
        return plain + jnp.sum(own, axis=0), cross + jnp.sum(own * hat[1 : rows + 1], axis=0)

    zero = jnp.zeros((images, chans), F32)
    inner = (zero, zero)
    for (a, b), pair in zip(steps, loads):
        for load in pair:
            load.wait()
        if a == 0:
            column(0, None)
        inner = lax.fori_loop(max(a, 1), min(b, cols + 1), column, inner)
        if b == wide:
            column(wide - 1, None)
        clear_border(act_ref, 1, a, b)
        mover.put(act_ref.at[a:b], act_far.at[a:b])
        mover.put(pre_ref.at[a:b], pre_far.at[a:b])
    plain, cross = inner
    sums_ref[0] = plain
    sums_ref[1] = cross
    send_payload(mover, pack_pair(group_total(plain * slope), group_total(cross * slope)), pay_far, stage_ref)
    mover.finish()


def kernel_two(
    act_far, gt_far, sums_ref, bias_ref, keep_far, send_far, act_ref, gt_ref, keep_ref, send_ref, sems
):
    mover = Mover(sems)
    for load in [mover.start(act_far, act_ref), mover.start(gt_far, gt_ref)]:
        load.wait()
    kernel_grad(act_ref, gt_ref, keep_ref, send_ref)
    images, chans = bias_ref.shape
    at = 9 * (chans // 2)
    total = jnp.sum(bias_ref[...], axis=0, keepdims=True)
    for ref in (keep_ref, send_ref):
        ref[at : at + images] = sums_ref[0]
        ref[at + images : at + 2 * images] = sums_ref[1]
        ref[at + 2 * images :] = jnp.broadcast_to(total, (ref.shape[0] - at - 2 * images, chans))
    mover.put(keep_ref, keep_far)
    mover.put(send_ref, send_far)
    mover.finish()


def mix(
    act_far, kernel_far, xt_far, vecs_ref, out_far, act_ref, kernel_ref, xt_ref, branch_ref, out_ref, pair_ref, sems
):
    images, rows, cols, chans = out_ref.shape
    mover = Mover(sems)
    loads = [mover.start(f, n) for f, n in ((kernel_far, kernel_ref), (act_far, act_ref), (xt_far, xt_ref))]
    for load in loads:
        load.wait()
    forward_weights(kernel_ref, pair_ref)
    convolve(act_ref, pair_ref, branch_ref, False, 0, cols, vecs_ref[5:6])
    for a, b in pieces(rows, 4):
        for row in range(a, b):
            mixed = jnp.swapaxes((xt_ref[:, row].astype(F32) + branch_ref[:, row]) * INV_ROOT, 0, 1)
            out_ref[:, row] = mixed.astype(BF16)
        mover.put(out_ref.at[:, a:b], out_far.at[:, a:b])
    mover.finish()


def middle_grad(
    mid_far, pre_far, act_far, keep_two_far, gathered_ref, stat_ref, vecs_ref, film_ref,
    low_far, keep_ref, send_ref, two_ref,
    mid_ref, pre_ref, act_ref, low_ref, sems,
):
    wide, tall, images, chans = mid_ref.shape
    cols, rows = wide - 2, tall - 2
    mover = Mover(sems)
    steps = pieces(wide, 9)
    loads = []
    for a, b in steps:
        loads.append([mover.start(f.at[a:b], n.at[a:b]) for f, n in ((mid_far, mid_ref), (pre_far, pre_ref))])
    late = [
        mover.start(f, n)
        for f, n in ((act_far, act_ref), (keep_two_far, two_ref))
    ]
    count = lax.axis_size("ha") * lax.axis_size("wa") * rows * cols * (chans // GROUPS)
    packed = jnp.sum(gathered_ref[...], axis=0) * (1.0 / count)
    plain = unpack_at(packed, 0)
    cross = unpack_at(packed, 1)
    mean = stat_ref[0]
    inv = stat_ref[1]
    slope = vecs_ref[3:4] * (1.0 + film_ref[:, 0:chans])

    def low_column(col, total):
        hat = (mid_ref[pl.ds(col, 1)].reshape(tall, images, chans) - mean) * inv
        grad = pre_ref[pl.ds(col, 1)].reshape(tall, images, chans) * slope
        low = (inv * (grad - plain - hat * cross)).astype(BF16)
        low_ref[pl.ds(col, 1)] = low.reshape(1, tall, images, chans)
        if total is None:
            return None
        return total + jnp.sum(low[1 : rows + 1].astype(F32), axis=0)

    kbias = jnp.zeros((images, chans), F32)
    for (a, b), pair in zip(steps, loads):
        for load in pair:
            load.wait()
        if a == 0:
            low_column(0, None)
        kbias = lax.fori_loop(max(a, 1), min(b, cols + 1), low_column, kbias)
        if b == wide:
            low_column(wide - 1, None)
        clear_border(low_ref, 1, a, b)
        mover.put(low_ref.at[a:b], low_far.at[a:b])
    for load in late:
        load.wait()
    own = low_ref.at[1 : wide - 1, 1 : tall - 1]
    kernel_grad(act_ref.at[1 : wide + 1, 1 : tall + 1], own, keep_ref, send_ref)
    at = 9 * (chans // 2)
    for ref in (keep_ref, send_ref):
        ref[at:] = jnp.broadcast_to(jnp.sum(kbias, axis=0, keepdims=True), (ref.shape[0] - at, chans))
    mover.finish()


def back_one(
    low_far, xt_far, kernel_far, stat_ref, vecs_ref, grad_far, pay_ref, low_ref, xt_ref, kernel_ref, out_ref, pair_ref, sems
):
    cols, rows, images, chans = xt_ref.shape
    mover = Mover(sems)
    loads = [mover.start(f, n) for f, n in ((kernel_far, kernel_ref), (low_far, low_ref), (xt_far, xt_ref))]
    loads[0].wait()
    backward_weights(kernel_ref, pair_ref)
    loads[1].wait()
    convolve(low_ref, pair_ref, out_ref, True, 0, cols)
    loads[2].wait()
    mean = stat_ref[0]
    inv = stat_ref[1]
    gain = vecs_ref[0:1]
    bias = vecs_ref[1:2]

    def column(col, carry):
        plain, cross = carry
        hat = (xt_ref[pl.ds(col, 1)].reshape(rows, images, chans).astype(F32) - mean) * inv
        norm = hat * gain + bias
        sigma = sigmoid(norm)
        grad = out_ref[pl.ds(col, 1)].reshape(rows, images, chans)
        grad = grad * (sigma * (1.0 + norm * (1.0 - sigma)))
        out_ref[pl.ds(col, 1)] = grad.reshape(1, rows, images, chans)
        return plain + jnp.sum(grad, axis=0), cross + jnp.sum(grad * hat, axis=0)

    zero = jnp.zeros((images, chans), F32)
    inner = (zero, zero)
    for a, b in pieces(cols, 8):
        inner = lax.fori_loop(a, b, column, inner)
        mover.put(out_ref.at[a:b], grad_far.at[a:b])
    plain, cross = inner
    half = images // 2
    pay_ref[0:half] = pack_pair(group_total(plain * gain), group_total(cross * gain))
    rest = [jnp.sum(v, axis=0, keepdims=True) for v in (cross, plain)]
    short = pay_ref.shape[0] - half - 2
    pay_ref[half:] = jnp.concatenate(rest + [jnp.zeros((short, chans), F32)], axis=0)
    mover.finish()


def pack_terms(
    keep_one_ref, came_one_ref, keep_two_ref, came_two_ref, out_far, token_ref,
    one_ref, two_ref, extra_ref, out_ref, sems, extras_one, extras_two,
):
    chips, rows, chans = out_ref.shape
    mover = Mover(sems)
    taps = 9 * (chans // 2)
    share = -(-taps // chips)
    more = -(-(extras_one + extras_two) // chips)
    one_ref[...] = keep_one_ref[...] + came_one_ref[...]
    two_ref[...] = keep_two_ref[...] + came_two_ref[...]
    extra_ref[...] = jnp.zeros(extra_ref.shape, F32)
    extra_ref[0:extras_two] = two_ref[taps : taps + extras_two]
    extra_ref[extras_two : extras_two + extras_one] = one_ref[taps : taps + extras_one]
    for chip in range(chips):
        for at, ref in ((0, one_ref), (share, two_ref)):
            a, b = chip * share, min((chip + 1) * share, taps)
            if a < b:
                out_ref[chip, at : at + b - a] = ref[a:b]
        out_ref[chip, 2 * share : 2 * share + more] = extra_ref[chip * more : (chip + 1) * more]
    token_ref[...] = extra_ref[0:8]
    mover.put(out_ref, out_far)
    mover.finish()


def two_terms(values):
    high = values.astype(BF16).astype(F32)
    return [high, values - high]


def add_terms(gathered_ref, pay_ref, came_ref, out_far, token_ref, out_ref, sems, more, whole):
    chips, rows, chans = gathered_ref.shape
    mover = Mover(sems)
    share = -(-9 * (chans // 2) // chips)
    total = jnp.sum(gathered_ref[...], axis=0)
    every = [total[0 : 2 * share]] + two_terms(total[2 * share : 2 * share + more])
    every = every + two_terms(pay_ref[0:whole] + came_ref[0:whole])
    short = out_ref.shape[1] - sum(v.shape[0] for v in every)
    if short:
        every.append(jnp.zeros((short, chans), F32))
    out_ref[...] = jnp.broadcast_to(jnp.concatenate(every, axis=0).astype(BF16)[None], out_ref.shape)
    token_ref[...] = total[0:8]
    mover.put(out_ref, out_far)
    mover.finish()


def sums_of(own_ref, at, whole):
    total = own_ref[0].astype(F32)
    for chip in range(1, own_ref.shape[0]):
        total = total + own_ref[chip].astype(F32)
    return total[at : at + whole] + total[at + whole : at + 2 * whole]


def three_terms(values):
    high = values.astype(BF16)
    rest = values - high.astype(F32)
    mid = rest.astype(BF16)
    low = (rest - mid.astype(F32)).astype(BF16)
    return jnp.concatenate([high, mid, low], axis=0)


def spread_out(own_ref, other_ref, one_far, two_far, one_ref, two_ref, half_ref, sems):
    chips, rows, chans = own_ref.shape
    mover = Mover(sems)
    half = chans // 2
    taps = 9 * half
    share = -(-taps // chips)
    core = lax.axis_index("ha") % 2
    for at, (out_ref, far) in enumerate(((one_ref, one_far), (two_ref, two_far))):
        for source, place in ((own_ref, core), (other_ref, 1 - core)):
            for chip in range(chips):
                piece = source[chip].astype(F32)[at * share : (at + 1) * share]
                half_ref[chip * share : (chip + 1) * share] = piece
            for tap in range(9):
                rows_at = pl.ds(pl.multiple_of(place * half, half), half)
                out_ref[tap, rows_at] = half_ref[tap * half : (tap + 1) * half]
        mover.put(out_ref, far)
    mover.finish()


def last_grads(
    grad_far, xt_far, c_far, weight_far, own_ref, stat_ref, vecs_ref, film_ref, ints_ref, text_ref,
    out_far, weight_grad_far, text_grad_far, bias_ref, *refs, more, whole,
):
    *vec_refs, grad_ref, xt_ref, c_ref, weight_ref, out_ref, weight_grad_ref, text_grad_ref, extra_ref, sems = refs
    images, rows, cols, chans = out_ref.shape
    chips = own_ref.shape[0]
    mover = Mover(sems)
    steps = pieces(rows, 4)
    loads = []
    for a, b in steps:
        both = [mover.start(f.at[:, a:b], n.at[:, a:b]) for f, n in ((grad_far, grad_ref), (xt_far, xt_ref))]
        loads.append(both + [mover.start(c_far.at[:, a:b], c_ref.at[:, a:b])])
    late = mover.start(weight_far, weight_ref)

    share = -(-9 * (chans // 2) // chips)
    start = 2 * share
    for chip in range(chips):
        piece = own_ref[chip].astype(F32)
        extra_ref[chip * more : (chip + 1) * more] = piece[start : start + more] + piece[start + more : start + 2 * more]
    plain = extra_ref[0:images]
    cross = extra_ref[images : 2 * images]
    scale = 1.0 + film_ref[:, 0:chans]
    scale_grad = vecs_ref[3:4] * cross + vecs_ref[4:5] * plain
    film_grad = jnp.concatenate([scale_grad, plain], axis=1)
    bias_ref[...] = jnp.sum(film_grad, axis=0, keepdims=True)
    sums = sums_of(own_ref, start + 2 * more, whole)
    vec_refs[0][...] = jnp.sum(scale * cross, axis=0, keepdims=True)
    vec_refs[1][...] = jnp.sum(scale * plain, axis=0, keepdims=True)
    for at, row in enumerate((extra_ref[2 * images : 2 * images + 1], extra_ref[2 * images + 1 : 2 * images + 2])):
        vec_refs[2 + at][...] = row
    vec_refs[4][...] = sums[whole - 2 : whole - 1]
    vec_refs[5][...] = sums[whole - 1 : whole]
    terms = three_terms(film_grad)
    ints = ints_ref.shape[1]

    depth = weight_grad_ref.shape[0]
    for at in range(0, depth, 512):
        if at < ints:
            act = ints_ref[:, at : at + 512]
        else:
            embed = text_ref[:, at - ints : at - ints + 512].astype(F32)
            act = (embed * sigmoid(embed)).astype(BF16)
        weight_grad_ref[at : at + 512] = lax.dot_general(
            jnp.concatenate([act, act, act], axis=0), terms, (((0,), (0,)), ((), ())), preferred_element_type=F32
        )
        mover.put(weight_grad_ref.at[at : at + 512], weight_grad_far.at[at : at + 512])

    count = lax.axis_size("ha") * lax.axis_size("wa") * rows * cols * (chans // GROUPS)
    packed = sums[0 : images // 2] * (1.0 / count)
    plain = unpack_at(packed, 0)
    cross = unpack_at(packed, 1)
    mean = stat_ref[0]
    inv = stat_ref[1]
    gain = vecs_ref[0:1]
    for (a, b), group in zip(steps, loads):
        for load in group:
            load.wait()
        for row in range(a, b):
            hat = (xt_ref[:, row].astype(F32) - mean) * inv
            path = jnp.swapaxes(inv * (grad_ref[:, row] * gain - plain - hat * cross), 0, 1)
            out_ref[:, row] = (c_ref[:, row].astype(F32) * INV_ROOT + path).astype(BF16)
        mover.put(out_ref.at[:, a:b], out_far.at[:, a:b])

    late.wait()
    for at in range(ints, depth, 512):
        embed = text_ref[:, at - ints : at - ints + 512].astype(F32)
        sigma = sigmoid(embed)
        made = lax.dot_general(
            terms, weight_ref[at : at + 512], (((1,), (1,)), ((), ())), preferred_element_type=F32
        )
        cond_grad = made[0:images] + made[images : 2 * images] + made[2 * images :]
        text_grad_ref[:, at - ints : at - ints + 512] = cond_grad * (sigma * (1.0 + embed * (1.0 - sigma)))
    mover.put(text_grad_ref, text_grad_far)
    mover.finish()


def to_all(payload):
    return lax.all_to_all(payload, AXES, 0, 0)


def to_chips(payload):
    tall, wide = lax.axis_size("ha"), lax.axis_size("wa")
    groups = [[h * wide + w for h in range(core, tall, 2) for w in range(wide)] for core in range(2)]
    return lax.all_to_all(payload, AXES, 0, 0, axis_index_groups=groups)


def to_sibling(payload):
    return lax.ppermute(payload, "ha", [(i, i ^ 1) for i in range(lax.axis_size("ha"))])


def shifted(cells, axis, step):
    count = lax.axis_size(axis)
    return lax.ppermute(cells, axis, [(i, (i + step) % count) for i in range(count)])


def side_halo(sides, top, bottom, after_near=()):
    four, rows, images, chans = sides.shape
    edge = shaped((2, rows + 4, images, chans), sides.dtype)
    right, left = kernel_call(
        edge_columns, (), (sides, top, bottom), (), (edge, edge), cost=0.4, after_near=after_near, limit=16
    )
    return shifted(right, "wa", 1), shifted(left, "wa", -1), right


def sinusoids(first, second):
    half = TEMB // 2
    freqs = jnp.exp(-math.log(10000.0) * jnp.arange(half, dtype=F32) / half)
    times = jnp.stack([first, second], axis=1).astype(F32)
    angles = times[:, :, None, None] * freqs[None, None, None, :]
    which = lax.broadcasted_iota(jnp.int32, (first.shape[0], 2, 2, half), 2)
    made = jnp.where(which == 0, jnp.sin(angles), jnp.cos(angles))
    return made.reshape(first.shape[0], 2 * TEMB)


def buffers(*arrays):
    return tuple(pltpu.VMEM(a.shape, a.dtype) for a in arrays)


def local(
    block_input,
    timesteps,
    aug_levels,
    text_pooled,
    gain_one,
    bias_one,
    conv_one,
    conv_one_bias,
    gain_two,
    bias_two,
    film_weight,
    film_bias,
    conv_two,
    conv_two_bias,
    cotangent,
):
    images, rows, cols, chans = block_input.shape
    parts = lax.axis_size("ha") * lax.axis_size("wa")
    chips = parts // 2
    half = images // 2
    vecs = (gain_one, bias_one, conv_one_bias, gain_two, bias_two, conv_two_bias, gain_one, gain_one)
    vecs = jnp.stack(vecs).astype(F32)
    payload = shaped((parts, half, chans), F32)
    per_image = shaped((images, chans), F32)
    two_images = shaped((2, images, chans), F32)
    block = shaped((cols, rows, images, chans), BF16)
    block_wide = shaped((cols, rows, images, chans), F32)
    rim = shaped((cols + 2, rows + 2, images, chans), BF16)
    rim_wide = shaped((cols + 2, rows + 2, images, chans), F32)
    far_rim = shaped((cols + 4, rows + 4, images, chans), BF16)
    given = shaped((images, rows, cols, chans), BF16)
    pair = pltpu.VMEM((12 * chans, 2 * chans), BF16)
    pair_back = pltpu.VMEM((2 * chans, 12 * chans), BF16)

    sides = shaped((4, rows, images, chans), BF16)
    row_halo = shaped((cols, 2, images, chans), BF16)
    xt, x_down, x_up, x_sides, moments = kernel_call(
        prepare_x, (block_input,), (), (block,), (row_halo, row_halo, sides, shaped((half, chans), F32)),
        scratch=buffers(given, block), sems=16, cost=2.3,
    )
    x_top = shifted(x_down, "ha", 1)
    x_bottom = shifted(x_up, "ha", -1)
    (pay_one,) = kernel_call(
        write_payload, (), (moments,), (payload,), scratch=buffers(payload), sems=1, cost=1.0,
        after_near=(to_sibling(moments),),
    )
    moments_one = to_all(pay_one)
    x_left, x_right, x_edge = side_halo(x_sides, x_top, x_bottom)
    gt, g_down, g_up, g_sides, kbias_two_local = kernel_call(
        prepare_g, (cotangent,), (), (block,), (row_halo, row_halo, sides, per_image),
        scratch=buffers(given, block), sems=16, cost=2.0, after_near=(x_edge,),
    )
    g_top = shifted(g_down, "ha", 1)
    g_bottom = shifted(g_up, "ha", -1)

    embed_ints = sinusoids(timesteps, aug_levels)
    act_ints = jax.nn.silu(embed_ints).astype(BF16)
    act_one, mid, pay_two, stat_one = kernel_call(
        first_half, (xt, conv_one), (x_top, x_bottom, x_left, x_right, moments_one, vecs), (far_rim, rim_wide, payload), (two_images,),
        scratch=buffers(xt, conv_one, far_rim, rim_wide, payload) + (pair,), sems=16, cost=5.5, after_near=(kbias_two_local,),
    )
    moments_two = to_all(pay_two)
    g_left, g_right, _ = side_halo(g_sides, g_top, g_bottom, after_near=(stat_one,))
    act_two_grad, film = kernel_call(
        back_two,
        (gt, conv_two, film_weight),
        (g_top, g_bottom, g_left, g_right, act_ints, text_pooled, film_bias.reshape(1, 2 * chans)),
        (rim_wide,),
        (shaped((images, 2 * chans), F32),),
        scratch=buffers(gt, conv_two, film_weight, far_rim, rim_wide) + (pair_back,), sems=16, cost=5.0,
    )
    act_two, pre_two_grad, pay_three, sums_two, stat_two = kernel_call(
        second_norm, (mid, act_two_grad), (moments_two, vecs, film), (rim, rim_wide, payload), (two_images, two_images),
        scratch=buffers(rim_wide, rim_wide, rim, rim_wide, payload), sems=24, cost=3.2,
    )
    moments_three = to_all(pay_three)

    taps = 9 * (chans // 2)
    share = -(-taps // chips)
    extras_two = 2 * images + 1
    extras_one = 1
    halves_two = shaped((taps + 2 * images + 8, chans), F32)
    halves_one = shaped((taps + 8, chans), F32)
    keep_two, send_two = kernel_call(
        kernel_two, (act_two, gt), (sums_two, kbias_two_local), (halves_two, halves_two),
        scratch=buffers(act_two, gt, halves_two, halves_two), sems=4, cost=3.0,
    )
    came_two = to_sibling(send_two)
    low, keep_one, send_one, keep_two = kernel_call(
        middle_grad,
        (mid, pre_two_grad, act_one, keep_two),
        (moments_three, stat_two, vecs, film),
        (rim,),
        (halves_one, halves_one, halves_two),
        scratch=buffers(mid, pre_two_grad, act_one, rim),
        sems=24, cost=6.0,
    )
    came_one = to_sibling(send_one)
    more = -(-(extras_one + extras_two) // chips)
    terms_shape = shaped((chips, -(-(2 * share + more) // 8) * 8, chans), F32)
    terms, token = kernel_call(
        functools.partial(pack_terms, extras_one=extras_one, extras_two=extras_two),
        (), (keep_one, came_one, keep_two, came_two), (terms_shape,), (shaped((8, chans), F32),),
        scratch=buffers(halves_one, halves_two, shaped((-(-chips * more // 8) * 8, chans), F32), terms_shape),
        sems=3, cost=1.0,
    )
    gathered = to_chips(terms)
    whole = half + 2
    norm_one_grad, pay_four = kernel_call(
        back_one, (low, xt, conv_one), (stat_one, vecs), (block_wide,), (shaped((2 * half, chans), F32),),
        scratch=buffers(rim, block, conv_one, block_wide) + (pair_back,), sems=16, cost=5.0,
        after_near=(to_sibling(token),),
    )
    came_four = to_sibling(pay_four)
    (mixed,) = kernel_call(
        mix, (act_two, conv_two, xt), (vecs,), (given,),
        scratch=buffers(act_two, conv_two, xt, block_wide, given) + (pair,), sems=8, cost=3.6, after_near=(pay_four,),
    )
    shares_shape = shaped((chips, -(-(2 * share + 2 * more + 2 * whole) // 8) * 8, chans), BF16)
    shares, token = kernel_call(
        functools.partial(add_terms, more=more, whole=whole),
        (), (gathered, pay_four, came_four), (shares_shape,), (shaped((8, chans), F32),),
        scratch=buffers(shares_shape), sems=1, cost=1.0, after=(mixed,),
    )
    own_half = to_chips(shares)
    other_half = to_sibling(own_half)
    weight_grad = shaped(film_weight.shape, F32)
    text_shape = shaped(text_pooled.shape, F32)
    row = shaped((1, chans), F32)
    input_grad, film_weight_grad, text_grad, film_bias_grad, *vec_grads = kernel_call(
        functools.partial(last_grads, more=more, whole=whole),
        (norm_one_grad, xt, cotangent, film_weight),
        (own_half, stat_one, vecs, film, act_ints, text_pooled),
        (given, weight_grad, text_shape),
        (shaped((1, 2 * chans), F32),) + (row,) * 6,
        scratch=buffers(block_wide, block, given, film_weight, given, weight_grad, text_shape)
        + (pltpu.VMEM((-(-chips * more // 8) * 8, chans), F32),),
        sems=32, cost=6.0,
    )
    full = shaped((9, chans, chans), F32)
    kernel_one_grad, kernel_two_grad = kernel_call(
        spread_out, (), (own_half, other_half), (full, full),
        scratch=buffers(full, full, shaped((chips * share, chans), F32)), sems=2, cost=2.0, after=(input_grad,),
    )
    return (
        mixed,
        input_grad,
        text_grad,
        vec_grads[4].reshape(chans),
        vec_grads[5].reshape(chans),
        kernel_one_grad.reshape(3, 3, chans, chans),
        vec_grads[3].reshape(chans),
        vec_grads[0].reshape(chans),
        vec_grads[1].reshape(chans),
        film_weight_grad,
        film_bias_grad.reshape(2 * chans),
        kernel_two_grad.reshape(3, 3, chans, chans),
        vec_grads[2].reshape(chans),
    )


def solution(mesh):
    split = P(None, "ha", "wa", None)
    return jax.shard_map(
        local,
        mesh=mesh,
        in_specs=(split,) + (P(),) * 13 + (split,),
        out_specs=(split, split) + (P(),) * 11,
        check_vma=False,
    )
```

```python
import functools
import math

import jax
import jax.numpy as jnp
import numpy as np
from jax import lax
from jax.experimental import pallas as pl
from jax.experimental.pallas import tpu as pltpu
from jax.sharding import PartitionSpec as P

GROUPS = 32
TEMB = 256
EPSILON = 1e-05
INV_ROOT = 1.0 / math.sqrt(2.0)
AXES = ("ha", "wa")
F32 = jnp.float32
BF16 = jnp.bfloat16
NEAR = pl.BlockSpec(memory_space=pltpu.VMEM)
FAR = pl.BlockSpec(memory_space=pl.ANY)
MIB = 1 << 20


def shaped(shape, dtype):
    return jax.ShapeDtypeStruct(shape, dtype)


def kernel_call(
    body, far=(), near=(), tiny=(), far_out=(), near_out=(), tiny_out=(), scratch=(), sems=0, cost=1.0,
    after=(), after_near=(), scalars=(), limit=48,
):
    pinned = lambda arrays: [pltpu.with_memory_space_constraint(array, pltpu.HBM) for array in arrays]
    given = len(far) + len(near)
    held = len(after) + len(after_near)
    copies = len(tiny) + len(tiny_out)

    def run(*refs):
        refs = list(refs)
        take = lambda count: [refs.pop(0) for _ in range(count)]
        inputs = take(given)
        tiny_far = take(len(tiny))
        scalar_refs = take(len(scalars))
        take(held)
        outputs = take(len(far_out) + len(near_out))
        tiny_out_far = take(len(tiny_out))
        tiny_refs = take(len(tiny))
        tiny_out_refs = take(len(tiny_out))
        mover = None
        if sems + copies:
            mover = Mover(refs.pop(), [(f, n) for f, n in zip(tiny_far, tiny_refs)])
        body(*inputs, *tiny_refs, *scalar_refs, *outputs, *tiny_out_refs, *refs, *([mover] if mover else []))
        if mover:
            for source, target in zip(tiny_out_refs, tiny_out_far):
                mover.put(source, target)
            mover.finish()

    return pl.pallas_call(
        run,
        out_shape=(
            *(pltpu.HBM(out.shape, out.dtype) for out in far_out),
            *near_out,
            *(pltpu.HBM(out.shape, out.dtype) for out in tiny_out),
        ),
        in_specs=[FAR] * len(far)
        + [NEAR] * len(near)
        + [FAR] * len(tiny)
        + [pl.BlockSpec(memory_space=pltpu.SMEM)] * len(scalars)
        + [FAR] * held,
        out_specs=(FAR,) * len(far_out) + (NEAR,) * len(near_out) + (FAR,) * len(tiny_out),
        scratch_shapes=buffers(*tiny, *tiny_out)
        + tuple(scratch)
        + ((pltpu.SemaphoreType.DMA((sems + copies,)),) if sems + copies else ()),
        compiler_params=pltpu.CompilerParams(vmem_limit_bytes=limit * MIB),
        name=getattr(body, "func", body).__name__,
        cost_estimate=pl.CostEstimate(flops=int(cost * 1.1e9), bytes_accessed=0, transcendentals=0),
    )(*pinned(far), *near, *pinned(tiny), *scalars, *pinned(after), *after_near)


def buffers(*arrays):
    return tuple(pltpu.VMEM(a.shape, a.dtype) for a in arrays)


class Mover:
    def __init__(self, sems, first):
        self.sems = sems
        self.used = 0
        self.open = []
        self.first = [self.start(source, target) for source, target in first]

    def start(self, source, target):
        copy = pltpu.make_async_copy(source, target, self.sems.at[self.used])
        self.used += 1
        copy.start()
        return copy

    def ready(self):
        for copy in self.first:
            copy.wait()

    def put(self, source, target):
        self.open.append(self.start(source, target))

    def finish(self):
        for copy in self.open:
            copy.wait()


def pieces(count, size):
    return [(at, min(at + size, count)) for at in range(0, count, size)]


def lanes_of(shape):
    return lax.broadcasted_iota(jnp.int32, shape, 1)


def group_total(values):
    chans = values.shape[1]
    lane = lanes_of(values.shape)
    step = 1
    while step < chans // GROUPS:
        up = pltpu.roll(values, chans - step, 1)
        down = pltpu.roll(values, step, 1)
        values = values + jnp.where((lane & step) == 0, up, down)
        step *= 2
    return values


def pack_pair(first, second):
    half = first.shape[0] // 2
    lane = lanes_of((half, first.shape[1])) & 3
    return jnp.where(
        lane == 0,
        first[:half],
        jnp.where(lane == 1, second[:half], jnp.where(lane == 2, first[half:], second[half:])),
    )


def unpack_at(packed, place):
    lane = lanes_of(packed.shape) & 3
    top = group_total(jnp.where(lane == place, packed, 0.0))
    low = group_total(jnp.where(lane == place + 2, packed, 0.0))
    return jnp.concatenate([top, low], axis=0)


def merge_moments(gathered_ref, local_count):
    parts = gathered_ref.shape[0]
    chans = gathered_ref.shape[2]
    every = gathered_ref[...]
    total = jnp.sum(every, axis=0)
    mean = total * (1.0 / parts)
    apart = every - mean[None]
    between = jnp.sum(apart * apart, axis=0)
    square = pltpu.roll(total, chans - 1, 1) + local_count * between
    inv = lax.rsqrt(square * (1.0 / (local_count * parts)) + EPSILON)
    return unpack_at(mean, 0), unpack_at(inv, 0)


def local_moments(total, square, pilot, pixels, per):
    off = total * (1.0 / pixels)
    mean = pilot + off
    apart = square - total * off
    group_mean = group_total(mean) * (1.0 / per)
    shift = mean - group_mean
    return group_mean, group_total(apart + pixels * shift * shift)


def sigmoid(values):
    return 0.5 + 0.5 * jnp.tanh(0.5 * values)


def forward_weights(kernel_ref, pair_ref):
    chans = kernel_ref.shape[2]
    zero = jnp.zeros((chans, chans), BF16)
    for row in range(3):
        for col in range(4):
            at = (row * 4 + col) * chans
            pair_ref[at : at + chans, 0:chans] = kernel_ref[row, col] if col < 3 else zero
            pair_ref[at : at + chans, chans:] = kernel_ref[row, col - 1] if col > 0 else zero


def backward_weights(kernel_ref, pair_ref):
    chans = kernel_ref.shape[2]
    zero = jnp.zeros((chans, chans), BF16)
    for row in range(3):
        for col in range(4):
            at = (row * 4 + col) * chans
            pair_ref[0:chans, at : at + chans] = kernel_ref[2 - row, 2 - col] if col < 3 else zero
            pair_ref[chans:, at : at + chans] = kernel_ref[2 - row, 3 - col] if col > 0 else zero


def convolve(cells_ref, pair_ref, transposed, rows, first, last, take):
    images, chans = cells_ref.shape[2:]
    pairs = (last - first) // 2
    parts = []
    for row in range(3):
        for col in range(4):
            window = [cells_ref[first + 2 * q + col, row : row + rows] for q in range(pairs)]
            parts.append(jnp.stack(window).reshape(pairs * rows * images, chans))
    wide = jnp.concatenate(parts, axis=1)
    contract = ((1,), (1,)) if transposed else ((1,), (0,))
    made = lax.dot_general(wide, pair_ref[...], (contract, ((), ())), preferred_element_type=F32)
    made = made.reshape(pairs, rows, images, 2 * chans)
    for q in range(pairs):
        for side in range(2):
            take(first + 2 * q + side, made[q, :, :, side * chans : (side + 1) * chans])


def grad_terms(cells_ref, grads_ref):
    cols, rows, images, chans = grads_ref.shape
    pixels = cols * rows * images
    windows = [
        cells_ref[col : col + cols, row : row + rows].reshape(pixels, chans) for row in range(3) for col in range(3)
    ]
    return lax.dot_general(
        grads_ref[...].reshape(pixels, chans),
        jnp.concatenate(windows, axis=1),
        (((0,), (0,)), ((), ())),
        preferred_element_type=F32,
    )


def split_taps(every, keep_ref, send_ref):
    chans = every.shape[0]
    half = chans // 2
    first = lax.axis_index("ha") % 2 == 0
    for tap in range(9):
        made = every[:, tap * chans : (tap + 1) * chans].T
        at = tap * half
        keep_ref[at : at + half, :] = jnp.where(first, made[:half], made[half:])
        send_ref[at : at + half, :] = jnp.where(first, made[half:], made[:half])


def at_edges():
    tall = lax.axis_index("ha")
    wide = lax.axis_index("wa")
    return (
        tall == 0,
        tall == lax.axis_size("ha") - 1,
        wide == 0,
        wide == lax.axis_size("wa") - 1,
    )


def clear_border(cells_ref, width, first=0, last=None):
    top, bottom, left, right = at_edges()
    cols, rows, images, chans = cells_ref.shape
    last = cols if last is None else last
    dtype = cells_ref.dtype

    @pl.when(top)
    def _():
        cells_ref[first:last, 0:width] = jnp.zeros((last - first, width, images, chans), dtype)

    @pl.when(bottom)
    def _():
        cells_ref[first:last, rows - width :] = jnp.zeros((last - first, width, images, chans), dtype)

    if first == 0:

        @pl.when(left)
        def _():
            cells_ref[0:width] = jnp.zeros((width, rows, images, chans), dtype)

    if last == cols:

        @pl.when(right)
        def _():
            cells_ref[cols - width :] = jnp.zeros((width, rows, images, chans), dtype)


def send_payload(mover, packed, pay_ref, stage_ref):
    stage_ref[...] = jnp.broadcast_to(packed[None], stage_ref.shape)
    mover.put(stage_ref, pay_ref)


def prepare_x(x_far, xt_far, near_ref, next_ref, sides_ref, moments_ref, x_ref, xt_ref, mover):
    images, rows, cols, chans = x_ref.shape
    steps = pieces(rows, 2)
    loads = [mover.start(x_far.at[:, a:b], x_ref.at[:, a:b]) for a, b in steps]
    total = jnp.zeros((images, chans), F32)
    square = total
    for (a, b), load in zip(steps, loads):
        load.wait()
        if a == 0:
            pilot = x_ref[:, 0, 0].astype(F32)
        for row in range(a, b):
            x = jnp.swapaxes(x_ref[:, row].astype(F32), 0, 1)
            xt_ref[:, row] = x.astype(BF16)
            apart = x - pilot[None]
            total = total + jnp.sum(apart, axis=0)
            square = square + jnp.sum(apart * apart, axis=0)
        mover.put(xt_ref.at[:, a:b], xt_far.at[:, a:b])
    mean, spread = local_moments(total, square, pilot, rows * cols, chans // GROUPS)
    moments_ref[...] = pack_pair(mean, spread)
    outer(xt_ref, near_ref, next_ref, sides_ref)


def is_even(axis="ha"):
    return lax.axis_index(axis) % 2 == 0


def outer(cells, near_ref, next_ref, sides_ref):
    cols, rows = cells.shape[0:2]
    down, up = cells[:, rows - 2 :], cells[:, 0:2]
    near_ref[...] = jnp.where(is_even(), down, up)
    next_ref[...] = jnp.where(is_even(), up, down)
    sides_ref[0:2] = cells[0:2]
    sides_ref[2:4] = cells[cols - 2 :]


def prepare_g(
    c_far, moments_ref, gt_far, pay_far, near_ref, next_ref, sides_ref, bias_ref, c_ref, gt_ref, stage_ref, mover
):
    images, rows, cols, chans = c_ref.shape
    steps = pieces(rows, 2)
    loads = [mover.start(c_far.at[:, a:b], c_ref.at[:, a:b]) for a, b in steps]
    send_payload(mover, moments_ref[...], pay_far, stage_ref)
    bias = jnp.zeros((images, chans), F32)
    for (a, b), load in zip(steps, loads):
        load.wait()
        for row in range(a, b):
            grad = jnp.swapaxes(c_ref[:, row].astype(F32) * INV_ROOT, 0, 1).astype(BF16)
            gt_ref[:, row] = grad
            bias = bias + jnp.sum(grad.astype(F32), axis=0)
        mover.put(gt_ref.at[:, a:b], gt_far.at[:, a:b])
    bias_ref[...] = bias
    outer(gt_ref, near_ref, next_ref, sides_ref)


def edge_columns(sides_ref, near_ref, next_ref, one_ref, other_ref):
    cols, rows = near_ref.shape[0], sides_ref.shape[1]
    even = is_even("wa")

    def piece(left, right):
        return jnp.where(even, right, left), jnp.where(even, left, right)

    near = piece(near_ref[0:2], near_ref[cols - 2 : cols])
    following = piece(next_ref[0:2], next_ref[cols - 2 : cols])
    own = piece(sides_ref[0:2], sides_ref[2:4])
    for at, ref in enumerate((one_ref, other_ref)):
        ref[:, 0:2] = jnp.where(is_even(), following[at], near[at])
        ref[:, 2 : rows + 2] = own[at]
        ref[:, rows + 2 :] = jnp.where(is_even(), near[at], following[at])


def assemble(mover, own_far, own_ref, near_ref, next_ref, one_ref, other_ref, cells_ref, change):
    cols, rows, images, chans = own_ref.shape
    steps = pieces(cols, 8)
    loads = [mover.start(own_far.at[a:b], own_ref.at[a:b]) for a, b in steps]

    def fill():
        def halo_column(col, _):
            near, next_ = near_ref[pl.ds(col, 1)], next_ref[pl.ds(col, 1)]
            cells_ref[pl.ds(col + 2, 1), 0:2] = change(jnp.where(is_even(), next_, near))
            cells_ref[pl.ds(col + 2, 1), rows + 2 :] = change(jnp.where(is_even(), near, next_))
            return 0

        def column(col, _):
            cells_ref[pl.ds(col + 2, 1), 2 : rows + 2] = change(own_ref[pl.ds(col, 1)])
            return 0

        even = is_even("wa")
        cells_ref[0:2] = change(jnp.where(even, other_ref[...], one_ref[...]))
        cells_ref[cols + 2 :] = change(jnp.where(even, one_ref[...], other_ref[...]))
        lax.fori_loop(0, cols, halo_column, 0, unroll=4)
        for (a, b), load in zip(steps, loads):
            load.wait()
            lax.fori_loop(a, b, column, 0, unroll=2)
        clear_border(cells_ref, 2)

    return fill


def first_half(
    xt_far, kernel_far, near_ref, next_ref, one_ref, other_ref, gathered_ref, gain_ref, bias_ref, kbias_ref,
    act_far, mid_far, pay_far, stat_ref,
    xt_ref, kernel_ref, act_ref, mid_ref, stage_ref, pair_ref, mover,
):
    cols, rows, images, chans = xt_ref.shape
    per = chans // GROUPS
    load = mover.start(kernel_far, kernel_ref)
    fill = assemble(
        mover, xt_far, xt_ref, near_ref, next_ref, one_ref, other_ref, act_ref, lambda cells: act(cells)
    )
    mean, inv = merge_moments(gathered_ref, rows * cols * per)
    stat_ref[0] = mean
    stat_ref[1] = inv
    mover.ready()
    slope = 0.5 * inv * gain_ref[...].astype(F32)
    offset = 0.5 * bias_ref[...].astype(F32)

    def act(cells):
        value = (cells.astype(F32) - mean) * slope + offset
        return (value + value * jnp.tanh(value)).astype(BF16)

    fill()
    load.wait()
    forward_weights(kernel_ref, pair_ref)
    mover.put(act_ref, act_far)

    wide = cols + 2
    kbias = kbias_ref[...].astype(F32)
    state = [None, jnp.zeros((images, chans), F32), jnp.zeros((images, chans), F32)]

    def take(col, values):
        values = values + kbias
        mid_ref[col] = values
        if 1 <= col <= cols:
            own = values[1 : rows + 1]
            if state[0] is None:
                state[0] = own[0]
            apart = own - state[0][None]
            state[1] = state[1] + jnp.sum(apart, axis=0)
            state[2] = state[2] + jnp.sum(apart * apart, axis=0)

    for a, b in pieces(wide, 10):
        convolve(act_ref, pair_ref, False, rows + 2, a, b, take)
        mover.put(mid_ref.at[a:b], mid_far.at[a:b])
    pilot, total, square = state
    mean, spread = local_moments(total, square, pilot, rows * cols, per)
    send_payload(mover, pack_pair(mean, spread), pay_far, stage_ref)


def back_two(
    gt_far, kernel_far, weight_far, near_ref, next_ref, one_ref, other_ref, *refs,
):
    text_ref, fbias_ref, freqs_ref, times_ref, levels_ref, out_far, film_ref, ints_ref, *refs = refs
    gt_ref, kernel_ref, weight_ref, cells_ref, out_ref, pair_ref, mover = refs
    load = mover.start(kernel_far, kernel_ref)
    fill = assemble(
        mover, gt_far, gt_ref, near_ref, next_ref, one_ref, other_ref, cells_ref, lambda cells: cells
    )
    late = mover.start(weight_far, weight_ref)
    load.wait()
    backward_weights(kernel_ref, pair_ref)
    fill()
    wide = out_ref.shape[0]
    for a, b in pieces(wide, 10):
        convolve(cells_ref, pair_ref, True, out_ref.shape[1], a, b, lambda col, values: out_ref.__setitem__(col, values))
        mover.put(out_ref.at[a:b], out_far.at[a:b])
    mover.ready()
    text = text_ref[...].astype(F32)
    half = TEMB // 2
    for at, source_ref in ((0, times_ref), (TEMB, levels_ref)):
        angles = [source_ref[image].astype(F32) * freqs_ref[...] for image in range(text_ref.shape[0])]
        angles = jnp.concatenate(angles, axis=0)
        for start, embed in ((at, jnp.sin(angles)), (at + half, jnp.cos(angles))):
            ints_ref[:, start : start + half] = (embed * sigmoid(embed)).astype(BF16)
    act = jnp.concatenate([ints_ref[...], (text * sigmoid(text)).astype(BF16)], axis=1)
    late.wait()
    film_ref[...] = jnp.dot(act, weight_ref[...], preferred_element_type=F32) + fbias_ref[...].astype(F32)


def second_values(stat, gain_ref, bias_ref, film_ref):
    mean, inv = stat
    chans = mean.shape[1]
    scale = 1.0 + film_ref[:, 0:chans]
    slope = gain_ref[...].astype(F32) * scale
    half_slope = 0.5 * slope
    half_offset = 0.5 * (bias_ref[...].astype(F32) * scale + film_ref[:, chans:])

    def values(mid, back):
        hat = (mid - mean) * inv
        pre = hat * half_slope + half_offset
        bend = jnp.tanh(pre)
        more = 1.0 + bend
        grad = back * (0.5 * more * (1.0 + pre * (1.0 - bend)))
        return hat, pre * more, grad

    return slope, values


def second_norm(
    mid_far, back_far, gathered_ref, gain_ref, bias_ref, film_ref,
    act_far, pre_far, pay_far, sums_ref, stat_ref,
    mid_ref, back_ref, act_ref, pre_ref, stage_ref, mover,
):
    wide, tall, images, chans = mid_ref.shape
    cols, rows = wide - 2, tall - 2
    per = chans // GROUPS
    steps = pieces(wide, 9)
    loads = []
    for a, b in steps:
        loads.append(
            [mover.start(f.at[a:b], n.at[a:b]) for f, n in ((mid_far, mid_ref), (back_far, back_ref))]
        )
    mean, inv = merge_moments(gathered_ref, rows * cols * per)
    stat_ref[0] = mean
    stat_ref[1] = inv
    mover.ready()
    slope, values = second_values((mean, inv), gain_ref, bias_ref, film_ref)

    def column(col, inner):
        hat, act, grad = values(mid_ref[col], back_ref[col])
        act_ref[col] = act.astype(BF16)
        pre_ref[col] = grad
        if inner is None:
            return None
        own = grad[1 : rows + 1]
        plain, cross = inner
        return plain + jnp.sum(own, axis=0), cross + jnp.sum(own * hat[1 : rows + 1], axis=0)

    zero = jnp.zeros((images, chans), F32)
    inner = (zero, zero)
    for (a, b), pair in zip(steps, loads):
        for load in pair:
            load.wait()
        if a == 0:
            column(0, None)
        inner = lax.fori_loop(max(a, 1), min(b, cols + 1), column, inner)
        if b == wide:
            column(wide - 1, None)
        clear_border(act_ref, 1, a, b)
        mover.put(act_ref.at[a:b], act_far.at[a:b])
        mover.put(pre_ref.at[a:b], pre_far.at[a:b])
    plain, cross = inner
    sums_ref[0] = plain
    sums_ref[1] = cross
    send_payload(mover, pack_pair(group_total(plain * slope), group_total(cross * slope)), pay_far, stage_ref)


def kernel_two(
    act_far, gt_far, sums_ref, bias_ref, keep_far, send_far, act_ref, gt_ref, keep_ref, send_ref, mover
):
    for load in [mover.start(act_far, act_ref), mover.start(gt_far, gt_ref)]:
        load.wait()
    split_taps(grad_terms(act_ref, gt_ref), keep_ref, send_ref)
    mover.ready()
    images, chans = bias_ref.shape
    at = 9 * (chans // 2)
    total = jnp.sum(bias_ref[...], axis=0, keepdims=True)
    for ref in (keep_ref, send_ref):
        ref[at : at + images] = sums_ref[0]
        ref[at + images : at + 2 * images] = sums_ref[1]
        ref[at + 2 * images :] = jnp.broadcast_to(total, (ref.shape[0] - at - 2 * images, chans))
    mover.put(keep_ref, keep_far)
    mover.put(send_ref, send_far)


def mix(
    act_far, kernel_far, xt_far, kbias_ref, out_far, act_ref, kernel_ref, xt_ref, branch_ref, out_ref, pair_ref, mover
):
    images, rows, cols, chans = out_ref.shape
    loads = [mover.start(f, n) for f, n in ((kernel_far, kernel_ref), (act_far, act_ref), (xt_far, xt_ref))]
    for load in loads:
        load.wait()
    forward_weights(kernel_ref, pair_ref)
    mover.ready()
    kbias = kbias_ref[...].astype(F32)
    convolve(
        act_ref, pair_ref, False, rows, 0, cols, lambda col, values: branch_ref.__setitem__(col, values + kbias)
    )
    for a, b in pieces(rows, 4):
        for row in range(a, b):
            mixed = jnp.swapaxes((xt_ref[:, row].astype(F32) + branch_ref[:, row]) * INV_ROOT, 0, 1)
            out_ref[:, row] = mixed.astype(BF16)
        mover.put(out_ref.at[:, a:b], out_far.at[:, a:b])


def middle_grad(
    mid_far, pre_far, act_far, keep_two_far, gathered_ref, stat_ref, gain_ref, film_ref,
    low_far, keep_ref, send_ref, two_ref,
    mid_ref, pre_ref, act_ref, low_ref, mover,
):
    wide, tall, images, chans = mid_ref.shape
    cols, rows = wide - 2, tall - 2
    steps = pieces(wide, 9)
    loads = []
    for a, b in steps:
        loads.append([mover.start(f.at[a:b], n.at[a:b]) for f, n in ((mid_far, mid_ref), (pre_far, pre_ref))])
    late = [mover.start(f, n) for f, n in ((act_far, act_ref), (keep_two_far, two_ref))]
    count = lax.axis_size("ha") * lax.axis_size("wa") * rows * cols * (chans // GROUPS)
    packed = jnp.sum(gathered_ref[...], axis=0) * (1.0 / count)
    mover.ready()
    mean = stat_ref[0]
    inv = stat_ref[1]
    plain = unpack_at(packed, 0) * inv
    cross = unpack_at(packed, 1) * inv * inv
    slope = gain_ref[...].astype(F32) * (1.0 + film_ref[:, 0:chans]) * inv

    def low_column(col, total):
        low = (pre_ref[col] * slope - plain - (mid_ref[col] - mean) * cross).astype(BF16)
        low_ref[col] = low
        if total is None:
            return None
        return total + jnp.sum(low[1 : rows + 1].astype(F32), axis=0)

    kbias = jnp.zeros((images, chans), F32)
    for (a, b), pair in zip(steps, loads):
        for load in pair:
            load.wait()
        if a == 0:
            low_column(0, None)
        kbias = lax.fori_loop(max(a, 1), min(b, cols + 1), low_column, kbias)
        if b == wide:
            low_column(wide - 1, None)
        clear_border(low_ref, 1, a, b)
        mover.put(low_ref.at[a:b], low_far.at[a:b])
    for load in late:
        load.wait()
    own = low_ref.at[1 : wide - 1, 1 : tall - 1]
    split_taps(grad_terms(act_ref.at[1 : wide + 1, 1 : tall + 1], own), keep_ref, send_ref)
    at = 9 * (chans // 2)
    for ref in (keep_ref, send_ref):
        ref[at:] = jnp.broadcast_to(jnp.sum(kbias, axis=0, keepdims=True), (ref.shape[0] - at, chans))


def back_one(
    low_far, xt_far, kernel_far, stat_ref, gain_ref, bias_ref, grad_far, pay_ref, low_ref, xt_ref, kernel_ref, out_ref, pair_ref, mover
):
    cols, rows, images, chans = xt_ref.shape
    loads = [mover.start(f, n) for f, n in ((kernel_far, kernel_ref), (low_far, low_ref), (xt_far, xt_ref))]
    loads[0].wait()
    backward_weights(kernel_ref, pair_ref)
    loads[1].wait()
    loads[2].wait()
    mover.ready()
    mean = stat_ref[0]
    inv = stat_ref[1]
    gain = gain_ref[...].astype(F32)
    bias = bias_ref[...].astype(F32)
    state = [jnp.zeros((images, chans), F32), jnp.zeros((images, chans), F32)]

    def take(col, values):
        hat = (xt_ref[col].astype(F32) - mean) * inv
        norm = hat * gain + bias
        sigma = sigmoid(norm)
        grad = values * (sigma * (1.0 + norm * (1.0 - sigma)))
        out_ref[col] = grad
        state[0] = state[0] + jnp.sum(grad, axis=0)
        state[1] = state[1] + jnp.sum(grad * hat, axis=0)

    for a, b in pieces(cols, 8):
        convolve(low_ref, pair_ref, True, rows, a, b, take)
        mover.put(out_ref.at[a:b], grad_far.at[a:b])
    plain, cross = state
    half = images // 2
    pay_ref[0:half] = pack_pair(group_total(plain * gain), group_total(cross * gain))
    rest = [jnp.sum(v, axis=0, keepdims=True) for v in (cross, plain)]
    short = pay_ref.shape[0] - half - 2
    pay_ref[half:] = jnp.concatenate(rest + [jnp.zeros((short, chans), F32)], axis=0)


CODE = 32767.0


def exponents(values):
    most = jnp.maximum(jnp.max(jnp.abs(values), axis=0, keepdims=True), 1e-30)
    return jnp.ceil(jnp.log2(most) + 1e-3)


def pack_terms(
    keep_one_ref, came_one_ref, keep_two_ref, came_two_ref, out_far, token_ref,
    one_ref, two_ref, extra_ref, rest_ref, out_ref, mover, extras_one, extras_two,
):
    chips, rows, chans = out_ref.shape
    taps = 9 * (chans // 2)
    share = -(-taps // chips)
    more = -(-(extras_one + extras_two) // chips)
    extra_ref[...] = jnp.zeros(extra_ref.shape, F32)
    one_ref[...] = keep_one_ref[...] + came_one_ref[...]
    two_ref[...] = keep_two_ref[...] + came_two_ref[...]
    extra_ref[0:extras_two] = two_ref[taps : taps + extras_two]
    extra_ref[extras_two : extras_two + extras_one] = one_ref[taps : taps + extras_one]
    token_ref[...] = extra_ref[0:8]
    powers = []
    for ref, count in ((one_ref, taps), (two_ref, taps), (extra_ref, extra_ref.shape[0])):
        values = ref[0:count]
        power = exponents(values)
        powers.append(power)
        scaled = values * (jnp.exp2(-power) * CODE)
        code = jnp.round(scaled)
        ref[0:count] = code
        if ref is extra_ref:
            rest_ref[...] = jnp.round((scaled - code) * (2.0 * CODE))
    short = rows - 2 * share - 2 * more - 3
    pad = [jnp.zeros((short, chans), F32)] if short else []
    for chip in range(chips):
        a, b = chip * share, min((chip + 1) * share, taps)
        mine = []
        for ref in (one_ref, two_ref):
            if a < b:
                mine.append(ref[a:b])
            if max(b - a, 0) < share:
                mine.append(jnp.zeros((share - max(b - a, 0), chans), F32))
        for ref in (extra_ref, rest_ref):
            mine.append(ref[chip * more : (chip + 1) * more])
        whole = jnp.concatenate(mine + powers + pad, axis=0)
        out_ref[chip] = whole.astype(jnp.int32).astype(jnp.int16)
    mover.put(out_ref, out_far)


def unpack_terms(gathered_ref, share, more):
    chips, rows, chans = gathered_ref.shape
    row = lax.broadcasted_iota(jnp.int32, (rows, chans), 0)
    base = 2 * share + 2 * more
    total = jnp.zeros((rows, chans), F32)
    for chip in range(chips):
        block = gathered_ref[chip].astype(jnp.int32).astype(F32)
        scales = jnp.exp2(block[base : base + 3]) * (1.0 / CODE)
        scale = jnp.where(row < share, scales[0:1], jnp.where(row < 2 * share, scales[1:2], scales[2:3]))
        scale = jnp.where(row < 2 * share + more, scale, scale * (0.5 / CODE))
        total = total + block * scale
    extra = total[2 * share : 2 * share + more] + total[2 * share + more : base]
    return total[0 : 2 * share], extra


def two_terms(values):
    high = values.astype(BF16).astype(F32)
    return [high, values - high]


def add_terms(gathered_ref, pay_ref, came_ref, out_far, out_ref, mover, more, whole):
    chips, rows, chans = gathered_ref.shape
    shares, extra = unpack_terms(gathered_ref, -(-9 * (chans // 2) // chips), more)
    every = [shares] + two_terms(extra) + two_terms(pay_ref[0:whole] + came_ref[0:whole])
    short = out_ref.shape[1] - sum(v.shape[0] for v in every)
    if short:
        every.append(jnp.zeros((short, chans), F32))
    out_ref[...] = jnp.broadcast_to(jnp.concatenate(every, axis=0).astype(BF16)[None], out_ref.shape)
    mover.put(out_ref, out_far)


def sums_of(own_ref, at, whole):
    total = own_ref[0].astype(F32)
    for chip in range(1, own_ref.shape[0]):
        total = total + own_ref[chip].astype(F32)
    return total[at : at + whole] + total[at + whole : at + 2 * whole]


def three_terms(values):
    high = values.astype(BF16)
    rest = values - high.astype(F32)
    mid = rest.astype(BF16)
    low = (rest - mid.astype(F32)).astype(BF16)
    return jnp.concatenate([high, mid, low], axis=0)


def spread_out(own_ref, other_ref, one_far, two_far, one_ref, two_ref, half_ref, mover):
    chips, rows, chans = own_ref.shape
    half = chans // 2
    taps = 9 * half
    share = -(-taps // chips)
    core = lax.axis_index("ha") % 2
    for at, (out_ref, far) in enumerate(((one_ref, one_far), (two_ref, two_far))):
        for source, place in ((own_ref, core), (other_ref, 1 - core)):
            for chip in range(chips):
                piece = source[chip].astype(F32)[at * share : (at + 1) * share]
                half_ref[chip * share : (chip + 1) * share] = piece
            for tap in range(9):
                rows_at = pl.ds(pl.multiple_of(place * half, half), half)
                out_ref[tap, rows_at] = half_ref[tap * half : (tap + 1) * half]
        mover.put(out_ref, far)


def last_grads(
    grad_far, xt_ref, c_ref, weight_ref, own_ref, stat_ref, gain_one_ref, gain_two_ref, bias_two_ref, film_ref, ints_ref, text_ref,
    out_far, weight_grad_far, text_grad_far, bias_ref, *refs, more, whole,
):
    *vec_refs, grad_ref, out_ref, weight_grad_ref, text_grad_ref, extra_ref, mover = refs
    images, rows, cols, chans = out_ref.shape
    chips = own_ref.shape[0]
    load = mover.start(grad_far, grad_ref)
    share = -(-9 * (chans // 2) // chips)
    start = 2 * share
    for chip in range(chips):
        piece = own_ref[chip].astype(F32)
        extra_ref[chip * more : (chip + 1) * more] = piece[start : start + more] + piece[start + more : start + 2 * more]
    plain = extra_ref[0:images]
    cross = extra_ref[images : 2 * images]
    mover.ready()
    scale = 1.0 + film_ref[:, 0:chans]
    scale_grad = gain_two_ref[...].astype(F32) * cross + bias_two_ref[...].astype(F32) * plain
    film_grad = jnp.concatenate([scale_grad, plain], axis=1)
    bias_ref[...] = jnp.sum(film_grad, axis=0, keepdims=True)
    sums = sums_of(own_ref, start + 2 * more, whole)
    vec_refs[0][...] = jnp.sum(scale * cross, axis=0, keepdims=True)
    vec_refs[1][...] = jnp.sum(scale * plain, axis=0, keepdims=True)
    for at, row in enumerate((extra_ref[2 * images : 2 * images + 1], extra_ref[2 * images + 1 : 2 * images + 2])):
        vec_refs[2 + at][...] = row
    vec_refs[4][...] = sums[whole - 2 : whole - 1]
    vec_refs[5][...] = sums[whole - 1 : whole]
    terms = three_terms(film_grad)
    ints = ints_ref.shape[1]

    depth = weight_grad_ref.shape[0]
    for at in range(0, depth, 512):
        if at < ints:
            act = ints_ref[:, at : at + 512]
        else:
            embed = text_ref[:, at - ints : at - ints + 512].astype(F32)
            act = (embed * sigmoid(embed)).astype(BF16)
        weight_grad_ref[at : at + 512] = lax.dot_general(
            jnp.concatenate([act, act, act], axis=0), terms, (((0,), (0,)), ((), ())), preferred_element_type=F32
        )
        mover.put(weight_grad_ref.at[at : at + 512], weight_grad_far.at[at : at + 512])

    count = lax.axis_size("ha") * lax.axis_size("wa") * rows * cols * (chans // GROUPS)
    packed = sums[0 : images // 2] * (1.0 / count)
    plain = unpack_at(packed, 0)
    cross = unpack_at(packed, 1)
    mean = stat_ref[0]
    inv = stat_ref[1]
    gain = gain_one_ref[...].astype(F32)
    load.wait()
    for a, b in pieces(rows, 2):
        for row in range(a, b):
            hat = (xt_ref[:, row].astype(F32) - mean) * inv
            path = jnp.swapaxes(inv * (grad_ref[:, row] * gain - plain - hat * cross), 0, 1)
            out_ref[:, row] = (c_ref[:, row].astype(F32) * INV_ROOT + path).astype(BF16)
        mover.put(out_ref.at[:, a:b], out_far.at[:, a:b])

    for at in range(ints, depth, 512):
        embed = text_ref[:, at - ints : at - ints + 512].astype(F32)
        sigma = sigmoid(embed)
        made = lax.dot_general(
            terms, weight_ref[at : at + 512], (((1,), (1,)), ((), ())), preferred_element_type=F32
        )
        cond_grad = made[0:images] + made[images : 2 * images] + made[2 * images :]
        text_grad_ref[:, at - ints : at - ints + 512] = cond_grad * (sigma * (1.0 + embed * (1.0 - sigma)))
    mover.put(text_grad_ref, text_grad_far)


def to_all(payload):
    return lax.all_to_all(payload, AXES, 0, 0)


def to_chips(payload):
    tall, wide = lax.axis_size("ha"), lax.axis_size("wa")
    groups = [[h * wide + w for h in range(core, tall, 2) for w in range(wide)] for core in range(2)]
    return lax.all_to_all(payload, AXES, 0, 0, axis_index_groups=groups)


def to_sibling(payload):
    return lax.ppermute(payload, "ha", [(i, i ^ 1) for i in range(lax.axis_size("ha"))])


def pair_exchange(one, other, axis):
    count = lax.axis_size(axis)
    pairs = [(i, (i + 1 if i % 2 else i - 1) % count) for i in range(count)]
    if axis == "wa":
        pairs = [(i, min(max(j, 0), count - 1) if abs(i - j) == 1 else i) for i, j in pairs]
    one = lax.ppermute(one, axis, [(i, i ^ 1) for i in range(count)])
    return one, lax.ppermute(other, axis, pairs)


def side_halo(sides, near, following, after=()):
    four, rows, images, chans = sides.shape
    edge = shaped((2, rows + 4, images, chans), sides.dtype)
    one, other = kernel_call(
        edge_columns, near=(sides, near, following), near_out=(edge, edge), cost=0.4, after=after, limit=16
    )
    return pair_exchange(one, other, "wa"), one


def local(
    block_input,
    timesteps,
    aug_levels,
    text_pooled,
    gain_one,
    bias_one,
    conv_one,
    conv_one_bias,
    gain_two,
    bias_two,
    film_weight,
    film_bias,
    conv_two,
    conv_two_bias,
    cotangent,
):
    images, rows, cols, chans = block_input.shape
    parts = lax.axis_size("ha") * lax.axis_size("wa")
    chips = parts // 2
    half = images // 2
    gain_one, bias_one, conv_one_bias, gain_two, bias_two, conv_two_bias = (
        v.reshape(1, chans) for v in (gain_one, bias_one, conv_one_bias, gain_two, bias_two, conv_two_bias)
    )
    freqs = np.exp(-math.log(10000.0) * np.arange(TEMB // 2) / (TEMB // 2)).astype(np.float32)[None]
    payload = shaped((parts, half, chans), F32)
    per_image = shaped((images, chans), F32)
    two_images = shaped((2, images, chans), F32)
    block = shaped((cols, rows, images, chans), BF16)
    block_wide = shaped((cols, rows, images, chans), F32)
    rim = shaped((cols + 2, rows + 2, images, chans), BF16)
    rim_wide = shaped((cols + 2, rows + 2, images, chans), F32)
    far_rim = shaped((cols + 4, rows + 4, images, chans), BF16)
    given = shaped((images, rows, cols, chans), BF16)
    pair = pltpu.VMEM((12 * chans, 2 * chans), BF16)
    pair_back = pltpu.VMEM((2 * chans, 12 * chans), BF16)

    sides = shaped((4, rows, images, chans), BF16)
    row_halo = shaped((cols, 2, images, chans), BF16)
    xt, x_near, x_next, x_sides, moments = kernel_call(
        prepare_x, far=(block_input,), far_out=(block,),
        near_out=(row_halo, row_halo, sides, shaped((half, chans), F32)),
        scratch=buffers(given, block), sems=16, cost=2.3,
    )
    x_near, x_next = pair_exchange(x_near, x_next, "ha")
    gt, pay_one, g_near, g_next, g_sides, kbias_two_local = kernel_call(
        prepare_g, far=(cotangent,), near=(moments,), far_out=(block, payload),
        near_out=(row_halo, row_halo, sides), tiny_out=(per_image,),
        scratch=buffers(given, block, payload), sems=16, cost=2.0,
    )
    moments_one = to_all(pay_one)
    x_cols, x_edge = side_halo(x_sides, x_near, x_next)
    g_near, g_next = pair_exchange(g_near, g_next, "ha")
    g_cols, g_edge = side_halo(g_sides, g_near, g_next)

    act_one, mid, pay_two, stat_one = kernel_call(
        first_half, far=(xt, conv_one), near=(x_near, x_next, *x_cols, moments_one),
        tiny=(gain_one, bias_one, conv_one_bias),
        far_out=(far_rim, rim_wide, payload), tiny_out=(two_images,),
        scratch=buffers(xt, conv_one, far_rim, rim_wide, payload) + (pair,), sems=16, cost=5.5,
        after_near=(g_edge,),
    )
    moments_two = to_all(pay_two)
    act_two_grad, film, act_ints = kernel_call(
        back_two, far=(gt, conv_two, film_weight), near=(g_near, g_next, *g_cols),
        tiny=(text_pooled, film_bias.reshape(1, 2 * chans), freqs), scalars=(timesteps, aug_levels),
        far_out=(rim_wide,), tiny_out=(shaped((images, 2 * chans), F32), shaped((images, 2 * TEMB), BF16)),
        scratch=buffers(gt, conv_two, film_weight, far_rim, rim_wide) + (pair_back,), sems=16, cost=5.0,
    )
    act_two, pre_two_grad, pay_three, sums_two, stat_two = kernel_call(
        second_norm, far=(mid, act_two_grad), near=(moments_two,), tiny=(gain_two, bias_two, film),
        far_out=(rim, rim_wide, payload), tiny_out=(two_images, two_images),
        scratch=buffers(rim_wide, rim_wide, rim, rim_wide, payload), sems=24, cost=3.2,
    )
    moments_three = to_all(pay_three)

    taps = 9 * (chans // 2)
    share = -(-taps // chips)
    extras_two = 2 * images + 1
    extras_one = 1
    halves_two = shaped((taps + 2 * images + 8, chans), F32)
    halves_one = shaped((taps + 8, chans), F32)
    keep_two, send_two = kernel_call(
        kernel_two, far=(act_two, gt), tiny=(sums_two, kbias_two_local), far_out=(halves_two, halves_two),
        scratch=buffers(act_two, gt, halves_two, halves_two), sems=4, cost=3.0,
    )
    came_two = to_sibling(send_two)
    low, keep_one, send_one, keep_two = kernel_call(
        middle_grad, far=(mid, pre_two_grad, act_one, keep_two), near=(moments_three,), tiny=(stat_two, gain_two, film),
        far_out=(rim,), near_out=(halves_one, halves_one, halves_two),
        scratch=buffers(mid, pre_two_grad, act_one, rim), sems=24, cost=6.0,
    )
    came_one = to_sibling(send_one)
    more = -(-(extras_one + extras_two) // chips)
    terms_shape = shaped((chips, -(-(2 * share + 2 * more + 3) // 8) * 8, chans), jnp.int16)
    extra_shape = shaped((-(-chips * more // 8) * 8, chans), F32)
    terms, token = kernel_call(
        functools.partial(pack_terms, extras_one=extras_one, extras_two=extras_two),
        near=(keep_one, came_one, keep_two, came_two), far_out=(terms_shape,), near_out=(shaped((8, chans), F32),),
        scratch=buffers(halves_one, halves_two, extra_shape, extra_shape, terms_shape),
        sems=3, cost=1.0,
    )
    gathered = to_chips(terms)
    whole = half + 2
    norm_one_grad, pay_four = kernel_call(
        back_one, far=(low, xt, conv_one), tiny=(stat_one, gain_one, bias_one), far_out=(block_wide,),
        near_out=(shaped((2 * half, chans), F32),),
        scratch=buffers(rim, block, conv_one, block_wide) + (pair_back,), sems=16, cost=5.0,
        after_near=(to_sibling(token),),
    )
    came_four = to_sibling(pay_four)
    (mixed,) = kernel_call(
        mix, far=(act_two, conv_two, xt), tiny=(conv_two_bias,), far_out=(given,),
        scratch=buffers(act_two, conv_two, xt, block_wide, given) + (pair,), sems=8, cost=3.6, after_near=(pay_four,),
    )
    shares_shape = shaped((chips, -(-(2 * share + 2 * more + 2 * whole) // 8) * 8, chans), BF16)
    (shares,) = kernel_call(
        functools.partial(add_terms, more=more, whole=whole),
        near=(gathered, pay_four, came_four), far_out=(shares_shape,),
        scratch=buffers(shares_shape), sems=1, cost=1.0, after=(mixed,),
    )
    own_half = to_chips(shares)
    other_half = to_sibling(own_half)
    weight_grad = shaped(film_weight.shape, F32)
    text_shape = shaped(text_pooled.shape, F32)
    row = shaped((1, chans), F32)
    input_grad, film_weight_grad, text_grad, film_bias_grad, *vec_grads = kernel_call(
        functools.partial(last_grads, more=more, whole=whole),
        far=(norm_one_grad,), near=(xt, cotangent, film_weight, own_half),
        tiny=(stat_one, gain_one, gain_two, bias_two, film, act_ints, text_pooled),
        far_out=(given, weight_grad, text_shape), tiny_out=(shaped((1, 2 * chans), F32),) + (row,) * 6,
        scratch=buffers(norm_one_grad, given, weight_grad, text_shape)
        + (pltpu.VMEM((-(-chips * more // 8) * 8, chans), F32),),
        sems=32, cost=6.0, limit=24,
    )
    full = shaped((9, chans, chans), F32)
    kernel_one_grad, kernel_two_grad = kernel_call(
        spread_out, near=(own_half, other_half), far_out=(full, full),
        scratch=buffers(full, full, shaped((chips * share, chans), F32)), sems=2, cost=2.0, after=(input_grad,), limit=24,
    )
    return (
        mixed,
        input_grad,
        text_grad,
        vec_grads[4].reshape(chans),
        vec_grads[5].reshape(chans),
        kernel_one_grad.reshape(3, 3, chans, chans),
        vec_grads[3].reshape(chans),
        vec_grads[0].reshape(chans),
        vec_grads[1].reshape(chans),
        film_weight_grad,
        film_bias_grad.reshape(2 * chans),
        kernel_two_grad.reshape(3, 3, chans, chans),
        vec_grads[2].reshape(chans),
    )


def solution(mesh):
    split = P(None, "ha", "wa", None)
    return jax.shard_map(
        local,
        mesh=mesh,
        in_specs=(split,) + (P(),) * 13 + (split,),
        out_specs=(split, split) + (P(),) * 11,
        check_vma=False,
    )
```

```python
import functools
import math

import jax
import jax.numpy as jnp
import numpy as np
from jax import lax
from jax.experimental import pallas as pl
from jax.experimental.pallas import tpu as pltpu
from jax.sharding import PartitionSpec as P

GROUPS = 32
TEMB = 256
EPSILON = 1e-05
INV_ROOT = 1.0 / math.sqrt(2.0)
AXES = ("ha", "wa")
F32 = jnp.float32
BF16 = jnp.bfloat16
NEAR = pl.BlockSpec(memory_space=pltpu.VMEM)
FAR = pl.BlockSpec(memory_space=pl.ANY)
MIB = 1 << 20


def shaped(shape, dtype):
    return jax.ShapeDtypeStruct(shape, dtype)


def kernel_call(
    body, far=(), near=(), tiny=(), far_out=(), near_out=(), tiny_out=(), scratch=(), sems=0, cost=1.0,
    after=(), after_near=(), scalars=(), limit=48,
):
    pinned = lambda arrays: [pltpu.with_memory_space_constraint(array, pltpu.HBM) for array in arrays]
    given = len(far) + len(near)
    held = len(after) + len(after_near)
    copies = len(tiny) + len(tiny_out)

    def run(*refs):
        refs = list(refs)
        take = lambda count: [refs.pop(0) for _ in range(count)]
        inputs = take(given)
        tiny_far = take(len(tiny))
        scalar_refs = take(len(scalars))
        take(held)
        outputs = take(len(far_out) + len(near_out))
        tiny_out_far = take(len(tiny_out))
        tiny_refs = take(len(tiny))
        tiny_out_refs = take(len(tiny_out))
        mover = None
        if sems + copies:
            mover = Mover(refs.pop(), [(f, n) for f, n in zip(tiny_far, tiny_refs)])
        body(*inputs, *tiny_refs, *scalar_refs, *outputs, *tiny_out_refs, *refs, *([mover] if mover else []))
        if mover:
            for source, target in zip(tiny_out_refs, tiny_out_far):
                mover.put(source, target)
            mover.finish()

    return pl.pallas_call(
        run,
        out_shape=(
            *(pltpu.HBM(out.shape, out.dtype) for out in far_out),
            *near_out,
            *(pltpu.HBM(out.shape, out.dtype) for out in tiny_out),
        ),
        in_specs=[FAR] * len(far)
        + [NEAR] * len(near)
        + [FAR] * len(tiny)
        + [pl.BlockSpec(memory_space=pltpu.SMEM)] * len(scalars)
        + [FAR] * held,
        out_specs=(FAR,) * len(far_out) + (NEAR,) * len(near_out) + (FAR,) * len(tiny_out),
        scratch_shapes=buffers(*tiny, *tiny_out)
        + tuple(scratch)
        + ((pltpu.SemaphoreType.DMA((sems + copies,)),) if sems + copies else ()),
        compiler_params=pltpu.CompilerParams(vmem_limit_bytes=limit * MIB),
        name=getattr(body, "func", body).__name__,
        cost_estimate=pl.CostEstimate(flops=int(cost * 1.1e9), bytes_accessed=0, transcendentals=0),
    )(*pinned(far), *near, *pinned(tiny), *scalars, *pinned(after), *after_near)


def buffers(*arrays):
    return tuple(pltpu.VMEM(a.shape, a.dtype) for a in arrays)


class Mover:
    def __init__(self, sems, first):
        self.sems = sems
        self.used = 0
        self.open = []
        self.first = [self.start(source, target) for source, target in first]

    def start(self, source, target):
        copy = pltpu.make_async_copy(source, target, self.sems.at[self.used])
        self.used += 1
        copy.start()
        return copy

    def ready(self):
        for copy in self.first:
            copy.wait()

    def put(self, source, target):
        self.open.append(self.start(source, target))

    def finish(self):
        for copy in self.open:
            copy.wait()


def pieces(count, size):
    return [(at, min(at + size, count)) for at in range(0, count, size)]


def lanes_of(shape):
    return lax.broadcasted_iota(jnp.int32, shape, 1)


def group_total(values):
    chans = values.shape[1]
    lane = lanes_of(values.shape)
    step = 1
    while step < chans // GROUPS:
        up = pltpu.roll(values, chans - step, 1)
        down = pltpu.roll(values, step, 1)
        values = values + jnp.where((lane & step) == 0, up, down)
        step *= 2
    return values


def pack_pair(first, second):
    half = first.shape[0] // 2
    lane = lanes_of((half, first.shape[1])) & 3
    return jnp.where(
        lane == 0,
        first[:half],
        jnp.where(lane == 1, second[:half], jnp.where(lane == 2, first[half:], second[half:])),
    )


def unpack_at(packed, place):
    lane = lanes_of(packed.shape) & 3
    top = group_total(jnp.where(lane == place, packed, 0.0))
    low = group_total(jnp.where(lane == place + 2, packed, 0.0))
    return jnp.concatenate([top, low], axis=0)


def merge_moments(gathered_ref, local_count):
    parts = gathered_ref.shape[0]
    chans = gathered_ref.shape[2]
    every = gathered_ref[...]
    total = jnp.sum(every, axis=0)
    mean = total * (1.0 / parts)
    apart = every - mean[None]
    between = jnp.sum(apart * apart, axis=0)
    square = pltpu.roll(total, chans - 1, 1) + local_count * between
    inv = lax.rsqrt(square * (1.0 / (local_count * parts)) + EPSILON)
    return unpack_at(mean, 0), unpack_at(inv, 0)


def local_moments(total, square, pilot, pixels, per):
    off = total * (1.0 / pixels)
    mean = pilot + off
    apart = square - total * off
    group_mean = group_total(mean) * (1.0 / per)
    shift = mean - group_mean
    return group_mean, group_total(apart + pixels * shift * shift)


def sigmoid(values):
    return 0.5 + 0.5 * jnp.tanh(0.5 * values)


def forward_weights(kernel_ref, pair_ref):
    chans = kernel_ref.shape[2]
    zero = jnp.zeros((chans, chans), BF16)
    for row in range(3):
        for col in range(4):
            at = (row * 4 + col) * chans
            pair_ref[at : at + chans, 0:chans] = kernel_ref[row, col] if col < 3 else zero
            pair_ref[at : at + chans, chans:] = kernel_ref[row, col - 1] if col > 0 else zero


def backward_weights(kernel_ref, pair_ref):
    chans = kernel_ref.shape[2]
    zero = jnp.zeros((chans, chans), BF16)
    for row in range(3):
        for col in range(4):
            at = (row * 4 + col) * chans
            pair_ref[0:chans, at : at + chans] = kernel_ref[2 - row, 2 - col] if col < 3 else zero
            pair_ref[chans:, at : at + chans] = kernel_ref[2 - row, 3 - col] if col > 0 else zero


def convolve(cells_ref, pair_ref, transposed, rows, first, last, take):
    images, chans = cells_ref.shape[2:]
    pairs = (last - first) // 2
    parts = []
    for row in range(3):
        for col in range(4):
            window = [cells_ref[first + 2 * q + col, row : row + rows] for q in range(pairs)]
            parts.append(jnp.stack(window).reshape(pairs * rows * images, chans))
    wide = jnp.concatenate(parts, axis=1)
    contract = ((1,), (1,)) if transposed else ((1,), (0,))
    made = lax.dot_general(wide, pair_ref[...], (contract, ((), ())), preferred_element_type=F32)
    made = made.reshape(pairs, rows, images, 2 * chans)
    for q in range(pairs):
        for side in range(2):
            take(first + 2 * q + side, made[q, :, :, side * chans : (side + 1) * chans])


def grad_terms(cells_ref, grads_ref):
    cols, rows, images, chans = grads_ref.shape
    pixels = cols * rows * images
    windows = [
        cells_ref[col : col + cols, row : row + rows].reshape(pixels, chans) for row in range(3) for col in range(3)
    ]
    return lax.dot_general(
        grads_ref[...].reshape(pixels, chans),
        jnp.concatenate(windows, axis=1),
        (((0,), (0,)), ((), ())),
        preferred_element_type=F32,
    )


def split_taps(every, keep_ref, send_ref):
    chans = every.shape[0]
    half = chans // 2
    first = lax.axis_index("ha") % 2 == 0
    for tap in range(9):
        made = every[:, tap * chans : (tap + 1) * chans].T
        at = tap * half
        keep_ref[at : at + half, :] = jnp.where(first, made[:half], made[half:])
        send_ref[at : at + half, :] = jnp.where(first, made[half:], made[:half])


def at_edges():
    tall = lax.axis_index("ha")
    wide = lax.axis_index("wa")
    return (
        tall == 0,
        tall == lax.axis_size("ha") - 1,
        wide == 0,
        wide == lax.axis_size("wa") - 1,
    )


def clear_border(cells_ref, width, first=0, last=None):
    top, bottom, left, right = at_edges()
    cols, rows, images, chans = cells_ref.shape
    last = cols if last is None else last
    dtype = cells_ref.dtype

    @pl.when(top)
    def _():
        cells_ref[first:last, 0:width] = jnp.zeros((last - first, width, images, chans), dtype)

    @pl.when(bottom)
    def _():
        cells_ref[first:last, rows - width :] = jnp.zeros((last - first, width, images, chans), dtype)

    if first == 0:

        @pl.when(left)
        def _():
            cells_ref[0:width] = jnp.zeros((width, rows, images, chans), dtype)

    if last == cols:

        @pl.when(right)
        def _():
            cells_ref[cols - width :] = jnp.zeros((width, rows, images, chans), dtype)


def send_payload(mover, packed, pay_ref, stage_ref):
    stage_ref[...] = jnp.broadcast_to(packed[None], stage_ref.shape)
    mover.put(stage_ref, pay_ref)


def prepare_x(x_far, xt_far, near_ref, next_ref, sides_ref, moments_ref, x_ref, xt_ref, mover):
    images, rows, cols, chans = x_ref.shape
    steps = pieces(rows, 2)
    loads = [mover.start(x_far.at[:, a:b], x_ref.at[:, a:b]) for a, b in steps]
    total = jnp.zeros((images, chans), F32)
    square = total
    for (a, b), load in zip(steps, loads):
        load.wait()
        if a == 0:
            pilot = x_ref[:, 0, 0].astype(F32)
        for row in range(a, b):
            x = jnp.swapaxes(x_ref[:, row].astype(F32), 0, 1)
            xt_ref[:, row] = x.astype(BF16)
            apart = x - pilot[None]
            total = total + jnp.sum(apart, axis=0)
            square = square + jnp.sum(apart * apart, axis=0)
        mover.put(xt_ref.at[:, a:b], xt_far.at[:, a:b])
    mean, spread = local_moments(total, square, pilot, rows * cols, chans // GROUPS)
    moments_ref[...] = pack_pair(mean, spread)
    outer(xt_ref, near_ref, next_ref, sides_ref)


def is_even(axis="ha"):
    return lax.axis_index(axis) % 2 == 0


def outer(cells, near_ref, next_ref, sides_ref):
    cols, rows = cells.shape[0:2]
    down, up = cells[:, rows - 2 :], cells[:, 0:2]
    near_ref[...] = jnp.where(is_even(), down, up)
    next_ref[...] = jnp.where(is_even(), up, down)
    sides_ref[0:2] = cells[0:2]
    sides_ref[2:4] = cells[cols - 2 :]


def prepare_g(
    c_far, moments_ref, gt_far, pay_far, near_ref, next_ref, sides_ref, bias_ref, c_ref, gt_ref, stage_ref, mover
):
    images, rows, cols, chans = c_ref.shape
    steps = pieces(rows, 2)
    loads = [mover.start(c_far.at[:, a:b], c_ref.at[:, a:b]) for a, b in steps]
    send_payload(mover, moments_ref[...], pay_far, stage_ref)
    bias = jnp.zeros((images, chans), F32)
    for (a, b), load in zip(steps, loads):
        load.wait()
        for row in range(a, b):
            grad = jnp.swapaxes(c_ref[:, row].astype(F32) * INV_ROOT, 0, 1).astype(BF16)
            gt_ref[:, row] = grad
            bias = bias + jnp.sum(grad.astype(F32), axis=0)
        mover.put(gt_ref.at[:, a:b], gt_far.at[:, a:b])
    bias_ref[...] = bias
    outer(gt_ref, near_ref, next_ref, sides_ref)


def edge_columns(sides_ref, near_ref, next_ref, one_ref, other_ref):
    cols, rows = near_ref.shape[0], sides_ref.shape[1]
    even = is_even("wa")

    def piece(left, right):
        return jnp.where(even, right, left), jnp.where(even, left, right)

    near = piece(near_ref[0:2], near_ref[cols - 2 : cols])
    following = piece(next_ref[0:2], next_ref[cols - 2 : cols])
    own = piece(sides_ref[0:2], sides_ref[2:4])
    for at, ref in enumerate((one_ref, other_ref)):
        ref[:, 0:2] = jnp.where(is_even(), following[at], near[at])
        ref[:, 2 : rows + 2] = own[at]
        ref[:, rows + 2 :] = jnp.where(is_even(), near[at], following[at])


def fill_halo(cells_ref, near_ref, next_ref, one_ref, other_ref, change):
    cols, rows = near_ref.shape[0], cells_ref.shape[1] - 4

    def halo_column(col, _):
        near, next_ = near_ref[pl.ds(col, 1)], next_ref[pl.ds(col, 1)]
        cells_ref[pl.ds(col + 2, 1), 0:2] = change(jnp.where(is_even(), next_, near))
        cells_ref[pl.ds(col + 2, 1), rows + 2 :] = change(jnp.where(is_even(), near, next_))
        return 0

    even = is_even("wa")
    cells_ref[0:2] = change(jnp.where(even, other_ref[...], one_ref[...]))
    cells_ref[cols + 2 :] = change(jnp.where(even, one_ref[...], other_ref[...]))
    lax.fori_loop(0, cols, halo_column, 0, unroll=4)


def first_half(
    xt_far, kernel_far, near_ref, next_ref, one_ref, other_ref, gathered_ref, gain_ref, bias_ref, kbias_ref,
    act_far, mid_far, pay_far, stat_ref,
    xt_ref, kernel_ref, act_ref, mid_ref, stage_ref, pair_ref, mover,
):
    cols, rows, images, chans = xt_ref.shape
    per = chans // GROUPS
    load = mover.start(kernel_far, kernel_ref)
    steps = pieces(cols, 8)
    own = [mover.start(xt_far.at[a:b], xt_ref.at[a:b]) for a, b in steps]
    mean, inv = merge_moments(gathered_ref, rows * cols * per)
    stat_ref[0] = mean
    stat_ref[1] = inv
    mover.ready()
    slope = 0.5 * inv * gain_ref[...].astype(F32)
    offset = 0.5 * bias_ref[...].astype(F32)

    def act(cells):
        value = (cells.astype(F32) - mean) * slope + offset
        return (value + value * jnp.tanh(value)).astype(BF16)

    def column(col, _):
        act_ref[pl.ds(col + 2, 1), 2 : rows + 2] = act(xt_ref[pl.ds(col, 1)])
        return 0

    fill_halo(act_ref, near_ref, next_ref, one_ref, other_ref, act)
    for (a, b), copy in zip(steps, own):
        copy.wait()
        lax.fori_loop(a, b, column, 0, unroll=2)
    clear_border(act_ref, 2)
    load.wait()
    forward_weights(kernel_ref, pair_ref)
    mover.put(act_ref, act_far)

    wide = cols + 2
    kbias = kbias_ref[...].astype(F32)
    state = [None, jnp.zeros((images, chans), F32), jnp.zeros((images, chans), F32)]

    def take(col, values):
        values = values + kbias
        mid_ref[col] = values
        if 1 <= col <= cols:
            own = values[1 : rows + 1]
            if state[0] is None:
                state[0] = own[0]
            apart = own - state[0][None]
            state[1] = state[1] + jnp.sum(apart, axis=0)
            state[2] = state[2] + jnp.sum(apart * apart, axis=0)

    for a, b in pieces(wide, 10):
        convolve(act_ref, pair_ref, False, rows + 2, a, b, take)
        mover.put(mid_ref.at[a:b], mid_far.at[a:b])
    pilot, total, square = state
    mean, spread = local_moments(total, square, pilot, rows * cols, per)
    send_payload(mover, pack_pair(mean, spread), pay_far, stage_ref)


def back_two(
    gt_far, kernel_far, weight_far, near_ref, next_ref, one_ref, other_ref, *refs,
):
    text_ref, fbias_ref, freqs_ref, times_ref, levels_ref, out_far, film_ref, ints_ref, *refs = refs
    gt_ref, kernel_ref, weight_ref, cells_ref, out_ref, pair_ref, mover = refs
    cols, rows = gt_ref.shape[0:2]
    load = mover.start(kernel_far, kernel_ref)
    steps = pieces(cols, 8)
    own = [mover.start(gt_far.at[a:b], gt_ref.at[a:b]) for a, b in steps]
    late = mover.start(weight_far, weight_ref)
    fill_halo(cells_ref, near_ref, next_ref, one_ref, other_ref, lambda cells: cells)
    load.wait()
    backward_weights(kernel_ref, pair_ref)
    mover.ready()
    text = text_ref[...].astype(F32)
    half = TEMB // 2
    for at, source_ref in ((0, times_ref), (TEMB, levels_ref)):
        angles = [source_ref[image].astype(F32) * freqs_ref[...] for image in range(text_ref.shape[0])]
        angles = jnp.concatenate(angles, axis=0)
        for start, embed in ((at, jnp.sin(angles)), (at + half, jnp.cos(angles))):
            ints_ref[:, start : start + half] = (embed * sigmoid(embed)).astype(BF16)
    act = jnp.concatenate([ints_ref[...], (text * sigmoid(text)).astype(BF16)], axis=1)
    for (a, b), copy in zip(steps, own):
        copy.wait()
        cells_ref[a + 2 : b + 2, 2 : rows + 2] = gt_ref[a:b]
    clear_border(cells_ref, 2)
    for a, b in pieces(cols + 2, 10):
        convolve(cells_ref, pair_ref, True, rows + 2, a, b, lambda col, values: out_ref.__setitem__(col, values))
        mover.put(out_ref.at[a:b], out_far.at[a:b])
    late.wait()
    film_ref[...] = jnp.dot(act, weight_ref[...], preferred_element_type=F32) + fbias_ref[...].astype(F32)


def second_values(stat, gain_ref, bias_ref, film_ref):
    mean, inv = stat
    chans = mean.shape[1]
    scale = 1.0 + film_ref[:, 0:chans]
    slope = gain_ref[...].astype(F32) * scale
    half_slope = 0.5 * slope
    half_offset = 0.5 * (bias_ref[...].astype(F32) * scale + film_ref[:, chans:])

    def values(mid, back):
        hat = (mid - mean) * inv
        pre = hat * half_slope + half_offset
        bend = jnp.tanh(pre)
        more = 1.0 + bend
        grad = back * (0.5 * more * (1.0 + pre * (1.0 - bend)))
        return hat, pre * more, grad

    return slope, values


def second_norm(
    mid_far, back_far, gathered_ref, gain_ref, bias_ref, film_ref,
    act_far, pre_far, pay_far, sums_ref, stat_ref,
    mid_ref, back_ref, act_ref, pre_ref, stage_ref, mover,
):
    wide, tall, images, chans = mid_ref.shape
    cols, rows = wide - 2, tall - 2
    per = chans // GROUPS
    steps = pieces(wide, 9)
    loads = []
    for a, b in steps:
        loads.append(
            [mover.start(f.at[a:b], n.at[a:b]) for f, n in ((mid_far, mid_ref), (back_far, back_ref))]
        )
    mean, inv = merge_moments(gathered_ref, rows * cols * per)
    stat_ref[0] = mean
    stat_ref[1] = inv
    mover.ready()
    slope, values = second_values((mean, inv), gain_ref, bias_ref, film_ref)

    def column(col, inner):
        hat, act, grad = values(mid_ref[col], back_ref[col])
        act_ref[col] = act.astype(BF16)
        pre_ref[col] = grad
        if inner is None:
            return None
        own = grad[1 : rows + 1]
        plain, cross = inner
        return plain + jnp.sum(own, axis=0), cross + jnp.sum(own * hat[1 : rows + 1], axis=0)

    zero = jnp.zeros((images, chans), F32)
    inner = (zero, zero)
    for (a, b), pair in zip(steps, loads):
        for load in pair:
            load.wait()
        if a == 0:
            column(0, None)
        inner = lax.fori_loop(max(a, 1), min(b, cols + 1), column, inner)
        if b == wide:
            column(wide - 1, None)
        clear_border(act_ref, 1, a, b)
        mover.put(act_ref.at[a:b], act_far.at[a:b])
        mover.put(pre_ref.at[a:b], pre_far.at[a:b])
    plain, cross = inner
    sums_ref[0] = plain
    sums_ref[1] = cross
    send_payload(mover, pack_pair(group_total(plain * slope), group_total(cross * slope)), pay_far, stage_ref)


def kernel_two(
    act_far, gt_far, sums_ref, bias_ref, keep_far, send_far, act_ref, gt_ref, keep_ref, send_ref, mover
):
    for load in [mover.start(act_far, act_ref), mover.start(gt_far, gt_ref)]:
        load.wait()
    split_taps(grad_terms(act_ref, gt_ref), keep_ref, send_ref)
    mover.ready()
    images, chans = bias_ref.shape
    at = 9 * (chans // 2)
    total = jnp.sum(bias_ref[...], axis=0, keepdims=True)
    for ref in (keep_ref, send_ref):
        ref[at : at + images] = sums_ref[0]
        ref[at + images : at + 2 * images] = sums_ref[1]
        ref[at + 2 * images :] = jnp.broadcast_to(total, (ref.shape[0] - at - 2 * images, chans))
    mover.put(keep_ref, keep_far)
    mover.put(send_ref, send_far)


def mix(
    act_far, kernel_far, xt_far, kbias_ref, out_far, act_ref, kernel_ref, xt_ref, branch_ref, out_ref, pair_ref, mover
):
    images, rows, cols, chans = out_ref.shape
    loads = [mover.start(f, n) for f, n in ((kernel_far, kernel_ref), (act_far, act_ref), (xt_far, xt_ref))]
    for load in loads:
        load.wait()
    forward_weights(kernel_ref, pair_ref)
    mover.ready()
    kbias = kbias_ref[...].astype(F32)
    convolve(
        act_ref, pair_ref, False, rows, 0, cols, lambda col, values: branch_ref.__setitem__(col, values + kbias)
    )
    for a, b in pieces(rows, 4):
        for row in range(a, b):
            mixed = jnp.swapaxes((xt_ref[:, row].astype(F32) + branch_ref[:, row]) * INV_ROOT, 0, 1)
            out_ref[:, row] = mixed.astype(BF16)
        mover.put(out_ref.at[:, a:b], out_far.at[:, a:b])


def middle_grad(
    mid_far, pre_far, act_far, keep_two_far, gathered_ref, stat_ref, gain_ref, film_ref,
    low_far, keep_ref, send_ref, two_ref,
    mid_ref, pre_ref, act_ref, low_ref, mover,
):
    wide, tall, images, chans = mid_ref.shape
    cols, rows = wide - 2, tall - 2
    steps = pieces(wide, 9)
    loads = []
    for a, b in steps:
        loads.append([mover.start(f.at[a:b], n.at[a:b]) for f, n in ((mid_far, mid_ref), (pre_far, pre_ref))])
    late = [mover.start(f, n) for f, n in ((act_far, act_ref), (keep_two_far, two_ref))]
    count = lax.axis_size("ha") * lax.axis_size("wa") * rows * cols * (chans // GROUPS)
    packed = jnp.sum(gathered_ref[...], axis=0) * (1.0 / count)
    mover.ready()
    mean = stat_ref[0]
    inv = stat_ref[1]
    plain = unpack_at(packed, 0) * inv
    cross = unpack_at(packed, 1) * inv * inv
    slope = gain_ref[...].astype(F32) * (1.0 + film_ref[:, 0:chans]) * inv

    def low_column(col, total):
        low = (pre_ref[col] * slope - plain - (mid_ref[col] - mean) * cross).astype(BF16)
        low_ref[col] = low
        if total is None:
            return None
        return total + jnp.sum(low[1 : rows + 1].astype(F32), axis=0)

    kbias = jnp.zeros((images, chans), F32)
    for (a, b), pair in zip(steps, loads):
        for load in pair:
            load.wait()
        if a == 0:
            low_column(0, None)
        kbias = lax.fori_loop(max(a, 1), min(b, cols + 1), low_column, kbias)
        if b == wide:
            low_column(wide - 1, None)
        clear_border(low_ref, 1, a, b)
        mover.put(low_ref.at[a:b], low_far.at[a:b])
    for load in late:
        load.wait()
    own = low_ref.at[1 : wide - 1, 1 : tall - 1]
    split_taps(grad_terms(act_ref.at[1 : wide + 1, 1 : tall + 1], own), keep_ref, send_ref)
    at = 9 * (chans // 2)
    for ref in (keep_ref, send_ref):
        ref[at:] = jnp.broadcast_to(jnp.sum(kbias, axis=0, keepdims=True), (ref.shape[0] - at, chans))


def back_one(
    low_far, xt_far, kernel_far, stat_ref, gain_ref, bias_ref, grad_far, pay_ref, low_ref, xt_ref, kernel_ref, out_ref, pair_ref, mover
):
    cols, rows, images, chans = xt_ref.shape
    loads = [mover.start(f, n) for f, n in ((kernel_far, kernel_ref), (low_far, low_ref), (xt_far, xt_ref))]
    loads[0].wait()
    backward_weights(kernel_ref, pair_ref)
    loads[1].wait()
    loads[2].wait()
    mover.ready()
    mean = stat_ref[0]
    inv = stat_ref[1]
    gain = gain_ref[...].astype(F32)
    bias = bias_ref[...].astype(F32)
    state = [jnp.zeros((images, chans), F32), jnp.zeros((images, chans), F32)]

    def take(col, values):
        hat = (xt_ref[col].astype(F32) - mean) * inv
        norm = hat * gain + bias
        sigma = sigmoid(norm)
        grad = values * (sigma * (1.0 + norm * (1.0 - sigma)))
        out_ref[col] = grad
        state[0] = state[0] + jnp.sum(grad, axis=0)
        state[1] = state[1] + jnp.sum(grad * hat, axis=0)

    for a, b in pieces(cols, 8):
        convolve(low_ref, pair_ref, True, rows, a, b, take)
        mover.put(out_ref.at[a:b], grad_far.at[a:b])
    plain, cross = state
    half = images // 2
    pay_ref[0:half] = pack_pair(group_total(plain * gain), group_total(cross * gain))
    rest = [jnp.sum(v, axis=0, keepdims=True) for v in (cross, plain)]
    short = pay_ref.shape[0] - half - 2
    pay_ref[half:] = jnp.concatenate(rest + [jnp.zeros((short, chans), F32)], axis=0)


CODE = 32767.0


def exponents(values):
    most = jnp.maximum(jnp.max(jnp.abs(values), axis=0, keepdims=True), 1e-30)
    return jnp.ceil(jnp.log2(most) + 1e-3)


def pack_terms(
    keep_one_ref, came_one_ref, keep_two_ref, came_two_ref, out_far, token_ref,
    one_ref, two_ref, extra_ref, rest_ref, out_ref, mover, extras_one, extras_two,
):
    chips, rows, chans = out_ref.shape
    taps = 9 * (chans // 2)
    share = -(-taps // chips)
    more = -(-(extras_one + extras_two) // chips)
    extra_ref[...] = jnp.zeros(extra_ref.shape, F32)
    one_ref[...] = keep_one_ref[...] + came_one_ref[...]
    two_ref[...] = keep_two_ref[...] + came_two_ref[...]
    extra_ref[0:extras_two] = two_ref[taps : taps + extras_two]
    extra_ref[extras_two : extras_two + extras_one] = one_ref[taps : taps + extras_one]
    token_ref[...] = extra_ref[0:8]
    powers = []
    for ref, count in ((one_ref, taps), (two_ref, taps), (extra_ref, extra_ref.shape[0])):
        values = ref[0:count]
        power = exponents(values)
        powers.append(power)
        scaled = values * (jnp.exp2(-power) * CODE)
        code = jnp.round(scaled)
        ref[0:count] = code
        if ref is extra_ref:
            rest_ref[...] = jnp.round((scaled - code) * (2.0 * CODE))
    short = rows - 2 * share - 2 * more - 3
    pad = [jnp.zeros((short, chans), F32)] if short else []
    for chip in range(chips):
        a, b = chip * share, min((chip + 1) * share, taps)
        mine = []
        for ref in (one_ref, two_ref):
            if a < b:
                mine.append(ref[a:b])
            if max(b - a, 0) < share:
                mine.append(jnp.zeros((share - max(b - a, 0), chans), F32))
        for ref in (extra_ref, rest_ref):
            mine.append(ref[chip * more : (chip + 1) * more])
        whole = jnp.concatenate(mine + powers + pad, axis=0)
        out_ref[chip] = whole.astype(jnp.int32).astype(jnp.int16)
    mover.put(out_ref, out_far)


def unpack_terms(gathered_ref, share, more):
    chips, rows, chans = gathered_ref.shape
    row = lax.broadcasted_iota(jnp.int32, (rows, chans), 0)
    base = 2 * share + 2 * more
    total = jnp.zeros((rows, chans), F32)
    for chip in range(chips):
        block = gathered_ref[chip].astype(jnp.int32).astype(F32)
        scales = jnp.exp2(block[base : base + 3]) * (1.0 / CODE)
        scale = jnp.where(row < share, scales[0:1], jnp.where(row < 2 * share, scales[1:2], scales[2:3]))
        scale = jnp.where(row < 2 * share + more, scale, scale * (0.5 / CODE))
        total = total + block * scale
    extra = total[2 * share : 2 * share + more] + total[2 * share + more : base]
    return total[0 : 2 * share], extra


def two_terms(values):
    high = values.astype(BF16).astype(F32)
    return [high, values - high]


def add_terms(gathered_ref, pay_ref, came_ref, out_far, out_ref, mover, more, whole):
    chips, rows, chans = gathered_ref.shape
    shares, extra = unpack_terms(gathered_ref, -(-9 * (chans // 2) // chips), more)
    every = [shares] + two_terms(extra) + two_terms(pay_ref[0:whole] + came_ref[0:whole])
    short = out_ref.shape[1] - sum(v.shape[0] for v in every)
    if short:
        every.append(jnp.zeros((short, chans), F32))
    out_ref[...] = jnp.broadcast_to(jnp.concatenate(every, axis=0).astype(BF16)[None], out_ref.shape)
    mover.put(out_ref, out_far)


def sums_of(own_ref, at, whole):
    total = own_ref[0].astype(F32)
    for chip in range(1, own_ref.shape[0]):
        total = total + own_ref[chip].astype(F32)
    return total[at : at + whole] + total[at + whole : at + 2 * whole]


def three_terms(values):
    high = values.astype(BF16)
    rest = values - high.astype(F32)
    mid = rest.astype(BF16)
    low = (rest - mid.astype(F32)).astype(BF16)
    return jnp.concatenate([high, mid, low], axis=0)


def spread_out(own_ref, other_ref, one_far, two_far, one_ref, two_ref, half_ref, mover):
    chips, rows, chans = own_ref.shape
    half = chans // 2
    taps = 9 * half
    share = -(-taps // chips)
    core = lax.axis_index("ha") % 2
    for at, (out_ref, far) in enumerate(((one_ref, one_far), (two_ref, two_far))):
        for source, place in ((own_ref, core), (other_ref, 1 - core)):
            for chip in range(chips):
                piece = source[chip].astype(F32)[at * share : (at + 1) * share]
                half_ref[chip * share : (chip + 1) * share] = piece
            for tap in range(9):
                rows_at = pl.ds(pl.multiple_of(place * half, half), half)
                out_ref[tap, rows_at] = half_ref[tap * half : (tap + 1) * half]
        mover.put(out_ref, far)


def last_grads(
    weight_far, grad_ref, xt_ref, c_ref, own_ref, stat_ref, gain_one_ref, gain_two_ref, bias_two_ref, film_ref, ints_ref, text_ref,
    out_far, weight_grad_far, text_grad_far, bias_ref, *refs, more, whole,
):
    *vec_refs, weight_ref, out_ref, weight_grad_ref, text_grad_ref, extra_ref, mover = refs
    images, rows, cols, chans = out_ref.shape
    chips = own_ref.shape[0]
    load = mover.start(weight_far, weight_ref)
    share = -(-9 * (chans // 2) // chips)
    start = 2 * share
    for chip in range(chips):
        piece = own_ref[chip].astype(F32)
        extra_ref[chip * more : (chip + 1) * more] = piece[start : start + more] + piece[start + more : start + 2 * more]
    plain = extra_ref[0:images]
    cross = extra_ref[images : 2 * images]
    mover.ready()
    scale = 1.0 + film_ref[:, 0:chans]
    scale_grad = gain_two_ref[...].astype(F32) * cross + bias_two_ref[...].astype(F32) * plain
    film_grad = jnp.concatenate([scale_grad, plain], axis=1)
    bias_ref[...] = jnp.sum(film_grad, axis=0, keepdims=True)
    sums = sums_of(own_ref, start + 2 * more, whole)
    vec_refs[0][...] = jnp.sum(scale * cross, axis=0, keepdims=True)
    vec_refs[1][...] = jnp.sum(scale * plain, axis=0, keepdims=True)
    for at, row in enumerate((extra_ref[2 * images : 2 * images + 1], extra_ref[2 * images + 1 : 2 * images + 2])):
        vec_refs[2 + at][...] = row
    vec_refs[4][...] = sums[whole - 2 : whole - 1]
    vec_refs[5][...] = sums[whole - 1 : whole]
    terms = three_terms(film_grad)
    ints = ints_ref.shape[1]

    depth = weight_grad_ref.shape[0]
    for at in range(0, depth, 512):
        if at < ints:
            act = ints_ref[:, at : at + 512]
        else:
            embed = text_ref[:, at - ints : at - ints + 512].astype(F32)
            act = (embed * sigmoid(embed)).astype(BF16)
        weight_grad_ref[at : at + 512] = lax.dot_general(
            jnp.concatenate([act, act, act], axis=0), terms, (((0,), (0,)), ((), ())), preferred_element_type=F32
        )
        mover.put(weight_grad_ref.at[at : at + 512], weight_grad_far.at[at : at + 512])

    count = lax.axis_size("ha") * lax.axis_size("wa") * rows * cols * (chans // GROUPS)
    packed = sums[0 : images // 2] * (1.0 / count)
    plain = unpack_at(packed, 0)
    cross = unpack_at(packed, 1)
    mean = stat_ref[0]
    inv = stat_ref[1]
    gain = gain_one_ref[...].astype(F32)
    for a, b in pieces(rows, 2):
        for row in range(a, b):
            hat = (xt_ref[:, row].astype(F32) - mean) * inv
            path = jnp.swapaxes(inv * (grad_ref[:, row] * gain - plain - hat * cross), 0, 1)
            out_ref[:, row] = (c_ref[:, row].astype(F32) * INV_ROOT + path).astype(BF16)
        mover.put(out_ref.at[:, a:b], out_far.at[:, a:b])

    load.wait()
    for at in range(ints, depth, 512):
        embed = text_ref[:, at - ints : at - ints + 512].astype(F32)
        sigma = sigmoid(embed)
        made = lax.dot_general(
            terms, weight_ref[at : at + 512], (((1,), (1,)), ((), ())), preferred_element_type=F32
        )
        cond_grad = made[0:images] + made[images : 2 * images] + made[2 * images :]
        text_grad_ref[:, at - ints : at - ints + 512] = cond_grad * (sigma * (1.0 + embed * (1.0 - sigma)))
    mover.put(text_grad_ref, text_grad_far)


def to_all(payload):
    return lax.all_to_all(payload, AXES, 0, 0)


def to_chips(payload):
    tall, wide = lax.axis_size("ha"), lax.axis_size("wa")
    groups = [[h * wide + w for h in range(core, tall, 2) for w in range(wide)] for core in range(2)]
    return lax.all_to_all(payload, AXES, 0, 0, axis_index_groups=groups)


def to_sibling(payload):
    return lax.ppermute(payload, "ha", [(i, i ^ 1) for i in range(lax.axis_size("ha"))])


def pair_exchange(one, other, axis):
    count = lax.axis_size(axis)
    pairs = [(i, (i + 1 if i % 2 else i - 1) % count) for i in range(count)]
    if axis == "wa":
        pairs = [(i, min(max(j, 0), count - 1) if abs(i - j) == 1 else i) for i, j in pairs]
    one = lax.ppermute(one, axis, [(i, i ^ 1) for i in range(count)])
    return one, lax.ppermute(other, axis, pairs)


def side_halo(sides, near, following, after=()):
    four, rows, images, chans = sides.shape
    edge = shaped((2, rows + 4, images, chans), sides.dtype)
    one, other = kernel_call(
        edge_columns, near=(sides, near, following), near_out=(edge, edge), cost=0.4, after=after, limit=16
    )
    return pair_exchange(one, other, "wa"), one


def local(
    block_input,
    timesteps,
    aug_levels,
    text_pooled,
    gain_one,
    bias_one,
    conv_one,
    conv_one_bias,
    gain_two,
    bias_two,
    film_weight,
    film_bias,
    conv_two,
    conv_two_bias,
    cotangent,
):
    images, rows, cols, chans = block_input.shape
    parts = lax.axis_size("ha") * lax.axis_size("wa")
    chips = parts // 2
    half = images // 2
    gain_one, bias_one, conv_one_bias, gain_two, bias_two, conv_two_bias = (
        v.reshape(1, chans) for v in (gain_one, bias_one, conv_one_bias, gain_two, bias_two, conv_two_bias)
    )
    freqs = np.exp(-math.log(10000.0) * np.arange(TEMB // 2) / (TEMB // 2)).astype(np.float32)[None]
    payload = shaped((parts, half, chans), F32)
    per_image = shaped((images, chans), F32)
    two_images = shaped((2, images, chans), F32)
    block = shaped((cols, rows, images, chans), BF16)
    block_wide = shaped((cols, rows, images, chans), F32)
    rim = shaped((cols + 2, rows + 2, images, chans), BF16)
    rim_wide = shaped((cols + 2, rows + 2, images, chans), F32)
    far_rim = shaped((cols + 4, rows + 4, images, chans), BF16)
    given = shaped((images, rows, cols, chans), BF16)
    pair = pltpu.VMEM((12 * chans, 2 * chans), BF16)
    pair_back = pltpu.VMEM((2 * chans, 12 * chans), BF16)

    sides = shaped((4, rows, images, chans), BF16)
    row_halo = shaped((cols, 2, images, chans), BF16)
    xt, x_near, x_next, x_sides, moments = kernel_call(
        prepare_x, far=(block_input,), far_out=(block,),
        near_out=(row_halo, row_halo, sides, shaped((half, chans), F32)),
        scratch=buffers(given, block), sems=16, cost=2.3,
    )
    x_near, x_next = pair_exchange(x_near, x_next, "ha")
    gt, pay_one, g_near, g_next, g_sides, kbias_two_local = kernel_call(
        prepare_g, far=(cotangent,), near=(moments,), far_out=(block, payload),
        near_out=(row_halo, row_halo, sides), tiny_out=(per_image,),
        scratch=buffers(given, block, payload), sems=16, cost=2.0,
    )
    moments_one = to_all(pay_one)
    x_cols, x_edge = side_halo(x_sides, x_near, x_next)
    g_near, g_next = pair_exchange(g_near, g_next, "ha")

    film_bias = film_bias.reshape(1, 2 * chans)
    act_one, mid, pay_two, stat_one = kernel_call(
        first_half, far=(xt, conv_one), near=(x_near, x_next, *x_cols, moments_one),
        tiny=(gain_one, bias_one, conv_one_bias),
        far_out=(far_rim, rim_wide, payload), tiny_out=(two_images,),
        scratch=buffers(xt, conv_one, far_rim, rim_wide, payload) + (pair,), sems=16, cost=5.5,
        after=(film_bias,),
    )
    moments_two = to_all(pay_two)
    g_cols, _ = side_halo(g_sides, g_near, g_next, after=(stat_one,))
    act_two_grad, film, act_ints = kernel_call(
        back_two, far=(gt, conv_two, film_weight), near=(g_near, g_next, *g_cols),
        tiny=(text_pooled, film_bias, freqs), scalars=(timesteps, aug_levels),
        far_out=(rim_wide,), tiny_out=(shaped((images, 2 * chans), F32), shaped((images, 2 * TEMB), BF16)),
        scratch=buffers(gt, conv_two, film_weight, far_rim, rim_wide) + (pair_back,), sems=16, cost=5.0,
    )
    act_two, pre_two_grad, pay_three, sums_two, stat_two = kernel_call(
        second_norm, far=(mid, act_two_grad), near=(moments_two,), tiny=(gain_two, bias_two, film),
        far_out=(rim, rim_wide, payload), tiny_out=(two_images, two_images),
        scratch=buffers(rim_wide, rim_wide, rim, rim_wide, payload), sems=24, cost=3.2,
    )
    moments_three = to_all(pay_three)

    taps = 9 * (chans // 2)
    share = -(-taps // chips)
    extras_two = 2 * images + 1
    extras_one = 1
    halves_two = shaped((taps + 2 * images + 8, chans), F32)
    halves_one = shaped((taps + 8, chans), F32)
    keep_two, send_two = kernel_call(
        kernel_two, far=(act_two, gt), tiny=(sums_two, kbias_two_local), far_out=(halves_two, halves_two),
        scratch=buffers(act_two, gt, halves_two, halves_two), sems=4, cost=3.0,
    )
    came_two = to_sibling(send_two)
    low, keep_one, send_one, keep_two = kernel_call(
        middle_grad, far=(mid, pre_two_grad, act_one, keep_two), near=(moments_three,), tiny=(stat_two, gain_two, film),
        far_out=(rim,), near_out=(halves_one, halves_one, halves_two),
        scratch=buffers(mid, pre_two_grad, act_one, rim), sems=24, cost=6.0,
    )
    came_one = to_sibling(send_one)
    more = -(-(extras_one + extras_two) // chips)
    terms_shape = shaped((chips, -(-(2 * share + 2 * more + 3) // 8) * 8, chans), jnp.int16)
    extra_shape = shaped((-(-chips * more // 8) * 8, chans), F32)
    terms, token = kernel_call(
        functools.partial(pack_terms, extras_one=extras_one, extras_two=extras_two),
        near=(keep_one, came_one, keep_two, came_two), far_out=(terms_shape,), near_out=(shaped((8, chans), F32),),
        scratch=buffers(halves_one, halves_two, extra_shape, extra_shape, terms_shape),
        sems=3, cost=1.0,
    )
    gathered = to_chips(terms)
    whole = half + 2
    norm_one_grad, pay_four = kernel_call(
        back_one, far=(low, xt, conv_one), tiny=(stat_one, gain_one, bias_one), far_out=(block_wide,),
        near_out=(shaped((2 * half, chans), F32),),
        scratch=buffers(rim, block, conv_one, block_wide) + (pair_back,), sems=16, cost=5.0,
        after_near=(to_sibling(token),),
    )
    came_four = to_sibling(pay_four)
    (mixed,) = kernel_call(
        mix, far=(act_two, conv_two, xt), tiny=(conv_two_bias,), far_out=(given,),
        scratch=buffers(act_two, conv_two, xt, block_wide, given) + (pair,), sems=8, cost=3.6, after_near=(pay_four,),
    )
    shares_shape = shaped((chips, -(-(2 * share + 2 * more + 2 * whole) // 8) * 8, chans), BF16)
    (shares,) = kernel_call(
        functools.partial(add_terms, more=more, whole=whole),
        near=(gathered, pay_four, came_four), far_out=(shares_shape,),
        scratch=buffers(shares_shape), sems=1, cost=1.0, after=(mixed,),
    )
    own_half = to_chips(shares)
    other_half = to_sibling(own_half)
    weight_grad = shaped(film_weight.shape, F32)
    text_shape = shaped(text_pooled.shape, F32)
    row = shaped((1, chans), F32)
    input_grad, film_weight_grad, text_grad, film_bias_grad, *vec_grads = kernel_call(
        functools.partial(last_grads, more=more, whole=whole),
        far=(film_weight,),
        near=(norm_one_grad, xt, cotangent, own_half, stat_one, gain_one, gain_two, bias_two, film, act_ints, text_pooled),
        far_out=(given, weight_grad, text_shape), tiny_out=(shaped((1, 2 * chans), F32),) + (row,) * 6,
        scratch=buffers(film_weight, given, weight_grad, text_shape)
        + (pltpu.VMEM((-(-chips * more // 8) * 8, chans), F32),),
        sems=32, cost=6.0, limit=24,
    )
    full = shaped((9, chans, chans), F32)
    kernel_one_grad, kernel_two_grad = kernel_call(
        spread_out, near=(own_half, other_half), far_out=(full, full),
        scratch=buffers(full, full, shaped((chips * share, chans), F32)), sems=2, cost=2.0, after=(input_grad,), limit=24,
    )
    return (
        mixed,
        input_grad,
        text_grad,
        vec_grads[4].reshape(chans),
        vec_grads[5].reshape(chans),
        kernel_one_grad.reshape(3, 3, chans, chans),
        vec_grads[3].reshape(chans),
        vec_grads[0].reshape(chans),
        vec_grads[1].reshape(chans),
        film_weight_grad,
        film_bias_grad.reshape(2 * chans),
        kernel_two_grad.reshape(3, 3, chans, chans),
        vec_grads[2].reshape(chans),
    )


def solution(mesh):
    split = P(None, "ha", "wa", None)
    return jax.shard_map(
        local,
        mesh=mesh,
        in_specs=(split,) + (P(),) * 13 + (split,),
        out_specs=(split, split) + (P(),) * 11,
        check_vma=False,
    )
```

```python
import functools
import math

import jax
import jax.numpy as jnp
import numpy as np
from jax import lax
from jax.experimental import pallas as pl
from jax.experimental.pallas import tpu as pltpu
from jax.sharding import PartitionSpec as P

GROUPS = 32
TEMB = 256
EPSILON = 1e-05
INV_ROOT = 1.0 / math.sqrt(2.0)
AXES = ("ha", "wa")
F32 = jnp.float32
BF16 = jnp.bfloat16
NEAR = pl.BlockSpec(memory_space=pltpu.VMEM)
FAR = pl.BlockSpec(memory_space=pl.ANY)
MIB = 1 << 20


def shaped(shape, dtype):
    return jax.ShapeDtypeStruct(shape, dtype)


def kernel_call(
    body, far=(), near=(), tiny=(), far_out=(), near_out=(), tiny_out=(), scratch=(), sems=0, cost=1.0,
    after=(), after_near=(), scalars=(), limit=48,
):
    pinned = lambda arrays: [pltpu.with_memory_space_constraint(array, pltpu.HBM) for array in arrays]
    given = len(far) + len(near)
    held = len(after) + len(after_near)
    copies = len(tiny) + len(tiny_out)

    def run(*refs):
        refs = list(refs)
        take = lambda count: [refs.pop(0) for _ in range(count)]
        inputs = take(given)
        tiny_far = take(len(tiny))
        scalar_refs = take(len(scalars))
        take(held)
        outputs = take(len(far_out) + len(near_out))
        tiny_out_far = take(len(tiny_out))
        tiny_refs = take(len(tiny))
        tiny_out_refs = take(len(tiny_out))
        mover = None
        if sems + copies:
            mover = Mover(refs.pop(), [(f, n) for f, n in zip(tiny_far, tiny_refs)])
        body(*inputs, *tiny_refs, *scalar_refs, *outputs, *tiny_out_refs, *refs, *([mover] if mover else []))
        if mover:
            for source, target in zip(tiny_out_refs, tiny_out_far):
                mover.put(source, target)
            mover.finish()

    return pl.pallas_call(
        run,
        out_shape=(
            *(pltpu.HBM(out.shape, out.dtype) for out in far_out),
            *near_out,
            *(pltpu.HBM(out.shape, out.dtype) for out in tiny_out),
        ),
        in_specs=[FAR] * len(far)
        + [NEAR] * len(near)
        + [FAR] * len(tiny)
        + [pl.BlockSpec(memory_space=pltpu.SMEM)] * len(scalars)
        + [FAR] * held,
        out_specs=(FAR,) * len(far_out) + (NEAR,) * len(near_out) + (FAR,) * len(tiny_out),
        scratch_shapes=buffers(*tiny, *tiny_out)
        + tuple(scratch)
        + ((pltpu.SemaphoreType.DMA((sems + copies,)),) if sems + copies else ()),
        compiler_params=pltpu.CompilerParams(vmem_limit_bytes=limit * MIB),
        name=getattr(body, "func", body).__name__,
        cost_estimate=pl.CostEstimate(flops=int(cost * 1.1e9), bytes_accessed=0, transcendentals=0),
    )(*pinned(far), *near, *pinned(tiny), *scalars, *pinned(after), *after_near)


def buffers(*arrays):
    return tuple(pltpu.VMEM(a.shape, a.dtype) for a in arrays)


class Mover:
    def __init__(self, sems, first):
        self.sems = sems
        self.used = 0
        self.open = []
        self.first = [self.start(source, target) for source, target in first]

    def start(self, source, target):
        copy = pltpu.make_async_copy(source, target, self.sems.at[self.used])
        self.used += 1
        copy.start()
        return copy

    def ready(self):
        for copy in self.first:
            copy.wait()

    def put(self, source, target):
        self.open.append(self.start(source, target))

    def finish(self):
        for copy in self.open:
            copy.wait()


def pieces(count, size):
    return [(at, min(at + size, count)) for at in range(0, count, size)]


def lanes_of(shape):
    return lax.broadcasted_iota(jnp.int32, shape, 1)


def group_total(values):
    chans = values.shape[1]
    lane = lanes_of(values.shape)
    step = 1
    while step < chans // GROUPS:
        up = pltpu.roll(values, chans - step, 1)
        down = pltpu.roll(values, step, 1)
        values = values + jnp.where((lane & step) == 0, up, down)
        step *= 2
    return values


def pack_pair(first, second):
    half = first.shape[0] // 2
    lane = lanes_of((half, first.shape[1])) & 3
    return jnp.where(
        lane == 0,
        first[:half],
        jnp.where(lane == 1, second[:half], jnp.where(lane == 2, first[half:], second[half:])),
    )


def unpack_at(packed, place):
    lane = lanes_of(packed.shape) & 3
    top = group_total(jnp.where(lane == place, packed, 0.0))
    low = group_total(jnp.where(lane == place + 2, packed, 0.0))
    return jnp.concatenate([top, low], axis=0)


def merge_moments(gathered_ref, local_count):
    parts = gathered_ref.shape[0]
    chans = gathered_ref.shape[2]
    every = gathered_ref[...]
    total = jnp.sum(every, axis=0)
    mean = total * (1.0 / parts)
    apart = every - mean[None]
    between = jnp.sum(apart * apart, axis=0)
    square = pltpu.roll(total, chans - 1, 1) + local_count * between
    inv = lax.rsqrt(square * (1.0 / (local_count * parts)) + EPSILON)
    return unpack_at(mean, 0), unpack_at(inv, 0)


def local_moments(total, square, pilot, pixels, per):
    off = total * (1.0 / pixels)
    mean = pilot + off
    apart = square - total * off
    group_mean = group_total(mean) * (1.0 / per)
    shift = mean - group_mean
    return group_mean, group_total(apart + pixels * shift * shift)


def sigmoid(values):
    return 0.5 + 0.5 * jnp.tanh(0.5 * values)


def forward_weights(kernel_ref, pair_ref):
    chans = kernel_ref.shape[2]
    zero = jnp.zeros((chans, chans), BF16)
    for row in range(3):
        for col in range(4):
            at = (row * 4 + col) * chans
            pair_ref[at : at + chans, 0:chans] = kernel_ref[row, col] if col < 3 else zero
            pair_ref[at : at + chans, chans:] = kernel_ref[row, col - 1] if col > 0 else zero


def backward_weights(kernel_ref, pair_ref):
    chans = kernel_ref.shape[2]
    zero = jnp.zeros((chans, chans), BF16)
    for row in range(3):
        for col in range(4):
            at = (row * 4 + col) * chans
            pair_ref[0:chans, at : at + chans] = kernel_ref[2 - row, 2 - col] if col < 3 else zero
            pair_ref[chans:, at : at + chans] = kernel_ref[2 - row, 3 - col] if col > 0 else zero


def convolve(cells_ref, pair_ref, transposed, rows, first, last, take):
    images, chans = cells_ref.shape[2:]
    pairs = (last - first) // 2
    parts = []
    for row in range(3):
        for col in range(4):
            window = [cells_ref[first + 2 * q + col, row : row + rows] for q in range(pairs)]
            parts.append(jnp.stack(window).reshape(pairs * rows * images, chans))
    wide = jnp.concatenate(parts, axis=1)
    contract = ((1,), (1,)) if transposed else ((1,), (0,))
    made = lax.dot_general(wide, pair_ref[...], (contract, ((), ())), preferred_element_type=F32)
    made = made.reshape(pairs, rows, images, 2 * chans)
    for q in range(pairs):
        for side in range(2):
            take(first + 2 * q + side, made[q, :, :, side * chans : (side + 1) * chans])


def grad_terms(cells_ref, grads_ref):
    cols, rows, images, chans = grads_ref.shape
    pixels = cols * rows * images
    windows = [
        cells_ref[col : col + cols, row : row + rows].reshape(pixels, chans) for row in range(3) for col in range(3)
    ]
    return lax.dot_general(
        grads_ref[...].reshape(pixels, chans),
        jnp.concatenate(windows, axis=1),
        (((0,), (0,)), ((), ())),
        preferred_element_type=F32,
    )


def split_taps(every, keep_ref, send_ref):
    chans = every.shape[0]
    half = chans // 2
    first = lax.axis_index("ha") % 2 == 0
    for tap in range(9):
        made = every[:, tap * chans : (tap + 1) * chans].T
        at = tap * half
        keep_ref[at : at + half, :] = jnp.where(first, made[:half], made[half:])
        send_ref[at : at + half, :] = jnp.where(first, made[half:], made[:half])


def at_edges():
    tall = lax.axis_index("ha")
    wide = lax.axis_index("wa")
    return (
        tall == 0,
        tall == lax.axis_size("ha") - 1,
        wide == 0,
        wide == lax.axis_size("wa") - 1,
    )


def clear_border(cells_ref, width, first=0, last=None):
    top, bottom, left, right = at_edges()
    cols, rows, images, chans = cells_ref.shape
    last = cols if last is None else last
    dtype = cells_ref.dtype

    @pl.when(top)
    def _():
        cells_ref[first:last, 0:width] = jnp.zeros((last - first, width, images, chans), dtype)

    @pl.when(bottom)
    def _():
        cells_ref[first:last, rows - width :] = jnp.zeros((last - first, width, images, chans), dtype)

    if first == 0:

        @pl.when(left)
        def _():
            cells_ref[0:width] = jnp.zeros((width, rows, images, chans), dtype)

    if last == cols:

        @pl.when(right)
        def _():
            cells_ref[cols - width :] = jnp.zeros((width, rows, images, chans), dtype)


def send_payload(mover, packed, pay_ref, stage_ref):
    stage_ref[...] = jnp.broadcast_to(packed[None], stage_ref.shape)
    mover.put(stage_ref, pay_ref)


def prepare_x(x_far, xt_far, near_ref, next_ref, sides_ref, moments_ref, x_ref, xt_ref, mover):
    images, rows, cols, chans = x_ref.shape
    steps = pieces(rows, 2)
    loads = [mover.start(x_far.at[:, a:b], x_ref.at[:, a:b]) for a, b in steps]
    total = jnp.zeros((images, chans), F32)
    square = total
    for (a, b), load in zip(steps, loads):
        load.wait()
        if a == 0:
            pilot = x_ref[:, 0, 0].astype(F32)
        for row in range(a, b):
            x = jnp.swapaxes(x_ref[:, row].astype(F32), 0, 1)
            xt_ref[:, row] = x.astype(BF16)
            apart = x - pilot[None]
            total = total + jnp.sum(apart, axis=0)
            square = square + jnp.sum(apart * apart, axis=0)
        mover.put(xt_ref.at[:, a:b], xt_far.at[:, a:b])
    mean, spread = local_moments(total, square, pilot, rows * cols, chans // GROUPS)
    moments_ref[...] = pack_pair(mean, spread)
    outer(xt_ref, near_ref, next_ref, sides_ref)


def is_even(axis="ha"):
    return lax.axis_index(axis) % 2 == 0


def outer(cells, near_ref, next_ref, sides_ref):
    cols, rows = cells.shape[0:2]
    down, up = cells[:, rows - 2 :], cells[:, 0:2]
    near_ref[...] = jnp.where(is_even(), down, up)
    next_ref[...] = jnp.where(is_even(), up, down)
    sides_ref[0:2] = cells[0:2]
    sides_ref[2:4] = cells[cols - 2 :]


def prepare_g(
    c_far, moments_ref, gt_far, pay_far, near_ref, next_ref, sides_ref, bias_ref, c_ref, gt_ref, stage_ref, mover
):
    images, rows, cols, chans = c_ref.shape
    steps = pieces(rows, 2)
    loads = [mover.start(c_far.at[:, a:b], c_ref.at[:, a:b]) for a, b in steps]
    send_payload(mover, moments_ref[...], pay_far, stage_ref)
    bias = jnp.zeros((images, chans), F32)
    for (a, b), load in zip(steps, loads):
        load.wait()
        for row in range(a, b):
            grad = jnp.swapaxes(c_ref[:, row].astype(F32) * INV_ROOT, 0, 1).astype(BF16)
            gt_ref[:, row] = grad
            bias = bias + jnp.sum(grad.astype(F32), axis=0)
        mover.put(gt_ref.at[:, a:b], gt_far.at[:, a:b])
    bias_ref[...] = bias
    outer(gt_ref, near_ref, next_ref, sides_ref)


def edge_columns(sides_ref, near_ref, next_ref, one_ref, other_ref):
    cols, rows = near_ref.shape[0], sides_ref.shape[1]
    even = is_even("wa")

    def piece(left, right):
        return jnp.where(even, right, left), jnp.where(even, left, right)

    near = piece(near_ref[0:2], near_ref[cols - 2 : cols])
    following = piece(next_ref[0:2], next_ref[cols - 2 : cols])
    own = piece(sides_ref[0:2], sides_ref[2:4])
    for at, ref in enumerate((one_ref, other_ref)):
        ref[:, 0:2] = jnp.where(is_even(), following[at], near[at])
        ref[:, 2 : rows + 2] = own[at]
        ref[:, rows + 2 :] = jnp.where(is_even(), near[at], following[at])


def fill_halo(cells_ref, near_ref, next_ref, one_ref, other_ref, change):
    cols, rows = near_ref.shape[0], cells_ref.shape[1] - 4

    def halo_column(col, _):
        near, next_ = near_ref[pl.ds(col, 1)], next_ref[pl.ds(col, 1)]
        cells_ref[pl.ds(col + 2, 1), 0:2] = change(jnp.where(is_even(), next_, near))
        cells_ref[pl.ds(col + 2, 1), rows + 2 :] = change(jnp.where(is_even(), near, next_))
        return 0

    even = is_even("wa")
    cells_ref[0:2] = change(jnp.where(even, other_ref[...], one_ref[...]))
    cells_ref[cols + 2 :] = change(jnp.where(even, one_ref[...], other_ref[...]))
    lax.fori_loop(0, cols, halo_column, 0, unroll=4)


def first_half(
    xt_far, kernel_far, near_ref, next_ref, one_ref, other_ref, gathered_ref, gain_ref, bias_ref, kbias_ref,
    act_far, mid_far, pay_far, stat_ref,
    xt_ref, kernel_ref, act_ref, mid_ref, stage_ref, pair_ref, mover,
):
    cols, rows, images, chans = xt_ref.shape
    per = chans // GROUPS
    load = mover.start(kernel_far, kernel_ref)
    steps = pieces(cols, 8)
    own = [mover.start(xt_far.at[a:b], xt_ref.at[a:b]) for a, b in steps]
    mean, inv = merge_moments(gathered_ref, rows * cols * per)
    stat_ref[0] = mean
    stat_ref[1] = inv
    mover.ready()
    slope = 0.5 * inv * gain_ref[...].astype(F32)
    offset = 0.5 * bias_ref[...].astype(F32)

    def act(cells):
        value = (cells.astype(F32) - mean) * slope + offset
        return (value + value * jnp.tanh(value)).astype(BF16)

    def column(col, _):
        act_ref[pl.ds(col + 2, 1), 2 : rows + 2] = act(xt_ref[pl.ds(col, 1)])
        return 0

    fill_halo(act_ref, near_ref, next_ref, one_ref, other_ref, act)
    for (a, b), copy in zip(steps, own):
        copy.wait()
        lax.fori_loop(a, b, column, 0, unroll=2)
    clear_border(act_ref, 2)
    load.wait()
    forward_weights(kernel_ref, pair_ref)
    mover.put(act_ref, act_far)

    wide = cols + 2
    kbias = kbias_ref[...].astype(F32)
    state = [None, jnp.zeros((images, chans), F32), jnp.zeros((images, chans), F32)]

    def take(col, values):
        values = values + kbias
        mid_ref[col] = values
        if 1 <= col <= cols:
            own = values[1 : rows + 1]
            if state[0] is None:
                state[0] = own[0]
            apart = own - state[0][None]
            state[1] = state[1] + jnp.sum(apart, axis=0)
            state[2] = state[2] + jnp.sum(apart * apart, axis=0)

    for a, b in pieces(wide, 10):
        convolve(act_ref, pair_ref, False, rows + 2, a, b, take)
        mover.put(mid_ref.at[a:b], mid_far.at[a:b])
    pilot, total, square = state
    mean, spread = local_moments(total, square, pilot, rows * cols, per)
    send_payload(mover, pack_pair(mean, spread), pay_far, stage_ref)


def back_two(
    gt_far, kernel_far, weight_far, near_ref, next_ref, one_ref, other_ref, *refs,
):
    text_ref, fbias_ref, freqs_ref, times_ref, levels_ref, out_far, film_ref, ints_ref, *refs = refs
    gt_ref, kernel_ref, weight_ref, cells_ref, out_ref, pair_ref, mover = refs
    cols, rows = gt_ref.shape[0:2]
    load = mover.start(kernel_far, kernel_ref)
    steps = pieces(cols, 8)
    own = [mover.start(gt_far.at[a:b], gt_ref.at[a:b]) for a, b in steps]
    late = mover.start(weight_far, weight_ref)
    fill_halo(cells_ref, near_ref, next_ref, one_ref, other_ref, lambda cells: cells)
    load.wait()
    backward_weights(kernel_ref, pair_ref)
    mover.ready()
    text = text_ref[...].astype(F32)
    half = TEMB // 2
    for at, source_ref in ((0, times_ref), (TEMB, levels_ref)):
        angles = [source_ref[image].astype(F32) * freqs_ref[...] for image in range(text_ref.shape[0])]
        angles = jnp.concatenate(angles, axis=0)
        for start, embed in ((at, jnp.sin(angles)), (at + half, jnp.cos(angles))):
            ints_ref[:, start : start + half] = (embed * sigmoid(embed)).astype(BF16)
    act = jnp.concatenate([ints_ref[...], (text * sigmoid(text)).astype(BF16)], axis=1)
    for (a, b), copy in zip(steps, own):
        copy.wait()
        cells_ref[a + 2 : b + 2, 2 : rows + 2] = gt_ref[a:b]
    clear_border(cells_ref, 2)
    for a, b in pieces(cols + 2, 10):
        convolve(cells_ref, pair_ref, True, rows + 2, a, b, lambda col, values: out_ref.__setitem__(col, values))
        mover.put(out_ref.at[a:b], out_far.at[a:b])
    late.wait()
    film_ref[...] = jnp.dot(act, weight_ref[...], preferred_element_type=F32) + fbias_ref[...].astype(F32)


def second_values(stat, gain_ref, bias_ref, film_ref):
    mean, inv = stat
    chans = mean.shape[1]
    scale = 1.0 + film_ref[:, 0:chans]
    slope = gain_ref[...].astype(F32) * scale
    half_slope = 0.5 * slope
    half_offset = 0.5 * (bias_ref[...].astype(F32) * scale + film_ref[:, chans:])

    def values(mid, back):
        hat = (mid - mean) * inv
        pre = hat * half_slope + half_offset
        bend = jnp.tanh(pre)
        more = 1.0 + bend
        grad = back * (0.5 * more * (1.0 + pre * (1.0 - bend)))
        return hat, pre * more, grad

    return slope, values


def second_norm(
    mid_far, back_far, gathered_ref, gain_ref, bias_ref, film_ref,
    act_far, pre_far, pay_far, sums_ref, stat_ref,
    mid_ref, back_ref, act_ref, pre_ref, stage_ref, mover,
):
    wide, tall, images, chans = mid_ref.shape
    cols, rows = wide - 2, tall - 2
    per = chans // GROUPS
    steps = pieces(wide, 9)
    loads = []
    for a, b in steps:
        loads.append(
            [mover.start(f.at[a:b], n.at[a:b]) for f, n in ((mid_far, mid_ref), (back_far, back_ref))]
        )
    mean, inv = merge_moments(gathered_ref, rows * cols * per)
    stat_ref[0] = mean
    stat_ref[1] = inv
    mover.ready()
    slope, values = second_values((mean, inv), gain_ref, bias_ref, film_ref)

    def column(col, inner):
        hat, act, grad = values(mid_ref[col], back_ref[col])
        act_ref[col] = act.astype(BF16)
        pre_ref[col] = grad
        if inner is None:
            return None
        own = grad[1 : rows + 1]
        plain, cross = inner
        return plain + jnp.sum(own, axis=0), cross + jnp.sum(own * hat[1 : rows + 1], axis=0)

    zero = jnp.zeros((images, chans), F32)
    inner = (zero, zero)
    for (a, b), pair in zip(steps, loads):
        for load in pair:
            load.wait()
        if a == 0:
            column(0, None)
        inner = lax.fori_loop(max(a, 1), min(b, cols + 1), column, inner)
        if b == wide:
            column(wide - 1, None)
        clear_border(act_ref, 1, a, b)
        mover.put(act_ref.at[a:b], act_far.at[a:b])
        mover.put(pre_ref.at[a:b], pre_far.at[a:b])
    plain, cross = inner
    sums_ref[0] = plain
    sums_ref[1] = cross
    send_payload(mover, pack_pair(group_total(plain * slope), group_total(cross * slope)), pay_far, stage_ref)


def kernel_two(
    act_far, gt_far, sums_ref, bias_ref, keep_far, send_far, act_ref, gt_ref, keep_ref, send_ref, mover
):
    for load in [mover.start(act_far, act_ref), mover.start(gt_far, gt_ref)]:
        load.wait()
    split_taps(grad_terms(act_ref, gt_ref), keep_ref, send_ref)
    mover.ready()
    images, chans = bias_ref.shape
    at = 9 * (chans // 2)
    total = jnp.sum(bias_ref[...], axis=0, keepdims=True)
    for ref in (keep_ref, send_ref):
        ref[at : at + images] = sums_ref[0]
        ref[at + images : at + 2 * images] = sums_ref[1]
        ref[at + 2 * images :] = jnp.broadcast_to(total, (ref.shape[0] - at - 2 * images, chans))
    mover.put(keep_ref, keep_far)
    mover.put(send_ref, send_far)


def mix(
    act_far, kernel_far, xt_far, kbias_ref, out_far, act_ref, kernel_ref, xt_ref, branch_ref, out_ref, pair_ref, mover
):
    images, rows, cols, chans = out_ref.shape
    loads = [mover.start(f, n) for f, n in ((kernel_far, kernel_ref), (act_far, act_ref), (xt_far, xt_ref))]
    loads[0].wait()
    forward_weights(kernel_ref, pair_ref)
    mover.ready()
    kbias = kbias_ref[...].astype(F32)
    loads[1].wait()
    convolve(
        act_ref, pair_ref, False, rows, 0, cols, lambda col, values: branch_ref.__setitem__(col, values + kbias)
    )
    loads[2].wait()
    for a, b in pieces(rows, 2):
        for row in range(a, b):
            mixed = jnp.swapaxes((xt_ref[:, row].astype(F32) + branch_ref[:, row]) * INV_ROOT, 0, 1)
            out_ref[:, row] = mixed.astype(BF16)
        mover.put(out_ref.at[:, a:b], out_far.at[:, a:b])


def middle_grad(
    mid_far, pre_far, act_far, keep_two_far, gathered_ref, stat_ref, gain_ref, film_ref,
    low_far, keep_ref, send_ref, two_ref,
    mid_ref, pre_ref, act_ref, low_ref, mover,
):
    wide, tall, images, chans = mid_ref.shape
    cols, rows = wide - 2, tall - 2
    steps = pieces(wide, 9)
    loads = []
    for a, b in steps:
        loads.append([mover.start(f.at[a:b], n.at[a:b]) for f, n in ((mid_far, mid_ref), (pre_far, pre_ref))])
    late = [mover.start(f, n) for f, n in ((act_far, act_ref), (keep_two_far, two_ref))]
    count = lax.axis_size("ha") * lax.axis_size("wa") * rows * cols * (chans // GROUPS)
    packed = jnp.sum(gathered_ref[...], axis=0) * (1.0 / count)
    mover.ready()
    mean = stat_ref[0]
    inv = stat_ref[1]
    plain = unpack_at(packed, 0) * inv
    cross = unpack_at(packed, 1) * inv * inv
    slope = gain_ref[...].astype(F32) * (1.0 + film_ref[:, 0:chans]) * inv

    def low_column(col, total):
        low = (pre_ref[col] * slope - plain - (mid_ref[col] - mean) * cross).astype(BF16)
        low_ref[col] = low
        if total is None:
            return None
        return total + jnp.sum(low[1 : rows + 1].astype(F32), axis=0)

    kbias = jnp.zeros((images, chans), F32)
    for (a, b), pair in zip(steps, loads):
        for load in pair:
            load.wait()
        if a == 0:
            low_column(0, None)
        kbias = lax.fori_loop(max(a, 1), min(b, cols + 1), low_column, kbias)
        if b == wide:
            low_column(wide - 1, None)
        clear_border(low_ref, 1, a, b)
        mover.put(low_ref.at[a:b], low_far.at[a:b])
    for load in late:
        load.wait()
    own = low_ref.at[1 : wide - 1, 1 : tall - 1]
    split_taps(grad_terms(act_ref.at[1 : wide + 1, 1 : tall + 1], own), keep_ref, send_ref)
    at = 9 * (chans // 2)
    for ref in (keep_ref, send_ref):
        ref[at:] = jnp.broadcast_to(jnp.sum(kbias, axis=0, keepdims=True), (ref.shape[0] - at, chans))


def back_one(
    low_far, xt_far, kernel_far, stat_ref, gain_ref, bias_ref, grad_far, pay_ref, low_ref, xt_ref, kernel_ref, out_ref, pair_ref, mover
):
    cols, rows, images, chans = xt_ref.shape
    loads = [mover.start(f, n) for f, n in ((kernel_far, kernel_ref), (low_far, low_ref), (xt_far, xt_ref))]
    loads[0].wait()
    backward_weights(kernel_ref, pair_ref)
    loads[1].wait()
    loads[2].wait()
    mover.ready()
    mean = stat_ref[0]
    inv = stat_ref[1]
    gain = gain_ref[...].astype(F32)
    bias = bias_ref[...].astype(F32)
    state = [jnp.zeros((images, chans), F32), jnp.zeros((images, chans), F32)]

    def take(col, values):
        hat = (xt_ref[col].astype(F32) - mean) * inv
        norm = hat * gain + bias
        sigma = sigmoid(norm)
        grad = values * (sigma * (1.0 + norm * (1.0 - sigma)))
        out_ref[col] = grad
        state[0] = state[0] + jnp.sum(grad, axis=0)
        state[1] = state[1] + jnp.sum(grad * hat, axis=0)

    for a, b in pieces(cols, 8):
        convolve(low_ref, pair_ref, True, rows, a, b, take)
        mover.put(out_ref.at[a:b], grad_far.at[a:b])
    plain, cross = state
    half = images // 2
    pay_ref[0:half] = pack_pair(group_total(plain * gain), group_total(cross * gain))
    rest = [jnp.sum(v, axis=0, keepdims=True) for v in (cross, plain)]
    short = pay_ref.shape[0] - half - 2
    pay_ref[half:] = jnp.concatenate(rest + [jnp.zeros((short, chans), F32)], axis=0)


CODE = 32767.0


def exponents(values):
    most = jnp.maximum(jnp.max(jnp.abs(values), axis=0, keepdims=True), 1e-30)
    return jnp.ceil(jnp.log2(most) + 1e-3)


def pack_terms(
    keep_one_ref, came_one_ref, keep_two_ref, came_two_ref, out_far, token_ref,
    one_ref, two_ref, extra_ref, rest_ref, out_ref, mover, extras_one, extras_two,
):
    chips, rows, chans = out_ref.shape
    taps = 9 * (chans // 2)
    share = -(-taps // chips)
    more = -(-(extras_one + extras_two) // chips)
    extra_ref[...] = jnp.zeros(extra_ref.shape, F32)
    one_ref[...] = keep_one_ref[...] + came_one_ref[...]
    two_ref[...] = keep_two_ref[...] + came_two_ref[...]
    extra_ref[0:extras_two] = two_ref[taps : taps + extras_two]
    extra_ref[extras_two : extras_two + extras_one] = one_ref[taps : taps + extras_one]
    token_ref[...] = extra_ref[0:8]
    powers = []
    for ref, count in ((one_ref, taps), (two_ref, taps), (extra_ref, extra_ref.shape[0])):
        values = ref[0:count]
        power = exponents(values)
        powers.append(power)
        scaled = values * (jnp.exp2(-power) * CODE)
        code = jnp.round(scaled)
        ref[0:count] = code
        if ref is extra_ref:
            rest_ref[...] = jnp.round((scaled - code) * (2.0 * CODE))
    short = rows - 2 * share - 2 * more - 3
    pad = [jnp.zeros((short, chans), F32)] if short else []
    for chip in range(chips):
        a, b = chip * share, min((chip + 1) * share, taps)
        mine = []
        for ref in (one_ref, two_ref):
            if a < b:
                mine.append(ref[a:b])
            if max(b - a, 0) < share:
                mine.append(jnp.zeros((share - max(b - a, 0), chans), F32))
        for ref in (extra_ref, rest_ref):
            mine.append(ref[chip * more : (chip + 1) * more])
        whole = jnp.concatenate(mine + powers + pad, axis=0)
        out_ref[chip] = whole.astype(jnp.int32).astype(jnp.int16)
    mover.put(out_ref, out_far)


def unpack_terms(gathered_ref, share, more):
    chips, rows, chans = gathered_ref.shape
    row = lax.broadcasted_iota(jnp.int32, (rows, chans), 0)
    base = 2 * share + 2 * more
    total = jnp.zeros((rows, chans), F32)
    for chip in range(chips):
        block = gathered_ref[chip].astype(jnp.int32).astype(F32)
        scales = jnp.exp2(block[base : base + 3]) * (1.0 / CODE)
        scale = jnp.where(row < share, scales[0:1], jnp.where(row < 2 * share, scales[1:2], scales[2:3]))
        scale = jnp.where(row < 2 * share + more, scale, scale * (0.5 / CODE))
        total = total + block * scale
    extra = total[2 * share : 2 * share + more] + total[2 * share + more : base]
    return total[0 : 2 * share], extra


def two_terms(values):
    high = values.astype(BF16).astype(F32)
    return [high, values - high]


def add_terms(gathered_ref, pay_ref, came_ref, out_far, out_ref, mover, more, whole):
    chips, rows, chans = gathered_ref.shape
    shares, extra = unpack_terms(gathered_ref, -(-9 * (chans // 2) // chips), more)
    every = [shares] + two_terms(extra) + two_terms(pay_ref[0:whole] + came_ref[0:whole])
    short = out_ref.shape[1] - sum(v.shape[0] for v in every)
    if short:
        every.append(jnp.zeros((short, chans), F32))
    out_ref[...] = jnp.broadcast_to(jnp.concatenate(every, axis=0).astype(BF16)[None], out_ref.shape)
    mover.put(out_ref, out_far)


def sums_of(own_ref, at, whole):
    total = own_ref[0].astype(F32)
    for chip in range(1, own_ref.shape[0]):
        total = total + own_ref[chip].astype(F32)
    return total[at : at + whole] + total[at + whole : at + 2 * whole]


def three_terms(values):
    high = values.astype(BF16)
    rest = values - high.astype(F32)
    mid = rest.astype(BF16)
    low = (rest - mid.astype(F32)).astype(BF16)
    return jnp.concatenate([high, mid, low], axis=0)


def spread_out(own_ref, other_ref, one_far, two_far, one_ref, two_ref, half_ref, mover):
    chips, rows, chans = own_ref.shape
    half = chans // 2
    taps = 9 * half
    share = -(-taps // chips)
    core = lax.axis_index("ha") % 2
    for at, (out_ref, far) in enumerate(((one_ref, one_far), (two_ref, two_far))):
        for source, place in ((own_ref, core), (other_ref, 1 - core)):
            for chip in range(chips):
                piece = source[chip].astype(F32)[at * share : (at + 1) * share]
                half_ref[chip * share : (chip + 1) * share] = piece
            for tap in range(9):
                rows_at = pl.ds(pl.multiple_of(place * half, half), half)
                out_ref[tap, rows_at] = half_ref[tap * half : (tap + 1) * half]
        mover.put(out_ref, far)


def last_grads(
    weight_far, grad_ref, xt_ref, c_ref, own_ref, stat_ref, gain_one_ref, gain_two_ref, bias_two_ref, film_ref, ints_ref, text_ref,
    out_far, weight_grad_far, text_grad_far, bias_ref, *refs, more, whole,
):
    *vec_refs, weight_ref, out_ref, weight_grad_ref, text_grad_ref, extra_ref, mover = refs
    images, rows, cols, chans = out_ref.shape
    chips = own_ref.shape[0]
    load = mover.start(weight_far, weight_ref)
    share = -(-9 * (chans // 2) // chips)
    start = 2 * share
    for chip in range(chips):
        piece = own_ref[chip].astype(F32)
        extra_ref[chip * more : (chip + 1) * more] = piece[start : start + more] + piece[start + more : start + 2 * more]
    plain = extra_ref[0:images]
    cross = extra_ref[images : 2 * images]
    mover.ready()
    scale = 1.0 + film_ref[:, 0:chans]
    scale_grad = gain_two_ref[...].astype(F32) * cross + bias_two_ref[...].astype(F32) * plain
    film_grad = jnp.concatenate([scale_grad, plain], axis=1)
    bias_ref[...] = jnp.sum(film_grad, axis=0, keepdims=True)
    sums = sums_of(own_ref, start + 2 * more, whole)
    vec_refs[0][...] = jnp.sum(scale * cross, axis=0, keepdims=True)
    vec_refs[1][...] = jnp.sum(scale * plain, axis=0, keepdims=True)
    for at, row in enumerate((extra_ref[2 * images : 2 * images + 1], extra_ref[2 * images + 1 : 2 * images + 2])):
        vec_refs[2 + at][...] = row
    vec_refs[4][...] = sums[whole - 2 : whole - 1]
    vec_refs[5][...] = sums[whole - 1 : whole]
    terms = three_terms(film_grad)
    ints = ints_ref.shape[1]

    depth = weight_grad_ref.shape[0]
    for at in range(0, depth, 512):
        if at < ints:
            act = ints_ref[:, at : at + 512]
        else:
            embed = text_ref[:, at - ints : at - ints + 512].astype(F32)
            act = (embed * sigmoid(embed)).astype(BF16)
        weight_grad_ref[at : at + 512] = lax.dot_general(
            jnp.concatenate([act, act, act], axis=0), terms, (((0,), (0,)), ((), ())), preferred_element_type=F32
        )
        mover.put(weight_grad_ref.at[at : at + 512], weight_grad_far.at[at : at + 512])

    count = lax.axis_size("ha") * lax.axis_size("wa") * rows * cols * (chans // GROUPS)
    packed = sums[0 : images // 2] * (1.0 / count)
    plain = unpack_at(packed, 0)
    cross = unpack_at(packed, 1)
    mean = stat_ref[0]
    inv = stat_ref[1]
    gain = gain_one_ref[...].astype(F32)
    for a, b in pieces(rows, 2):
        for row in range(a, b):
            hat = (xt_ref[:, row].astype(F32) - mean) * inv
            path = jnp.swapaxes(inv * (grad_ref[:, row] * gain - plain - hat * cross), 0, 1)
            out_ref[:, row] = (c_ref[:, row].astype(F32) * INV_ROOT + path).astype(BF16)
        mover.put(out_ref.at[:, a:b], out_far.at[:, a:b])

    load.wait()
    for at in range(ints, depth, 512):
        embed = text_ref[:, at - ints : at - ints + 512].astype(F32)
        sigma = sigmoid(embed)
        made = lax.dot_general(
            terms, weight_ref[at : at + 512], (((1,), (1,)), ((), ())), preferred_element_type=F32
        )
        cond_grad = made[0:images] + made[images : 2 * images] + made[2 * images :]
        text_grad_ref[:, at - ints : at - ints + 512] = cond_grad * (sigma * (1.0 + embed * (1.0 - sigma)))
    mover.put(text_grad_ref, text_grad_far)


def to_all(payload):
    return lax.all_to_all(payload, AXES, 0, 0)


def to_chips(payload):
    tall, wide = lax.axis_size("ha"), lax.axis_size("wa")
    groups = [[h * wide + w for h in range(core, tall, 2) for w in range(wide)] for core in range(2)]
    return lax.all_to_all(payload, AXES, 0, 0, axis_index_groups=groups)


def to_sibling(payload):
    return lax.ppermute(payload, "ha", [(i, i ^ 1) for i in range(lax.axis_size("ha"))])


def pair_exchange(one, other, axis):
    count = lax.axis_size(axis)
    pairs = [(i, (i + 1 if i % 2 else i - 1) % count) for i in range(count)]
    if axis == "wa":
        pairs = [(i, min(max(j, 0), count - 1) if abs(i - j) == 1 else i) for i, j in pairs]
    one = lax.ppermute(one, axis, [(i, i ^ 1) for i in range(count)])
    return one, lax.ppermute(other, axis, pairs)


def side_halo(sides, near, following, after=()):
    four, rows, images, chans = sides.shape
    edge = shaped((2, rows + 4, images, chans), sides.dtype)
    one, other = kernel_call(
        edge_columns, near=(sides, near, following), near_out=(edge, edge), cost=0.4, after=after, limit=16
    )
    return pair_exchange(one, other, "wa"), one


def local(
    block_input,
    timesteps,
    aug_levels,
    text_pooled,
    gain_one,
    bias_one,
    conv_one,
    conv_one_bias,
    gain_two,
    bias_two,
    film_weight,
    film_bias,
    conv_two,
    conv_two_bias,
    cotangent,
):
    images, rows, cols, chans = block_input.shape
    parts = lax.axis_size("ha") * lax.axis_size("wa")
    chips = parts // 2
    half = images // 2
    gain_one, bias_one, conv_one_bias, gain_two, bias_two, conv_two_bias = (
        v.reshape(1, chans) for v in (gain_one, bias_one, conv_one_bias, gain_two, bias_two, conv_two_bias)
    )
    freqs = np.exp(-math.log(10000.0) * np.arange(TEMB // 2) / (TEMB // 2)).astype(np.float32)[None]
    payload = shaped((parts, half, chans), F32)
    per_image = shaped((images, chans), F32)
    two_images = shaped((2, images, chans), F32)
    block = shaped((cols, rows, images, chans), BF16)
    block_wide = shaped((cols, rows, images, chans), F32)
    rim = shaped((cols + 2, rows + 2, images, chans), BF16)
    rim_wide = shaped((cols + 2, rows + 2, images, chans), F32)
    far_rim = shaped((cols + 4, rows + 4, images, chans), BF16)
    given = shaped((images, rows, cols, chans), BF16)
    pair = pltpu.VMEM((12 * chans, 2 * chans), BF16)
    pair_back = pltpu.VMEM((2 * chans, 12 * chans), BF16)

    sides = shaped((4, rows, images, chans), BF16)
    row_halo = shaped((cols, 2, images, chans), BF16)
    xt, x_near, x_next, x_sides, moments = kernel_call(
        prepare_x, far=(block_input,), far_out=(block,),
        near_out=(row_halo, row_halo, sides, shaped((half, chans), F32)),
        scratch=buffers(given, block), sems=16, cost=2.3,
    )
    x_near, x_next = pair_exchange(x_near, x_next, "ha")
    gt, pay_one, g_near, g_next, g_sides, kbias_two_local = kernel_call(
        prepare_g, far=(cotangent,), near=(moments,), far_out=(block, payload),
        near_out=(row_halo, row_halo, sides), tiny_out=(per_image,),
        scratch=buffers(given, block, payload), sems=16, cost=2.0,
    )
    moments_one = to_all(pay_one)
    x_cols, x_edge = side_halo(x_sides, x_near, x_next)
    g_near, g_next = pair_exchange(g_near, g_next, "ha")

    film_bias = film_bias.reshape(1, 2 * chans)
    act_one, mid, pay_two, stat_one = kernel_call(
        first_half, far=(xt, conv_one), near=(x_near, x_next, *x_cols, moments_one),
        tiny=(gain_one, bias_one, conv_one_bias),
        far_out=(far_rim, rim_wide, payload), tiny_out=(two_images,),
        scratch=buffers(xt, conv_one, far_rim, rim_wide, payload) + (pair,), sems=16, cost=5.5,
        after=(film_bias,),
    )
    moments_two = to_all(pay_two)
    g_cols, _ = side_halo(g_sides, g_near, g_next, after=(stat_one,))
    act_two_grad, film, act_ints = kernel_call(
        back_two, far=(gt, conv_two, film_weight), near=(g_near, g_next, *g_cols),
        tiny=(text_pooled, film_bias, freqs), scalars=(timesteps, aug_levels),
        far_out=(rim_wide,), tiny_out=(shaped((images, 2 * chans), F32), shaped((images, 2 * TEMB), BF16)),
        scratch=buffers(gt, conv_two, film_weight, far_rim, rim_wide) + (pair_back,), sems=16, cost=5.0,
    )
    act_two, pre_two_grad, pay_three, sums_two, stat_two = kernel_call(
        second_norm, far=(mid, act_two_grad), near=(moments_two,), tiny=(gain_two, bias_two, film),
        far_out=(rim, rim_wide, payload), tiny_out=(two_images, two_images),
        scratch=buffers(rim_wide, rim_wide, rim, rim_wide, payload), sems=24, cost=3.2,
    )
    moments_three = to_all(pay_three)

    taps = 9 * (chans // 2)
    share = -(-taps // chips)
    extras_two = 2 * images + 1
    extras_one = 1
    halves_two = shaped((taps + 2 * images + 8, chans), F32)
    halves_one = shaped((taps + 8, chans), F32)
    keep_two, send_two = kernel_call(
        kernel_two, far=(act_two, gt), tiny=(sums_two, kbias_two_local), far_out=(halves_two, halves_two),
        scratch=buffers(act_two, gt, halves_two, halves_two), sems=4, cost=3.0,
    )
    came_two = to_sibling(send_two)
    low, keep_one, send_one, keep_two = kernel_call(
        middle_grad, far=(mid, pre_two_grad, act_one, keep_two), near=(moments_three,), tiny=(stat_two, gain_two, film),
        far_out=(rim,), near_out=(halves_one, halves_one, halves_two),
        scratch=buffers(mid, pre_two_grad, act_one, rim), sems=24, cost=6.0,
    )
    came_one = to_sibling(send_one)
    more = -(-(extras_one + extras_two) // chips)
    terms_shape = shaped((chips, -(-(2 * share + 2 * more + 3) // 8) * 8, chans), jnp.int16)
    extra_shape = shaped((-(-chips * more // 8) * 8, chans), F32)
    terms, token = kernel_call(
        functools.partial(pack_terms, extras_one=extras_one, extras_two=extras_two),
        near=(keep_one, came_one, keep_two, came_two), far_out=(terms_shape,), near_out=(shaped((8, chans), F32),),
        scratch=buffers(halves_one, halves_two, extra_shape, extra_shape, terms_shape),
        sems=3, cost=1.0,
    )
    gathered = to_chips(terms)
    whole = half + 2
    norm_one_grad, pay_four = kernel_call(
        back_one, far=(low, xt, conv_one), tiny=(stat_one, gain_one, bias_one), far_out=(block_wide,),
        near_out=(shaped((2 * half, chans), F32),),
        scratch=buffers(rim, block, conv_one, block_wide) + (pair_back,), sems=16, cost=5.0,
        after_near=(to_sibling(token),),
    )
    came_four = to_sibling(pay_four)
    (mixed,) = kernel_call(
        mix, far=(act_two, conv_two, xt), tiny=(conv_two_bias,), far_out=(given,),
        scratch=buffers(act_two, conv_two, xt, block_wide, given) + (pair,), sems=8, cost=3.6, after_near=(pay_four,),
    )
    shares_shape = shaped((chips, -(-(2 * share + 2 * more + 2 * whole) // 8) * 8, chans), BF16)
    (shares,) = kernel_call(
        functools.partial(add_terms, more=more, whole=whole),
        near=(gathered, pay_four, came_four), far_out=(shares_shape,),
        scratch=buffers(shares_shape), sems=1, cost=1.0, after=(mixed,),
    )
    own_half = to_chips(shares)
    other_half = to_sibling(own_half)
    weight_grad = shaped(film_weight.shape, F32)
    text_shape = shaped(text_pooled.shape, F32)
    row = shaped((1, chans), F32)
    input_grad, film_weight_grad, text_grad, film_bias_grad, *vec_grads = kernel_call(
        functools.partial(last_grads, more=more, whole=whole),
        far=(film_weight,),
        near=(norm_one_grad, xt, cotangent, own_half, stat_one, gain_one, gain_two, bias_two, film, act_ints, text_pooled),
        far_out=(given, weight_grad, text_shape), tiny_out=(shaped((1, 2 * chans), F32),) + (row,) * 6,
        scratch=buffers(film_weight, given, weight_grad, text_shape)
        + (pltpu.VMEM((-(-chips * more // 8) * 8, chans), F32),),
        sems=32, cost=6.0, limit=24,
    )
    full = shaped((9, chans, chans), F32)
    kernel_one_grad, kernel_two_grad = kernel_call(
        spread_out, near=(own_half, other_half), far_out=(full, full),
        scratch=buffers(full, full, shaped((chips * share, chans), F32)), sems=2, cost=2.0, after=(input_grad,), limit=24,
    )
    return (
        mixed,
        input_grad,
        text_grad,
        vec_grads[4].reshape(chans),
        vec_grads[5].reshape(chans),
        kernel_one_grad.reshape(3, 3, chans, chans),
        vec_grads[3].reshape(chans),
        vec_grads[0].reshape(chans),
        vec_grads[1].reshape(chans),
        film_weight_grad,
        film_bias_grad.reshape(2 * chans),
        kernel_two_grad.reshape(3, 3, chans, chans),
        vec_grads[2].reshape(chans),
    )


def solution(mesh):
    split = P(None, "ha", "wa", None)
    return jax.shard_map(
        local,
        mesh=mesh,
        in_specs=(split,) + (P(),) * 13 + (split,),
        out_specs=(split, split) + (P(),) * 11,
        check_vma=False,
    )
```

```python
import functools
import math

import jax
import jax.numpy as jnp
import numpy as np
from jax import lax
from jax.experimental import pallas as pl
from jax.experimental.pallas import tpu as pltpu
from jax.sharding import PartitionSpec as P

GROUPS = 32
TEMB = 256
EPSILON = 1e-05
INV_ROOT = 1.0 / math.sqrt(2.0)
AXES = ("ha", "wa")
F32 = jnp.float32
BF16 = jnp.bfloat16
NEAR = pl.BlockSpec(memory_space=pltpu.VMEM)
FAR = pl.BlockSpec(memory_space=pl.ANY)
MIB = 1 << 20


def shaped(shape, dtype):
    return jax.ShapeDtypeStruct(shape, dtype)


def kernel_call(
    body, far=(), near=(), tiny=(), far_out=(), near_out=(), tiny_out=(), scratch=(), sems=0, cost=1.0,
    after=(), after_near=(), scalars=(), limit=48,
):
    pinned = lambda arrays: [pltpu.with_memory_space_constraint(array, pltpu.HBM) for array in arrays]
    given = len(far) + len(near)
    held = len(after) + len(after_near)
    copies = len(tiny) + len(tiny_out)

    def run(*refs):
        refs = list(refs)
        take = lambda count: [refs.pop(0) for _ in range(count)]
        inputs = take(given)
        tiny_far = take(len(tiny))
        scalar_refs = take(len(scalars))
        take(held)
        outputs = take(len(far_out) + len(near_out))
        tiny_out_far = take(len(tiny_out))
        tiny_refs = take(len(tiny))
        tiny_out_refs = take(len(tiny_out))
        mover = None
        if sems + copies:
            mover = Mover(refs.pop(), [(f, n) for f, n in zip(tiny_far, tiny_refs)])
        body(*inputs, *tiny_refs, *scalar_refs, *outputs, *tiny_out_refs, *refs, *([mover] if mover else []))
        if mover:
            for source, target in zip(tiny_out_refs, tiny_out_far):
                mover.put(source, target)
            mover.finish()

    return pl.pallas_call(
        run,
        out_shape=(
            *(pltpu.HBM(out.shape, out.dtype) for out in far_out),
            *near_out,
            *(pltpu.HBM(out.shape, out.dtype) for out in tiny_out),
        ),
        in_specs=[FAR] * len(far)
        + [NEAR] * len(near)
        + [FAR] * len(tiny)
        + [pl.BlockSpec(memory_space=pltpu.SMEM)] * len(scalars)
        + [FAR] * held,
        out_specs=(FAR,) * len(far_out) + (NEAR,) * len(near_out) + (FAR,) * len(tiny_out),
        scratch_shapes=buffers(*tiny, *tiny_out)
        + tuple(scratch)
        + ((pltpu.SemaphoreType.DMA((sems + copies,)),) if sems + copies else ()),
        compiler_params=pltpu.CompilerParams(vmem_limit_bytes=limit * MIB),
        name=getattr(body, "func", body).__name__,
        cost_estimate=pl.CostEstimate(flops=int(cost * 1.1e9), bytes_accessed=0, transcendentals=0),
    )(*pinned(far), *near, *pinned(tiny), *scalars, *pinned(after), *after_near)


def buffers(*arrays):
    return tuple(pltpu.VMEM(a.shape, a.dtype) for a in arrays)


class Mover:
    def __init__(self, sems, first):
        self.sems = sems
        self.used = 0
        self.open = []
        self.first = [self.start(source, target) for source, target in first]

    def start(self, source, target):
        copy = pltpu.make_async_copy(source, target, self.sems.at[self.used])
        self.used += 1
        copy.start()
        return copy

    def ready(self):
        for copy in self.first:
            copy.wait()

    def put(self, source, target):
        self.open.append(self.start(source, target))

    def finish(self):
        for copy in self.open:
            copy.wait()


def pieces(count, size):
    return [(at, min(at + size, count)) for at in range(0, count, size)]


def lanes_of(shape):
    return lax.broadcasted_iota(jnp.int32, shape, 1)


def group_total(values):
    chans = values.shape[1]
    lane = lanes_of(values.shape)
    step = 1
    while step < chans // GROUPS:
        up = pltpu.roll(values, chans - step, 1)
        down = pltpu.roll(values, step, 1)
        values = values + jnp.where((lane & step) == 0, up, down)
        step *= 2
    return values


def pack_pair(first, second):
    half = first.shape[0] // 2
    lane = lanes_of((half, first.shape[1])) & 3
    return jnp.where(
        lane == 0,
        first[:half],
        jnp.where(lane == 1, second[:half], jnp.where(lane == 2, first[half:], second[half:])),
    )


def unpack_at(packed, place):
    lane = lanes_of(packed.shape) & 3
    top = group_total(jnp.where(lane == place, packed, 0.0))
    low = group_total(jnp.where(lane == place + 2, packed, 0.0))
    return jnp.concatenate([top, low], axis=0)


def merge_moments(gathered_ref, local_count):
    parts = gathered_ref.shape[0]
    chans = gathered_ref.shape[2]
    every = gathered_ref[...]
    total = jnp.sum(every, axis=0)
    mean = total * (1.0 / parts)
    apart = every - mean[None]
    between = jnp.sum(apart * apart, axis=0)
    square = pltpu.roll(total, chans - 1, 1) + local_count * between
    inv = lax.rsqrt(square * (1.0 / (local_count * parts)) + EPSILON)
    return unpack_at(mean, 0), unpack_at(inv, 0)


def local_moments(total, square, pilot, pixels, per):
    off = total * (1.0 / pixels)
    mean = pilot + off
    apart = square - total * off
    group_mean = group_total(mean) * (1.0 / per)
    shift = mean - group_mean
    return group_mean, group_total(apart + pixels * shift * shift)


def sigmoid(values):
    return 0.5 + 0.5 * jnp.tanh(0.5 * values)


def forward_weights(kernel_ref, pair_ref):
    chans = kernel_ref.shape[2]
    zero = jnp.zeros((chans, chans), BF16)
    for row in range(3):
        for col in range(4):
            at = (row * 4 + col) * chans
            pair_ref[at : at + chans, 0:chans] = kernel_ref[row, col] if col < 3 else zero
            pair_ref[at : at + chans, chans:] = kernel_ref[row, col - 1] if col > 0 else zero


def backward_weights(kernel_ref, pair_ref):
    chans = kernel_ref.shape[2]
    zero = jnp.zeros((chans, chans), BF16)
    for row in range(3):
        for col in range(4):
            at = (row * 4 + col) * chans
            pair_ref[0:chans, at : at + chans] = kernel_ref[2 - row, 2 - col] if col < 3 else zero
            pair_ref[chans:, at : at + chans] = kernel_ref[2 - row, 3 - col] if col > 0 else zero


def convolve(cells_ref, pair_ref, transposed, rows, first, last, take):
    images, chans = cells_ref.shape[2:]
    pairs = (last - first) // 2
    parts = []
    for row in range(3):
        for col in range(4):
            window = [cells_ref[first + 2 * q + col, row : row + rows] for q in range(pairs)]
            parts.append(jnp.stack(window).reshape(pairs * rows * images, chans))
    wide = jnp.concatenate(parts, axis=1)
    contract = ((1,), (1,)) if transposed else ((1,), (0,))
    made = lax.dot_general(wide, pair_ref[...], (contract, ((), ())), preferred_element_type=F32)
    made = made.reshape(pairs, rows, images, 2 * chans)
    for q in range(pairs):
        for side in range(2):
            take(first + 2 * q + side, made[q, :, :, side * chans : (side + 1) * chans])


def grad_terms(cells_ref, grads_ref):
    cols, rows, images, chans = grads_ref.shape
    pixels = cols * rows * images
    windows = [
        cells_ref[col : col + cols, row : row + rows].reshape(pixels, chans) for row in range(3) for col in range(3)
    ]
    return lax.dot_general(
        grads_ref[...].reshape(pixels, chans),
        jnp.concatenate(windows, axis=1),
        (((0,), (0,)), ((), ())),
        preferred_element_type=F32,
    )


def split_taps(every, keep_ref, send_ref):
    chans = every.shape[0]
    half = chans // 2
    first = lax.axis_index("ha") % 2 == 0
    for tap in range(9):
        made = every[:, tap * chans : (tap + 1) * chans].T
        at = tap * half
        keep_ref[at : at + half, :] = jnp.where(first, made[:half], made[half:])
        send_ref[at : at + half, :] = jnp.where(first, made[half:], made[:half])


def at_edges():
    tall = lax.axis_index("ha")
    wide = lax.axis_index("wa")
    return (
        tall == 0,
        tall == lax.axis_size("ha") - 1,
        wide == 0,
        wide == lax.axis_size("wa") - 1,
    )


def clear_border(cells_ref, width, first=0, last=None):
    top, bottom, left, right = at_edges()
    cols, rows, images, chans = cells_ref.shape
    last = cols if last is None else last
    dtype = cells_ref.dtype

    @pl.when(top)
    def _():
        cells_ref[first:last, 0:width] = jnp.zeros((last - first, width, images, chans), dtype)

    @pl.when(bottom)
    def _():
        cells_ref[first:last, rows - width :] = jnp.zeros((last - first, width, images, chans), dtype)

    if first == 0:

        @pl.when(left)
        def _():
            cells_ref[0:width] = jnp.zeros((width, rows, images, chans), dtype)

    if last == cols:

        @pl.when(right)
        def _():
            cells_ref[cols - width :] = jnp.zeros((width, rows, images, chans), dtype)


def send_payload(mover, packed, pay_ref, stage_ref):
    stage_ref[...] = jnp.broadcast_to(packed[None], stage_ref.shape)
    mover.put(stage_ref, pay_ref)


def prepare_x(x_far, xt_far, near_ref, next_ref, sides_ref, moments_ref, x_ref, xt_ref, mover):
    images, rows, cols, chans = x_ref.shape
    steps = pieces(rows, 2)
    loads = [mover.start(x_far.at[:, a:b], x_ref.at[:, a:b]) for a, b in steps]
    total = jnp.zeros((images, chans), F32)
    square = total
    for (a, b), load in zip(steps, loads):
        load.wait()
        if a == 0:
            pilot = x_ref[:, 0, 0].astype(F32)
        for row in range(a, b):
            x = jnp.swapaxes(x_ref[:, row].astype(F32), 0, 1)
            xt_ref[:, row] = x.astype(BF16)
            apart = x - pilot[None]
            total = total + jnp.sum(apart, axis=0)
            square = square + jnp.sum(apart * apart, axis=0)
        mover.put(xt_ref.at[:, a:b], xt_far.at[:, a:b])
    mean, spread = local_moments(total, square, pilot, rows * cols, chans // GROUPS)
    moments_ref[...] = pack_pair(mean, spread)
    outer(xt_ref, near_ref, next_ref, sides_ref)


def is_even(axis="ha"):
    return lax.axis_index(axis) % 2 == 0


def outer(cells, near_ref, next_ref, sides_ref):
    cols, rows = cells.shape[0:2]
    down, up = cells[:, rows - 2 :], cells[:, 0:2]
    near_ref[...] = jnp.where(is_even(), down, up)
    next_ref[...] = jnp.where(is_even(), up, down)
    sides_ref[0:2] = cells[0:2]
    sides_ref[2:4] = cells[cols - 2 :]


def prepare_g(
    c_far, moments_ref, gt_far, pay_far, near_ref, next_ref, sides_ref, bias_ref, c_ref, gt_ref, stage_ref, mover
):
    images, rows, cols, chans = c_ref.shape
    steps = pieces(rows, 2)
    loads = [mover.start(c_far.at[:, a:b], c_ref.at[:, a:b]) for a, b in steps]
    send_payload(mover, moments_ref[...], pay_far, stage_ref)
    bias = jnp.zeros((images, chans), F32)
    for (a, b), load in zip(steps, loads):
        load.wait()
        for row in range(a, b):
            grad = jnp.swapaxes(c_ref[:, row].astype(F32) * INV_ROOT, 0, 1).astype(BF16)
            gt_ref[:, row] = grad
            bias = bias + jnp.sum(grad.astype(F32), axis=0)
        mover.put(gt_ref.at[:, a:b], gt_far.at[:, a:b])
    bias_ref[...] = bias
    outer(gt_ref, near_ref, next_ref, sides_ref)


def edge_columns(sides_ref, near_ref, next_ref, one_ref, other_ref):
    cols, rows = near_ref.shape[0], sides_ref.shape[1]
    even = is_even("wa")

    def piece(left, right):
        return jnp.where(even, right, left), jnp.where(even, left, right)

    near = piece(near_ref[0:2], near_ref[cols - 2 : cols])
    following = piece(next_ref[0:2], next_ref[cols - 2 : cols])
    own = piece(sides_ref[0:2], sides_ref[2:4])
    for at, ref in enumerate((one_ref, other_ref)):
        ref[:, 0:2] = jnp.where(is_even(), following[at], near[at])
        ref[:, 2 : rows + 2] = own[at]
        ref[:, rows + 2 :] = jnp.where(is_even(), near[at], following[at])


def fill_halo(cells_ref, near_ref, next_ref, one_ref, other_ref, change):
    cols, rows = near_ref.shape[0], cells_ref.shape[1] - 4

    def halo_column(col, _):
        near, next_ = near_ref[pl.ds(col, 1)], next_ref[pl.ds(col, 1)]
        cells_ref[pl.ds(col + 2, 1), 0:2] = change(jnp.where(is_even(), next_, near))
        cells_ref[pl.ds(col + 2, 1), rows + 2 :] = change(jnp.where(is_even(), near, next_))
        return 0

    even = is_even("wa")
    cells_ref[0:2] = change(jnp.where(even, other_ref[...], one_ref[...]))
    cells_ref[cols + 2 :] = change(jnp.where(even, one_ref[...], other_ref[...]))
    lax.fori_loop(0, cols, halo_column, 0, unroll=4)


def first_half(
    xt_far, kernel_far, near_ref, next_ref, one_ref, other_ref, gathered_ref, gain_ref, bias_ref, kbias_ref,
    act_far, mid_far, pay_far, stat_ref,
    xt_ref, kernel_ref, act_ref, mid_ref, stage_ref, pair_ref, mover,
):
    cols, rows, images, chans = xt_ref.shape
    per = chans // GROUPS
    load = mover.start(kernel_far, kernel_ref)
    steps = pieces(cols, 8)
    own = [mover.start(xt_far.at[a:b], xt_ref.at[a:b]) for a, b in steps]
    mean, inv = merge_moments(gathered_ref, rows * cols * per)
    stat_ref[0] = mean
    stat_ref[1] = inv
    mover.ready()
    slope = 0.5 * inv * gain_ref[...].astype(F32)
    offset = 0.5 * bias_ref[...].astype(F32)

    def act(cells):
        value = (cells.astype(F32) - mean) * slope + offset
        return (value + value * jnp.tanh(value)).astype(BF16)

    def column(col, _):
        act_ref[pl.ds(col + 2, 1), 2 : rows + 2] = act(xt_ref[pl.ds(col, 1)])
        return 0

    fill_halo(act_ref, near_ref, next_ref, one_ref, other_ref, act)
    for (a, b), copy in zip(steps, own):
        copy.wait()
        lax.fori_loop(a, b, column, 0, unroll=2)
    clear_border(act_ref, 2)
    load.wait()
    forward_weights(kernel_ref, pair_ref)
    mover.put(act_ref, act_far)

    wide = cols + 2
    kbias = kbias_ref[...].astype(F32)
    state = [None, jnp.zeros((images, chans), F32), jnp.zeros((images, chans), F32)]

    def take(col, values):
        values = values + kbias
        mid_ref[col] = values
        if 1 <= col <= cols:
            own = values[1 : rows + 1]
            if state[0] is None:
                state[0] = own[0]
            apart = own - state[0][None]
            state[1] = state[1] + jnp.sum(apart, axis=0)
            state[2] = state[2] + jnp.sum(apart * apart, axis=0)

    for a, b in pieces(wide, 10):
        convolve(act_ref, pair_ref, False, rows + 2, a, b, take)
        mover.put(mid_ref.at[a:b], mid_far.at[a:b])
    pilot, total, square = state
    mean, spread = local_moments(total, square, pilot, rows * cols, per)
    send_payload(mover, pack_pair(mean, spread), pay_far, stage_ref)


def back_two(
    gt_far, kernel_far, weight_far, near_ref, next_ref, one_ref, other_ref, *refs,
):
    text_ref, fbias_ref, freqs_ref, times_ref, levels_ref, out_far, film_ref, ints_ref, *refs = refs
    gt_ref, kernel_ref, weight_ref, cells_ref, out_ref, pair_ref, mover = refs
    cols, rows = gt_ref.shape[0:2]
    load = mover.start(kernel_far, kernel_ref)
    steps = pieces(cols, 8)
    own = [mover.start(gt_far.at[a:b], gt_ref.at[a:b]) for a, b in steps]
    late = mover.start(weight_far, weight_ref)
    fill_halo(cells_ref, near_ref, next_ref, one_ref, other_ref, lambda cells: cells)
    load.wait()
    backward_weights(kernel_ref, pair_ref)
    mover.ready()
    text = text_ref[...].astype(F32)
    half = TEMB // 2
    for at, source_ref in ((0, times_ref), (TEMB, levels_ref)):
        angles = [source_ref[image].astype(F32) * freqs_ref[...] for image in range(text_ref.shape[0])]
        angles = jnp.concatenate(angles, axis=0)
        for start, embed in ((at, jnp.sin(angles)), (at + half, jnp.cos(angles))):
            ints_ref[:, start : start + half] = (embed * sigmoid(embed)).astype(BF16)
    act = jnp.concatenate([ints_ref[...], (text * sigmoid(text)).astype(BF16)], axis=1)
    for (a, b), copy in zip(steps, own):
        copy.wait()
        cells_ref[a + 2 : b + 2, 2 : rows + 2] = gt_ref[a:b]
    clear_border(cells_ref, 2)
    for a, b in pieces(cols + 2, 10):
        convolve(cells_ref, pair_ref, True, rows + 2, a, b, lambda col, values: out_ref.__setitem__(col, values))
        mover.put(out_ref.at[a:b], out_far.at[a:b])
    late.wait()
    film_ref[...] = jnp.dot(act, weight_ref[...], preferred_element_type=F32) + fbias_ref[...].astype(F32)


def second_values(stat, gain_ref, bias_ref, film_ref):
    mean, inv = stat
    chans = mean.shape[1]
    scale = 1.0 + film_ref[:, 0:chans]
    slope = gain_ref[...].astype(F32) * scale
    half_slope = 0.5 * slope
    half_offset = 0.5 * (bias_ref[...].astype(F32) * scale + film_ref[:, chans:])

    def values(mid, back):
        hat = (mid - mean) * inv
        pre = hat * half_slope + half_offset
        bend = jnp.tanh(pre)
        more = 1.0 + bend
        grad = back * (0.5 * more * (1.0 + pre * (1.0 - bend)))
        return hat, pre * more, grad

    return slope, values


def second_norm(
    mid_far, back_far, gathered_ref, gain_ref, bias_ref, film_ref,
    act_far, pre_far, pay_far, sums_ref, stat_ref,
    mid_ref, back_ref, act_ref, pre_ref, stage_ref, mover,
):
    wide, tall, images, chans = mid_ref.shape
    cols, rows = wide - 2, tall - 2
    per = chans // GROUPS
    steps = pieces(wide, 9)
    loads = []
    for a, b in steps:
        loads.append(
            [mover.start(f.at[a:b], n.at[a:b]) for f, n in ((mid_far, mid_ref), (back_far, back_ref))]
        )
    mean, inv = merge_moments(gathered_ref, rows * cols * per)
    stat_ref[0] = mean
    stat_ref[1] = inv
    mover.ready()
    slope, values = second_values((mean, inv), gain_ref, bias_ref, film_ref)

    def column(col, inner):
        hat, act, grad = values(mid_ref[col], back_ref[col])
        act_ref[col] = act.astype(BF16)
        pre_ref[col] = grad
        if inner is None:
            return None
        own = grad[1 : rows + 1]
        plain, cross = inner
        return plain + jnp.sum(own, axis=0), cross + jnp.sum(own * hat[1 : rows + 1], axis=0)

    zero = jnp.zeros((images, chans), F32)
    inner = (zero, zero)
    for (a, b), pair in zip(steps, loads):
        for load in pair:
            load.wait()
        if a == 0:
            column(0, None)
        inner = lax.fori_loop(max(a, 1), min(b, cols + 1), column, inner)
        if b == wide:
            column(wide - 1, None)
        clear_border(act_ref, 1, a, b)
        mover.put(act_ref.at[a:b], act_far.at[a:b])
        mover.put(pre_ref.at[a:b], pre_far.at[a:b])
    plain, cross = inner
    sums_ref[0] = plain
    sums_ref[1] = cross
    send_payload(mover, pack_pair(group_total(plain * slope), group_total(cross * slope)), pay_far, stage_ref)


def kernel_two(
    act_far, gt_far, sums_ref, bias_ref, keep_far, send_far, act_ref, gt_ref, keep_ref, send_ref, mover
):
    for load in [mover.start(act_far, act_ref), mover.start(gt_far, gt_ref)]:
        load.wait()
    split_taps(grad_terms(act_ref, gt_ref), keep_ref, send_ref)
    mover.ready()
    images, chans = bias_ref.shape
    at = 9 * (chans // 2)
    total = jnp.sum(bias_ref[...], axis=0, keepdims=True)
    for ref in (keep_ref, send_ref):
        ref[at : at + images] = sums_ref[0]
        ref[at + images : at + 2 * images] = sums_ref[1]
        ref[at + 2 * images :] = jnp.broadcast_to(total, (ref.shape[0] - at - 2 * images, chans))
    mover.put(keep_ref, keep_far)
    mover.put(send_ref, send_far)


def mix(
    act_far, kernel_far, xt_far, kbias_ref, out_far, act_ref, kernel_ref, xt_ref, branch_ref, out_ref, pair_ref, mover
):
    images, rows, cols, chans = out_ref.shape
    loads = [mover.start(f, n) for f, n in ((kernel_far, kernel_ref), (act_far, act_ref), (xt_far, xt_ref))]
    loads[0].wait()
    forward_weights(kernel_ref, pair_ref)
    mover.ready()
    kbias = kbias_ref[...].astype(F32)
    loads[1].wait()
    convolve(
        act_ref, pair_ref, False, rows, 0, cols, lambda col, values: branch_ref.__setitem__(col, values + kbias)
    )
    loads[2].wait()
    for a, b in pieces(rows, 2):
        for row in range(a, b):
            mixed = jnp.swapaxes((xt_ref[:, row].astype(F32) + branch_ref[:, row]) * INV_ROOT, 0, 1)
            out_ref[:, row] = mixed.astype(BF16)
        mover.put(out_ref.at[:, a:b], out_far.at[:, a:b])


def middle_grad(
    mid_far, pre_far, act_far, keep_two_far, gathered_ref, stat_ref, gain_ref, film_ref,
    low_far, keep_ref, send_ref, two_ref,
    mid_ref, pre_ref, act_ref, low_ref, mover,
):
    wide, tall, images, chans = mid_ref.shape
    cols, rows = wide - 2, tall - 2
    steps = pieces(wide, 9)
    loads = []
    for a, b in steps:
        loads.append([mover.start(f.at[a:b], n.at[a:b]) for f, n in ((mid_far, mid_ref), (pre_far, pre_ref))])
    late = [mover.start(f, n) for f, n in ((act_far, act_ref), (keep_two_far, two_ref))]
    count = lax.axis_size("ha") * lax.axis_size("wa") * rows * cols * (chans // GROUPS)
    packed = jnp.sum(gathered_ref[...], axis=0) * (1.0 / count)
    mover.ready()
    mean = stat_ref[0]
    inv = stat_ref[1]
    plain = unpack_at(packed, 0) * inv
    cross = unpack_at(packed, 1) * inv * inv
    slope = gain_ref[...].astype(F32) * (1.0 + film_ref[:, 0:chans]) * inv

    def low_column(col, total):
        low = (pre_ref[col] * slope - plain - (mid_ref[col] - mean) * cross).astype(BF16)
        low_ref[col] = low
        if total is None:
            return None
        return total + jnp.sum(low[1 : rows + 1].astype(F32), axis=0)

    kbias = jnp.zeros((images, chans), F32)
    for (a, b), pair in zip(steps, loads):
        for load in pair:
            load.wait()
        if a == 0:
            low_column(0, None)
        kbias = lax.fori_loop(max(a, 1), min(b, cols + 1), low_column, kbias)
        if b == wide:
            low_column(wide - 1, None)
        clear_border(low_ref, 1, a, b)
        mover.put(low_ref.at[a:b], low_far.at[a:b])
    for load in late:
        load.wait()
    own = low_ref.at[1 : wide - 1, 1 : tall - 1]
    split_taps(grad_terms(act_ref.at[1 : wide + 1, 1 : tall + 1], own), keep_ref, send_ref)
    at = 9 * (chans // 2)
    for ref in (keep_ref, send_ref):
        ref[at:] = jnp.broadcast_to(jnp.sum(kbias, axis=0, keepdims=True), (ref.shape[0] - at, chans))


def back_one(
    low_far, xt_far, kernel_far, stat_ref, gain_ref, bias_ref, grad_far, pay_ref, low_ref, xt_ref, kernel_ref, out_ref, pair_ref, mover
):
    cols, rows, images, chans = xt_ref.shape
    loads = [mover.start(f, n) for f, n in ((kernel_far, kernel_ref), (low_far, low_ref), (xt_far, xt_ref))]
    loads[0].wait()
    backward_weights(kernel_ref, pair_ref)
    loads[1].wait()
    loads[2].wait()
    mover.ready()
    mean = stat_ref[0]
    inv = stat_ref[1]
    gain = gain_ref[...].astype(F32)
    bias = bias_ref[...].astype(F32)
    state = [jnp.zeros((images, chans), F32), jnp.zeros((images, chans), F32)]

    def take(col, values):
        hat = (xt_ref[col].astype(F32) - mean) * inv
        norm = hat * gain + bias
        sigma = sigmoid(norm)
        grad = values * (sigma * (1.0 + norm * (1.0 - sigma)))
        out_ref[col] = grad
        state[0] = state[0] + jnp.sum(grad, axis=0)
        state[1] = state[1] + jnp.sum(grad * hat, axis=0)

    for a, b in pieces(cols, 8):
        convolve(low_ref, pair_ref, True, rows, a, b, take)
        mover.put(out_ref.at[a:b], grad_far.at[a:b])
    plain, cross = state
    half = images // 2
    pay_ref[0:half] = pack_pair(group_total(plain * gain), group_total(cross * gain))
    rest = [jnp.sum(v, axis=0, keepdims=True) for v in (cross, plain)]
    short = pay_ref.shape[0] - half - 2
    pay_ref[half:] = jnp.concatenate(rest + [jnp.zeros((short, chans), F32)], axis=0)


CODE = 32768.0


def exponents(values):
    most = jnp.clip(jnp.max(jnp.abs(values), axis=0, keepdims=True), 1e-30, 1e30)
    return jnp.ceil(jnp.log2(most) + 2e-3)


def two_to(powers):
    powers = powers.astype(jnp.int32)
    first = powers >> 1
    made = None
    for part in (first, powers - first):
        shifted = part + 64
        for bit in range(7):
            factor = jnp.where((shifted >> bit) & 1 == 1, 2.0 ** (1 << bit), 1.0)
            if bit == 0:
                piece = factor * 2.0**-64
            else:
                piece = piece * factor
        made = piece if made is None else made * piece
    return made


def pack_terms(
    keep_one_ref, came_one_ref, keep_two_ref, came_two_ref, out_far, token_ref,
    one_ref, two_ref, extra_ref, rest_ref, out_ref, mover, extras_one, extras_two,
):
    chips, rows, chans = out_ref.shape
    taps = 9 * (chans // 2)
    share = -(-taps // chips)
    more = -(-(extras_one + extras_two) // chips)
    extra_ref[...] = jnp.zeros(extra_ref.shape, F32)
    one_ref[...] = keep_one_ref[...] + came_one_ref[...]
    two_ref[...] = keep_two_ref[...] + came_two_ref[...]
    extra_ref[0:extras_two] = two_ref[taps : taps + extras_two]
    extra_ref[extras_two : extras_two + extras_one] = one_ref[taps : taps + extras_one]
    token_ref[...] = extra_ref[0:8]
    powers = []
    for ref, count in ((one_ref, taps), (two_ref, taps), (extra_ref, extra_ref.shape[0])):
        values = ref[0:count]
        power = exponents(values)
        powers.append(power)
        scaled = values * (two_to(-power) * CODE)
        code = jnp.round(scaled)
        ref[0:count] = code
        if ref is extra_ref:
            rest_ref[...] = jnp.round((scaled - code) * CODE)
    short = rows - 2 * share - 2 * more - 3
    pad = [jnp.zeros((short, chans), F32)] if short else []
    for chip in range(chips):
        a, b = chip * share, min((chip + 1) * share, taps)
        mine = []
        for ref in (one_ref, two_ref):
            if a < b:
                mine.append(ref[a:b])
            if max(b - a, 0) < share:
                mine.append(jnp.zeros((share - max(b - a, 0), chans), F32))
        for ref in (extra_ref, rest_ref):
            mine.append(ref[chip * more : (chip + 1) * more])
        whole = jnp.concatenate(mine + powers + pad, axis=0)
        out_ref[chip] = whole.astype(jnp.int32).astype(jnp.int16)
    mover.put(out_ref, out_far)


def unpack_terms(gathered_ref, share, more):
    chips, rows, chans = gathered_ref.shape
    row = lax.broadcasted_iota(jnp.int32, (rows, chans), 0)
    base = 2 * share + 2 * more
    total = jnp.zeros((rows, chans), F32)
    blocks = [gathered_ref[chip].astype(jnp.int32).astype(F32) for chip in range(chips)]
    every = two_to(jnp.concatenate([block[base : base + 3] for block in blocks], axis=0)) * (1.0 / CODE)
    for chip, block in enumerate(blocks):
        scales = every[3 * chip : 3 * chip + 3]
        scale = jnp.where(row < share, scales[0:1], jnp.where(row < 2 * share, scales[1:2], scales[2:3]))
        scale = jnp.where(row < 2 * share + more, scale, scale * (1.0 / CODE))
        total = total + block * scale
    extra = total[2 * share : 2 * share + more] + total[2 * share + more : base]
    return total[0 : 2 * share], extra


def two_terms(values):
    high = values.astype(BF16).astype(F32)
    return [high, values - high]


def add_terms(gathered_ref, pay_ref, came_ref, out_far, out_ref, mover, more, whole):
    chips, rows, chans = gathered_ref.shape
    shares, extra = unpack_terms(gathered_ref, -(-9 * (chans // 2) // chips), more)
    every = [shares] + two_terms(extra) + two_terms(pay_ref[0:whole] + came_ref[0:whole])
    short = out_ref.shape[1] - sum(v.shape[0] for v in every)
    if short:
        every.append(jnp.zeros((short, chans), F32))
    out_ref[...] = jnp.broadcast_to(jnp.concatenate(every, axis=0).astype(BF16)[None], out_ref.shape)
    mover.put(out_ref, out_far)


def sums_of(own_ref, at, whole):
    total = own_ref[0].astype(F32)
    for chip in range(1, own_ref.shape[0]):
        total = total + own_ref[chip].astype(F32)
    return total[at : at + whole] + total[at + whole : at + 2 * whole]


def three_terms(values):
    high = values.astype(BF16)
    rest = values - high.astype(F32)
    mid = rest.astype(BF16)
    low = (rest - mid.astype(F32)).astype(BF16)
    return jnp.concatenate([high, mid, low], axis=0)


def spread_out(own_ref, other_ref, one_far, two_far, one_ref, two_ref, half_ref, mover):
    chips, rows, chans = own_ref.shape
    half = chans // 2
    taps = 9 * half
    share = -(-taps // chips)
    core = lax.axis_index("ha") % 2
    for at, (out_ref, far) in enumerate(((one_ref, one_far), (two_ref, two_far))):
        for source, place in ((own_ref, core), (other_ref, 1 - core)):
            for chip in range(chips):
                piece = source[chip].astype(F32)[at * share : (at + 1) * share]
                half_ref[chip * share : (chip + 1) * share] = piece
            for tap in range(9):
                rows_at = pl.ds(pl.multiple_of(place * half, half), half)
                out_ref[tap, rows_at] = half_ref[tap * half : (tap + 1) * half]
        mover.put(out_ref, far)


def last_grads(
    weight_far, grad_ref, xt_ref, c_ref, own_ref, stat_ref, gain_one_ref, gain_two_ref, bias_two_ref, film_ref, ints_ref, text_ref,
    out_far, weight_grad_far, text_grad_far, bias_ref, *refs, more, whole,
):
    *vec_refs, weight_ref, out_ref, weight_grad_ref, text_grad_ref, extra_ref, mover = refs
    images, rows, cols, chans = out_ref.shape
    chips = own_ref.shape[0]
    load = mover.start(weight_far, weight_ref)
    share = -(-9 * (chans // 2) // chips)
    start = 2 * share
    for chip in range(chips):
        piece = own_ref[chip].astype(F32)
        extra_ref[chip * more : (chip + 1) * more] = piece[start : start + more] + piece[start + more : start + 2 * more]
    plain = extra_ref[0:images]
    cross = extra_ref[images : 2 * images]
    mover.ready()
    scale = 1.0 + film_ref[:, 0:chans]
    scale_grad = gain_two_ref[...].astype(F32) * cross + bias_two_ref[...].astype(F32) * plain
    film_grad = jnp.concatenate([scale_grad, plain], axis=1)
    bias_ref[...] = jnp.sum(film_grad, axis=0, keepdims=True)
    sums = sums_of(own_ref, start + 2 * more, whole)
    vec_refs[0][...] = jnp.sum(scale * cross, axis=0, keepdims=True)
    vec_refs[1][...] = jnp.sum(scale * plain, axis=0, keepdims=True)
    for at, row in enumerate((extra_ref[2 * images : 2 * images + 1], extra_ref[2 * images + 1 : 2 * images + 2])):
        vec_refs[2 + at][...] = row
    vec_refs[4][...] = sums[whole - 2 : whole - 1]
    vec_refs[5][...] = sums[whole - 1 : whole]
    terms = three_terms(film_grad)
    ints = ints_ref.shape[1]

    depth = weight_grad_ref.shape[0]
    for at in range(0, depth, 512):
        if at < ints:
            act = ints_ref[:, at : at + 512]
        else:
            embed = text_ref[:, at - ints : at - ints + 512].astype(F32)
            act = (embed * sigmoid(embed)).astype(BF16)
        weight_grad_ref[at : at + 512] = lax.dot_general(
            jnp.concatenate([act, act, act], axis=0), terms, (((0,), (0,)), ((), ())), preferred_element_type=F32
        )
        mover.put(weight_grad_ref.at[at : at + 512], weight_grad_far.at[at : at + 512])

    count = lax.axis_size("ha") * lax.axis_size("wa") * rows * cols * (chans // GROUPS)
    packed = sums[0 : images // 2] * (1.0 / count)
    plain = unpack_at(packed, 0)
    cross = unpack_at(packed, 1)
    mean = stat_ref[0]
    inv = stat_ref[1]
    gain = gain_one_ref[...].astype(F32)
    for a, b in pieces(rows, 2):
        for row in range(a, b):
            hat = (xt_ref[:, row].astype(F32) - mean) * inv
            path = jnp.swapaxes(inv * (grad_ref[:, row] * gain - plain - hat * cross), 0, 1)
            out_ref[:, row] = (c_ref[:, row].astype(F32) * INV_ROOT + path).astype(BF16)
        mover.put(out_ref.at[:, a:b], out_far.at[:, a:b])

    load.wait()
    for at in range(ints, depth, 512):
        embed = text_ref[:, at - ints : at - ints + 512].astype(F32)
        sigma = sigmoid(embed)
        made = lax.dot_general(
            terms, weight_ref[at : at + 512], (((1,), (1,)), ((), ())), preferred_element_type=F32
        )
        cond_grad = made[0:images] + made[images : 2 * images] + made[2 * images :]
        text_grad_ref[:, at - ints : at - ints + 512] = cond_grad * (sigma * (1.0 + embed * (1.0 - sigma)))
    mover.put(text_grad_ref, text_grad_far)


def to_all(payload):
    return lax.all_to_all(payload, AXES, 0, 0)


def to_chips(payload):
    tall, wide = lax.axis_size("ha"), lax.axis_size("wa")
    groups = [[h * wide + w for h in range(core, tall, 2) for w in range(wide)] for core in range(2)]
    return lax.all_to_all(payload, AXES, 0, 0, axis_index_groups=groups)


def to_sibling(payload):
    return lax.ppermute(payload, "ha", [(i, i ^ 1) for i in range(lax.axis_size("ha"))])


def pair_exchange(one, other, axis):
    count = lax.axis_size(axis)
    pairs = [(i, (i + 1 if i % 2 else i - 1) % count) for i in range(count)]
    if axis == "wa":
        pairs = [(i, min(max(j, 0), count - 1) if abs(i - j) == 1 else i) for i, j in pairs]
    one = lax.ppermute(one, axis, [(i, i ^ 1) for i in range(count)])
    return one, lax.ppermute(other, axis, pairs)


def side_halo(sides, near, following, after=()):
    four, rows, images, chans = sides.shape
    edge = shaped((2, rows + 4, images, chans), sides.dtype)
    one, other = kernel_call(
        edge_columns, near=(sides, near, following), near_out=(edge, edge), cost=0.4, after=after, limit=16
    )
    return pair_exchange(one, other, "wa"), one


def local(
    block_input,
    timesteps,
    aug_levels,
    text_pooled,
    gain_one,
    bias_one,
    conv_one,
    conv_one_bias,
    gain_two,
    bias_two,
    film_weight,
    film_bias,
    conv_two,
    conv_two_bias,
    cotangent,
):
    images, rows, cols, chans = block_input.shape
    parts = lax.axis_size("ha") * lax.axis_size("wa")
    chips = parts // 2
    half = images // 2
    gain_one, bias_one, conv_one_bias, gain_two, bias_two, conv_two_bias = (
        v.reshape(1, chans) for v in (gain_one, bias_one, conv_one_bias, gain_two, bias_two, conv_two_bias)
    )
    freqs = np.exp(-math.log(10000.0) * np.arange(TEMB // 2) / (TEMB // 2)).astype(np.float32)[None]
    payload = shaped((parts, half, chans), F32)
    per_image = shaped((images, chans), F32)
    two_images = shaped((2, images, chans), F32)
    block = shaped((cols, rows, images, chans), BF16)
    block_wide = shaped((cols, rows, images, chans), F32)
    rim = shaped((cols + 2, rows + 2, images, chans), BF16)
    rim_wide = shaped((cols + 2, rows + 2, images, chans), F32)
    far_rim = shaped((cols + 4, rows + 4, images, chans), BF16)
    given = shaped((images, rows, cols, chans), BF16)
    pair = pltpu.VMEM((12 * chans, 2 * chans), BF16)
    pair_back = pltpu.VMEM((2 * chans, 12 * chans), BF16)

    sides = shaped((4, rows, images, chans), BF16)
    row_halo = shaped((cols, 2, images, chans), BF16)
    xt, x_near, x_next, x_sides, moments = kernel_call(
        prepare_x, far=(block_input,), far_out=(block,),
        near_out=(row_halo, row_halo, sides, shaped((half, chans), F32)),
        scratch=buffers(given, block), sems=16, cost=2.3,
    )
    x_near, x_next = pair_exchange(x_near, x_next, "ha")
    gt, pay_one, g_near, g_next, g_sides, kbias_two_local = kernel_call(
        prepare_g, far=(cotangent,), near=(moments,), far_out=(block, payload),
        near_out=(row_halo, row_halo, sides), tiny_out=(per_image,),
        scratch=buffers(given, block, payload), sems=16, cost=2.0,
    )
    moments_one = to_all(pay_one)
    x_cols, x_edge = side_halo(x_sides, x_near, x_next)
    g_near, g_next = pair_exchange(g_near, g_next, "ha")

    film_bias = film_bias.reshape(1, 2 * chans)
    act_one, mid, pay_two, stat_one = kernel_call(
        first_half, far=(xt, conv_one), near=(x_near, x_next, *x_cols, moments_one),
        tiny=(gain_one, bias_one, conv_one_bias),
        far_out=(far_rim, rim_wide, payload), tiny_out=(two_images,),
        scratch=buffers(xt, conv_one, far_rim, rim_wide, payload) + (pair,), sems=16, cost=5.5,
        after=(film_bias,),
    )
    moments_two = to_all(pay_two)
    g_cols, _ = side_halo(g_sides, g_near, g_next, after=(stat_one,))
    act_two_grad, film, act_ints = kernel_call(
        back_two, far=(gt, conv_two, film_weight), near=(g_near, g_next, *g_cols),
        tiny=(text_pooled, film_bias, freqs), scalars=(timesteps, aug_levels),
        far_out=(rim_wide,), tiny_out=(shaped((images, 2 * chans), F32), shaped((images, 2 * TEMB), BF16)),
        scratch=buffers(gt, conv_two, film_weight, far_rim, rim_wide) + (pair_back,), sems=16, cost=5.0,
    )
    act_two, pre_two_grad, pay_three, sums_two, stat_two = kernel_call(
        second_norm, far=(mid, act_two_grad), near=(moments_two,), tiny=(gain_two, bias_two, film),
        far_out=(rim, rim_wide, payload), tiny_out=(two_images, two_images),
        scratch=buffers(rim_wide, rim_wide, rim, rim_wide, payload), sems=24, cost=3.2,
    )
    moments_three = to_all(pay_three)

    taps = 9 * (chans // 2)
    share = -(-taps // chips)
    extras_two = 2 * images + 1
    extras_one = 1
    halves_two = shaped((taps + 2 * images + 8, chans), F32)
    halves_one = shaped((taps + 8, chans), F32)
    keep_two, send_two = kernel_call(
        kernel_two, far=(act_two, gt), tiny=(sums_two, kbias_two_local), far_out=(halves_two, halves_two),
        scratch=buffers(act_two, gt, halves_two, halves_two), sems=4, cost=3.0,
    )
    came_two = to_sibling(send_two)
    low, keep_one, send_one, keep_two = kernel_call(
        middle_grad, far=(mid, pre_two_grad, act_one, keep_two), near=(moments_three,), tiny=(stat_two, gain_two, film),
        far_out=(rim,), near_out=(halves_one, halves_one, halves_two),
        scratch=buffers(mid, pre_two_grad, act_one, rim), sems=24, cost=6.0,
    )
    came_one = to_sibling(send_one)
    more = -(-(extras_one + extras_two) // chips)
    terms_shape = shaped((chips, -(-(2 * share + 2 * more + 3) // 8) * 8, chans), jnp.int16)
    extra_shape = shaped((-(-chips * more // 8) * 8, chans), F32)
    terms, token = kernel_call(
        functools.partial(pack_terms, extras_one=extras_one, extras_two=extras_two),
        near=(keep_one, came_one, keep_two, came_two), far_out=(terms_shape,), near_out=(shaped((8, chans), F32),),
        scratch=buffers(halves_one, halves_two, extra_shape, extra_shape, terms_shape),
        sems=3, cost=1.0,
    )
    gathered = to_chips(terms)
    whole = half + 2
    norm_one_grad, pay_four = kernel_call(
        back_one, far=(low, xt, conv_one), tiny=(stat_one, gain_one, bias_one), far_out=(block_wide,),
        near_out=(shaped((2 * half, chans), F32),),
        scratch=buffers(rim, block, conv_one, block_wide) + (pair_back,), sems=16, cost=5.0,
        after_near=(to_sibling(token),),
    )
    came_four = to_sibling(pay_four)
    (mixed,) = kernel_call(
        mix, far=(act_two, conv_two, xt), tiny=(conv_two_bias,), far_out=(given,),
        scratch=buffers(act_two, conv_two, xt, block_wide, given) + (pair,), sems=8, cost=3.6, after_near=(pay_four,),
    )
    shares_shape = shaped((chips, -(-(2 * share + 2 * more + 2 * whole) // 8) * 8, chans), BF16)
    (shares,) = kernel_call(
        functools.partial(add_terms, more=more, whole=whole),
        near=(gathered, pay_four, came_four), far_out=(shares_shape,),
        scratch=buffers(shares_shape), sems=1, cost=1.0, after=(mixed,),
    )
    own_half = to_chips(shares)
    other_half = to_sibling(own_half)
    weight_grad = shaped(film_weight.shape, F32)
    text_shape = shaped(text_pooled.shape, F32)
    row = shaped((1, chans), F32)
    input_grad, film_weight_grad, text_grad, film_bias_grad, *vec_grads = kernel_call(
        functools.partial(last_grads, more=more, whole=whole),
        far=(film_weight,),
        near=(norm_one_grad, xt, cotangent, own_half, stat_one, gain_one, gain_two, bias_two, film, act_ints, text_pooled),
        far_out=(given, weight_grad, text_shape), tiny_out=(shaped((1, 2 * chans), F32),) + (row,) * 6,
        scratch=buffers(film_weight, given, weight_grad, text_shape)
        + (pltpu.VMEM((-(-chips * more // 8) * 8, chans), F32),),
        sems=32, cost=6.0, limit=24,
    )
    full = shaped((9, chans, chans), F32)
    kernel_one_grad, kernel_two_grad = kernel_call(
        spread_out, near=(own_half, other_half), far_out=(full, full),
        scratch=buffers(full, full, shaped((chips * share, chans), F32)), sems=2, cost=2.0, after=(input_grad,), limit=24,
    )
    return (
        mixed,
        input_grad,
        text_grad,
        vec_grads[4].reshape(chans),
        vec_grads[5].reshape(chans),
        kernel_one_grad.reshape(3, 3, chans, chans),
        vec_grads[3].reshape(chans),
        vec_grads[0].reshape(chans),
        vec_grads[1].reshape(chans),
        film_weight_grad,
        film_bias_grad.reshape(2 * chans),
        kernel_two_grad.reshape(3, 3, chans, chans),
        vec_grads[2].reshape(chans),
    )


def solution(mesh):
    split = P(None, "ha", "wa", None)
    return jax.shard_map(
        local,
        mesh=mesh,
        in_specs=(split,) + (P(),) * 13 + (split,),
        out_specs=(split, split) + (P(),) * 11,
        check_vma=False,
    )
```

```python
import functools
import math

import jax
import jax.numpy as jnp
import numpy as np
from jax import lax
from jax.experimental import pallas as pl
from jax.experimental.pallas import tpu as pltpu
from jax.sharding import PartitionSpec as P

GROUPS = 32
TEMB = 256
EPSILON = 1e-05
INV_ROOT = 1.0 / math.sqrt(2.0)
AXES = ("ha", "wa")
F32 = jnp.float32
BF16 = jnp.bfloat16
NEAR = pl.BlockSpec(memory_space=pltpu.VMEM)
FAR = pl.BlockSpec(memory_space=pl.ANY)
MIB = 1 << 20


def shaped(shape, dtype):
    return jax.ShapeDtypeStruct(shape, dtype)


def kernel_call(
    body, far=(), near=(), tiny=(), far_out=(), near_out=(), tiny_out=(), scratch=(), sems=0, cost=1.0,
    after=(), after_near=(), scalars=(), limit=48,
):
    pinned = lambda arrays: [pltpu.with_memory_space_constraint(array, pltpu.HBM) for array in arrays]
    given = len(far) + len(near)
    held = len(after) + len(after_near)
    copies = len(tiny) + len(tiny_out)

    def run(*refs):
        refs = list(refs)
        take = lambda count: [refs.pop(0) for _ in range(count)]
        inputs = take(given)
        tiny_far = take(len(tiny))
        scalar_refs = take(len(scalars))
        take(held)
        outputs = take(len(far_out) + len(near_out))
        tiny_out_far = take(len(tiny_out))
        tiny_refs = take(len(tiny))
        tiny_out_refs = take(len(tiny_out))
        mover = None
        if sems + copies:
            mover = Mover(refs.pop(), [(f, n) for f, n in zip(tiny_far, tiny_refs)])
        body(*inputs, *tiny_refs, *scalar_refs, *outputs, *tiny_out_refs, *refs, *([mover] if mover else []))
        if mover:
            for source, target in zip(tiny_out_refs, tiny_out_far):
                mover.put(source, target)
            mover.finish()

    return pl.pallas_call(
        run,
        out_shape=(
            *(pltpu.HBM(out.shape, out.dtype) for out in far_out),
            *near_out,
            *(pltpu.HBM(out.shape, out.dtype) for out in tiny_out),
        ),
        in_specs=[FAR] * len(far)
        + [NEAR] * len(near)
        + [FAR] * len(tiny)
        + [pl.BlockSpec(memory_space=pltpu.SMEM)] * len(scalars)
        + [FAR] * held,
        out_specs=(FAR,) * len(far_out) + (NEAR,) * len(near_out) + (FAR,) * len(tiny_out),
        scratch_shapes=buffers(*tiny, *tiny_out)
        + tuple(scratch)
        + ((pltpu.SemaphoreType.DMA((sems + copies,)),) if sems + copies else ()),
        compiler_params=pltpu.CompilerParams(vmem_limit_bytes=limit * MIB),
        name=getattr(body, "func", body).__name__,
        cost_estimate=pl.CostEstimate(flops=int(cost * 1.1e9), bytes_accessed=0, transcendentals=0),
    )(*pinned(far), *near, *pinned(tiny), *scalars, *pinned(after), *after_near)


def buffers(*arrays):
    return tuple(pltpu.VMEM(a.shape, a.dtype) for a in arrays)


class Mover:
    def __init__(self, sems, first):
        self.sems = sems
        self.used = 0
        self.open = []
        self.first = [self.start(source, target) for source, target in first]

    def start(self, source, target):
        copy = pltpu.make_async_copy(source, target, self.sems.at[self.used])
        self.used += 1
        copy.start()
        return copy

    def ready(self):
        for copy in self.first:
            copy.wait()

    def put(self, source, target):
        self.open.append(self.start(source, target))

    def finish(self):
        for copy in self.open:
            copy.wait()


def pieces(count, size):
    return [(at, min(at + size, count)) for at in range(0, count, size)]


def lanes_of(shape):
    return lax.broadcasted_iota(jnp.int32, shape, 1)


def group_total(values):
    chans = values.shape[1]
    lane = lanes_of(values.shape)
    step = 1
    while step < chans // GROUPS:
        up = pltpu.roll(values, chans - step, 1)
        down = pltpu.roll(values, step, 1)
        values = values + jnp.where((lane & step) == 0, up, down)
        step *= 2
    return values


def pack_pair(first, second):
    half = first.shape[0] // 2
    lane = lanes_of((half, first.shape[1])) & 3
    return jnp.where(
        lane == 0,
        first[:half],
        jnp.where(lane == 1, second[:half], jnp.where(lane == 2, first[half:], second[half:])),
    )


def unpack_at(packed, place):
    lane = lanes_of(packed.shape) & 3
    top = group_total(jnp.where(lane == place, packed, 0.0))
    low = group_total(jnp.where(lane == place + 2, packed, 0.0))
    return jnp.concatenate([top, low], axis=0)


def merge_moments(gathered_ref, local_count):
    parts = gathered_ref.shape[0]
    chans = gathered_ref.shape[2]
    every = gathered_ref[...]
    total = jnp.sum(every, axis=0)
    mean = total * (1.0 / parts)
    apart = every - mean[None]
    between = jnp.sum(apart * apart, axis=0)
    square = pltpu.roll(total, chans - 1, 1) + local_count * between
    inv = lax.rsqrt(square * (1.0 / (local_count * parts)) + EPSILON)
    return unpack_at(mean, 0), unpack_at(inv, 0)


def local_moments(total, square, pilot, pixels, per):
    off = total * (1.0 / pixels)
    mean = pilot + off
    apart = square - total * off
    group_mean = group_total(mean) * (1.0 / per)
    shift = mean - group_mean
    return group_mean, group_total(apart + pixels * shift * shift)


def sigmoid(values):
    return 0.5 + 0.5 * jnp.tanh(0.5 * values)


def forward_weights(kernel_ref, pair_ref):
    chans = kernel_ref.shape[2]
    zero = jnp.zeros((chans, chans), BF16)
    for row in range(3):
        for col in range(4):
            at = (row * 4 + col) * chans
            pair_ref[at : at + chans, 0:chans] = kernel_ref[row, col] if col < 3 else zero
            pair_ref[at : at + chans, chans:] = kernel_ref[row, col - 1] if col > 0 else zero


def backward_weights(kernel_ref, pair_ref):
    chans = kernel_ref.shape[2]
    zero = jnp.zeros((chans, chans), BF16)
    for row in range(3):
        for col in range(4):
            at = (row * 4 + col) * chans
            pair_ref[0:chans, at : at + chans] = kernel_ref[2 - row, 2 - col] if col < 3 else zero
            pair_ref[chans:, at : at + chans] = kernel_ref[2 - row, 3 - col] if col > 0 else zero


def convolve(cells_ref, pair_ref, transposed, rows, first, last, take):
    images, chans = cells_ref.shape[2:]
    pairs = (last - first) // 2
    parts = []
    for row in range(3):
        for col in range(4):
            window = [cells_ref[first + 2 * q + col, row : row + rows] for q in range(pairs)]
            parts.append(jnp.stack(window).reshape(pairs * rows * images, chans))
    wide = jnp.concatenate(parts, axis=1)
    contract = ((1,), (1,)) if transposed else ((1,), (0,))
    made = lax.dot_general(wide, pair_ref[...], (contract, ((), ())), preferred_element_type=F32)
    made = made.reshape(pairs, rows, images, 2 * chans)
    for q in range(pairs):
        for side in range(2):
            take(first + 2 * q + side, made[q, :, :, side * chans : (side + 1) * chans])


def grad_terms(cells_ref, grads_ref):
    cols, rows, images, chans = grads_ref.shape
    pixels = cols * rows * images
    windows = [
        cells_ref[col : col + cols, row : row + rows].reshape(pixels, chans) for row in range(3) for col in range(3)
    ]
    return lax.dot_general(
        grads_ref[...].reshape(pixels, chans),
        jnp.concatenate(windows, axis=1),
        (((0,), (0,)), ((), ())),
        preferred_element_type=F32,
    )


def split_taps(every, keep_ref, send_ref):
    chans = every.shape[0]
    half = chans // 2
    first = lax.axis_index("ha") % 2 == 0
    for tap in range(9):
        made = every[:, tap * chans : (tap + 1) * chans].T
        at = tap * half
        keep_ref[at : at + half, :] = jnp.where(first, made[:half], made[half:])
        send_ref[at : at + half, :] = jnp.where(first, made[half:], made[:half])


def at_edges():
    tall = lax.axis_index("ha")
    wide = lax.axis_index("wa")
    return (
        tall == 0,
        tall == lax.axis_size("ha") - 1,
        wide == 0,
        wide == lax.axis_size("wa") - 1,
    )


def clear_border(cells_ref, width, first=0, last=None):
    top, bottom, left, right = at_edges()
    cols, rows, images, chans = cells_ref.shape
    last = cols if last is None else last
    dtype = cells_ref.dtype

    @pl.when(top)
    def _():
        cells_ref[first:last, 0:width] = jnp.zeros((last - first, width, images, chans), dtype)

    @pl.when(bottom)
    def _():
        cells_ref[first:last, rows - width :] = jnp.zeros((last - first, width, images, chans), dtype)

    if first == 0:

        @pl.when(left)
        def _():
            cells_ref[0:width] = jnp.zeros((width, rows, images, chans), dtype)

    if last == cols:

        @pl.when(right)
        def _():
            cells_ref[cols - width :] = jnp.zeros((width, rows, images, chans), dtype)


def send_payload(mover, packed, pay_ref, stage_ref):
    stage_ref[...] = jnp.broadcast_to(packed[None], stage_ref.shape)
    mover.put(stage_ref, pay_ref)


def prepare_x(x_far, xt_far, near_ref, next_ref, sides_ref, moments_ref, x_ref, xt_ref, mover):
    images, rows, cols, chans = x_ref.shape
    steps = pieces(rows, 2)
    loads = [mover.start(x_far.at[:, a:b], x_ref.at[:, a:b]) for a, b in steps]
    total = jnp.zeros((images, chans), F32)
    square = total
    for (a, b), load in zip(steps, loads):
        load.wait()
        if a == 0:
            pilot = x_ref[:, 0, 0].astype(F32)
        for row in range(a, b):
            x = jnp.swapaxes(x_ref[:, row].astype(F32), 0, 1)
            xt_ref[:, row] = x.astype(BF16)
            apart = x - pilot[None]
            total = total + jnp.sum(apart, axis=0)
            square = square + jnp.sum(apart * apart, axis=0)
        mover.put(xt_ref.at[:, a:b], xt_far.at[:, a:b])
    mean, spread = local_moments(total, square, pilot, rows * cols, chans // GROUPS)
    moments_ref[...] = pack_pair(mean, spread)
    outer(xt_ref, near_ref, next_ref, sides_ref)


def is_even(axis="ha"):
    return lax.axis_index(axis) % 2 == 0


def outer(cells, near_ref, next_ref, sides_ref):
    cols, rows = cells.shape[0:2]
    down, up = cells[:, rows - 2 :], cells[:, 0:2]
    near_ref[...] = jnp.where(is_even(), down, up)
    next_ref[...] = jnp.where(is_even(), up, down)
    sides_ref[0:2] = cells[0:2]
    sides_ref[2:4] = cells[cols - 2 :]


def prepare_g(
    c_far, moments_ref, gt_far, pay_far, near_ref, next_ref, sides_ref, bias_ref, c_ref, gt_ref, stage_ref, mover
):
    images, rows, cols, chans = c_ref.shape
    steps = pieces(rows, 2)
    loads = [mover.start(c_far.at[:, a:b], c_ref.at[:, a:b]) for a, b in steps]
    send_payload(mover, moments_ref[...], pay_far, stage_ref)
    bias = jnp.zeros((images, chans), F32)
    for (a, b), load in zip(steps, loads):
        load.wait()
        for row in range(a, b):
            grad = jnp.swapaxes(c_ref[:, row].astype(F32) * INV_ROOT, 0, 1).astype(BF16)
            gt_ref[:, row] = grad
            bias = bias + jnp.sum(grad.astype(F32), axis=0)
        mover.put(gt_ref.at[:, a:b], gt_far.at[:, a:b])
    bias_ref[...] = bias
    outer(gt_ref, near_ref, next_ref, sides_ref)


def edge_columns(sides_ref, near_ref, next_ref, one_ref, other_ref):
    cols, rows = near_ref.shape[0], sides_ref.shape[1]
    even = is_even("wa")

    def piece(left, right):
        return jnp.where(even, right, left), jnp.where(even, left, right)

    near = piece(near_ref[0:2], near_ref[cols - 2 : cols])
    following = piece(next_ref[0:2], next_ref[cols - 2 : cols])
    own = piece(sides_ref[0:2], sides_ref[2:4])
    for at, ref in enumerate((one_ref, other_ref)):
        ref[:, 0:2] = jnp.where(is_even(), following[at], near[at])
        ref[:, 2 : rows + 2] = own[at]
        ref[:, rows + 2 :] = jnp.where(is_even(), near[at], following[at])


def fill_halo(cells_ref, near_ref, next_ref, one_ref, other_ref, change):
    cols, rows = near_ref.shape[0], cells_ref.shape[1] - 4

    def halo_column(col, _):
        near, next_ = near_ref[pl.ds(col, 1)], next_ref[pl.ds(col, 1)]
        cells_ref[pl.ds(col + 2, 1), 0:2] = change(jnp.where(is_even(), next_, near))
        cells_ref[pl.ds(col + 2, 1), rows + 2 :] = change(jnp.where(is_even(), near, next_))
        return 0

    even = is_even("wa")
    cells_ref[0:2] = change(jnp.where(even, other_ref[...], one_ref[...]))
    cells_ref[cols + 2 :] = change(jnp.where(even, one_ref[...], other_ref[...]))
    lax.fori_loop(0, cols, halo_column, 0, unroll=4)


def first_half(
    xt_far, kernel_far, near_ref, next_ref, one_ref, other_ref, gathered_ref, gain_ref, bias_ref, kbias_ref,
    act_far, mid_far, pay_far, stat_ref,
    xt_ref, kernel_ref, act_ref, mid_ref, stage_ref, pair_ref, mover,
):
    cols, rows, images, chans = xt_ref.shape
    per = chans // GROUPS
    load = mover.start(kernel_far, kernel_ref)
    steps = pieces(cols, 8)
    own = [mover.start(xt_far.at[a:b], xt_ref.at[a:b]) for a, b in steps]
    mean, inv = merge_moments(gathered_ref, rows * cols * per)
    stat_ref[0] = mean
    stat_ref[1] = inv
    mover.ready()
    slope = 0.5 * inv * gain_ref[...].astype(F32)
    offset = 0.5 * bias_ref[...].astype(F32)

    def act(cells):
        value = (cells.astype(F32) - mean) * slope + offset
        return (value + value * jnp.tanh(value)).astype(BF16)

    def column(col, _):
        act_ref[pl.ds(col + 2, 1), 2 : rows + 2] = act(xt_ref[pl.ds(col, 1)])
        return 0

    fill_halo(act_ref, near_ref, next_ref, one_ref, other_ref, act)
    for (a, b), copy in zip(steps, own):
        copy.wait()
        lax.fori_loop(a, b, column, 0, unroll=2)
    clear_border(act_ref, 2)
    load.wait()
    forward_weights(kernel_ref, pair_ref)
    mover.put(act_ref, act_far)

    wide = cols + 2
    kbias = kbias_ref[...].astype(F32)
    state = [None, jnp.zeros((images, chans), F32), jnp.zeros((images, chans), F32)]

    def take(col, values):
        values = values + kbias
        mid_ref[col] = values
        if 1 <= col <= cols:
            own = values[1 : rows + 1]
            if state[0] is None:
                state[0] = own[0]
            apart = own - state[0][None]
            state[1] = state[1] + jnp.sum(apart, axis=0)
            state[2] = state[2] + jnp.sum(apart * apart, axis=0)

    for a, b in pieces(wide, 10):
        convolve(act_ref, pair_ref, False, rows + 2, a, b, take)
        mover.put(mid_ref.at[a:b], mid_far.at[a:b])
    pilot, total, square = state
    mean, spread = local_moments(total, square, pilot, rows * cols, per)
    send_payload(mover, pack_pair(mean, spread), pay_far, stage_ref)


def back_two(
    gt_far, kernel_far, weight_far, near_ref, next_ref, one_ref, other_ref, *refs,
):
    text_ref, fbias_ref, freqs_ref, times_ref, levels_ref, out_far, film_ref, ints_ref, *refs = refs
    gt_ref, kernel_ref, weight_ref, cells_ref, out_ref, pair_ref, mover = refs
    cols, rows = gt_ref.shape[0:2]
    load = mover.start(kernel_far, kernel_ref)
    steps = pieces(cols, 8)
    own = [mover.start(gt_far.at[a:b], gt_ref.at[a:b]) for a, b in steps]
    late = mover.start(weight_far, weight_ref)
    fill_halo(cells_ref, near_ref, next_ref, one_ref, other_ref, lambda cells: cells)
    load.wait()
    backward_weights(kernel_ref, pair_ref)
    mover.ready()
    text = text_ref[...].astype(F32)
    half = TEMB // 2
    for at, source_ref in ((0, times_ref), (TEMB, levels_ref)):
        angles = [source_ref[image].astype(F32) * freqs_ref[...] for image in range(text_ref.shape[0])]
        angles = jnp.concatenate(angles, axis=0)
        for start, embed in ((at, jnp.sin(angles)), (at + half, jnp.cos(angles))):
            ints_ref[:, start : start + half] = (embed * sigmoid(embed)).astype(BF16)
    act = jnp.concatenate([ints_ref[...], (text * sigmoid(text)).astype(BF16)], axis=1)
    for (a, b), copy in zip(steps, own):
        copy.wait()
        cells_ref[a + 2 : b + 2, 2 : rows + 2] = gt_ref[a:b]
    clear_border(cells_ref, 2)
    for a, b in pieces(cols + 2, 10):
        convolve(cells_ref, pair_ref, True, rows + 2, a, b, lambda col, values: out_ref.__setitem__(col, values))
        mover.put(out_ref.at[a:b], out_far.at[a:b])
    late.wait()
    film_ref[...] = jnp.dot(act, weight_ref[...], preferred_element_type=F32) + fbias_ref[...].astype(F32)


def second_values(stat, gain_ref, bias_ref, film_ref):
    mean, inv = stat
    chans = mean.shape[1]
    scale = 1.0 + film_ref[:, 0:chans]
    slope = gain_ref[...].astype(F32) * scale
    half_slope = 0.5 * slope
    half_offset = 0.5 * (bias_ref[...].astype(F32) * scale + film_ref[:, chans:])

    def values(mid, back):
        hat = (mid - mean) * inv
        pre = hat * half_slope + half_offset
        bend = jnp.tanh(pre)
        more = 1.0 + bend
        grad = back * (0.5 * more * (1.0 + pre * (1.0 - bend)))
        return hat, pre * more, grad

    return slope, values


def second_norm(
    mid_far, back_far, gathered_ref, gain_ref, bias_ref, film_ref,
    act_far, pre_far, pay_far, sums_ref, stat_ref,
    mid_ref, back_ref, act_ref, pre_ref, stage_ref, mover,
):
    wide, tall, images, chans = mid_ref.shape
    cols, rows = wide - 2, tall - 2
    per = chans // GROUPS
    steps = pieces(wide, 9)
    loads = []
    for a, b in steps:
        loads.append(
            [mover.start(f.at[a:b], n.at[a:b]) for f, n in ((mid_far, mid_ref), (back_far, back_ref))]
        )
    mean, inv = merge_moments(gathered_ref, rows * cols * per)
    stat_ref[0] = mean
    stat_ref[1] = inv
    mover.ready()
    slope, values = second_values((mean, inv), gain_ref, bias_ref, film_ref)

    def column(col, inner):
        hat, act, grad = values(mid_ref[col], back_ref[col])
        act_ref[col] = act.astype(BF16)
        pre_ref[col] = grad.astype(BF16)
        if inner is None:
            return None
        own = grad[1 : rows + 1]
        plain, cross = inner
        return plain + jnp.sum(own, axis=0), cross + jnp.sum(own * hat[1 : rows + 1], axis=0)

    zero = jnp.zeros((images, chans), F32)
    inner = (zero, zero)
    for (a, b), pair in zip(steps, loads):
        for load in pair:
            load.wait()
        if a == 0:
            column(0, None)
        inner = lax.fori_loop(max(a, 1), min(b, cols + 1), column, inner)
        if b == wide:
            column(wide - 1, None)
        clear_border(act_ref, 1, a, b)
        mover.put(act_ref.at[a:b], act_far.at[a:b])
        mover.put(pre_ref.at[a:b], pre_far.at[a:b])
    plain, cross = inner
    sums_ref[0] = plain
    sums_ref[1] = cross
    send_payload(mover, pack_pair(group_total(plain * slope), group_total(cross * slope)), pay_far, stage_ref)


def kernel_two(
    act_far, gt_far, sums_ref, bias_ref, keep_far, send_far, act_ref, gt_ref, keep_ref, send_ref, mover
):
    for load in [mover.start(act_far, act_ref), mover.start(gt_far, gt_ref)]:
        load.wait()
    split_taps(grad_terms(act_ref, gt_ref), keep_ref, send_ref)
    mover.ready()
    images, chans = bias_ref.shape
    at = 9 * (chans // 2)
    total = jnp.sum(bias_ref[...], axis=0, keepdims=True)
    for ref in (keep_ref, send_ref):
        ref[at : at + images] = sums_ref[0]
        ref[at + images : at + 2 * images] = sums_ref[1]
        ref[at + 2 * images :] = jnp.broadcast_to(total, (ref.shape[0] - at - 2 * images, chans))
    mover.put(keep_ref, keep_far)
    mover.put(send_ref, send_far)


def mix(
    act_far, kernel_far, xt_far, kbias_ref, out_far, act_ref, kernel_ref, xt_ref, branch_ref, out_ref, pair_ref, mover
):
    images, rows, cols, chans = out_ref.shape
    loads = [mover.start(f, n) for f, n in ((kernel_far, kernel_ref), (act_far, act_ref), (xt_far, xt_ref))]
    loads[0].wait()
    forward_weights(kernel_ref, pair_ref)
    mover.ready()
    kbias = kbias_ref[...].astype(F32)
    loads[1].wait()
    convolve(
        act_ref, pair_ref, False, rows, 0, cols, lambda col, values: branch_ref.__setitem__(col, values + kbias)
    )
    loads[2].wait()
    for a, b in pieces(rows, 2):
        for row in range(a, b):
            mixed = jnp.swapaxes((xt_ref[:, row].astype(F32) + branch_ref[:, row]) * INV_ROOT, 0, 1)
            out_ref[:, row] = mixed.astype(BF16)
        mover.put(out_ref.at[:, a:b], out_far.at[:, a:b])


def middle_grad(
    mid_far, pre_far, act_far, keep_two_far, gathered_ref, stat_ref, gain_ref, film_ref,
    low_far, keep_ref, send_ref, two_ref,
    mid_ref, pre_ref, act_ref, low_ref, mover,
):
    wide, tall, images, chans = mid_ref.shape
    cols, rows = wide - 2, tall - 2
    steps = pieces(wide, 9)
    loads = []
    for a, b in steps:
        loads.append([mover.start(f.at[a:b], n.at[a:b]) for f, n in ((mid_far, mid_ref), (pre_far, pre_ref))])
    late = [mover.start(f, n) for f, n in ((act_far, act_ref), (keep_two_far, two_ref))]
    count = lax.axis_size("ha") * lax.axis_size("wa") * rows * cols * (chans // GROUPS)
    packed = jnp.sum(gathered_ref[...], axis=0) * (1.0 / count)
    mover.ready()
    mean = stat_ref[0]
    inv = stat_ref[1]
    plain = unpack_at(packed, 0) * inv
    cross = unpack_at(packed, 1) * inv * inv
    slope = gain_ref[...].astype(F32) * (1.0 + film_ref[:, 0:chans]) * inv

    def low_column(col, total):
        low = (pre_ref[col].astype(F32) * slope - plain - (mid_ref[col] - mean) * cross).astype(BF16)
        low_ref[col] = low
        if total is None:
            return None
        return total + jnp.sum(low[1 : rows + 1].astype(F32), axis=0)

    kbias = jnp.zeros((images, chans), F32)
    for (a, b), pair in zip(steps, loads):
        for load in pair:
            load.wait()
        if a == 0:
            low_column(0, None)
        kbias = lax.fori_loop(max(a, 1), min(b, cols + 1), low_column, kbias)
        if b == wide:
            low_column(wide - 1, None)
        clear_border(low_ref, 1, a, b)
        mover.put(low_ref.at[a:b], low_far.at[a:b])
    for load in late:
        load.wait()
    own = low_ref.at[1 : wide - 1, 1 : tall - 1]
    split_taps(grad_terms(act_ref.at[1 : wide + 1, 1 : tall + 1], own), keep_ref, send_ref)
    at = 9 * (chans // 2)
    for ref in (keep_ref, send_ref):
        ref[at:] = jnp.broadcast_to(jnp.sum(kbias, axis=0, keepdims=True), (ref.shape[0] - at, chans))


def back_one(
    low_far, xt_far, kernel_far, stat_ref, gain_ref, bias_ref, grad_far, pay_ref, low_ref, xt_ref, kernel_ref, out_ref, pair_ref, mover
):
    cols, rows, images, chans = xt_ref.shape
    loads = [mover.start(f, n) for f, n in ((kernel_far, kernel_ref), (low_far, low_ref), (xt_far, xt_ref))]
    loads[0].wait()
    backward_weights(kernel_ref, pair_ref)
    loads[1].wait()
    loads[2].wait()
    mover.ready()
    mean = stat_ref[0]
    inv = stat_ref[1]
    gain = gain_ref[...].astype(F32)
    bias = bias_ref[...].astype(F32)
    state = [jnp.zeros((images, chans), F32), jnp.zeros((images, chans), F32)]

    def take(col, values):
        hat = (xt_ref[col].astype(F32) - mean) * inv
        norm = hat * gain + bias
        sigma = sigmoid(norm)
        grad = values * (sigma * (1.0 + norm * (1.0 - sigma)))
        out_ref[col] = grad
        state[0] = state[0] + jnp.sum(grad, axis=0)
        state[1] = state[1] + jnp.sum(grad * hat, axis=0)

    for a, b in pieces(cols, 8):
        convolve(low_ref, pair_ref, True, rows, a, b, take)
        mover.put(out_ref.at[a:b], grad_far.at[a:b])
    plain, cross = state
    half = images // 2
    pay_ref[0:half] = pack_pair(group_total(plain * gain), group_total(cross * gain))
    rest = [jnp.sum(v, axis=0, keepdims=True) for v in (cross, plain)]
    short = pay_ref.shape[0] - half - 2
    pay_ref[half:] = jnp.concatenate(rest + [jnp.zeros((short, chans), F32)], axis=0)


CODE = 32768.0


def exponents(values):
    most = jnp.clip(jnp.max(jnp.abs(values), axis=0, keepdims=True), 1e-30, 1e30)
    return jnp.ceil(jnp.log2(most) + 2e-3)


def two_to(powers):
    powers = powers.astype(jnp.int32)
    first = powers >> 1
    made = None
    for part in (first, powers - first):
        shifted = part + 64
        for bit in range(7):
            factor = jnp.where((shifted >> bit) & 1 == 1, 2.0 ** (1 << bit), 1.0)
            if bit == 0:
                piece = factor * 2.0**-64
            else:
                piece = piece * factor
        made = piece if made is None else made * piece
    return made


def pack_terms(
    keep_one_ref, came_one_ref, keep_two_ref, came_two_ref, out_far, token_ref,
    one_ref, two_ref, extra_ref, rest_ref, out_ref, mover, extras_one, extras_two,
):
    chips, rows, chans = out_ref.shape
    taps = 9 * (chans // 2)
    share = -(-taps // chips)
    more = -(-(extras_one + extras_two) // chips)
    extra_ref[...] = jnp.zeros(extra_ref.shape, F32)
    one_ref[...] = keep_one_ref[...] + came_one_ref[...]
    two_ref[...] = keep_two_ref[...] + came_two_ref[...]
    extra_ref[0:extras_two] = two_ref[taps : taps + extras_two]
    extra_ref[extras_two : extras_two + extras_one] = one_ref[taps : taps + extras_one]
    token_ref[...] = extra_ref[0:8]
    powers = []
    for ref, count in ((one_ref, taps), (two_ref, taps), (extra_ref, extra_ref.shape[0])):
        values = ref[0:count]
        power = exponents(values)
        powers.append(power)
        scaled = values * (two_to(-power) * CODE)
        code = jnp.round(scaled)
        ref[0:count] = code
        if ref is extra_ref:
            rest_ref[...] = jnp.round((scaled - code) * CODE)
    short = rows - 2 * share - 2 * more - 3
    pad = [jnp.zeros((short, chans), F32)] if short else []
    for chip in range(chips):
        a, b = chip * share, min((chip + 1) * share, taps)
        mine = []
        for ref in (one_ref, two_ref):
            if a < b:
                mine.append(ref[a:b])
            if max(b - a, 0) < share:
                mine.append(jnp.zeros((share - max(b - a, 0), chans), F32))
        for ref in (extra_ref, rest_ref):
            mine.append(ref[chip * more : (chip + 1) * more])
        whole = jnp.concatenate(mine + powers + pad, axis=0)
        out_ref[chip] = whole.astype(jnp.int32).astype(jnp.int16)
    mover.put(out_ref, out_far)


def unpack_terms(gathered_ref, share, more):
    chips, rows, chans = gathered_ref.shape
    row = lax.broadcasted_iota(jnp.int32, (rows, chans), 0)
    base = 2 * share + 2 * more
    total = jnp.zeros((rows, chans), F32)
    blocks = [gathered_ref[chip].astype(jnp.int32).astype(F32) for chip in range(chips)]
    every = two_to(jnp.concatenate([block[base : base + 3] for block in blocks], axis=0)) * (1.0 / CODE)
    for chip, block in enumerate(blocks):
        scales = every[3 * chip : 3 * chip + 3]
        scale = jnp.where(row < share, scales[0:1], jnp.where(row < 2 * share, scales[1:2], scales[2:3]))
        scale = jnp.where(row < 2 * share + more, scale, scale * (1.0 / CODE))
        total = total + block * scale
    extra = total[2 * share : 2 * share + more] + total[2 * share + more : base]
    return total[0 : 2 * share], extra


def two_terms(values):
    high = values.astype(BF16).astype(F32)
    return [high, values - high]


def add_terms(gathered_ref, pay_ref, came_ref, out_far, out_ref, mover, more, whole):
    chips, rows, chans = gathered_ref.shape
    shares, extra = unpack_terms(gathered_ref, -(-9 * (chans // 2) // chips), more)
    every = [shares] + two_terms(extra) + two_terms(pay_ref[0:whole] + came_ref[0:whole])
    short = out_ref.shape[1] - sum(v.shape[0] for v in every)
    if short:
        every.append(jnp.zeros((short, chans), F32))
    out_ref[...] = jnp.broadcast_to(jnp.concatenate(every, axis=0).astype(BF16)[None], out_ref.shape)
    mover.put(out_ref, out_far)


def sums_of(own_ref, at, whole):
    total = own_ref[0].astype(F32)
    for chip in range(1, own_ref.shape[0]):
        total = total + own_ref[chip].astype(F32)
    return total[at : at + whole] + total[at + whole : at + 2 * whole]


def three_terms(values):
    high = values.astype(BF16)
    rest = values - high.astype(F32)
    mid = rest.astype(BF16)
    low = (rest - mid.astype(F32)).astype(BF16)
    return jnp.concatenate([high, mid, low], axis=0)


def spread_out(own_ref, other_ref, one_far, two_far, one_ref, two_ref, half_ref, mover):
    chips, rows, chans = own_ref.shape
    half = chans // 2
    taps = 9 * half
    share = -(-taps // chips)
    core = lax.axis_index("ha") % 2
    for at, (out_ref, far) in enumerate(((one_ref, one_far), (two_ref, two_far))):
        for source, place in ((own_ref, core), (other_ref, 1 - core)):
            for chip in range(chips):
                piece = source[chip].astype(F32)[at * share : (at + 1) * share]
                half_ref[chip * share : (chip + 1) * share] = piece
            for tap in range(9):
                rows_at = pl.ds(pl.multiple_of(place * half, half), half)
                out_ref[tap, rows_at] = half_ref[tap * half : (tap + 1) * half]
        mover.put(out_ref, far)


def last_grads(
    weight_far, grad_ref, xt_ref, c_ref, own_ref, stat_ref, gain_one_ref, gain_two_ref, bias_two_ref, film_ref, ints_ref, text_ref,
    out_far, weight_grad_far, text_grad_far, bias_ref, *refs, more, whole,
):
    *vec_refs, weight_ref, out_ref, weight_grad_ref, text_grad_ref, extra_ref, mover = refs
    images, rows, cols, chans = out_ref.shape
    chips = own_ref.shape[0]
    load = mover.start(weight_far, weight_ref)
    share = -(-9 * (chans // 2) // chips)
    start = 2 * share
    for chip in range(chips):
        piece = own_ref[chip].astype(F32)
        extra_ref[chip * more : (chip + 1) * more] = piece[start : start + more] + piece[start + more : start + 2 * more]
    plain = extra_ref[0:images]
    cross = extra_ref[images : 2 * images]
    mover.ready()
    scale = 1.0 + film_ref[:, 0:chans]
    scale_grad = gain_two_ref[...].astype(F32) * cross + bias_two_ref[...].astype(F32) * plain
    film_grad = jnp.concatenate([scale_grad, plain], axis=1)
    bias_ref[...] = jnp.sum(film_grad, axis=0, keepdims=True)
    sums = sums_of(own_ref, start + 2 * more, whole)
    vec_refs[0][...] = jnp.sum(scale * cross, axis=0, keepdims=True)
    vec_refs[1][...] = jnp.sum(scale * plain, axis=0, keepdims=True)
    for at, row in enumerate((extra_ref[2 * images : 2 * images + 1], extra_ref[2 * images + 1 : 2 * images + 2])):
        vec_refs[2 + at][...] = row
    vec_refs[4][...] = sums[whole - 2 : whole - 1]
    vec_refs[5][...] = sums[whole - 1 : whole]
    terms = three_terms(film_grad)
    ints = ints_ref.shape[1]

    depth = weight_grad_ref.shape[0]
    for at in range(0, depth, 512):
        if at < ints:
            act = ints_ref[:, at : at + 512]
        else:
            embed = text_ref[:, at - ints : at - ints + 512].astype(F32)
            act = (embed * sigmoid(embed)).astype(BF16)
        weight_grad_ref[at : at + 512] = lax.dot_general(
            jnp.concatenate([act, act, act], axis=0), terms, (((0,), (0,)), ((), ())), preferred_element_type=F32
        )
        mover.put(weight_grad_ref.at[at : at + 512], weight_grad_far.at[at : at + 512])

    count = lax.axis_size("ha") * lax.axis_size("wa") * rows * cols * (chans // GROUPS)
    packed = sums[0 : images // 2] * (1.0 / count)
    plain = unpack_at(packed, 0)
    cross = unpack_at(packed, 1)
    mean = stat_ref[0]
    inv = stat_ref[1]
    gain = gain_one_ref[...].astype(F32)
    for a, b in pieces(rows, 2):
        for row in range(a, b):
            hat = (xt_ref[:, row].astype(F32) - mean) * inv
            path = jnp.swapaxes(inv * (grad_ref[:, row] * gain - plain - hat * cross), 0, 1)
            out_ref[:, row] = (c_ref[:, row].astype(F32) * INV_ROOT + path).astype(BF16)
        mover.put(out_ref.at[:, a:b], out_far.at[:, a:b])

    load.wait()
    for at in range(ints, depth, 512):
        embed = text_ref[:, at - ints : at - ints + 512].astype(F32)
        sigma = sigmoid(embed)
        made = lax.dot_general(
            terms, weight_ref[at : at + 512], (((1,), (1,)), ((), ())), preferred_element_type=F32
        )
        cond_grad = made[0:images] + made[images : 2 * images] + made[2 * images :]
        text_grad_ref[:, at - ints : at - ints + 512] = cond_grad * (sigma * (1.0 + embed * (1.0 - sigma)))
    mover.put(text_grad_ref, text_grad_far)


def to_all(payload):
    return lax.all_to_all(payload, AXES, 0, 0)


def to_chips(payload):
    tall, wide = lax.axis_size("ha"), lax.axis_size("wa")
    groups = [[h * wide + w for h in range(core, tall, 2) for w in range(wide)] for core in range(2)]
    return lax.all_to_all(payload, AXES, 0, 0, axis_index_groups=groups)


def to_sibling(payload):
    return lax.ppermute(payload, "ha", [(i, i ^ 1) for i in range(lax.axis_size("ha"))])


def pair_exchange(one, other, axis):
    count = lax.axis_size(axis)
    pairs = [(i, (i + 1 if i % 2 else i - 1) % count) for i in range(count)]
    if axis == "wa":
        pairs = [(i, min(max(j, 0), count - 1) if abs(i - j) == 1 else i) for i, j in pairs]
    one = lax.ppermute(one, axis, [(i, i ^ 1) for i in range(count)])
    return one, lax.ppermute(other, axis, pairs)


def side_halo(sides, near, following, after=()):
    four, rows, images, chans = sides.shape
    edge = shaped((2, rows + 4, images, chans), sides.dtype)
    one, other = kernel_call(
        edge_columns, near=(sides, near, following), near_out=(edge, edge), cost=0.4, after=after, limit=16
    )
    return pair_exchange(one, other, "wa"), one


def local(
    block_input,
    timesteps,
    aug_levels,
    text_pooled,
    gain_one,
    bias_one,
    conv_one,
    conv_one_bias,
    gain_two,
    bias_two,
    film_weight,
    film_bias,
    conv_two,
    conv_two_bias,
    cotangent,
):
    images, rows, cols, chans = block_input.shape
    parts = lax.axis_size("ha") * lax.axis_size("wa")
    chips = parts // 2
    half = images // 2
    gain_one, bias_one, conv_one_bias, gain_two, bias_two, conv_two_bias = (
        v.reshape(1, chans) for v in (gain_one, bias_one, conv_one_bias, gain_two, bias_two, conv_two_bias)
    )
    freqs = np.exp(-math.log(10000.0) * np.arange(TEMB // 2) / (TEMB // 2)).astype(np.float32)[None]
    payload = shaped((parts, half, chans), F32)
    per_image = shaped((images, chans), F32)
    two_images = shaped((2, images, chans), F32)
    block = shaped((cols, rows, images, chans), BF16)
    block_wide = shaped((cols, rows, images, chans), F32)
    rim = shaped((cols + 2, rows + 2, images, chans), BF16)
    rim_wide = shaped((cols + 2, rows + 2, images, chans), F32)
    far_rim = shaped((cols + 4, rows + 4, images, chans), BF16)
    given = shaped((images, rows, cols, chans), BF16)
    pair = pltpu.VMEM((12 * chans, 2 * chans), BF16)
    pair_back = pltpu.VMEM((2 * chans, 12 * chans), BF16)

    sides = shaped((4, rows, images, chans), BF16)
    row_halo = shaped((cols, 2, images, chans), BF16)
    xt, x_near, x_next, x_sides, moments = kernel_call(
        prepare_x, far=(block_input,), far_out=(block,),
        near_out=(row_halo, row_halo, sides, shaped((half, chans), F32)),
        scratch=buffers(given, block), sems=16, cost=2.3,
    )
    x_near, x_next = pair_exchange(x_near, x_next, "ha")
    gt, pay_one, g_near, g_next, g_sides, kbias_two_local = kernel_call(
        prepare_g, far=(cotangent,), near=(moments,), far_out=(block, payload),
        near_out=(row_halo, row_halo, sides), tiny_out=(per_image,),
        scratch=buffers(given, block, payload), sems=16, cost=2.0,
    )
    moments_one = to_all(pay_one)
    x_cols, x_edge = side_halo(x_sides, x_near, x_next)
    g_near, g_next = pair_exchange(g_near, g_next, "ha")

    film_bias = film_bias.reshape(1, 2 * chans)
    act_one, mid, pay_two, stat_one = kernel_call(
        first_half, far=(xt, conv_one), near=(x_near, x_next, *x_cols, moments_one),
        tiny=(gain_one, bias_one, conv_one_bias),
        far_out=(far_rim, rim_wide, payload), tiny_out=(two_images,),
        scratch=buffers(xt, conv_one, far_rim, rim_wide, payload) + (pair,), sems=16, cost=5.5,
        after=(film_bias,),
    )
    moments_two = to_all(pay_two)
    g_cols, _ = side_halo(g_sides, g_near, g_next, after=(stat_one,))
    act_two_grad, film, act_ints = kernel_call(
        back_two, far=(gt, conv_two, film_weight), near=(g_near, g_next, *g_cols),
        tiny=(text_pooled, film_bias, freqs), scalars=(timesteps, aug_levels),
        far_out=(rim_wide,), tiny_out=(shaped((images, 2 * chans), F32), shaped((images, 2 * TEMB), BF16)),
        scratch=buffers(gt, conv_two, film_weight, far_rim, rim_wide) + (pair_back,), sems=16, cost=5.0,
    )
    act_two, pre_two_grad, pay_three, sums_two, stat_two = kernel_call(
        second_norm, far=(mid, act_two_grad), near=(moments_two,), tiny=(gain_two, bias_two, film),
        far_out=(rim, rim, payload), tiny_out=(two_images, two_images),
        scratch=buffers(rim_wide, rim_wide, rim, rim, payload), sems=24, cost=3.2,
    )
    moments_three = to_all(pay_three)

    taps = 9 * (chans // 2)
    share = -(-taps // chips)
    extras_two = 2 * images + 1
    extras_one = 1
    halves_two = shaped((taps + 2 * images + 8, chans), F32)
    halves_one = shaped((taps + 8, chans), F32)
    keep_two, send_two = kernel_call(
        kernel_two, far=(act_two, gt), tiny=(sums_two, kbias_two_local), far_out=(halves_two, halves_two),
        scratch=buffers(act_two, gt, halves_two, halves_two), sems=4, cost=3.0,
    )
    came_two = to_sibling(send_two)
    low, keep_one, send_one, keep_two = kernel_call(
        middle_grad, far=(mid, pre_two_grad, act_one, keep_two), near=(moments_three,), tiny=(stat_two, gain_two, film),
        far_out=(rim,), near_out=(halves_one, halves_one, halves_two),
        scratch=buffers(mid, pre_two_grad, act_one, rim), sems=24, cost=6.0,
    )
    came_one = to_sibling(send_one)
    more = -(-(extras_one + extras_two) // chips)
    terms_shape = shaped((chips, -(-(2 * share + 2 * more + 3) // 8) * 8, chans), jnp.int16)
    extra_shape = shaped((-(-chips * more // 8) * 8, chans), F32)
    terms, token = kernel_call(
        functools.partial(pack_terms, extras_one=extras_one, extras_two=extras_two),
        near=(keep_one, came_one, keep_two, came_two), far_out=(terms_shape,), near_out=(shaped((8, chans), F32),),
        scratch=buffers(halves_one, halves_two, extra_shape, extra_shape, terms_shape),
        sems=3, cost=1.0,
    )
    gathered = to_chips(terms)
    whole = half + 2
    norm_one_grad, pay_four = kernel_call(
        back_one, far=(low, xt, conv_one), tiny=(stat_one, gain_one, bias_one), far_out=(block_wide,),
        near_out=(shaped((2 * half, chans), F32),),
        scratch=buffers(rim, block, conv_one, block_wide) + (pair_back,), sems=16, cost=5.0,
        after_near=(to_sibling(token),),
    )
    came_four = to_sibling(pay_four)
    (mixed,) = kernel_call(
        mix, far=(act_two, conv_two, xt), tiny=(conv_two_bias,), far_out=(given,),
        scratch=buffers(act_two, conv_two, xt, block_wide, given) + (pair,), sems=8, cost=3.6, after_near=(pay_four,),
    )
    shares_shape = shaped((chips, -(-(2 * share + 2 * more + 2 * whole) // 8) * 8, chans), BF16)
    (shares,) = kernel_call(
        functools.partial(add_terms, more=more, whole=whole),
        near=(gathered, pay_four, came_four), far_out=(shares_shape,),
        scratch=buffers(shares_shape), sems=1, cost=1.0, after=(mixed,),
    )
    own_half = to_chips(shares)
    other_half = to_sibling(own_half)
    weight_grad = shaped(film_weight.shape, F32)
    text_shape = shaped(text_pooled.shape, F32)
    row = shaped((1, chans), F32)
    input_grad, film_weight_grad, text_grad, film_bias_grad, *vec_grads = kernel_call(
        functools.partial(last_grads, more=more, whole=whole),
        far=(film_weight,),
        near=(norm_one_grad, xt, cotangent, own_half, stat_one, gain_one, gain_two, bias_two, film, act_ints, text_pooled),
        far_out=(given, weight_grad, text_shape), tiny_out=(shaped((1, 2 * chans), F32),) + (row,) * 6,
        scratch=buffers(film_weight, given, weight_grad, text_shape)
        + (pltpu.VMEM((-(-chips * more // 8) * 8, chans), F32),),
        sems=32, cost=6.0, limit=24,
    )
    full = shaped((9, chans, chans), F32)
    kernel_one_grad, kernel_two_grad = kernel_call(
        spread_out, near=(own_half, other_half), far_out=(full, full),
        scratch=buffers(full, full, shaped((chips * share, chans), F32)), sems=2, cost=2.0, after=(input_grad,), limit=24,
    )
    return (
        mixed,
        input_grad,
        text_grad,
        vec_grads[4].reshape(chans),
        vec_grads[5].reshape(chans),
        kernel_one_grad.reshape(3, 3, chans, chans),
        vec_grads[3].reshape(chans),
        vec_grads[0].reshape(chans),
        vec_grads[1].reshape(chans),
        film_weight_grad,
        film_bias_grad.reshape(2 * chans),
        kernel_two_grad.reshape(3, 3, chans, chans),
        vec_grads[2].reshape(chans),
    )


def solution(mesh):
    split = P(None, "ha", "wa", None)
    return jax.shard_map(
        local,
        mesh=mesh,
        in_specs=(split,) + (P(),) * 13 + (split,),
        out_specs=(split, split) + (P(),) * 11,
        check_vma=False,
    )
```

```python
import functools
import math

import jax
import jax.numpy as jnp
import numpy as np
from jax import lax
from jax.experimental import pallas as pl
from jax.experimental.pallas import tpu as pltpu
from jax.sharding import PartitionSpec as P

GROUPS = 32
TEMB = 256
EPSILON = 1e-05
INV_ROOT = 1.0 / math.sqrt(2.0)
AXES = ("ha", "wa")
F32 = jnp.float32
BF16 = jnp.bfloat16
NEAR = pl.BlockSpec(memory_space=pltpu.VMEM)
FAR = pl.BlockSpec(memory_space=pl.ANY)
MIB = 1 << 20


def shaped(shape, dtype):
    return jax.ShapeDtypeStruct(shape, dtype)


def kernel_call(
    body, far=(), near=(), tiny=(), far_out=(), near_out=(), tiny_out=(), scratch=(), sems=0, cost=1.0,
    after=(), after_near=(), scalars=(), limit=48,
):
    pinned = lambda arrays: [pltpu.with_memory_space_constraint(array, pltpu.HBM) for array in arrays]
    given = len(far) + len(near)
    held = len(after) + len(after_near)
    copies = len(tiny) + len(tiny_out)

    def run(*refs):
        refs = list(refs)
        take = lambda count: [refs.pop(0) for _ in range(count)]
        inputs = take(given)
        tiny_far = take(len(tiny))
        scalar_refs = take(len(scalars))
        take(held)
        outputs = take(len(far_out) + len(near_out))
        tiny_out_far = take(len(tiny_out))
        tiny_refs = take(len(tiny))
        tiny_out_refs = take(len(tiny_out))
        mover = None
        if sems + copies:
            mover = Mover(refs.pop(), [(f, n) for f, n in zip(tiny_far, tiny_refs)])
        body(*inputs, *tiny_refs, *scalar_refs, *outputs, *tiny_out_refs, *refs, *([mover] if mover else []))
        if mover:
            for source, target in zip(tiny_out_refs, tiny_out_far):
                mover.put(source, target)
            mover.finish()

    return pl.pallas_call(
        run,
        out_shape=(
            *(pltpu.HBM(out.shape, out.dtype) for out in far_out),
            *near_out,
            *(pltpu.HBM(out.shape, out.dtype) for out in tiny_out),
        ),
        in_specs=[FAR] * len(far)
        + [NEAR] * len(near)
        + [FAR] * len(tiny)
        + [pl.BlockSpec(memory_space=pltpu.SMEM)] * len(scalars)
        + [FAR] * held,
        out_specs=(FAR,) * len(far_out) + (NEAR,) * len(near_out) + (FAR,) * len(tiny_out),
        scratch_shapes=buffers(*tiny, *tiny_out)
        + tuple(scratch)
        + ((pltpu.SemaphoreType.DMA((sems + copies,)),) if sems + copies else ()),
        compiler_params=pltpu.CompilerParams(vmem_limit_bytes=limit * MIB),
        name=getattr(body, "func", body).__name__,
        cost_estimate=pl.CostEstimate(flops=int(cost * 1.1e9), bytes_accessed=0, transcendentals=0),
    )(*pinned(far), *near, *pinned(tiny), *scalars, *pinned(after), *after_near)


def buffers(*arrays):
    return tuple(pltpu.VMEM(a.shape, a.dtype) for a in arrays)


class Mover:
    def __init__(self, sems, first):
        self.sems = sems
        self.used = 0
        self.open = []
        self.first = [self.start(source, target) for source, target in first]

    def start(self, source, target):
        copy = pltpu.make_async_copy(source, target, self.sems.at[self.used])
        self.used += 1
        copy.start()
        return copy

    def ready(self):
        for copy in self.first:
            copy.wait()

    def put(self, source, target):
        self.open.append(self.start(source, target))

    def finish(self):
        for copy in self.open:
            copy.wait()


def pieces(count, size):
    return [(at, min(at + size, count)) for at in range(0, count, size)]


def lanes_of(shape):
    return lax.broadcasted_iota(jnp.int32, shape, 1)


def group_total(values):
    chans = values.shape[1]
    lane = lanes_of(values.shape)
    step = 1
    while step < chans // GROUPS:
        up = pltpu.roll(values, chans - step, 1)
        down = pltpu.roll(values, step, 1)
        values = values + jnp.where((lane & step) == 0, up, down)
        step *= 2
    return values


def pack_pair(first, second):
    half = first.shape[0] // 2
    lane = lanes_of((half, first.shape[1])) & 3
    return jnp.where(
        lane == 0,
        first[:half],
        jnp.where(lane == 1, second[:half], jnp.where(lane == 2, first[half:], second[half:])),
    )


def unpack_at(packed, place):
    lane = lanes_of(packed.shape) & 3
    top = group_total(jnp.where(lane == place, packed, 0.0))
    low = group_total(jnp.where(lane == place + 2, packed, 0.0))
    return jnp.concatenate([top, low], axis=0)


def merge_moments(gathered_ref, local_count):
    parts = gathered_ref.shape[0]
    chans = gathered_ref.shape[2]
    every = gathered_ref[...]
    total = jnp.sum(every, axis=0)
    mean = total * (1.0 / parts)
    apart = every - mean[None]
    between = jnp.sum(apart * apart, axis=0)
    square = pltpu.roll(total, chans - 1, 1) + local_count * between
    inv = lax.rsqrt(square * (1.0 / (local_count * parts)) + EPSILON)
    return unpack_at(mean, 0), unpack_at(inv, 0)


def local_moments(total, square, pilot, pixels, per):
    off = total * (1.0 / pixels)
    mean = pilot + off
    apart = square - total * off
    group_mean = group_total(mean) * (1.0 / per)
    shift = mean - group_mean
    return group_mean, group_total(apart + pixels * shift * shift)


def sigmoid(values):
    return 0.5 + 0.5 * jnp.tanh(0.5 * values)


def forward_weights(kernel_ref, pair_ref):
    chans = kernel_ref.shape[2]
    zero = jnp.zeros((chans, chans), BF16)
    for row in range(3):
        for col in range(4):
            at = (row * 4 + col) * chans
            pair_ref[at : at + chans, 0:chans] = kernel_ref[row, col] if col < 3 else zero
            pair_ref[at : at + chans, chans:] = kernel_ref[row, col - 1] if col > 0 else zero


def backward_weights(kernel_ref, pair_ref):
    chans = kernel_ref.shape[2]
    zero = jnp.zeros((chans, chans), BF16)
    for row in range(3):
        for col in range(4):
            at = (row * 4 + col) * chans
            pair_ref[0:chans, at : at + chans] = kernel_ref[2 - row, 2 - col] if col < 3 else zero
            pair_ref[chans:, at : at + chans] = kernel_ref[2 - row, 3 - col] if col > 0 else zero


def convolve(cells_ref, pair_ref, transposed, rows, first, last, take):
    images, chans = cells_ref.shape[2:]
    pairs = (last - first) // 2
    parts = []
    for row in range(3):
        for col in range(4):
            window = [cells_ref[first + 2 * q + col, row : row + rows] for q in range(pairs)]
            parts.append(jnp.stack(window).reshape(pairs * rows * images, chans))
    wide = jnp.concatenate(parts, axis=1)
    contract = ((1,), (1,)) if transposed else ((1,), (0,))
    made = lax.dot_general(wide, pair_ref[...], (contract, ((), ())), preferred_element_type=F32)
    made = made.reshape(pairs, rows, images, 2 * chans)
    for q in range(pairs):
        for side in range(2):
            take(first + 2 * q + side, made[q, :, :, side * chans : (side + 1) * chans])


def grad_terms(cells_ref, grads_ref):
    cols, rows, images, chans = grads_ref.shape
    pixels = cols * rows * images
    windows = [
        cells_ref[col : col + cols, row : row + rows].reshape(pixels, chans) for row in range(3) for col in range(3)
    ]
    return lax.dot_general(
        grads_ref[...].reshape(pixels, chans),
        jnp.concatenate(windows, axis=1),
        (((0,), (0,)), ((), ())),
        preferred_element_type=F32,
    )


def split_taps(every, keep_ref, send_ref):
    chans = every.shape[0]
    half = chans // 2
    first = lax.axis_index("ha") % 2 == 0
    for tap in range(9):
        made = every[:, tap * chans : (tap + 1) * chans].T
        at = tap * half
        keep_ref[at : at + half, :] = jnp.where(first, made[:half], made[half:])
        send_ref[at : at + half, :] = jnp.where(first, made[half:], made[:half])


def at_edges():
    tall = lax.axis_index("ha")
    wide = lax.axis_index("wa")
    return (
        tall == 0,
        tall == lax.axis_size("ha") - 1,
        wide == 0,
        wide == lax.axis_size("wa") - 1,
    )


def clear_border(cells_ref, width, first=0, last=None):
    top, bottom, left, right = at_edges()
    cols, rows, images, chans = cells_ref.shape
    last = cols if last is None else last
    dtype = cells_ref.dtype

    @pl.when(top)
    def _():
        cells_ref[first:last, 0:width] = jnp.zeros((last - first, width, images, chans), dtype)

    @pl.when(bottom)
    def _():
        cells_ref[first:last, rows - width :] = jnp.zeros((last - first, width, images, chans), dtype)

    if first == 0:

        @pl.when(left)
        def _():
            cells_ref[0:width] = jnp.zeros((width, rows, images, chans), dtype)

    if last == cols:

        @pl.when(right)
        def _():
            cells_ref[cols - width :] = jnp.zeros((width, rows, images, chans), dtype)


def send_payload(mover, packed, pay_ref, stage_ref):
    stage_ref[...] = jnp.broadcast_to(packed[None], stage_ref.shape)
    mover.put(stage_ref, pay_ref)


def prepare_x(x_far, xt_far, near_ref, next_ref, sides_ref, moments_ref, x_ref, xt_ref, mover):
    images, rows, cols, chans = x_ref.shape
    steps = pieces(rows, 2)
    loads = [mover.start(x_far.at[:, a:b], x_ref.at[:, a:b]) for a, b in steps]
    total = jnp.zeros((images, chans), F32)
    square = total
    for (a, b), load in zip(steps, loads):
        load.wait()
        if a == 0:
            pilot = x_ref[:, 0, 0].astype(F32)
        for row in range(a, b):
            x = jnp.swapaxes(x_ref[:, row].astype(F32), 0, 1)
            xt_ref[:, row] = x.astype(BF16)
            apart = x - pilot[None]
            total = total + jnp.sum(apart, axis=0)
            square = square + jnp.sum(apart * apart, axis=0)
        mover.put(xt_ref.at[:, a:b], xt_far.at[:, a:b])
    mean, spread = local_moments(total, square, pilot, rows * cols, chans // GROUPS)
    moments_ref[...] = pack_pair(mean, spread)
    outer(xt_ref, near_ref, next_ref, sides_ref)


def is_even(axis="ha"):
    return lax.axis_index(axis) % 2 == 0


def outer(cells, near_ref, next_ref, sides_ref):
    cols, rows = cells.shape[0:2]
    down, up = cells[:, rows - 2 :], cells[:, 0:2]
    near_ref[...] = jnp.where(is_even(), down, up)
    next_ref[...] = jnp.where(is_even(), up, down)
    sides_ref[0:2] = cells[0:2]
    sides_ref[2:4] = cells[cols - 2 :]


def prepare_g(
    c_far, moments_ref, gt_far, pay_far, near_ref, next_ref, sides_ref, bias_ref, c_ref, gt_ref, stage_ref, mover
):
    images, rows, cols, chans = c_ref.shape
    steps = pieces(rows, 2)
    loads = [mover.start(c_far.at[:, a:b], c_ref.at[:, a:b]) for a, b in steps]
    send_payload(mover, moments_ref[...], pay_far, stage_ref)
    bias = jnp.zeros((images, chans), F32)
    for (a, b), load in zip(steps, loads):
        load.wait()
        for row in range(a, b):
            grad = jnp.swapaxes(c_ref[:, row].astype(F32) * INV_ROOT, 0, 1).astype(BF16)
            gt_ref[:, row] = grad
            bias = bias + jnp.sum(grad.astype(F32), axis=0)
        mover.put(gt_ref.at[:, a:b], gt_far.at[:, a:b])
    bias_ref[...] = bias
    outer(gt_ref, near_ref, next_ref, sides_ref)


def edge_columns(sides_ref, near_ref, next_ref, one_ref, other_ref):
    cols, rows = near_ref.shape[0], sides_ref.shape[1]
    even = is_even("wa")

    def piece(left, right):
        return jnp.where(even, right, left), jnp.where(even, left, right)

    near = piece(near_ref[0:2], near_ref[cols - 2 : cols])
    following = piece(next_ref[0:2], next_ref[cols - 2 : cols])
    own = piece(sides_ref[0:2], sides_ref[2:4])
    for at, ref in enumerate((one_ref, other_ref)):
        ref[:, 0:2] = jnp.where(is_even(), following[at], near[at])
        ref[:, 2 : rows + 2] = own[at]
        ref[:, rows + 2 :] = jnp.where(is_even(), near[at], following[at])


def fill_halo(cells_ref, near_ref, next_ref, one_ref, other_ref, change):
    cols, rows = near_ref.shape[0], cells_ref.shape[1] - 4

    def halo_column(col, _):
        near, next_ = near_ref[pl.ds(col, 1)], next_ref[pl.ds(col, 1)]
        cells_ref[pl.ds(col + 2, 1), 0:2] = change(jnp.where(is_even(), next_, near))
        cells_ref[pl.ds(col + 2, 1), rows + 2 :] = change(jnp.where(is_even(), near, next_))
        return 0

    even = is_even("wa")
    cells_ref[0:2] = change(jnp.where(even, other_ref[...], one_ref[...]))
    cells_ref[cols + 2 :] = change(jnp.where(even, one_ref[...], other_ref[...]))
    lax.fori_loop(0, cols, halo_column, 0, unroll=4)


def first_half(
    xt_far, kernel_far, near_ref, next_ref, one_ref, other_ref, gathered_ref, gain_ref, bias_ref, kbias_ref,
    act_far, mid_far, pay_far, stat_ref,
    xt_ref, kernel_ref, act_ref, mid_ref, stage_ref, pair_ref, mover,
):
    cols, rows, images, chans = xt_ref.shape
    per = chans // GROUPS
    load = mover.start(kernel_far, kernel_ref)
    steps = pieces(cols, 8)
    own = [mover.start(xt_far.at[a:b], xt_ref.at[a:b]) for a, b in steps]
    mean, inv = merge_moments(gathered_ref, rows * cols * per)
    stat_ref[0] = mean
    stat_ref[1] = inv
    mover.ready()
    slope = 0.5 * inv * gain_ref[...].astype(F32)
    offset = 0.5 * bias_ref[...].astype(F32)

    def act(cells):
        value = (cells.astype(F32) - mean) * slope + offset
        return (value + value * jnp.tanh(value)).astype(BF16)

    def column(col, _):
        act_ref[pl.ds(col + 2, 1), 2 : rows + 2] = act(xt_ref[pl.ds(col, 1)])
        return 0

    fill_halo(act_ref, near_ref, next_ref, one_ref, other_ref, act)
    for (a, b), copy in zip(steps, own):
        copy.wait()
        lax.fori_loop(a, b, column, 0, unroll=2)
    clear_border(act_ref, 2)
    load.wait()
    forward_weights(kernel_ref, pair_ref)
    mover.put(act_ref, act_far)

    wide = cols + 2
    kbias = kbias_ref[...].astype(F32)
    state = [None, jnp.zeros((images, chans), F32), jnp.zeros((images, chans), F32)]

    def take(col, values):
        values = values + kbias
        mid_ref[col] = values
        if 1 <= col <= cols:
            own = values[1 : rows + 1]
            if state[0] is None:
                state[0] = own[0]
            apart = own - state[0][None]
            state[1] = state[1] + jnp.sum(apart, axis=0)
            state[2] = state[2] + jnp.sum(apart * apart, axis=0)

    for a, b in pieces(wide, 10):
        convolve(act_ref, pair_ref, False, rows + 2, a, b, take)
        mover.put(mid_ref.at[a:b], mid_far.at[a:b])
    pilot, total, square = state
    mean, spread = local_moments(total, square, pilot, rows * cols, per)
    send_payload(mover, pack_pair(mean, spread), pay_far, stage_ref)


def back_two(
    gt_far, kernel_far, weight_far, near_ref, next_ref, one_ref, other_ref, *refs,
):
    text_ref, fbias_ref, freqs_ref, times_ref, levels_ref, out_far, film_ref, ints_ref, *refs = refs
    gt_ref, kernel_ref, weight_ref, cells_ref, out_ref, pair_ref, mover = refs
    cols, rows = gt_ref.shape[0:2]
    load = mover.start(kernel_far, kernel_ref)
    steps = pieces(cols, 8)
    own = [mover.start(gt_far.at[a:b], gt_ref.at[a:b]) for a, b in steps]
    late = mover.start(weight_far, weight_ref)
    fill_halo(cells_ref, near_ref, next_ref, one_ref, other_ref, lambda cells: cells)
    load.wait()
    backward_weights(kernel_ref, pair_ref)
    mover.ready()
    text = text_ref[...].astype(F32)
    half = TEMB // 2
    for at, source_ref in ((0, times_ref), (TEMB, levels_ref)):
        angles = [source_ref[image].astype(F32) * freqs_ref[...] for image in range(text_ref.shape[0])]
        angles = jnp.concatenate(angles, axis=0)
        for start, embed in ((at, jnp.sin(angles)), (at + half, jnp.cos(angles))):
            ints_ref[:, start : start + half] = (embed * sigmoid(embed)).astype(BF16)
    act = jnp.concatenate([ints_ref[...], (text * sigmoid(text)).astype(BF16)], axis=1)
    for (a, b), copy in zip(steps, own):
        copy.wait()
        cells_ref[a + 2 : b + 2, 2 : rows + 2] = gt_ref[a:b]
    clear_border(cells_ref, 2)
    for a, b in pieces(cols + 2, 10):
        convolve(cells_ref, pair_ref, True, rows + 2, a, b, lambda col, values: out_ref.__setitem__(col, values))
        mover.put(out_ref.at[a:b], out_far.at[a:b])
    late.wait()
    film_ref[...] = jnp.dot(act, weight_ref[...], preferred_element_type=F32) + fbias_ref[...].astype(F32)


def second_values(stat, gain_ref, bias_ref, film_ref):
    mean, inv = stat
    chans = mean.shape[1]
    scale = 1.0 + film_ref[:, 0:chans]
    slope = gain_ref[...].astype(F32) * scale
    half_slope = 0.5 * slope
    half_offset = 0.5 * (bias_ref[...].astype(F32) * scale + film_ref[:, chans:])

    def values(mid, back):
        hat = (mid - mean) * inv
        pre = hat * half_slope + half_offset
        bend = jnp.tanh(pre)
        more = 1.0 + bend
        grad = back * (0.5 * more * (1.0 + pre * (1.0 - bend)))
        return hat, pre * more, grad

    return slope, values


def second_norm(
    mid_far, back_far, gathered_ref, gain_ref, bias_ref, film_ref,
    act_far, pre_far, pay_far, sums_ref, stat_ref,
    mid_ref, back_ref, act_ref, pre_ref, stage_ref, mover,
):
    wide, tall, images, chans = mid_ref.shape
    cols, rows = wide - 2, tall - 2
    per = chans // GROUPS
    steps = pieces(wide, 9)
    loads = []
    for a, b in steps:
        loads.append(
            [mover.start(f.at[a:b], n.at[a:b]) for f, n in ((mid_far, mid_ref), (back_far, back_ref))]
        )
    mean, inv = merge_moments(gathered_ref, rows * cols * per)
    stat_ref[0] = mean
    stat_ref[1] = inv
    mover.ready()
    slope, values = second_values((mean, inv), gain_ref, bias_ref, film_ref)

    def column(col, inner):
        hat, act, grad = values(mid_ref[col], back_ref[col])
        act_ref[col] = act.astype(BF16)
        pre_ref[col] = grad.astype(BF16)
        if inner is None:
            return None
        own = grad[1 : rows + 1]
        plain, cross = inner
        return plain + jnp.sum(own, axis=0), cross + jnp.sum(own * hat[1 : rows + 1], axis=0)

    zero = jnp.zeros((images, chans), F32)
    inner = (zero, zero)
    for (a, b), pair in zip(steps, loads):
        for load in pair:
            load.wait()
        if a == 0:
            column(0, None)
        inner = lax.fori_loop(max(a, 1), min(b, cols + 1), column, inner)
        if b == wide:
            column(wide - 1, None)
        clear_border(act_ref, 1, a, b)
        mover.put(act_ref.at[a:b], act_far.at[a:b])
        mover.put(pre_ref.at[a:b], pre_far.at[a:b])
    plain, cross = inner
    sums_ref[0] = plain
    sums_ref[1] = cross
    send_payload(mover, pack_pair(group_total(plain * slope), group_total(cross * slope)), pay_far, stage_ref)


def kernel_two(
    act_far, gt_far, sums_ref, bias_ref, keep_far, send_far, act_ref, gt_ref, keep_ref, send_ref, mover
):
    for load in [mover.start(act_far, act_ref), mover.start(gt_far, gt_ref)]:
        load.wait()
    split_taps(grad_terms(act_ref, gt_ref), keep_ref, send_ref)
    mover.ready()
    images, chans = bias_ref.shape
    at = 9 * (chans // 2)
    total = jnp.sum(bias_ref[...], axis=0, keepdims=True)
    for ref in (keep_ref, send_ref):
        ref[at : at + images] = sums_ref[0]
        ref[at + images : at + 2 * images] = sums_ref[1]
        ref[at + 2 * images :] = jnp.broadcast_to(total, (ref.shape[0] - at - 2 * images, chans))
    mover.put(keep_ref, keep_far)
    mover.put(send_ref, send_far)


def mix(
    act_far, kernel_far, xt_far, kbias_ref, out_far, act_ref, kernel_ref, xt_ref, branch_ref, out_ref, pair_ref, mover
):
    images, rows, cols, chans = out_ref.shape
    loads = [mover.start(f, n) for f, n in ((kernel_far, kernel_ref), (act_far, act_ref), (xt_far, xt_ref))]
    loads[0].wait()
    forward_weights(kernel_ref, pair_ref)
    mover.ready()
    kbias = kbias_ref[...].astype(F32)
    loads[1].wait()
    convolve(
        act_ref, pair_ref, False, rows, 0, cols, lambda col, values: branch_ref.__setitem__(col, values + kbias)
    )
    loads[2].wait()
    for a, b in pieces(rows, 2):
        for row in range(a, b):
            mixed = jnp.swapaxes((xt_ref[:, row].astype(F32) + branch_ref[:, row]) * INV_ROOT, 0, 1)
            out_ref[:, row] = mixed.astype(BF16)
        mover.put(out_ref.at[:, a:b], out_far.at[:, a:b])


def middle_grad(
    mid_far, pre_far, act_far, keep_two_far, gathered_ref, stat_ref, gain_ref, film_ref,
    low_far, keep_ref, send_ref, two_ref, bias_ref,
    mid_ref, pre_ref, act_ref, low_ref, mover,
):
    wide, tall, images, chans = mid_ref.shape
    cols, rows = wide - 2, tall - 2
    steps = pieces(wide, 9)
    loads = []
    for a, b in steps:
        loads.append([mover.start(f.at[a:b], n.at[a:b]) for f, n in ((mid_far, mid_ref), (pre_far, pre_ref))])
    late = [mover.start(f, n) for f, n in ((act_far, act_ref), (keep_two_far, two_ref))]
    count = lax.axis_size("ha") * lax.axis_size("wa") * rows * cols * (chans // GROUPS)
    packed = jnp.sum(gathered_ref[...], axis=0) * (1.0 / count)
    mover.ready()
    mean = stat_ref[0]
    inv = stat_ref[1]
    plain = unpack_at(packed, 0) * inv
    cross = unpack_at(packed, 1) * inv * inv
    slope = gain_ref[...].astype(F32) * (1.0 + film_ref[:, 0:chans]) * inv

    def low_column(col, total):
        low = (pre_ref[col].astype(F32) * slope - plain - (mid_ref[col] - mean) * cross).astype(BF16)
        low_ref[col] = low
        if total is None:
            return None
        return total + jnp.sum(low[1 : rows + 1].astype(F32), axis=0)

    kbias = jnp.zeros((images, chans), F32)
    for (a, b), pair in zip(steps, loads):
        for load in pair:
            load.wait()
        if a == 0:
            low_column(0, None)
        kbias = lax.fori_loop(max(a, 1), min(b, cols + 1), low_column, kbias)
        if b == wide:
            low_column(wide - 1, None)
        clear_border(low_ref, 1, a, b)
        mover.put(low_ref.at[a:b], low_far.at[a:b])
    for load in late:
        load.wait()
    own = low_ref.at[1 : wide - 1, 1 : tall - 1]
    split_taps(grad_terms(act_ref.at[1 : wide + 1, 1 : tall + 1], own), keep_ref, send_ref)
    at = 9 * (chans // 2)
    for ref in (keep_ref, send_ref):
        ref[at:] = jnp.broadcast_to(jnp.sum(kbias, axis=0, keepdims=True), (ref.shape[0] - at, chans))
    bias_ref[...] = kbias


def back_one(
    low_far, xt_far, kernel_far, stat_ref, gain_ref, bias_ref, gbias_ref, lbias_ref, grad_far, pay_ref, low_ref, xt_ref, kernel_ref, out_ref, pair_ref, mover
):
    cols, rows, images, chans = xt_ref.shape
    loads = [mover.start(f, n) for f, n in ((kernel_far, kernel_ref), (low_far, low_ref), (xt_far, xt_ref))]
    loads[0].wait()
    backward_weights(kernel_ref, pair_ref)
    loads[1].wait()
    loads[2].wait()
    mover.ready()
    mean = stat_ref[0]
    inv = stat_ref[1]
    gain = gain_ref[...].astype(F32)
    bias = bias_ref[...].astype(F32)
    state = [jnp.zeros((images, chans), F32), jnp.zeros((images, chans), F32)]

    def take(col, values):
        hat = (xt_ref[col].astype(F32) - mean) * inv
        norm = hat * gain + bias
        sigma = sigmoid(norm)
        grad = values * (sigma * (1.0 + norm * (1.0 - sigma)))
        out_ref[col] = grad
        state[0] = state[0] + jnp.sum(grad, axis=0)
        state[1] = state[1] + jnp.sum(grad * hat, axis=0)

    for a, b in pieces(cols, 8):
        convolve(low_ref, pair_ref, True, rows, a, b, take)
        mover.put(out_ref.at[a:b], grad_far.at[a:b])
    plain, cross = state
    half = images // 2
    pay_ref[0:half] = pack_pair(group_total(plain * gain), group_total(cross * gain))
    rest = [jnp.sum(v, axis=0, keepdims=True) for v in (cross, plain, gbias_ref[...], lbias_ref[...])]
    short = pay_ref.shape[0] - half - 4
    pay_ref[half:] = jnp.concatenate(rest + [jnp.zeros((short, chans), F32)], axis=0)


CODE = 32768.0


def exponents(values):
    most = jnp.clip(jnp.max(jnp.abs(values), axis=0, keepdims=True), 1e-30, 1e30)
    return jnp.ceil(jnp.log2(most) + 2e-3)


def two_to(powers):
    powers = powers.astype(jnp.int32)
    first = powers >> 1
    made = None
    for part in (first, powers - first):
        shifted = part + 64
        for bit in range(7):
            factor = jnp.where((shifted >> bit) & 1 == 1, 2.0 ** (1 << bit), 1.0)
            if bit == 0:
                piece = factor * 2.0**-64
            else:
                piece = piece * factor
        made = piece if made is None else made * piece
    return made


def pack_terms(
    keep_one_ref, came_one_ref, keep_two_ref, came_two_ref, out_far, token_ref,
    one_ref, two_ref, extra_ref, rest_ref, out_ref, mover, extras_one, extras_two,
):
    chips, rows, chans = out_ref.shape
    taps = 9 * (chans // 2)
    share = -(-taps // chips)
    more = -(-(extras_one + extras_two) // chips)
    extra_ref[...] = jnp.zeros(extra_ref.shape, F32)
    one_ref[...] = keep_one_ref[...] + came_one_ref[...]
    two_ref[...] = keep_two_ref[...] + came_two_ref[...]
    extra_ref[0:extras_two] = two_ref[taps : taps + extras_two]
    if extras_one:
        extra_ref[extras_two : extras_two + extras_one] = one_ref[taps : taps + extras_one]
    token_ref[...] = extra_ref[0:8]
    powers = []
    for ref, count in ((one_ref, taps), (two_ref, taps), (extra_ref, extra_ref.shape[0])):
        values = ref[0:count]
        power = exponents(values)
        powers.append(power)
        scaled = values * (two_to(-power) * CODE)
        code = jnp.round(scaled)
        ref[0:count] = code
        if ref is extra_ref:
            rest_ref[...] = jnp.round((scaled - code) * CODE)
    short = rows - 2 * share - 2 * more - 3
    pad = [jnp.zeros((short, chans), F32)] if short else []
    for chip in range(chips):
        a, b = chip * share, min((chip + 1) * share, taps)
        mine = []
        for ref in (one_ref, two_ref):
            if a < b:
                mine.append(ref[a:b])
            if max(b - a, 0) < share:
                mine.append(jnp.zeros((share - max(b - a, 0), chans), F32))
        for ref in (extra_ref, rest_ref):
            mine.append(ref[chip * more : (chip + 1) * more])
        whole = jnp.concatenate(mine + powers + pad, axis=0)
        out_ref[chip] = whole.astype(jnp.int32).astype(jnp.int16)
    mover.put(out_ref, out_far)


def unpack_terms(gathered_ref, share, more):
    chips, rows, chans = gathered_ref.shape
    row = lax.broadcasted_iota(jnp.int32, (rows, chans), 0)
    base = 2 * share + 2 * more
    total = jnp.zeros((rows, chans), F32)
    blocks = [gathered_ref[chip].astype(jnp.int32).astype(F32) for chip in range(chips)]
    every = two_to(jnp.concatenate([block[base : base + 3] for block in blocks], axis=0)) * (1.0 / CODE)
    for chip, block in enumerate(blocks):
        scales = every[3 * chip : 3 * chip + 3]
        scale = jnp.where(row < share, scales[0:1], jnp.where(row < 2 * share, scales[1:2], scales[2:3]))
        scale = jnp.where(row < 2 * share + more, scale, scale * (1.0 / CODE))
        total = total + block * scale
    extra = total[2 * share : 2 * share + more] + total[2 * share + more : base]
    return total[0 : 2 * share], extra


def two_terms(values):
    high = values.astype(BF16).astype(F32)
    return [high, values - high]


def add_terms(gathered_ref, pay_ref, came_ref, out_far, out_ref, mover, more, whole):
    chips, rows, chans = gathered_ref.shape
    shares, extra = unpack_terms(gathered_ref, -(-9 * (chans // 2) // chips), more)
    every = [shares] + two_terms(extra) + two_terms(pay_ref[0:whole] + came_ref[0:whole])
    short = out_ref.shape[1] - sum(v.shape[0] for v in every)
    if short:
        every.append(jnp.zeros((short, chans), F32))
    out_ref[...] = jnp.broadcast_to(jnp.concatenate(every, axis=0).astype(BF16)[None], out_ref.shape)
    mover.put(out_ref, out_far)


def sums_of(own_ref, at, whole):
    total = own_ref[0].astype(F32)
    for chip in range(1, own_ref.shape[0]):
        total = total + own_ref[chip].astype(F32)
    return total[at : at + whole] + total[at + whole : at + 2 * whole]


def three_terms(values):
    high = values.astype(BF16)
    rest = values - high.astype(F32)
    mid = rest.astype(BF16)
    low = (rest - mid.astype(F32)).astype(BF16)
    return jnp.concatenate([high, mid, low], axis=0)


def spread_out(own_ref, other_ref, one_far, two_far, one_ref, two_ref, half_ref, mover):
    chips, rows, chans = own_ref.shape
    half = chans // 2
    taps = 9 * half
    share = -(-taps // chips)
    core = lax.axis_index("ha") % 2
    for at, (out_ref, far) in enumerate(((one_ref, one_far), (two_ref, two_far))):
        for source, place in ((own_ref, core), (other_ref, 1 - core)):
            for chip in range(chips):
                piece = source[chip].astype(F32)[at * share : (at + 1) * share]
                half_ref[chip * share : (chip + 1) * share] = piece
            for tap in range(9):
                rows_at = pl.ds(pl.multiple_of(place * half, half), half)
                out_ref[tap, rows_at] = half_ref[tap * half : (tap + 1) * half]
        mover.put(out_ref, far)


def last_grads(
    weight_far, grad_ref, xt_ref, c_ref, own_ref, stat_ref, gain_one_ref, gain_two_ref, bias_two_ref, film_ref, ints_ref, text_ref,
    out_far, weight_grad_far, text_grad_far, bias_ref, *refs, more, whole,
):
    *vec_refs, weight_ref, out_ref, weight_grad_ref, text_grad_ref, extra_ref, mover = refs
    images, rows, cols, chans = out_ref.shape
    chips = own_ref.shape[0]
    load = mover.start(weight_far, weight_ref)
    share = -(-9 * (chans // 2) // chips)
    start = 2 * share
    for chip in range(chips):
        piece = own_ref[chip].astype(F32)
        extra_ref[chip * more : (chip + 1) * more] = piece[start : start + more] + piece[start + more : start + 2 * more]
    plain = extra_ref[0:images]
    cross = extra_ref[images : 2 * images]
    mover.ready()
    scale = 1.0 + film_ref[:, 0:chans]
    scale_grad = gain_two_ref[...].astype(F32) * cross + bias_two_ref[...].astype(F32) * plain
    film_grad = jnp.concatenate([scale_grad, plain], axis=1)
    bias_ref[...] = jnp.sum(film_grad, axis=0, keepdims=True)
    sums = sums_of(own_ref, start + 2 * more, whole)
    vec_refs[0][...] = jnp.sum(scale * cross, axis=0, keepdims=True)
    vec_refs[1][...] = jnp.sum(scale * plain, axis=0, keepdims=True)
    for at, row in ((4, whole - 4), (5, whole - 3), (2, whole - 2), (3, whole - 1)):
        vec_refs[at][...] = sums[row : row + 1]
    terms = three_terms(film_grad)
    ints = ints_ref.shape[1]

    depth = weight_grad_ref.shape[0]
    for at in range(0, depth, 512):
        if at < ints:
            act = ints_ref[:, at : at + 512]
        else:
            embed = text_ref[:, at - ints : at - ints + 512].astype(F32)
            act = (embed * sigmoid(embed)).astype(BF16)
        weight_grad_ref[at : at + 512] = lax.dot_general(
            jnp.concatenate([act, act, act], axis=0), terms, (((0,), (0,)), ((), ())), preferred_element_type=F32
        )
        mover.put(weight_grad_ref.at[at : at + 512], weight_grad_far.at[at : at + 512])

    count = lax.axis_size("ha") * lax.axis_size("wa") * rows * cols * (chans // GROUPS)
    packed = sums[0 : images // 2] * (1.0 / count)
    plain = unpack_at(packed, 0)
    cross = unpack_at(packed, 1)
    mean = stat_ref[0]
    inv = stat_ref[1]
    gain = gain_one_ref[...].astype(F32)
    for a, b in pieces(rows, 2):
        for row in range(a, b):
            hat = (xt_ref[:, row].astype(F32) - mean) * inv
            path = jnp.swapaxes(inv * (grad_ref[:, row] * gain - plain - hat * cross), 0, 1)
            out_ref[:, row] = (c_ref[:, row].astype(F32) * INV_ROOT + path).astype(BF16)
        mover.put(out_ref.at[:, a:b], out_far.at[:, a:b])

    load.wait()
    for at in range(ints, depth, 512):
        embed = text_ref[:, at - ints : at - ints + 512].astype(F32)
        sigma = sigmoid(embed)
        made = lax.dot_general(
            terms, weight_ref[at : at + 512], (((1,), (1,)), ((), ())), preferred_element_type=F32
        )
        cond_grad = made[0:images] + made[images : 2 * images] + made[2 * images :]
        text_grad_ref[:, at - ints : at - ints + 512] = cond_grad * (sigma * (1.0 + embed * (1.0 - sigma)))
    mover.put(text_grad_ref, text_grad_far)


def to_all(payload):
    return lax.all_to_all(payload, AXES, 0, 0)


def to_chips(payload):
    tall, wide = lax.axis_size("ha"), lax.axis_size("wa")
    groups = [[h * wide + w for h in range(core, tall, 2) for w in range(wide)] for core in range(2)]
    return lax.all_to_all(payload, AXES, 0, 0, axis_index_groups=groups)


def to_sibling(payload):
    return lax.ppermute(payload, "ha", [(i, i ^ 1) for i in range(lax.axis_size("ha"))])


def pair_exchange(one, other, axis):
    count = lax.axis_size(axis)
    pairs = [(i, (i + 1 if i % 2 else i - 1) % count) for i in range(count)]
    if axis == "wa":
        pairs = [(i, min(max(j, 0), count - 1) if abs(i - j) == 1 else i) for i, j in pairs]
    one = lax.ppermute(one, axis, [(i, i ^ 1) for i in range(count)])
    return one, lax.ppermute(other, axis, pairs)


def side_halo(sides, near, following, after=()):
    four, rows, images, chans = sides.shape
    edge = shaped((2, rows + 4, images, chans), sides.dtype)
    one, other = kernel_call(
        edge_columns, near=(sides, near, following), near_out=(edge, edge), cost=0.4, after=after, limit=16
    )
    return pair_exchange(one, other, "wa"), one


def local(
    block_input,
    timesteps,
    aug_levels,
    text_pooled,
    gain_one,
    bias_one,
    conv_one,
    conv_one_bias,
    gain_two,
    bias_two,
    film_weight,
    film_bias,
    conv_two,
    conv_two_bias,
    cotangent,
):
    images, rows, cols, chans = block_input.shape
    parts = lax.axis_size("ha") * lax.axis_size("wa")
    chips = parts // 2
    half = images // 2
    gain_one, bias_one, conv_one_bias, gain_two, bias_two, conv_two_bias = (
        v.reshape(1, chans) for v in (gain_one, bias_one, conv_one_bias, gain_two, bias_two, conv_two_bias)
    )
    freqs = np.exp(-math.log(10000.0) * np.arange(TEMB // 2) / (TEMB // 2)).astype(np.float32)[None]
    payload = shaped((parts, half, chans), F32)
    per_image = shaped((images, chans), F32)
    two_images = shaped((2, images, chans), F32)
    block = shaped((cols, rows, images, chans), BF16)
    block_wide = shaped((cols, rows, images, chans), F32)
    rim = shaped((cols + 2, rows + 2, images, chans), BF16)
    rim_wide = shaped((cols + 2, rows + 2, images, chans), F32)
    far_rim = shaped((cols + 4, rows + 4, images, chans), BF16)
    given = shaped((images, rows, cols, chans), BF16)
    pair = pltpu.VMEM((12 * chans, 2 * chans), BF16)
    pair_back = pltpu.VMEM((2 * chans, 12 * chans), BF16)

    sides = shaped((4, rows, images, chans), BF16)
    row_halo = shaped((cols, 2, images, chans), BF16)
    xt, x_near, x_next, x_sides, moments = kernel_call(
        prepare_x, far=(block_input,), far_out=(block,),
        near_out=(row_halo, row_halo, sides, shaped((half, chans), F32)),
        scratch=buffers(given, block), sems=16, cost=2.3,
    )
    x_near, x_next = pair_exchange(x_near, x_next, "ha")
    gt, pay_one, g_near, g_next, g_sides, kbias_two_local = kernel_call(
        prepare_g, far=(cotangent,), near=(moments,), far_out=(block, payload),
        near_out=(row_halo, row_halo, sides), tiny_out=(per_image,),
        scratch=buffers(given, block, payload), sems=16, cost=2.0,
    )
    moments_one = to_all(pay_one)
    x_cols, x_edge = side_halo(x_sides, x_near, x_next)
    g_near, g_next = pair_exchange(g_near, g_next, "ha")

    film_bias = film_bias.reshape(1, 2 * chans)
    act_one, mid, pay_two, stat_one = kernel_call(
        first_half, far=(xt, conv_one), near=(x_near, x_next, *x_cols, moments_one),
        tiny=(gain_one, bias_one, conv_one_bias),
        far_out=(far_rim, rim_wide, payload), tiny_out=(two_images,),
        scratch=buffers(xt, conv_one, far_rim, rim_wide, payload) + (pair,), sems=16, cost=5.5,
        after=(film_bias,),
    )
    moments_two = to_all(pay_two)
    g_cols, _ = side_halo(g_sides, g_near, g_next, after=(stat_one,))
    act_two_grad, film, act_ints = kernel_call(
        back_two, far=(gt, conv_two, film_weight), near=(g_near, g_next, *g_cols),
        tiny=(text_pooled, film_bias, freqs), scalars=(timesteps, aug_levels),
        far_out=(rim_wide,), tiny_out=(shaped((images, 2 * chans), F32), shaped((images, 2 * TEMB), BF16)),
        scratch=buffers(gt, conv_two, film_weight, far_rim, rim_wide) + (pair_back,), sems=16, cost=5.0,
    )
    act_two, pre_two_grad, pay_three, sums_two, stat_two = kernel_call(
        second_norm, far=(mid, act_two_grad), near=(moments_two,), tiny=(gain_two, bias_two, film),
        far_out=(rim, rim, payload), tiny_out=(two_images, two_images),
        scratch=buffers(rim_wide, rim_wide, rim, rim, payload), sems=24, cost=3.2,
    )
    moments_three = to_all(pay_three)

    taps = 9 * (chans // 2)
    share = -(-taps // chips)
    extras_two = 2 * images
    extras_one = 0
    halves_two = shaped((taps + 2 * images + 8, chans), F32)
    halves_one = shaped((taps + 8, chans), F32)
    keep_two, send_two = kernel_call(
        kernel_two, far=(act_two, gt), tiny=(sums_two, kbias_two_local), far_out=(halves_two, halves_two),
        scratch=buffers(act_two, gt, halves_two, halves_two), sems=4, cost=3.0,
    )
    came_two = to_sibling(send_two)
    low, keep_one, send_one, keep_two, kbias_one_local = kernel_call(
        middle_grad, far=(mid, pre_two_grad, act_one, keep_two), near=(moments_three,), tiny=(stat_two, gain_two, film),
        far_out=(rim,), near_out=(halves_one, halves_one, halves_two), tiny_out=(per_image,),
        scratch=buffers(mid, pre_two_grad, act_one, rim), sems=24, cost=6.0,
    )
    came_one = to_sibling(send_one)
    more = -(-(extras_one + extras_two) // chips)
    terms_shape = shaped((chips, -(-(2 * share + 2 * more + 3) // 8) * 8, chans), jnp.int16)
    extra_shape = shaped((-(-chips * more // 8) * 8, chans), F32)
    terms, token = kernel_call(
        functools.partial(pack_terms, extras_one=extras_one, extras_two=extras_two),
        near=(keep_one, came_one, keep_two, came_two), far_out=(terms_shape,), near_out=(shaped((8, chans), F32),),
        scratch=buffers(halves_one, halves_two, extra_shape, extra_shape, terms_shape),
        sems=3, cost=1.0,
    )
    gathered = to_chips(terms)
    whole = half + 4
    norm_one_grad, pay_four = kernel_call(
        back_one, far=(low, xt, conv_one), tiny=(stat_one, gain_one, bias_one, kbias_two_local, kbias_one_local), far_out=(block_wide,),
        near_out=(shaped((2 * half, chans), F32),),
        scratch=buffers(rim, block, conv_one, block_wide) + (pair_back,), sems=16, cost=5.0,
        after_near=(to_sibling(token),),
    )
    came_four = to_sibling(pay_four)
    (mixed,) = kernel_call(
        mix, far=(act_two, conv_two, xt), tiny=(conv_two_bias,), far_out=(given,),
        scratch=buffers(act_two, conv_two, xt, block_wide, given) + (pair,), sems=8, cost=3.6, after_near=(pay_four,),
    )
    shares_shape = shaped((chips, -(-(2 * share + 2 * more + 2 * whole) // 8) * 8, chans), BF16)
    (shares,) = kernel_call(
        functools.partial(add_terms, more=more, whole=whole),
        near=(gathered, pay_four, came_four), far_out=(shares_shape,),
        scratch=buffers(shares_shape), sems=1, cost=1.0, after=(mixed,),
    )
    own_half = to_chips(shares)
    other_half = to_sibling(own_half)
    weight_grad = shaped(film_weight.shape, F32)
    text_shape = shaped(text_pooled.shape, F32)
    row = shaped((1, chans), F32)
    input_grad, film_weight_grad, text_grad, film_bias_grad, *vec_grads = kernel_call(
        functools.partial(last_grads, more=more, whole=whole),
        far=(film_weight,),
        near=(norm_one_grad, xt, cotangent, own_half, stat_one, gain_one, gain_two, bias_two, film, act_ints, text_pooled),
        far_out=(given, weight_grad, text_shape), tiny_out=(shaped((1, 2 * chans), F32),) + (row,) * 6,
        scratch=buffers(film_weight, given, weight_grad, text_shape)
        + (pltpu.VMEM((-(-chips * more // 8) * 8, chans), F32),),
        sems=32, cost=6.0, limit=24,
    )
    full = shaped((9, chans, chans), F32)
    kernel_one_grad, kernel_two_grad = kernel_call(
        spread_out, near=(own_half, other_half), far_out=(full, full),
        scratch=buffers(full, full, shaped((chips * share, chans), F32)), sems=2, cost=2.0, after=(input_grad,), limit=24,
    )
    return (
        mixed,
        input_grad,
        text_grad,
        vec_grads[4].reshape(chans),
        vec_grads[5].reshape(chans),
        kernel_one_grad.reshape(3, 3, chans, chans),
        vec_grads[3].reshape(chans),
        vec_grads[0].reshape(chans),
        vec_grads[1].reshape(chans),
        film_weight_grad,
        film_bias_grad.reshape(2 * chans),
        kernel_two_grad.reshape(3, 3, chans, chans),
        vec_grads[2].reshape(chans),
    )


def solution(mesh):
    split = P(None, "ha", "wa", None)
    return jax.shard_map(
        local,
        mesh=mesh,
        in_specs=(split,) + (P(),) * 13 + (split,),
        out_specs=(split, split) + (P(),) * 11,
        check_vma=False,
    )
```

```python
import functools
import math

import jax
import jax.numpy as jnp
import numpy as np
from jax import lax
from jax.experimental import pallas as pl
from jax.experimental.pallas import tpu as pltpu
from jax.sharding import PartitionSpec as P

GROUPS = 32
TEMB = 256
EPSILON = 1e-05
INV_ROOT = 1.0 / math.sqrt(2.0)
AXES = ("ha", "wa")
F32 = jnp.float32
BF16 = jnp.bfloat16
NEAR = pl.BlockSpec(memory_space=pltpu.VMEM)
FAR = pl.BlockSpec(memory_space=pl.ANY)
MIB = 1 << 20


def shaped(shape, dtype):
    return jax.ShapeDtypeStruct(shape, dtype)


def kernel_call(
    body, far=(), near=(), tiny=(), far_out=(), near_out=(), tiny_out=(), scratch=(), sems=0, cost=1.0,
    after=(), after_near=(), scalars=(), limit=48,
):
    pinned = lambda arrays: [pltpu.with_memory_space_constraint(array, pltpu.HBM) for array in arrays]
    given = len(far) + len(near)
    held = len(after) + len(after_near)
    copies = len(tiny) + len(tiny_out)

    def run(*refs):
        refs = list(refs)
        take = lambda count: [refs.pop(0) for _ in range(count)]
        inputs = take(given)
        tiny_far = take(len(tiny))
        scalar_refs = take(len(scalars))
        take(held)
        outputs = take(len(far_out) + len(near_out))
        tiny_out_far = take(len(tiny_out))
        tiny_refs = take(len(tiny))
        tiny_out_refs = take(len(tiny_out))
        mover = None
        if sems + copies:
            mover = Mover(refs.pop(), [(f, n) for f, n in zip(tiny_far, tiny_refs)])
        body(*inputs, *tiny_refs, *scalar_refs, *outputs, *tiny_out_refs, *refs, *([mover] if mover else []))
        if mover:
            for source, target in zip(tiny_out_refs, tiny_out_far):
                mover.put(source, target)
            mover.finish()

    return pl.pallas_call(
        run,
        out_shape=(
            *(pltpu.HBM(out.shape, out.dtype) for out in far_out),
            *near_out,
            *(pltpu.HBM(out.shape, out.dtype) for out in tiny_out),
        ),
        in_specs=[FAR] * len(far)
        + [NEAR] * len(near)
        + [FAR] * len(tiny)
        + [pl.BlockSpec(memory_space=pltpu.SMEM)] * len(scalars)
        + [FAR] * held,
        out_specs=(FAR,) * len(far_out) + (NEAR,) * len(near_out) + (FAR,) * len(tiny_out),
        scratch_shapes=buffers(*tiny, *tiny_out)
        + tuple(scratch)
        + ((pltpu.SemaphoreType.DMA((sems + copies,)),) if sems + copies else ()),
        compiler_params=pltpu.CompilerParams(vmem_limit_bytes=limit * MIB),
        name=getattr(body, "func", body).__name__,
        cost_estimate=pl.CostEstimate(flops=int(cost * 1.1e9), bytes_accessed=0, transcendentals=0),
    )(*pinned(far), *near, *pinned(tiny), *scalars, *pinned(after), *after_near)


def buffers(*arrays):
    return tuple(pltpu.VMEM(a.shape, a.dtype) for a in arrays)


class Mover:
    def __init__(self, sems, first):
        self.sems = sems
        self.used = 0
        self.open = []
        self.first = [self.start(source, target) for source, target in first]

    def start(self, source, target):
        copy = pltpu.make_async_copy(source, target, self.sems.at[self.used])
        self.used += 1
        copy.start()
        return copy

    def ready(self):
        for copy in self.first:
            copy.wait()

    def put(self, source, target):
        self.open.append(self.start(source, target))

    def finish(self):
        for copy in self.open:
            copy.wait()


def pieces(count, size):
    return [(at, min(at + size, count)) for at in range(0, count, size)]


def lanes_of(shape):
    return lax.broadcasted_iota(jnp.int32, shape, 1)


def group_total(values):
    chans = values.shape[1]
    lane = lanes_of(values.shape)
    step = 1
    while step < chans // GROUPS:
        up = pltpu.roll(values, chans - step, 1)
        down = pltpu.roll(values, step, 1)
        values = values + jnp.where((lane & step) == 0, up, down)
        step *= 2
    return values


def pack_pair(first, second):
    half = first.shape[0] // 2
    lane = lanes_of((half, first.shape[1])) & 3
    return jnp.where(
        lane == 0,
        first[:half],
        jnp.where(lane == 1, second[:half], jnp.where(lane == 2, first[half:], second[half:])),
    )


def unpack_at(packed, place):
    lane = lanes_of(packed.shape) & 3
    top = group_total(jnp.where(lane == place, packed, 0.0))
    low = group_total(jnp.where(lane == place + 2, packed, 0.0))
    return jnp.concatenate([top, low], axis=0)


def merge_moments(gathered_ref, local_count):
    parts = gathered_ref.shape[0]
    chans = gathered_ref.shape[2]
    every = gathered_ref[...]
    total = jnp.sum(every, axis=0)
    mean = total * (1.0 / parts)
    apart = every - mean[None]
    between = jnp.sum(apart * apart, axis=0)
    square = pltpu.roll(total, chans - 1, 1) + local_count * between
    inv = lax.rsqrt(square * (1.0 / (local_count * parts)) + EPSILON)
    return unpack_at(mean, 0), unpack_at(inv, 0)


def local_moments(total, square, pilot, pixels, per):
    off = total * (1.0 / pixels)
    mean = pilot + off
    apart = square - total * off
    group_mean = group_total(mean) * (1.0 / per)
    shift = mean - group_mean
    return group_mean, group_total(apart + pixels * shift * shift)


def sigmoid(values):
    return 0.5 + 0.5 * jnp.tanh(0.5 * values)


def forward_weights(kernel_ref, pair_ref):
    chans = kernel_ref.shape[2]
    zero = jnp.zeros((chans, chans), BF16)
    for row in range(3):
        for col in range(4):
            at = (row * 4 + col) * chans
            pair_ref[at : at + chans, 0:chans] = kernel_ref[row, col] if col < 3 else zero
            pair_ref[at : at + chans, chans:] = kernel_ref[row, col - 1] if col > 0 else zero


def backward_weights(kernel_ref, pair_ref):
    chans = kernel_ref.shape[2]
    zero = jnp.zeros((chans, chans), BF16)
    for row in range(3):
        for col in range(4):
            at = (row * 4 + col) * chans
            pair_ref[0:chans, at : at + chans] = kernel_ref[2 - row, 2 - col] if col < 3 else zero
            pair_ref[chans:, at : at + chans] = kernel_ref[2 - row, 3 - col] if col > 0 else zero


def convolve(cells_ref, pair_ref, transposed, rows, first, last, take):
    images, chans = cells_ref.shape[2:]
    pairs = (last - first) // 2
    parts = []
    for row in range(3):
        for col in range(4):
            window = [cells_ref[first + 2 * q + col, row : row + rows] for q in range(pairs)]
            parts.append(jnp.stack(window).reshape(pairs * rows * images, chans))
    wide = jnp.concatenate(parts, axis=1)
    contract = ((1,), (1,)) if transposed else ((1,), (0,))
    made = lax.dot_general(wide, pair_ref[...], (contract, ((), ())), preferred_element_type=F32)
    made = made.reshape(pairs, rows, images, 2 * chans)
    for q in range(pairs):
        for side in range(2):
            take(first + 2 * q + side, made[q, :, :, side * chans : (side + 1) * chans])


def grad_terms(cells_ref, grads_ref):
    cols, rows, images, chans = grads_ref.shape
    pixels = cols * rows * images
    windows = [
        cells_ref[col : col + cols, row : row + rows].reshape(pixels, chans) for row in range(3) for col in range(3)
    ]
    return lax.dot_general(
        grads_ref[...].reshape(pixels, chans),
        jnp.concatenate(windows, axis=1),
        (((0,), (0,)), ((), ())),
        preferred_element_type=F32,
    )


def split_taps(every, keep_ref, send_ref):
    chans = every.shape[0]
    half = chans // 2
    first = lax.axis_index("ha") % 2 == 0
    for tap in range(9):
        made = every[:, tap * chans : (tap + 1) * chans].T
        at = tap * half
        keep_ref[at : at + half, :] = jnp.where(first, made[:half], made[half:])
        send_ref[at : at + half, :] = jnp.where(first, made[half:], made[:half])


def at_edges():
    tall = lax.axis_index("ha")
    wide = lax.axis_index("wa")
    return (
        tall == 0,
        tall == lax.axis_size("ha") - 1,
        wide == 0,
        wide == lax.axis_size("wa") - 1,
    )


def clear_border(cells_ref, width, first=0, last=None):
    top, bottom, left, right = at_edges()
    cols, rows, images, chans = cells_ref.shape
    last = cols if last is None else last
    dtype = cells_ref.dtype

    @pl.when(top)
    def _():
        cells_ref[first:last, 0:width] = jnp.zeros((last - first, width, images, chans), dtype)

    @pl.when(bottom)
    def _():
        cells_ref[first:last, rows - width :] = jnp.zeros((last - first, width, images, chans), dtype)

    if first == 0:

        @pl.when(left)
        def _():
            cells_ref[0:width] = jnp.zeros((width, rows, images, chans), dtype)

    if last == cols:

        @pl.when(right)
        def _():
            cells_ref[cols - width :] = jnp.zeros((width, rows, images, chans), dtype)


def send_payload(mover, packed, pay_ref, stage_ref):
    stage_ref[...] = jnp.broadcast_to(packed[None], stage_ref.shape)
    mover.put(stage_ref, pay_ref)


def prepare_x(x_far, xt_far, near_ref, next_ref, sides_ref, moments_ref, x_ref, xt_ref, mover):
    images, rows, cols, chans = x_ref.shape
    steps = pieces(rows, 2)
    loads = [mover.start(x_far.at[:, a:b], x_ref.at[:, a:b]) for a, b in steps]
    total = jnp.zeros((images, chans), F32)
    square = total
    for (a, b), load in zip(steps, loads):
        load.wait()
        if a == 0:
            pilot = x_ref[:, 0, 0].astype(F32)
        for row in range(a, b):
            x = jnp.swapaxes(x_ref[:, row].astype(F32), 0, 1)
            xt_ref[:, row] = x.astype(BF16)
            apart = x - pilot[None]
            total = total + jnp.sum(apart, axis=0)
            square = square + jnp.sum(apart * apart, axis=0)
        mover.put(xt_ref.at[:, a:b], xt_far.at[:, a:b])
    mean, spread = local_moments(total, square, pilot, rows * cols, chans // GROUPS)
    moments_ref[...] = pack_pair(mean, spread)
    outer(xt_ref, near_ref, next_ref, sides_ref)


def is_even(axis="ha"):
    return lax.axis_index(axis) % 2 == 0


def outer(cells, near_ref, next_ref, sides_ref):
    cols, rows = cells.shape[0:2]
    down, up = cells[:, rows - 2 :], cells[:, 0:2]
    near_ref[...] = jnp.where(is_even(), down, up)
    next_ref[...] = jnp.where(is_even(), up, down)
    sides_ref[0:2] = cells[0:2]
    sides_ref[2:4] = cells[cols - 2 :]


def prepare_g(
    c_far, moments_ref, gt_far, pay_far, near_ref, next_ref, sides_ref, bias_ref, c_ref, gt_ref, stage_ref, mover
):
    images, rows, cols, chans = c_ref.shape
    steps = pieces(rows, 2)
    loads = [mover.start(c_far.at[:, a:b], c_ref.at[:, a:b]) for a, b in steps]
    send_payload(mover, moments_ref[...], pay_far, stage_ref)
    bias = jnp.zeros((images, chans), F32)
    for (a, b), load in zip(steps, loads):
        load.wait()
        for row in range(a, b):
            grad = jnp.swapaxes(c_ref[:, row].astype(F32) * INV_ROOT, 0, 1).astype(BF16)
            gt_ref[:, row] = grad
            bias = bias + jnp.sum(grad.astype(F32), axis=0)
        mover.put(gt_ref.at[:, a:b], gt_far.at[:, a:b])
    bias_ref[...] = bias
    outer(gt_ref, near_ref, next_ref, sides_ref)


def edge_columns(sides_ref, near_ref, next_ref, one_ref, other_ref):
    cols, rows = near_ref.shape[0], sides_ref.shape[1]
    even = is_even("wa")

    def piece(left, right):
        return jnp.where(even, right, left), jnp.where(even, left, right)

    near = piece(near_ref[0:2], near_ref[cols - 2 : cols])
    following = piece(next_ref[0:2], next_ref[cols - 2 : cols])
    own = piece(sides_ref[0:2], sides_ref[2:4])
    for at, ref in enumerate((one_ref, other_ref)):
        ref[:, 0:2] = jnp.where(is_even(), following[at], near[at])
        ref[:, 2 : rows + 2] = own[at]
        ref[:, rows + 2 :] = jnp.where(is_even(), near[at], following[at])


def fill_halo(cells_ref, near_ref, next_ref, one_ref, other_ref, change):
    cols, rows = near_ref.shape[0], cells_ref.shape[1] - 4

    def halo_column(col, _):
        near, next_ = near_ref[pl.ds(col, 1)], next_ref[pl.ds(col, 1)]
        cells_ref[pl.ds(col + 2, 1), 0:2] = change(jnp.where(is_even(), next_, near))
        cells_ref[pl.ds(col + 2, 1), rows + 2 :] = change(jnp.where(is_even(), near, next_))
        return 0

    even = is_even("wa")
    cells_ref[0:2] = change(jnp.where(even, other_ref[...], one_ref[...]))
    cells_ref[cols + 2 :] = change(jnp.where(even, one_ref[...], other_ref[...]))
    lax.fori_loop(0, cols, halo_column, 0, unroll=4)


def first_half(
    xt_far, kernel_far, near_ref, next_ref, one_ref, other_ref, gathered_ref, gain_ref, bias_ref, kbias_ref,
    act_far, mid_far, pay_far, stat_ref,
    xt_ref, kernel_ref, act_ref, mid_ref, stage_ref, pair_ref, mover,
):
    cols, rows, images, chans = xt_ref.shape
    per = chans // GROUPS
    load = mover.start(kernel_far, kernel_ref)
    steps = pieces(cols, 8)
    own = [mover.start(xt_far.at[a:b], xt_ref.at[a:b]) for a, b in steps]
    mean, inv = merge_moments(gathered_ref, rows * cols * per)
    stat_ref[0] = mean
    stat_ref[1] = inv
    mover.ready()
    slope = 0.5 * inv * gain_ref[...].astype(F32)
    offset = 0.5 * bias_ref[...].astype(F32)

    def act(cells):
        value = (cells.astype(F32) - mean) * slope + offset
        return (value + value * jnp.tanh(value)).astype(BF16)

    def column(col, _):
        act_ref[pl.ds(col + 2, 1), 2 : rows + 2] = act(xt_ref[pl.ds(col, 1)])
        return 0

    fill_halo(act_ref, near_ref, next_ref, one_ref, other_ref, act)
    for (a, b), copy in zip(steps, own):
        copy.wait()
        lax.fori_loop(a, b, column, 0, unroll=2)
    clear_border(act_ref, 2)
    load.wait()
    forward_weights(kernel_ref, pair_ref)
    mover.put(act_ref, act_far)

    wide = cols + 2
    kbias = kbias_ref[...].astype(F32)
    state = [None, jnp.zeros((images, chans), F32), jnp.zeros((images, chans), F32)]

    def take(col, values):
        values = values + kbias
        mid_ref[col] = values
        if 1 <= col <= cols:
            own = values[1 : rows + 1]
            if state[0] is None:
                state[0] = own[0]
            apart = own - state[0][None]
            state[1] = state[1] + jnp.sum(apart, axis=0)
            state[2] = state[2] + jnp.sum(apart * apart, axis=0)

    for a, b in pieces(wide, 6):
        convolve(act_ref, pair_ref, False, rows + 2, a, b, take)
        mover.put(mid_ref.at[a:b], mid_far.at[a:b])
    pilot, total, square = state
    mean, spread = local_moments(total, square, pilot, rows * cols, per)
    send_payload(mover, pack_pair(mean, spread), pay_far, stage_ref)


def back_two(
    gt_far, kernel_far, weight_far, near_ref, next_ref, one_ref, other_ref, *refs,
):
    text_ref, fbias_ref, freqs_ref, times_ref, levels_ref, out_far, film_ref, ints_ref, *refs = refs
    gt_ref, kernel_ref, weight_ref, cells_ref, out_ref, pair_ref, mover = refs
    cols, rows = gt_ref.shape[0:2]
    load = mover.start(kernel_far, kernel_ref)
    steps = pieces(cols, 8)
    own = [mover.start(gt_far.at[a:b], gt_ref.at[a:b]) for a, b in steps]
    late = mover.start(weight_far, weight_ref)
    fill_halo(cells_ref, near_ref, next_ref, one_ref, other_ref, lambda cells: cells)
    load.wait()
    backward_weights(kernel_ref, pair_ref)
    mover.ready()
    text = text_ref[...].astype(F32)
    half = TEMB // 2
    for at, source_ref in ((0, times_ref), (TEMB, levels_ref)):
        angles = [source_ref[image].astype(F32) * freqs_ref[...] for image in range(text_ref.shape[0])]
        angles = jnp.concatenate(angles, axis=0)
        for start, embed in ((at, jnp.sin(angles)), (at + half, jnp.cos(angles))):
            ints_ref[:, start : start + half] = (embed * sigmoid(embed)).astype(BF16)
    act = jnp.concatenate([ints_ref[...], (text * sigmoid(text)).astype(BF16)], axis=1)
    for (a, b), copy in zip(steps, own):
        copy.wait()
        cells_ref[a + 2 : b + 2, 2 : rows + 2] = gt_ref[a:b]
    clear_border(cells_ref, 2)
    for a, b in pieces(cols + 2, 10):
        convolve(cells_ref, pair_ref, True, rows + 2, a, b, lambda col, values: out_ref.__setitem__(col, values))
        mover.put(out_ref.at[a:b], out_far.at[a:b])
    late.wait()
    film_ref[...] = jnp.dot(act, weight_ref[...], preferred_element_type=F32) + fbias_ref[...].astype(F32)


def second_values(stat, gain_ref, bias_ref, film_ref):
    mean, inv = stat
    chans = mean.shape[1]
    scale = 1.0 + film_ref[:, 0:chans]
    slope = gain_ref[...].astype(F32) * scale
    half_slope = 0.5 * slope
    half_offset = 0.5 * (bias_ref[...].astype(F32) * scale + film_ref[:, chans:])

    def values(mid, back):
        hat = (mid - mean) * inv
        pre = hat * half_slope + half_offset
        bend = jnp.tanh(pre)
        more = 1.0 + bend
        grad = back * (0.5 * more * (1.0 + pre * (1.0 - bend)))
        return hat, pre * more, grad

    return slope, values


def second_norm(
    mid_far, back_far, gathered_ref, gain_ref, bias_ref, film_ref,
    act_far, pre_far, pay_far, sums_ref, stat_ref,
    mid_ref, back_ref, act_ref, pre_ref, stage_ref, mover,
):
    wide, tall, images, chans = mid_ref.shape
    cols, rows = wide - 2, tall - 2
    per = chans // GROUPS
    steps = pieces(wide, 9)
    loads = []
    for a, b in steps:
        loads.append(
            [mover.start(f.at[a:b], n.at[a:b]) for f, n in ((mid_far, mid_ref), (back_far, back_ref))]
        )
    mean, inv = merge_moments(gathered_ref, rows * cols * per)
    stat_ref[0] = mean
    stat_ref[1] = inv
    mover.ready()
    slope, values = second_values((mean, inv), gain_ref, bias_ref, film_ref)

    def column(col, inner):
        hat, act, grad = values(mid_ref[col], back_ref[col])
        act_ref[col] = act.astype(BF16)
        pre_ref[col] = grad.astype(BF16)
        if inner is None:
            return None
        own = grad[1 : rows + 1]
        plain, cross = inner
        return plain + jnp.sum(own, axis=0), cross + jnp.sum(own * hat[1 : rows + 1], axis=0)

    zero = jnp.zeros((images, chans), F32)
    inner = (zero, zero)
    for (a, b), pair in zip(steps, loads):
        for load in pair:
            load.wait()
        if a == 0:
            column(0, None)
        inner = lax.fori_loop(max(a, 1), min(b, cols + 1), column, inner)
        if b == wide:
            column(wide - 1, None)
        clear_border(act_ref, 1, a, b)
        mover.put(act_ref.at[a:b], act_far.at[a:b])
        mover.put(pre_ref.at[a:b], pre_far.at[a:b])
    plain, cross = inner
    sums_ref[0] = plain
    sums_ref[1] = cross
    send_payload(mover, pack_pair(group_total(plain * slope), group_total(cross * slope)), pay_far, stage_ref)


def kernel_two(
    act_far, gt_far, sums_ref, bias_ref, keep_far, send_far, act_ref, gt_ref, keep_ref, send_ref, mover
):
    for load in [mover.start(act_far, act_ref), mover.start(gt_far, gt_ref)]:
        load.wait()
    split_taps(grad_terms(act_ref, gt_ref), keep_ref, send_ref)
    mover.ready()
    images, chans = bias_ref.shape
    at = 9 * (chans // 2)
    total = jnp.sum(bias_ref[...], axis=0, keepdims=True)
    for ref in (keep_ref, send_ref):
        ref[at : at + images] = sums_ref[0]
        ref[at + images : at + 2 * images] = sums_ref[1]
        ref[at + 2 * images :] = jnp.broadcast_to(total, (ref.shape[0] - at - 2 * images, chans))
    mover.put(keep_ref, keep_far)
    mover.put(send_ref, send_far)


def mix(
    act_far, kernel_far, xt_far, kbias_ref, out_far, act_ref, kernel_ref, xt_ref, branch_ref, out_ref, pair_ref, mover
):
    images, rows, cols, chans = out_ref.shape
    loads = [mover.start(f, n) for f, n in ((kernel_far, kernel_ref), (act_far, act_ref), (xt_far, xt_ref))]
    loads[0].wait()
    forward_weights(kernel_ref, pair_ref)
    mover.ready()
    kbias = kbias_ref[...].astype(F32)
    loads[1].wait()
    convolve(
        act_ref, pair_ref, False, rows, 0, cols, lambda col, values: branch_ref.__setitem__(col, values + kbias)
    )
    loads[2].wait()
    for a, b in pieces(rows, 2):
        for row in range(a, b):
            mixed = jnp.swapaxes((xt_ref[:, row].astype(F32) + branch_ref[:, row]) * INV_ROOT, 0, 1)
            out_ref[:, row] = mixed.astype(BF16)
        mover.put(out_ref.at[:, a:b], out_far.at[:, a:b])


def middle_grad(
    mid_far, pre_far, act_far, keep_two_far, gathered_ref, stat_ref, gain_ref, film_ref,
    low_far, keep_ref, send_ref, two_ref, bias_ref,
    mid_ref, pre_ref, act_ref, low_ref, mover,
):
    wide, tall, images, chans = mid_ref.shape
    cols, rows = wide - 2, tall - 2
    steps = pieces(wide, 9)
    loads = []
    for a, b in steps:
        loads.append([mover.start(f.at[a:b], n.at[a:b]) for f, n in ((mid_far, mid_ref), (pre_far, pre_ref))])
    late = [mover.start(f, n) for f, n in ((act_far, act_ref), (keep_two_far, two_ref))]
    count = lax.axis_size("ha") * lax.axis_size("wa") * rows * cols * (chans // GROUPS)
    packed = jnp.sum(gathered_ref[...], axis=0) * (1.0 / count)
    mover.ready()
    mean = stat_ref[0]
    inv = stat_ref[1]
    plain = unpack_at(packed, 0) * inv
    cross = unpack_at(packed, 1) * inv * inv
    slope = gain_ref[...].astype(F32) * (1.0 + film_ref[:, 0:chans]) * inv

    def low_column(col, total):
        low = (pre_ref[col].astype(F32) * slope - plain - (mid_ref[col] - mean) * cross).astype(BF16)
        low_ref[col] = low
        if total is None:
            return None
        return total + jnp.sum(low[1 : rows + 1].astype(F32), axis=0)

    kbias = jnp.zeros((images, chans), F32)
    for (a, b), pair in zip(steps, loads):
        for load in pair:
            load.wait()
        if a == 0:
            low_column(0, None)
        kbias = lax.fori_loop(max(a, 1), min(b, cols + 1), low_column, kbias)
        if b == wide:
            low_column(wide - 1, None)
        clear_border(low_ref, 1, a, b)
        mover.put(low_ref.at[a:b], low_far.at[a:b])
    for load in late:
        load.wait()
    own = low_ref.at[1 : wide - 1, 1 : tall - 1]
    split_taps(grad_terms(act_ref.at[1 : wide + 1, 1 : tall + 1], own), keep_ref, send_ref)
    at = 9 * (chans // 2)
    for ref in (keep_ref, send_ref):
        ref[at:] = jnp.broadcast_to(jnp.sum(kbias, axis=0, keepdims=True), (ref.shape[0] - at, chans))
    bias_ref[...] = kbias


def back_one(
    low_far, xt_far, kernel_far, stat_ref, gain_ref, bias_ref, gbias_ref, lbias_ref, grad_far, pay_ref, low_ref, xt_ref, kernel_ref, out_ref, pair_ref, mover
):
    cols, rows, images, chans = xt_ref.shape
    loads = [mover.start(f, n) for f, n in ((kernel_far, kernel_ref), (low_far, low_ref), (xt_far, xt_ref))]
    loads[0].wait()
    backward_weights(kernel_ref, pair_ref)
    loads[1].wait()
    loads[2].wait()
    mover.ready()
    mean = stat_ref[0]
    inv = stat_ref[1]
    gain = gain_ref[...].astype(F32)
    bias = bias_ref[...].astype(F32)
    state = [jnp.zeros((images, chans), F32), jnp.zeros((images, chans), F32)]

    def take(col, values):
        hat = (xt_ref[col].astype(F32) - mean) * inv
        norm = hat * gain + bias
        sigma = sigmoid(norm)
        grad = values * (sigma * (1.0 + norm * (1.0 - sigma)))
        out_ref[col] = grad
        state[0] = state[0] + jnp.sum(grad, axis=0)
        state[1] = state[1] + jnp.sum(grad * hat, axis=0)

    for a, b in pieces(cols, 8):
        convolve(low_ref, pair_ref, True, rows, a, b, take)
        mover.put(out_ref.at[a:b], grad_far.at[a:b])
    plain, cross = state
    half = images // 2
    pay_ref[0:half] = pack_pair(group_total(plain * gain), group_total(cross * gain))
    rest = [jnp.sum(v, axis=0, keepdims=True) for v in (cross, plain, gbias_ref[...], lbias_ref[...])]
    short = pay_ref.shape[0] - half - 4
    pay_ref[half:] = jnp.concatenate(rest + [jnp.zeros((short, chans), F32)], axis=0)


CODE = 32768.0


def exponents(values):
    most = jnp.clip(jnp.max(jnp.abs(values), axis=0, keepdims=True), 1e-30, 1e30)
    return jnp.ceil(jnp.log2(most) + 2e-3)


def two_to(powers):
    powers = powers.astype(jnp.int32)
    first = powers >> 1
    made = None
    for part in (first, powers - first):
        shifted = part + 64
        for bit in range(7):
            factor = jnp.where((shifted >> bit) & 1 == 1, 2.0 ** (1 << bit), 1.0)
            if bit == 0:
                piece = factor * 2.0**-64
            else:
                piece = piece * factor
        made = piece if made is None else made * piece
    return made


def pack_terms(
    keep_one_ref, came_one_ref, keep_two_ref, came_two_ref, out_far, token_ref,
    one_ref, two_ref, extra_ref, rest_ref, out_ref, mover, extras_one, extras_two,
):
    chips, rows, chans = out_ref.shape
    taps = 9 * (chans // 2)
    share = -(-taps // chips)
    more = -(-(extras_one + extras_two) // chips)
    extra_ref[...] = jnp.zeros(extra_ref.shape, F32)
    one_ref[...] = keep_one_ref[...] + came_one_ref[...]
    two_ref[...] = keep_two_ref[...] + came_two_ref[...]
    extra_ref[0:extras_two] = two_ref[taps : taps + extras_two]
    if extras_one:
        extra_ref[extras_two : extras_two + extras_one] = one_ref[taps : taps + extras_one]
    token_ref[...] = extra_ref[0:8]
    powers = []
    for ref, count in ((one_ref, taps), (two_ref, taps), (extra_ref, extra_ref.shape[0])):
        values = ref[0:count]
        power = exponents(values)
        powers.append(power)
        scaled = values * (two_to(-power) * CODE)
        code = jnp.round(scaled)
        ref[0:count] = code
        if ref is extra_ref:
            rest_ref[...] = jnp.round((scaled - code) * CODE)
    short = rows - 2 * share - 2 * more - 3
    pad = [jnp.zeros((short, chans), F32)] if short else []
    for chip in range(chips):
        a, b = chip * share, min((chip + 1) * share, taps)
        mine = []
        for ref in (one_ref, two_ref):
            if a < b:
                mine.append(ref[a:b])
            if max(b - a, 0) < share:
                mine.append(jnp.zeros((share - max(b - a, 0), chans), F32))
        for ref in (extra_ref, rest_ref):
            mine.append(ref[chip * more : (chip + 1) * more])
        whole = jnp.concatenate(mine + powers + pad, axis=0)
        out_ref[chip] = whole.astype(jnp.int32).astype(jnp.int16)
    mover.put(out_ref, out_far)


def unpack_terms(gathered_ref, share, more):
    chips, rows, chans = gathered_ref.shape
    row = lax.broadcasted_iota(jnp.int32, (rows, chans), 0)
    base = 2 * share + 2 * more
    total = jnp.zeros((rows, chans), F32)
    blocks = [gathered_ref[chip].astype(jnp.int32).astype(F32) for chip in range(chips)]
    every = two_to(jnp.concatenate([block[base : base + 3] for block in blocks], axis=0)) * (1.0 / CODE)
    for chip, block in enumerate(blocks):
        scales = every[3 * chip : 3 * chip + 3]
        scale = jnp.where(row < share, scales[0:1], jnp.where(row < 2 * share, scales[1:2], scales[2:3]))
        scale = jnp.where(row < 2 * share + more, scale, scale * (1.0 / CODE))
        total = total + block * scale
    extra = total[2 * share : 2 * share + more] + total[2 * share + more : base]
    return total[0 : 2 * share], extra


def two_terms(values):
    high = values.astype(BF16).astype(F32)
    return [high, values - high]


def add_terms(gathered_ref, pay_ref, came_ref, out_far, out_ref, mover, more, whole):
    chips, rows, chans = gathered_ref.shape
    shares, extra = unpack_terms(gathered_ref, -(-9 * (chans // 2) // chips), more)
    every = [shares] + two_terms(extra) + two_terms(pay_ref[0:whole] + came_ref[0:whole])
    short = out_ref.shape[1] - sum(v.shape[0] for v in every)
    if short:
        every.append(jnp.zeros((short, chans), F32))
    out_ref[...] = jnp.broadcast_to(jnp.concatenate(every, axis=0).astype(BF16)[None], out_ref.shape)
    mover.put(out_ref, out_far)


def sums_of(own_ref, at, whole):
    total = own_ref[0].astype(F32)
    for chip in range(1, own_ref.shape[0]):
        total = total + own_ref[chip].astype(F32)
    return total[at : at + whole] + total[at + whole : at + 2 * whole]


def three_terms(values):
    high = values.astype(BF16)
    rest = values - high.astype(F32)
    mid = rest.astype(BF16)
    low = (rest - mid.astype(F32)).astype(BF16)
    return jnp.concatenate([high, mid, low], axis=0)


def spread_out(own_ref, other_ref, one_far, two_far, one_ref, two_ref, half_ref, mover):
    chips, rows, chans = own_ref.shape
    half = chans // 2
    taps = 9 * half
    share = -(-taps // chips)
    core = lax.axis_index("ha") % 2
    for at, (out_ref, far) in enumerate(((one_ref, one_far), (two_ref, two_far))):
        for source, place in ((own_ref, core), (other_ref, 1 - core)):
            for chip in range(chips):
                piece = source[chip].astype(F32)[at * share : (at + 1) * share]
                half_ref[chip * share : (chip + 1) * share] = piece
            for tap in range(9):
                rows_at = pl.ds(pl.multiple_of(place * half, half), half)
                out_ref[tap, rows_at] = half_ref[tap * half : (tap + 1) * half]
        mover.put(out_ref, far)


def last_grads(
    weight_far, grad_ref, xt_ref, c_ref, own_ref, stat_ref, gain_one_ref, gain_two_ref, bias_two_ref, film_ref, ints_ref, text_ref,
    out_far, weight_grad_far, text_grad_far, bias_ref, *refs, more, whole,
):
    *vec_refs, weight_ref, out_ref, weight_grad_ref, text_grad_ref, extra_ref, mover = refs
    images, rows, cols, chans = out_ref.shape
    chips = own_ref.shape[0]
    load = mover.start(weight_far, weight_ref)
    share = -(-9 * (chans // 2) // chips)
    start = 2 * share
    for chip in range(chips):
        piece = own_ref[chip].astype(F32)
        extra_ref[chip * more : (chip + 1) * more] = piece[start : start + more] + piece[start + more : start + 2 * more]
    plain = extra_ref[0:images]
    cross = extra_ref[images : 2 * images]
    mover.ready()
    scale = 1.0 + film_ref[:, 0:chans]
    scale_grad = gain_two_ref[...].astype(F32) * cross + bias_two_ref[...].astype(F32) * plain
    film_grad = jnp.concatenate([scale_grad, plain], axis=1)
    bias_ref[...] = jnp.sum(film_grad, axis=0, keepdims=True)
    sums = sums_of(own_ref, start + 2 * more, whole)
    vec_refs[0][...] = jnp.sum(scale * cross, axis=0, keepdims=True)
    vec_refs[1][...] = jnp.sum(scale * plain, axis=0, keepdims=True)
    for at, row in ((4, whole - 4), (5, whole - 3), (2, whole - 2), (3, whole - 1)):
        vec_refs[at][...] = sums[row : row + 1]
    terms = three_terms(film_grad)
    ints = ints_ref.shape[1]

    depth = weight_grad_ref.shape[0]
    for at in range(0, depth, 512):
        if at < ints:
            act = ints_ref[:, at : at + 512]
        else:
            embed = text_ref[:, at - ints : at - ints + 512].astype(F32)
            act = (embed * sigmoid(embed)).astype(BF16)
        weight_grad_ref[at : at + 512] = lax.dot_general(
            jnp.concatenate([act, act, act], axis=0), terms, (((0,), (0,)), ((), ())), preferred_element_type=F32
        )
        mover.put(weight_grad_ref.at[at : at + 512], weight_grad_far.at[at : at + 512])

    count = lax.axis_size("ha") * lax.axis_size("wa") * rows * cols * (chans // GROUPS)
    packed = sums[0 : images // 2] * (1.0 / count)
    plain = unpack_at(packed, 0)
    cross = unpack_at(packed, 1)
    mean = stat_ref[0]
    inv = stat_ref[1]
    gain = gain_one_ref[...].astype(F32)
    for a, b in pieces(rows, 2):
        for row in range(a, b):
            hat = (xt_ref[:, row].astype(F32) - mean) * inv
            path = jnp.swapaxes(inv * (grad_ref[:, row] * gain - plain - hat * cross), 0, 1)
            out_ref[:, row] = (c_ref[:, row].astype(F32) * INV_ROOT + path).astype(BF16)
        mover.put(out_ref.at[:, a:b], out_far.at[:, a:b])

    load.wait()
    for at in range(ints, depth, 512):
        embed = text_ref[:, at - ints : at - ints + 512].astype(F32)
        sigma = sigmoid(embed)
        made = lax.dot_general(
            terms, weight_ref[at : at + 512], (((1,), (1,)), ((), ())), preferred_element_type=F32
        )
        cond_grad = made[0:images] + made[images : 2 * images] + made[2 * images :]
        text_grad_ref[:, at - ints : at - ints + 512] = cond_grad * (sigma * (1.0 + embed * (1.0 - sigma)))
    mover.put(text_grad_ref, text_grad_far)


def to_all(payload):
    return lax.all_to_all(payload, AXES, 0, 0)


def to_chips(payload):
    tall, wide = lax.axis_size("ha"), lax.axis_size("wa")
    groups = [[h * wide + w for h in range(core, tall, 2) for w in range(wide)] for core in range(2)]
    return lax.all_to_all(payload, AXES, 0, 0, axis_index_groups=groups)


def to_sibling(payload):
    return lax.ppermute(payload, "ha", [(i, i ^ 1) for i in range(lax.axis_size("ha"))])


def pair_exchange(one, other, axis):
    count = lax.axis_size(axis)
    pairs = [(i, (i + 1 if i % 2 else i - 1) % count) for i in range(count)]
    if axis == "wa":
        pairs = [(i, min(max(j, 0), count - 1) if abs(i - j) == 1 else i) for i, j in pairs]
    one = lax.ppermute(one, axis, [(i, i ^ 1) for i in range(count)])
    return one, lax.ppermute(other, axis, pairs)


def side_halo(sides, near, following, after=()):
    four, rows, images, chans = sides.shape
    edge = shaped((2, rows + 4, images, chans), sides.dtype)
    one, other = kernel_call(
        edge_columns, near=(sides, near, following), near_out=(edge, edge), cost=0.4, after=after, limit=16
    )
    return pair_exchange(one, other, "wa"), one


def local(
    block_input,
    timesteps,
    aug_levels,
    text_pooled,
    gain_one,
    bias_one,
    conv_one,
    conv_one_bias,
    gain_two,
    bias_two,
    film_weight,
    film_bias,
    conv_two,
    conv_two_bias,
    cotangent,
):
    images, rows, cols, chans = block_input.shape
    parts = lax.axis_size("ha") * lax.axis_size("wa")
    chips = parts // 2
    half = images // 2
    gain_one, bias_one, conv_one_bias, gain_two, bias_two, conv_two_bias = (
        v.reshape(1, chans) for v in (gain_one, bias_one, conv_one_bias, gain_two, bias_two, conv_two_bias)
    )
    freqs = np.exp(-math.log(10000.0) * np.arange(TEMB // 2) / (TEMB // 2)).astype(np.float32)[None]
    payload = shaped((parts, half, chans), F32)
    per_image = shaped((images, chans), F32)
    two_images = shaped((2, images, chans), F32)
    block = shaped((cols, rows, images, chans), BF16)
    block_wide = shaped((cols, rows, images, chans), F32)
    rim = shaped((cols + 2, rows + 2, images, chans), BF16)
    rim_wide = shaped((cols + 2, rows + 2, images, chans), F32)
    far_rim = shaped((cols + 4, rows + 4, images, chans), BF16)
    given = shaped((images, rows, cols, chans), BF16)
    pair = pltpu.VMEM((12 * chans, 2 * chans), BF16)
    pair_back = pltpu.VMEM((2 * chans, 12 * chans), BF16)

    sides = shaped((4, rows, images, chans), BF16)
    row_halo = shaped((cols, 2, images, chans), BF16)
    xt, x_near, x_next, x_sides, moments = kernel_call(
        prepare_x, far=(block_input,), far_out=(block,),
        near_out=(row_halo, row_halo, sides, shaped((half, chans), F32)),
        scratch=buffers(given, block), sems=16, cost=2.3,
    )
    x_near, x_next = pair_exchange(x_near, x_next, "ha")
    gt, pay_one, g_near, g_next, g_sides, kbias_two_local = kernel_call(
        prepare_g, far=(cotangent,), near=(moments,), far_out=(block, payload),
        near_out=(row_halo, row_halo, sides), tiny_out=(per_image,),
        scratch=buffers(given, block, payload), sems=16, cost=2.0,
    )
    moments_one = to_all(pay_one)
    x_cols, x_edge = side_halo(x_sides, x_near, x_next)
    g_near, g_next = pair_exchange(g_near, g_next, "ha")

    film_bias = film_bias.reshape(1, 2 * chans)
    act_one, mid, pay_two, stat_one = kernel_call(
        first_half, far=(xt, conv_one), near=(x_near, x_next, *x_cols, moments_one),
        tiny=(gain_one, bias_one, conv_one_bias),
        far_out=(far_rim, rim_wide, payload), tiny_out=(two_images,),
        scratch=buffers(xt, conv_one, far_rim, rim_wide, payload) + (pair,), sems=16, cost=5.5,
        after=(film_bias,),
    )
    moments_two = to_all(pay_two)
    g_cols, _ = side_halo(g_sides, g_near, g_next, after=(stat_one,))
    act_two_grad, film, act_ints = kernel_call(
        back_two, far=(gt, conv_two, film_weight), near=(g_near, g_next, *g_cols),
        tiny=(text_pooled, film_bias, freqs), scalars=(timesteps, aug_levels),
        far_out=(rim_wide,), tiny_out=(shaped((images, 2 * chans), F32), shaped((images, 2 * TEMB), BF16)),
        scratch=buffers(gt, conv_two, film_weight, far_rim, rim_wide) + (pair_back,), sems=16, cost=5.0,
    )
    act_two, pre_two_grad, pay_three, sums_two, stat_two = kernel_call(
        second_norm, far=(mid, act_two_grad), near=(moments_two,), tiny=(gain_two, bias_two, film),
        far_out=(rim, rim, payload), tiny_out=(two_images, two_images),
        scratch=buffers(rim_wide, rim_wide, rim, rim, payload), sems=24, cost=3.2,
    )
    moments_three = to_all(pay_three)

    taps = 9 * (chans // 2)
    share = -(-taps // chips)
    extras_two = 2 * images
    extras_one = 0
    halves_two = shaped((taps + 2 * images + 8, chans), F32)
    halves_one = shaped((taps + 8, chans), F32)
    keep_two, send_two = kernel_call(
        kernel_two, far=(act_two, gt), tiny=(sums_two, kbias_two_local), far_out=(halves_two, halves_two),
        scratch=buffers(act_two, gt, halves_two, halves_two), sems=4, cost=3.0,
    )
    came_two = to_sibling(send_two)
    low, keep_one, send_one, keep_two, kbias_one_local = kernel_call(
        middle_grad, far=(mid, pre_two_grad, act_one, keep_two), near=(moments_three,), tiny=(stat_two, gain_two, film),
        far_out=(rim,), near_out=(halves_one, halves_one, halves_two), tiny_out=(per_image,),
        scratch=buffers(mid, pre_two_grad, act_one, rim), sems=24, cost=6.0,
    )
    came_one = to_sibling(send_one)
    more = -(-(extras_one + extras_two) // chips)
    terms_shape = shaped((chips, -(-(2 * share + 2 * more + 3) // 8) * 8, chans), jnp.int16)
    extra_shape = shaped((-(-chips * more // 8) * 8, chans), F32)
    terms, token = kernel_call(
        functools.partial(pack_terms, extras_one=extras_one, extras_two=extras_two),
        near=(keep_one, came_one, keep_two, came_two), far_out=(terms_shape,), near_out=(shaped((8, chans), F32),),
        scratch=buffers(halves_one, halves_two, extra_shape, extra_shape, terms_shape),
        sems=3, cost=1.0,
    )
    gathered = to_chips(terms)
    whole = half + 4
    norm_one_grad, pay_four = kernel_call(
        back_one, far=(low, xt, conv_one), tiny=(stat_one, gain_one, bias_one, kbias_two_local, kbias_one_local), far_out=(block_wide,),
        near_out=(shaped((2 * half, chans), F32),),
        scratch=buffers(rim, block, conv_one, block_wide) + (pair_back,), sems=16, cost=5.0,
        after_near=(to_sibling(token),),
    )
    came_four = to_sibling(pay_four)
    (mixed,) = kernel_call(
        mix, far=(act_two, conv_two, xt), tiny=(conv_two_bias,), far_out=(given,),
        scratch=buffers(act_two, conv_two, xt, block_wide, given) + (pair,), sems=8, cost=3.6, after_near=(pay_four,),
    )
    shares_shape = shaped((chips, -(-(2 * share + 2 * more + 2 * whole) // 8) * 8, chans), BF16)
    (shares,) = kernel_call(
        functools.partial(add_terms, more=more, whole=whole),
        near=(gathered, pay_four, came_four), far_out=(shares_shape,),
        scratch=buffers(shares_shape), sems=1, cost=1.0, after=(mixed,),
    )
    own_half = to_chips(shares)
    other_half = to_sibling(own_half)
    weight_grad = shaped(film_weight.shape, F32)
    text_shape = shaped(text_pooled.shape, F32)
    row = shaped((1, chans), F32)
    input_grad, film_weight_grad, text_grad, film_bias_grad, *vec_grads = kernel_call(
        functools.partial(last_grads, more=more, whole=whole),
        far=(film_weight,),
        near=(norm_one_grad, xt, cotangent, own_half, stat_one, gain_one, gain_two, bias_two, film, act_ints, text_pooled),
        far_out=(given, weight_grad, text_shape), tiny_out=(shaped((1, 2 * chans), F32),) + (row,) * 6,
        scratch=buffers(film_weight, given, weight_grad, text_shape)
        + (pltpu.VMEM((-(-chips * more // 8) * 8, chans), F32),),
        sems=32, cost=6.0, limit=24,
    )
    full = shaped((9, chans, chans), F32)
    kernel_one_grad, kernel_two_grad = kernel_call(
        spread_out, near=(own_half, other_half), far_out=(full, full),
        scratch=buffers(full, full, shaped((chips * share, chans), F32)), sems=2, cost=2.0, after=(input_grad,), limit=24,
    )
    return (
        mixed,
        input_grad,
        text_grad,
        vec_grads[4].reshape(chans),
        vec_grads[5].reshape(chans),
        kernel_one_grad.reshape(3, 3, chans, chans),
        vec_grads[3].reshape(chans),
        vec_grads[0].reshape(chans),
        vec_grads[1].reshape(chans),
        film_weight_grad,
        film_bias_grad.reshape(2 * chans),
        kernel_two_grad.reshape(3, 3, chans, chans),
        vec_grads[2].reshape(chans),
    )


def solution(mesh):
    split = P(None, "ha", "wa", None)
    return jax.shard_map(
        local,
        mesh=mesh,
        in_specs=(split,) + (P(),) * 13 + (split,),
        out_specs=(split, split) + (P(),) * 11,
        check_vma=False,
    )
```
